32 devices in a mesh: dp: 16 (over z, y, x), mp: 2 (over core).
Axes of the slice: x: 2, y: 2, z: 4, core: 2. Of those that a mesh axis runs over, the one named last changes fastest.
Arguments:
- layer_input: bfloat16 [32, 512, 768], P('dp'), may hold values from -6 to 6
- segments: int32 [32, 512], P('dp'), may hold values from 0 to 15, never falling along the last dimension, each value on 1 to 256 neighbouring positions
- modality: int32 [32, 16], P('dp'), may hold values from 0 to 2, as said below
- ln_gain: float32 [2, 768], replicated, may hold values from 0.1 to 1.9
- ln_bias: float32 [2, 768], replicated, may hold values from -3 to 3
- w_qkv: bfloat16 [3, 768, 768], P(None, 'dp', 'mp'), may hold values from -0.21875 to 0.21875
- qv_bias: float32 [2, 768], replicated, may hold values from -3 to 3
- w_out: bfloat16 [768, 768], P('dp', 'mp'), may hold values from -0.875 to 0.875
- out_bias: float32 [768], replicated, may hold values from -3 to 3
- w_up: bfloat16 [3, 768, 3072], P(None, 'dp', 'mp'), may hold values from -0.21875 to 0.21875
- up_bias: float32 [3, 3072], replicated, may hold values from -3 to 3
- w_down: bfloat16 [3, 768, 3072], P(None, 'dp', 'mp'), may hold values from -0.21875 to 0.21875
- down_bias: float32 [3, 768], replicated, may hold values from -3 to 3
- cotangent: bfloat16 [32, 512, 768], P('dp'), may hold values from -6 to 6
Outputs:
- layer_output: bfloat16 [32, 512, 768], P('dp')
- grad_input: float32 [32, 512, 768], P('dp')
- grad_ln_gain: float32 [2, 768], replicated
- grad_ln_bias: float32 [2, 768], replicated
- grad_w_qkv: float32 [3, 768, 768], P(None, 'dp', 'mp')
- grad_qv_bias: float32 [2, 768], replicated
- grad_w_out: float32 [768, 768], P('dp', 'mp')
- grad_out_bias: float32 [768], replicated
- grad_w_up: float32 [3, 768, 3072], P(None, 'dp', 'mp')
- grad_up_bias: float32 [3, 3072], replicated
- grad_w_down: float32 [3, 768, 3072], P(None, 'dp', 'mp')
- grad_down_bias: float32 [3, 768], replicated
The draws below stay inside these ranges and needn't reach their ends.
Inputs may be any that keep to these rules, and one draw needn't show every extreme that they name: `segments`: within a row the document ids never fall; each document holds at most 256 tokens and one holds exactly that many. `modality`: every token of a document goes to the document's one expert (vision, language or vision-language); most documents are language, and any document may be of any kind.
All inputs are finite; a program needn't handle non-finite values.
Results may differ from the reference program's by a relative error of at most 0.015.
Values may be sent and summed in bfloat16 or wider, within the bound.
No kernel may reach another device: no remote copies, remote signals or barrier semaphores. Data moves between devices by JAX's collectives and lax.ppermute only.
A program may use at most 256 MiB of HBM per device.

```python
import math
import jax
import jax.numpy as jnp
import numpy as np
from jax import lax

D = 768
HEADS = 12
HD = 64
FF = 3072
EXPERTS = 3
SEQ = 512
ROWS = 32


def draw_modality(key, part):
    key = jax.random.fold_in(key, 7)
    drawn = jax.random.randint(key, (ROWS, SEQ // 32), 0, 5, dtype=jnp.int32)
    return jnp.where(drawn == 0, 0, jnp.where(drawn == 4, 2, 1)).astype(jnp.int32)


def block_levels(key, extent, split, smallest, top_value):
    level = 1.0
    for dim, blocks in split:
        draws = jax.random.uniform(jax.random.fold_in(jax.random.fold_in(key, 6), dim), (blocks,), jnp.float32, smallest / len(split), top_value / len(split))
        level = level * jnp.repeat(jnp.exp(draws), extent[dim] // blocks).reshape((-1,) + (1,) * (len(extent) - 1 - dim))
    return level


def profile(count, total, limit, skew):
    weights = [(1 << 20) // math.isqrt(rank ** skew) + 1 for rank in range(2, count + 1)]
    rest, holding = total - limit - (count - 1), [1] * (count - 1)
    while rest > 0:
        free = [i for i in range(count - 1) if holding[i] < limit]
        whole, budget = sum([weights[i] for i in free]), rest
        for i in free:
            extra = min(limit - holding[i], max(1, budget * weights[i] // whole), rest)
            holding[i] = holding[i] + extra
            rest = rest - extra
    return np.array([limit] + holding)


def uneven_parts(own_key, number_of, total, limit, lean):
    if number_of == 2:
        one = jax.random.randint(own_key, (), max(1, total - limit), min(limit, total - 1) + 1)
        return jnp.stack([one, total - one])
    lengths = jnp.asarray(profile(number_of, total, limit, lean), jnp.int32)
    couples = (number_of - 1) // 2
    source_of, taker = lengths[1:1 + 2 * couples:2], lengths[2:2 + 2 * couples:2]
    room = jnp.minimum(source_of - 1, limit - taker)
    passed = jax.random.randint(jax.random.fold_in(own_key, 1), (couples,), 0, 1 << 20) % (room + 1)
    lengths = lengths.at[1:1 + 2 * couples:2].set(source_of - passed).at[2:2 + 2 * couples:2].set(taker + passed)
    return lengths[jax.random.permutation(jax.random.fold_in(own_key, 2), number_of)]


def bell_draw(key, shape, spread, bound, pieces=(), kind=jnp.bfloat16):
    level = block_levels(key, shape, pieces, -0.22, 0.18) if pieces else 1.0
    array = jax.random.normal(key, shape, jnp.float32) * spread * level
    return jnp.minimum(jnp.maximum(array, -bound), bound).astype(kind)


def setup_inputs(seed: int = 0) -> dict:
    arg_keys = jax.random.split(jax.random.key(seed), 15)
    layer_input = bell_draw(arg_keys[0], (ROWS, SEQ, D), 1.0, 6.0, ((0, 16),))
    segments = jax.vmap(lambda own: jnp.searchsorted(jnp.cumsum(uneven_parts(own, SEQ // 32, SEQ, SEQ // 2, 0)), jnp.arange(SEQ), side="right"))(jax.random.split(arg_keys[1], ROWS)).reshape((ROWS, SEQ)).astype(jnp.int32)
    modality = draw_modality(jax.random.fold_in(arg_keys[14], 71), 0)
    ln_gain = jnp.clip(1.0 + 0.18 * jax.random.normal(arg_keys[3], (2, D), jnp.float32), 0.1, 1.9)
    ln_bias = bell_draw(arg_keys[4], (2, D), 0.3, 3.0, (), jnp.float32)
    w_qkv = bell_draw(arg_keys[5], (3, D, D), D ** -0.5, 0.21875, ((1, 16), (2, 2)))
    qv_bias = bell_draw(arg_keys[6], (2, D), 0.3, 3.0, (), jnp.float32)
    w_out = bell_draw(arg_keys[7], (D, D), (D // 16) ** -0.5, 0.875, ((0, 16), (1, 2)))
    out_bias = bell_draw(arg_keys[8], (D,), 0.3, 3.0, (), jnp.float32)
    w_up = bell_draw(arg_keys[9], (EXPERTS, D, FF), D ** -0.5, 0.21875, ((1, 16), (2, 2)))
    up_bias = bell_draw(arg_keys[10], (EXPERTS, FF), 0.3, 3.0, (), jnp.float32)
    w_down = bell_draw(arg_keys[11], (EXPERTS, D, FF), (FF // 4) ** -0.5, 0.21875, ((1, 16), (2, 2)))
    down_bias = bell_draw(arg_keys[12], (EXPERTS, D), 0.3, 3.0, (), jnp.float32)
    cotangent = bell_draw(arg_keys[13], (ROWS, SEQ, D), 1.0, 6.0, ((0, 16),))
    return dict(layer_input=layer_input, segments=segments, modality=modality, ln_gain=ln_gain, ln_bias=ln_bias, w_qkv=w_qkv, qv_bias=qv_bias, w_out=w_out, out_bias=out_bias, w_up=w_up, up_bias=up_bias, w_down=w_down, down_bias=down_bias, cotangent=cotangent)


@jax.custom_vjp
def low(v):
    return lax.optimization_barrier(v.astype(jnp.bfloat16)).astype(jnp.float32)

@jax.custom_vjp
def low_back(v):
    return v

def low_keep(v):
    return (low(v), None)

def low_pass(kept, grad):
    return (grad,)

def back_keep(v):
    return (v, None)

def back_low(kept, grad):
    return (low(grad),)
low.defvjp(low_keep, low_pass)
low_back.defvjp(back_keep, back_low)
EPS = 1e-05

def layer_norm(v, gain, shift):
    mean = lax.optimization_barrier(jnp.mean(v, axis=-1, keepdims=True))
    cent = v - mean
    var = lax.optimization_barrier(jnp.mean(cent * cent, axis=-1, keepdims=True))
    return cent * lax.rsqrt(var + EPS) * gain + shift

def token_modality(segg, docg):
    doc_ids = jnp.arange(docg.shape[-1], dtype=jnp.int32)
    match = segg[..., None] == doc_ids
    return lax.optimization_barrier(jnp.sum(jnp.where(match, docg[..., None, :], jnp.int32(0)), axis=-1)).astype(jnp.int32)

def forward(xg, segg, docg, params):
    ln_gain, ln_bias, w_qkv, qv_bias, w_out, out_bias, w_up, up_bias, w_down, down_bias = params
    highest = lax.Precision.HIGHEST
    scale = HD ** (-0.5)
    rows_here = xg.shape[0]
    modg = token_modality(segg, docg)
    h1 = layer_norm(xg, ln_gain[0], ln_bias[0])
    a1 = low(h1)
    query = low(low_back(jnp.einsum('rsd,de->rse', a1, w_qkv[0], precision=highest) + qv_bias[0]))
    keys = low(low_back(jnp.einsum('rsd,de->rse', a1, w_qkv[1], precision=highest)))
    values = low(low_back(jnp.einsum('rsd,de->rse', a1, w_qkv[2], precision=highest) + qv_bias[1]))
    query = query.reshape(rows_here, SEQ, HEADS, HD)
    keys = keys.reshape(rows_here, SEQ, HEADS, HD)
    values = values.reshape(rows_here, SEQ, HEADS, HD)
    scores = low_back(jnp.einsum('rqhc,rkhc->rhqk', query, keys, precision=highest) * scale)
    same = segg[:, None, :, None] == segg[:, None, None, :]
    scores = jnp.where(same, scores, jnp.float32(-1e+30))
    top = lax.optimization_barrier(jnp.max(scores, axis=-1, keepdims=True))
    expo = jnp.exp(scores - top)
    probs = expo / lax.optimization_barrier(jnp.sum(expo, axis=-1, keepdims=True))
    mixed = jnp.einsum('rhqk,rkhc->rqhc', low(probs), values, precision=highest)
    attended = low(low_back(mixed.reshape(rows_here, SEQ, D)))
    branch = low_back(jnp.einsum('rsi,oi->rso', attended, w_out, precision=highest)) + out_bias
    x2 = xg + branch
    a2 = low(layer_norm(x2, ln_gain[1], ln_bias[1]))
    onehot = (modg[..., None] == jnp.arange(EXPERTS, dtype=jnp.int32)).astype(jnp.float32)
    upper = low_back(jnp.einsum('rsd,edf->rsef', a2, w_up, precision=highest) + up_bias)
    active = low(jax.nn.gelu(upper, approximate=False)) * onehot[..., None]
    down = low_back(jnp.einsum('rsef,eof->rso', active, w_down, precision=highest))
    down = down + jnp.einsum('rse,eo->rso', onehot, down_bias, precision=highest)
    return x2 + down

def reference(layer_input, segments, modality, ln_gain, ln_bias, w_qkv, qv_bias, w_out, out_bias, w_up, up_bias, w_down, down_bias, cotangent):
    params = (ln_gain, ln_bias, w_qkv.astype(jnp.float32), qv_bias, w_out.astype(jnp.float32), out_bias, w_up.astype(jnp.float32), up_bias, w_down.astype(jnp.float32), down_bias)
    group = math.gcd(ROWS, max(1, 4096 // SEQ))
    count = ROWS // group
    inputs = layer_input.astype(jnp.float32).reshape(count, group, SEQ, D)
    segs = segments.reshape(count, group, SEQ)
    mods = modality.reshape(count, group, modality.shape[-1])
    cots = cotangent.astype(jnp.float32).reshape(count, group, SEQ, D)

    def step(acc, item):
        xg, sg, mg, cg = item

        def run(xv, *ps):
            return forward(xv, sg, mg, ps)
        out, pull = jax.vjp(run, xg, *params)
        grads = pull(cg)
        acc = tuple((a + b for a, b in zip(acc, grads[1:])))
        return (acc, (out.astype(jnp.bfloat16), grads[0]))
    zeros = tuple((jnp.zeros(p.shape, jnp.float32) for p in params))
    acc, outs = lax.scan(step, zeros, (inputs, segs, mods, cots))
    g_gain, g_lnb, g_qkv, g_qvb, g_out, g_outb, g_up, g_upb, g_down, g_downb = acc
    layer_output = outs[0].reshape(ROWS, SEQ, D)
    grad_input = outs[1].reshape(ROWS, SEQ, D)
    return (layer_output, grad_input, g_gain, g_lnb, g_qkv, g_qvb, g_out, g_outb, g_up, g_upb, g_down, g_downb)
```

```python
import functools
import math

import jax
import jax.numpy as jnp
from jax import lax
from jax.experimental import pallas as pl
from jax.experimental.pallas import tpu as pltpu
from jax.sharding import PartitionSpec as P

HD = 64
EPS = 1e-05
TILE = 256
CHUNKS = 2
VMEM = 58 * 1024 * 1024
LOG2E = math.log2(math.e)
f32 = jnp.float32
bf16 = jnp.bfloat16
ANY = pl.BlockSpec(memory_space=pl.ANY)


def full_spec(shape):
    zeros = (0,) * len(shape)
    return pl.BlockSpec(shape, lambda *_: zeros)


def nt_dot(a, b):
    return lax.dot_general(a, b, (((1,), (1,)), ((), ())), preferred_element_type=f32)


def nn_dot(a, b):
    return lax.dot_general(a, b, (((1,), (0,)), ((), ())), preferred_element_type=f32)


def params(grid_rank):
    return pltpu.CompilerParams(
        dimension_semantics=("arbitrary",) * grid_rank, vmem_limit_bytes=VMEM
    )


def cost(flops, nbytes, trans=0):
    return pl.CostEstimate(flops=int(flops), bytes_accessed=int(nbytes), transcendentals=int(trans))


def place(c_ref, kind, outer, inner, rz):
    ry, rx = (outer, inner) if kind == "a" else (inner, outer)
    return (c_ref[0] ^ rz) * 4 + (c_ref[1] ^ ry) * 2 + (c_ref[2] ^ rx)


def load_pieces(c_ref, jobs, sems):
    copies = []
    for kind, pair, view, target in jobs:
        for outer in range(2):
            for inner in range(2):
                for rz in range(4):
                    rows = place(c_ref, kind, outer, inner, rz)
                    copies.append(
                        pltpu.make_async_copy(
                            view(pair[outer], inner, rz), target(rows), sems.at[len(copies)]
                        )
                    )
    for c in copies:
        c.start()
    return copies


def gelu_parts(u):
    mag = jnp.abs(u)
    t = 1.0 / (1.0 + (0.3275911 * math.sqrt(0.5)) * mag)
    poly = t * (
        0.254829592
        + t * (-0.284496736 + t * (1.421413741 + t * (-1.453152027 + t * 1.061405429)))
    )
    gauss = jnp.exp(-0.5 * u * u)
    half = 0.5 * poly * gauss
    cdf = jnp.where(u >= 0, 1.0 - half, half)
    return u * cdf, cdf + u * gauss * (1.0 / math.sqrt(2.0 * math.pi))


def norm_parts(v):
    mean = jnp.mean(v, axis=-1, keepdims=True)
    cent = v - mean
    var = jnp.mean(cent * cent, axis=-1, keepdims=True)
    rstd = lax.rsqrt(var + EPS)
    return cent * rstd, rstd


def norm_back(d_out, xhat, rstd, gain):
    d_hat = d_out * gain
    m1 = jnp.mean(d_hat, axis=-1, keepdims=True)
    m2 = jnp.mean(d_hat * xhat, axis=-1, keepdims=True)
    return rstd * (d_hat - m1 - xhat * m2)


def attn_fwd_kernel(
    heads, piece, c_ref, x_ref, srow_ref, scol_ref, g_ref, b_ref, pb_ref, a0, a1_, b0, b1_,
    att_ref, qkv_ref, kt_ref, o_ref, ot_ref, lse_ref,
    w_s, wo_s, bias_s, sems,
):
    cols = heads * HD
    pairs = cols // 128
    seq, width = x_ref.shape[1], x_ref.shape[2]

    def into(block, j):
        return w_s.at[pl.ds(pl.multiple_of(block * piece, 16), piece), pl.ds(j * cols, cols)]

    def into_out(block):
        return wo_s.at[pl.ds(pl.multiple_of(block * piece, 16), piece), :]

    @pl.when(pl.program_id(0) == 0)
    def _():
        jobs = [
            ("a", (a0, a1_), lambda r, i, z: r.at[i, z, 0], lambda k: into(k, 0)),
            ("a", (a0, a1_), lambda r, i, z: r.at[i, z, 1], lambda k: into(k, 1)),
            ("b", (b0, b1_), lambda r, i, z: r.at[i, z, 0], lambda k: into(k, 2)),
            ("b", (b0, b1_), lambda r, i, z: r.at[i, z, 1], into_out),
        ]
        for c in load_pieces(c_ref, jobs, sems):
            c.wait()

    xhat, _ = norm_parts(x_ref[0].astype(f32))
    a1 = (xhat * g_ref[...] + b_ref[...]).astype(bf16)
    proj = (nn_dot(a1, w_s[...]) + pb_ref[...]).astype(bf16)
    for j in range(3):
        for p in range(pairs):
            qkv_ref[0, j, p] = proj[:, j * cols + p * 128 : j * cols + (p + 1) * 128]
    for p in range(pairs):
        kt_ref[0, p] = proj[:, cols + p * 128 : cols + (p + 1) * 128].T
    bias_s[...] = jnp.where(scol_ref[0] == srow_ref[0], 0.0, -1e30)
    lane = lax.broadcasted_iota(jnp.int32, (1, 128), 1)
    scale2 = HD ** (-0.5) * LOG2E

    @pl.loop(0, pairs)
    def _(p):
        q_p = qkv_ref[0, 0, p]
        k_p = qkv_ref[0, 1, p]
        v_t = qkv_ref[0, 2, p].T
        for h in range(2):
            keep = (lane < HD) if h == 0 else (lane >= HD)
            q_h = jnp.where(keep, q_p, jnp.zeros_like(q_p))
            s_t = nt_dot(k_p, q_h) + bias_s[...]
            top = jnp.max(s_t, axis=0, keepdims=True)
            e_t = jnp.exp2((s_t - top) * scale2)
            total = jnp.sum(e_t, axis=0, keepdims=True)
            p_t = (e_t * (1.0 / total)).astype(bf16)
            o_t = nn_dot(v_t[h * HD : (h + 1) * HD], p_t)
            ot_ref[0, p, h * HD : (h + 1) * HD] = o_t.astype(bf16)
            lse_ref[0, p, pl.ds(h, 1), :] = top * scale2 + jnp.log2(total)

    for p in range(pairs):
        o_ref[0, :, p * 128 : (p + 1) * 128] = ot_ref[0, p].T
    att_ref[0] = nt_dot(o_ref[0], wo_s[...]).astype(bf16)


def attn_fwd(coords, x, seg_row, seg_col, gain, bias, proj_bias, pa, pb):
    rows, seq, width = x.shape
    cols = proj_bias.shape[-1] // 3
    heads = cols // HD
    pairs = cols // 128
    piece = pa[0].shape[-2]
    row3 = lambda r, *_: (r, 0, 0)
    row4 = lambda r, *_: (r, 0, 0, 0)
    row5 = lambda r, *_: (r, 0, 0, 0, 0)
    outs = [
        ((rows, seq, width), bf16, (1, seq, width), row3),
        ((rows, 3, pairs, seq, 128), bf16, (1, 3, pairs, seq, 128), row5),
        ((rows, pairs, 128, seq), bf16, (1, pairs, 128, seq), row4),
        ((rows, seq, cols), bf16, (1, seq, cols), row3),
        ((rows, pairs, 128, seq), bf16, (1, pairs, 128, seq), row4),
        ((rows, pairs, 2, seq), f32, (1, pairs, 2, seq), row4),
    ]
    return pl.pallas_call(
        functools.partial(attn_fwd_kernel, heads, piece),
        out_shape=[jax.ShapeDtypeStruct(s, d) for s, d, _, _ in outs],
        grid_spec=pltpu.PrefetchScalarGridSpec(
            num_scalar_prefetch=1,
            grid=(rows,),
            in_specs=[
                pl.BlockSpec((1, seq, width), row3),
                pl.BlockSpec((1, 1, seq), row3),
                pl.BlockSpec((1, seq, 1), row3),
                full_spec((1, width)),
                full_spec((1, width)),
                full_spec((1, 3 * cols)),
                ANY, ANY, ANY, ANY,
            ],
            out_specs=[pl.BlockSpec(b, m) for _, _, b, m in outs],
            scratch_shapes=[
                pltpu.VMEM((width, 3 * cols), bf16),
                pltpu.VMEM((width, cols), bf16),
                pltpu.VMEM((seq, seq), f32),
                pltpu.SemaphoreType.DMA((64,)),
            ],
        ),
        compiler_params=params(1),
        cost_estimate=cost(2e10, 1e7, 3e6),
        name="attn_fwd",
    )(coords, x, seg_row, seg_col, gain, bias, proj_bias, *pa, *pb)


def attn_bwd_kernel(
    heads, piece, c_ref, own_ref, recv_ref, x2_ref, dy_ref, x_ref, srow_ref, scol_ref,
    ln_ref, qkv_ref, kt_ref, o_ref, ot_ref, lse_ref, a0, a1_, b0, b1_,
    da1_ref, dx2_ref, ga0_ref, ga1_ref, gb0_ref, gb1_ref, sums_ref, bsum_ref,
    w_s, wo_s, bias_s, dp_s, gw_s, go_s, sems,
):
    cols = heads * HD
    pairs = cols // 128
    step = pl.program_id(0)

    def into(block, j):
        return w_s.at[pl.ds(pl.multiple_of(block * piece, 16), piece), pl.ds(j * cols, cols)]

    def into_out(block):
        return wo_s.at[pl.ds(pl.multiple_of(block * piece, 16), piece), :]

    @pl.when(step == 0)
    def _():
        jobs = [
            ("a", (a0, a1_), lambda r, i, z: r.at[i, z, 0], lambda k: into(k, 0)),
            ("a", (a0, a1_), lambda r, i, z: r.at[i, z, 1], lambda k: into(k, 1)),
            ("b", (b0, b1_), lambda r, i, z: r.at[i, z, 0], lambda k: into(k, 2)),
            ("b", (b0, b1_), lambda r, i, z: r.at[i, z, 1], into_out),
        ]
        for c in load_pieces(c_ref, jobs, sems):
            c.wait()
        gw_s[...] = jnp.zeros_like(gw_s)
        go_s[...] = jnp.zeros_like(go_s)
        sums_ref[...] = jnp.zeros_like(sums_ref)
        bsum_ref[...] = jnp.zeros_like(bsum_ref)

    da2 = own_ref[0].astype(f32) + recv_ref[0].astype(f32)
    xhat2, rstd2 = norm_parts(x2_ref[0])
    dx2 = dy_ref[0].astype(f32) + norm_back(da2, xhat2, rstd2, ln_ref[2:3])
    dx2_ref[0] = dx2
    sums_ref[0:1] += jnp.sum(da2 * xhat2, axis=0, keepdims=True)
    sums_ref[1:2] += jnp.sum(da2, axis=0, keepdims=True)
    sums_ref[2:3] += jnp.sum(dx2, axis=0, keepdims=True)
    dxr = dx2.astype(bf16)
    do = nn_dot(dxr, wo_s[...]).astype(bf16)
    go_s[...] += nn_dot(dxr.T, o_ref[0])
    bias_s[...] = jnp.where(scol_ref[0] == srow_ref[0], 0.0, -1e30)
    lane = lax.broadcasted_iota(jnp.int32, (1, 128), 1)
    scale = HD ** (-0.5)
    scale2 = scale * LOG2E

    for p in range(pairs):
        q_p = qkv_ref[0, 0, p]
        k_p = qkv_ref[0, 1, p]
        v_p = qkv_ref[0, 2, p]
        do_p = do[:, p * 128 : (p + 1) * 128]
        prod = do_p.T.astype(f32) * ot_ref[0, p].astype(f32)
        dv = None
        for h in range(2):
            keep = (lane < HD) if h == 0 else (lane >= HD)
            q_h = jnp.where(keep, q_p, jnp.zeros_like(q_p))
            do_h = jnp.where(keep, do_p, jnp.zeros_like(do_p))
            row = jnp.sum(prod[h * HD : (h + 1) * HD], axis=0, keepdims=True)
            s_t = nt_dot(k_p, q_h)
            p_t = jnp.exp2(s_t * scale2 + (bias_s[...] - lse_ref[0, p, h : h + 1, :]))
            d_t = nt_dot(v_p, do_h)
            ds_t = (p_t * (d_t - row)).astype(bf16)
            dv_h = nn_dot(p_t.astype(bf16), do_h)
            dk_h = nn_dot(ds_t, q_h)
            dq_h = nn_dot(kt_ref[0, p, h * HD : (h + 1) * HD], ds_t)
            dv, dk, dq = (dv_h, dk_h, [dq_h]) if dv is None else (dv + dv_h, dk + dk_h, dq + [dq_h])
        dq = (jnp.concatenate(dq, axis=0) * scale).astype(bf16).T
        dp_s[:, p * 128 : (p + 1) * 128] = dq
        dp_s[:, cols + p * 128 : cols + (p + 1) * 128] = (dk * scale).astype(bf16)
        dp_s[:, 2 * cols + p * 128 : 2 * cols + (p + 1) * 128] = dv.astype(bf16)

    dproj = dp_s[...]
    da1_ref[0] = nt_dot(dproj, w_s[...]).astype(bf16)
    bsum_ref[...] += jnp.sum(dproj.astype(f32), axis=0, keepdims=True)
    xhat1, _ = norm_parts(x_ref[0].astype(f32))
    a1 = (xhat1 * ln_ref[0:1] + ln_ref[1:2]).astype(bf16)
    gw_s[...] += nn_dot(a1.T, dproj)

    @pl.when(step == pl.num_programs(0) - 1)
    def _():
        for outer in range(2):
            for inner in range(2):
                for rz in range(4):
                    ra = pl.ds(pl.multiple_of(place(c_ref, "a", outer, inner, rz) * piece, 16), piece)
                    rb = pl.ds(pl.multiple_of(place(c_ref, "b", outer, inner, rz) * piece, 16), piece)
                    ga, gb = ((ga0_ref, gb0_ref), (ga1_ref, gb1_ref))[outer]
                    ga[inner, rz, 0] = gw_s[ra, :cols].astype(bf16)
                    ga[inner, rz, 1] = gw_s[ra, cols : 2 * cols].astype(bf16)
                    gb[inner, rz, 0] = gw_s[rb, 2 * cols :].astype(bf16)
                    gb[inner, rz, 1] = go_s[rb, :].astype(bf16)


def attn_bwd(coords, own, recv, x2, dy, x, seg_row, seg_col, ln, saved, pa, pb):
    rows, seq, width = x.shape
    qkv, kt, o, ot, lse = saved
    cols = o.shape[-1]
    heads = cols // HD
    pairs = cols // 128
    piece = pa[0].shape[-2]
    row3 = lambda r, *_: (r, 0, 0)
    row4 = lambda r, *_: (r, 0, 0, 0)
    row5 = lambda r, *_: (r, 0, 0, 0, 0)
    tok = pl.BlockSpec((1, seq, width), row3)
    gshape = pa[0].shape
    return pl.pallas_call(
        functools.partial(attn_bwd_kernel, heads, piece),
        out_shape=[
            jax.ShapeDtypeStruct((rows, seq, width), bf16),
            jax.ShapeDtypeStruct((rows, seq, width), f32),
            *[jax.ShapeDtypeStruct(gshape, bf16)] * 4,
            jax.ShapeDtypeStruct((8, width), f32),
            jax.ShapeDtypeStruct((1, 3 * cols), f32),
        ],
        grid_spec=pltpu.PrefetchScalarGridSpec(
            num_scalar_prefetch=1,
            grid=(rows,),
            in_specs=[
                tok, tok, tok, tok, tok,
                pl.BlockSpec((1, 1, seq), row3),
                pl.BlockSpec((1, seq, 1), row3),
                full_spec((4, width)),
                pl.BlockSpec((1, 3, pairs, seq, 128), row5),
                pl.BlockSpec((1, pairs, 128, seq), row4),
                pl.BlockSpec((1, seq, cols), row3),
                pl.BlockSpec((1, pairs, 128, seq), row4),
                pl.BlockSpec((1, pairs, 2, seq), row4),
                ANY, ANY, ANY, ANY,
            ],
            out_specs=[
                tok, tok,
                *[full_spec(gshape)] * 4,
                full_spec((8, width)),
                full_spec((1, 3 * cols)),
            ],
            scratch_shapes=[
                pltpu.VMEM((width, 3 * cols), bf16),
                pltpu.VMEM((width, cols), bf16),
                pltpu.VMEM((seq, seq), f32),
                pltpu.VMEM((seq, 3 * cols), bf16),
                pltpu.VMEM((width, 3 * cols), f32),
                pltpu.VMEM((width, cols), f32),
                pltpu.SemaphoreType.DMA((64,)),
            ],
        ),
        compiler_params=params(1),
        cost_estimate=cost(4e10, 2e7, 3e6),
        name="attn_bwd",
    )(coords, own, recv, x2, dy, x, seg_row, seg_col, ln, qkv, kt, o, ot, lse, *pa, *pb)


def sort_kernel(pos_row, pos_col, v_ref, vs_ref, vst_ref, vt_s):
    _sort_tile(pos_row, pos_col, v_ref, vs_ref, vst_ref, vt_s)


def _sort_tile(pos_row, pos_col, v_ref, vs_ref, vst_ref, vt_s):
    i = pl.program_id(0)
    tokens = v_ref.shape[0]

    @pl.when(i == 0)
    def _():
        vt_s[...] = v_ref[...].T

    slot_c = lax.broadcasted_iota(jnp.int32, (TILE, tokens), 0) + i * TILE
    pick = (slot_c == pos_row[...]).astype(f32).astype(bf16)
    vs_ref[...] = nn_dot(pick, v_ref[...]).astype(bf16)
    slot_r = lax.broadcasted_iota(jnp.int32, (tokens, TILE), 1) + i * TILE
    pick_t = (slot_r == pos_col[...]).astype(f32).astype(bf16)
    vst_ref[...] = nn_dot(vt_s[...], pick_t).astype(bf16)


def sort_tokens(pos_row, pos_col, v, tiles):
    tokens, width = v.shape
    return pl.pallas_call(
        sort_kernel,
        out_shape=[
            jax.ShapeDtypeStruct((tiles * TILE, width), bf16),
            jax.ShapeDtypeStruct((width, tiles * TILE), bf16),
        ],
        grid=(tiles,),
        in_specs=[full_spec((1, tokens)), full_spec((tokens, 1)), full_spec((tokens, width))],
        out_specs=[
            pl.BlockSpec((TILE, width), lambda i: (i, 0)),
            pl.BlockSpec((width, TILE), lambda i: (0, i)),
        ],
        scratch_shapes=[pltpu.VMEM((width, tokens), bf16)],
        compiler_params=params(1),
        cost_estimate=cost(4 * tiles * TILE * tokens * width, 1e7),
        name="sort_tokens",
    )(pos_row, pos_col, v)


def mid_kernel(pos_row, pos_col, x_ref, own_ref, recv_ref, vec_ref, x2_ref, vs_ref, vst_ref, a2_s, vt_s):
    @pl.when(pl.program_id(0) == 0)
    def _():
        tokens = x_ref.shape[0]
        block = math.gcd(tokens, 256)
        for start in range(0, tokens, block):
            rows = slice(start, start + block)
            x2 = (
                x_ref[rows].astype(f32)
                + (own_ref[rows].astype(f32) + recv_ref[rows].astype(f32))
                + vec_ref[0:1]
            )
            x2_ref[rows] = x2
            xhat, _ = norm_parts(x2)
            a2_s[rows] = (xhat * vec_ref[1:2] + vec_ref[2:3]).astype(bf16)

    _sort_tile(pos_row, pos_col, a2_s, vs_ref, vst_ref, vt_s)


def mid(pos_row, pos_col, x, own, recv, vec, tiles):
    tokens, width = x.shape
    whole = full_spec((tokens, width))
    return pl.pallas_call(
        mid_kernel,
        out_shape=[
            jax.ShapeDtypeStruct((tokens, width), f32),
            jax.ShapeDtypeStruct((tiles * TILE, width), bf16),
            jax.ShapeDtypeStruct((width, tiles * TILE), bf16),
        ],
        grid=(tiles,),
        in_specs=[
            full_spec((1, tokens)), full_spec((tokens, 1)), whole, whole, whole, full_spec((4, width)),
        ],
        out_specs=[
            whole,
            pl.BlockSpec((TILE, width), lambda i: (i, 0)),
            pl.BlockSpec((width, TILE), lambda i: (0, i)),
        ],
        scratch_shapes=[pltpu.VMEM((tokens, width), bf16), pltpu.VMEM((width, tokens), bf16)],
        compiler_params=params(1),
        cost_estimate=cost(4 * tiles * TILE * tokens * width, 2e7),
        name="norm_sort",
    )(pos_row, pos_col, x, own, recv, vec)


def unsort_kernel(pos_col, vs_ref, out_ref):
    slots = vs_ref.shape[0]
    slot_r = lax.broadcasted_iota(jnp.int32, (TILE, slots), 1)
    pick = (slot_r == pos_col[...]).astype(f32).astype(bf16)
    out_ref[...] = nn_dot(pick, vs_ref[...]).astype(bf16)


def unsort_tokens(pos_col, vs):
    slots, width = vs.shape
    tokens = pos_col.shape[0]
    return pl.pallas_call(
        unsort_kernel,
        out_shape=jax.ShapeDtypeStruct((tokens, width), bf16),
        grid=(tokens // TILE,),
        in_specs=[pl.BlockSpec((TILE, 1), lambda i: (i, 0)), full_spec((slots, width))],
        out_specs=pl.BlockSpec((TILE, width), lambda i: (i, 0)),
        compiler_params=params(1),
        cost_estimate=cost(2 * slots * tokens * width, 1e7),
        name="unsort_tokens",
    )(pos_col, vs)


def ffn_kernel(first, last, piece, c_ref, te_ref, n_ref, *refs):
    xs_ref, xst_ref, dys_ref, dyst_ref, ub_ref, a0, a1_, b0, b1_, *rest = refs
    if not first:
        zin_ref, din_ref, *rest = rest
    (z_ref, da_ref, ga0_ref, ga1_ref, gb0_ref, gb1_ref, gub_ref,
     wu_s, wd_s, gu_s, gd_s, sems) = rest
    experts = wu_s.shape[0]
    i = pl.program_id(0)

    @pl.when(i == 0)
    def _():
        jobs = [
            ("a", (a0, a1_), lambda r, k, z: r.at[k, z],
             lambda k: wu_s.at[:, pl.ds(pl.multiple_of(k * piece, 16), piece), :]),
            ("b", (b0, b1_), lambda r, k, z: r.at[k, z],
             lambda k: wd_s.at[:, pl.ds(pl.multiple_of(k * piece, 16), piece), :]),
        ]
        copies = load_pieces(c_ref, jobs, sems)
        gu_s[...] = jnp.zeros_like(gu_s)
        gd_s[...] = jnp.zeros_like(gd_s)
        gub_ref[...] = jnp.zeros_like(gub_ref)
        for c in copies:
            c.wait()

    @pl.when(i < n_ref[0])
    def _():
        e = te_ref[i]
        dy = dys_ref[...]
        u = nn_dot(xs_ref[...], wu_s[e]) + ub_ref[e]
        act, slope = gelu_parts(u)
        act = act.astype(bf16)
        du = nn_dot(dy, wd_s[e]) * slope
        du = du.astype(bf16)
        z = nt_dot(act, wd_s[e])
        da = nt_dot(du, wu_s[e])
        if not first:
            z = z + zin_ref[...]
            da = da + din_ref[...]
        z_ref[...] = z.astype(z_ref.dtype)
        da_ref[...] = da.astype(da_ref.dtype)
        gd_s[e] += nn_dot(dyst_ref[...], act)
        gu_s[e] += nn_dot(xst_ref[...], du)
        gub_ref[e] += jnp.sum(du.astype(f32), axis=0, keepdims=True)

    @pl.when(i >= n_ref[0])
    def _():
        z_ref[...] = jnp.zeros_like(z_ref)
        da_ref[...] = jnp.zeros_like(da_ref)

    @pl.when(i == pl.num_programs(0) - 1)
    def _():
        for outer in range(2):
            for inner in range(2):
                for rz in range(4):
                    ra = pl.ds(pl.multiple_of(place(c_ref, "a", outer, inner, rz) * piece, 16), piece)
                    rb = pl.ds(pl.multiple_of(place(c_ref, "b", outer, inner, rz) * piece, 16), piece)
                    ga, gb = ((ga0_ref, gb0_ref), (ga1_ref, gb1_ref))[outer]
                    for e in range(experts):
                        ga[inner, rz, e] = gu_s[e, ra, :].astype(bf16)
                        gb[inner, rz, e] = gd_s[e, rb, :].astype(bf16)


def ffn(first, last, coords, tile_expert, used, xs, xst, dys, dyst, up_b, pa, pb, carry):
    slots, width = xs.shape
    tiles = slots // TILE
    gshape = pa[0].shape
    experts, piece, hid = gshape[2:]
    tile = pl.BlockSpec((TILE, width), lambda i, *_: (i, 0))
    tile_t = pl.BlockSpec((width, TILE), lambda i, *_: (0, i))
    kept = bf16 if last else f32
    return pl.pallas_call(
        functools.partial(ffn_kernel, first, last, piece),
        out_shape=[
            jax.ShapeDtypeStruct((slots, width), kept),
            jax.ShapeDtypeStruct((slots, width), kept),
            *[jax.ShapeDtypeStruct(gshape, bf16)] * 4,
            jax.ShapeDtypeStruct((experts, 1, hid), f32),
        ],
        grid_spec=pltpu.PrefetchScalarGridSpec(
            num_scalar_prefetch=3,
            grid=(tiles,),
            in_specs=[
                tile, tile_t, tile, tile_t, full_spec((experts, 1, hid)), ANY, ANY, ANY, ANY,
                *([] if first else [tile, tile]),
            ],
            out_specs=[tile, tile, *[full_spec(gshape)] * 4, full_spec((experts, 1, hid))],
            scratch_shapes=[
                pltpu.VMEM((experts, width, hid), bf16),
                pltpu.VMEM((experts, width, hid), bf16),
                pltpu.VMEM((experts, width, hid), f32),
                pltpu.VMEM((experts, width, hid), f32),
                pltpu.SemaphoreType.DMA((32,)),
            ],
        ),
        compiler_params=params(1),
        cost_estimate=cost(12 * slots * width * hid * 1.5, 4e7, 2 * slots * hid),
        name="ffn",
    )(coords, tile_expert, used, xs, xst, dys, dyst, up_b, *pa, *pb, *carry)


def input_grad_kernel(own_ref, recv_ref, x_ref, dx2_ref, gain_ref, out_ref, sums_ref):
    @pl.when(pl.program_id(0) == 0)
    def _():
        sums_ref[...] = jnp.zeros_like(sums_ref)

    da1 = own_ref[...].astype(f32) + recv_ref[...].astype(f32)
    xhat, rstd = norm_parts(x_ref[...].astype(f32))
    out_ref[...] = dx2_ref[...] + norm_back(da1, xhat, rstd, gain_ref[...])
    sums_ref[0:1] += jnp.sum(da1 * xhat, axis=0, keepdims=True)
    sums_ref[1:2] += jnp.sum(da1, axis=0, keepdims=True)


def input_grad(own, recv, x, dx2, gain):
    tokens, width = x.shape
    tile = pl.BlockSpec((TILE, width), lambda i: (i, 0))
    return pl.pallas_call(
        input_grad_kernel,
        out_shape=[
            jax.ShapeDtypeStruct((tokens, width), f32),
            jax.ShapeDtypeStruct((8, width), f32),
        ],
        grid=(tokens // TILE,),
        in_specs=[tile, tile, tile, tile, full_spec((1, width))],
        out_specs=[tile, full_spec((8, width))],
        compiler_params=params(1),
        cost_estimate=cost(2e7, 1.3e7),
        name="input_grad",
    )(own, recv, x, dx2, gain)


def flip(x, mask, size):
    return lax.ppermute(x, "dp", [(i, i ^ mask) for i in range(size)])


def swap(x, parts):
    if parts == 2:
        return lax.ppermute(x, "mp", [(0, 1), (1, 0)])
    return (lax.psum(x.astype(f32), "mp") - x.astype(f32)).astype(x.dtype)


def gather_staged(a, b, size):
    both = jnp.stack([a, b])
    blocks = [both] + [flip(both, 4 * rz, size) for rz in (1, 2, 3)]
    a0 = jnp.stack([v[0] for v in blocks])
    b0 = jnp.stack([v[1] for v in blocks])
    a0 = jnp.stack([a0, flip(a0, 1, size)])
    b0 = jnp.stack([b0, flip(b0, 2, size)])
    return (a0, flip(a0, 2, size)), (b0, flip(b0, 1, size))


def scatter_staged(ga, gb, size):
    ra = ga[0].astype(f32) + flip(ga[1], 2, size).astype(f32)
    rb = gb[0].astype(f32) + flip(gb[1], 1, size).astype(f32)
    sa = ra[0] + flip(ra[1].astype(bf16), 1, size).astype(f32)
    sb = rb[0] + flip(rb[1].astype(bf16), 2, size).astype(f32)
    own = jnp.stack([sa[0], sb[0]])
    for rz in (1, 2, 3):
        sent = jnp.stack([sa[rz].astype(bf16), sb[rz].astype(bf16)])
        own = own + flip(sent, 4 * rz, size).astype(f32)
    return own[0], own[1]


def gather_plain(w):
    full = lax.all_gather(w, "dp", axis=1, tiled=True)
    n, rows, cols = full.shape
    return full.reshape(n, 16, rows // 16, cols).swapaxes(0, 1)


def gather_pieces(a, b, size, staged):
    if staged:
        return gather_staged(a, b, size)
    blocks = [gather_plain(v) for v in (a, b)]
    blocks = [v.reshape((4, 2, 2) + v.shape[1:]) for v in blocks]
    fa = jnp.moveaxis(blocks[0], 0, 2)
    fb = jnp.swapaxes(jnp.moveaxis(blocks[1], 0, 2), 0, 1)
    return (fa[0], fa[1]), (fb[0], fb[1])


def scatter_pieces(ga, gb, size, staged):
    if staged:
        return scatter_staged(ga, gb, size)
    fa = jnp.moveaxis(jnp.stack(ga), 2, 0)
    fb = jnp.moveaxis(jnp.swapaxes(jnp.stack(gb), 0, 1), 2, 0)
    outs = []
    for v in (fa, fb):
        v = v.reshape((16,) + v.shape[3:]).swapaxes(0, 1)
        v = v.reshape(v.shape[0], -1, v.shape[-1]).astype(f32)
        outs.append(lax.psum_scatter(v, "dp", scatter_dimension=1, tiled=True))
    return outs


def sum_small(v, size, parts):
    if size & (size - 1) or parts != 2:
        return lax.psum(v, ("dp", "mp"))
    v = v + swap(v, parts)
    mask = 1
    while mask < size:
        v = v + flip(v, mask, size)
        mask *= 2
    return v


def body(
    layer_input, segments, modality, ln_gain, ln_bias, w_qkv, qv_bias, w_out, out_bias,
    w_up, up_bias, w_down, down_bias, cotangent,
):
    part = lax.axis_index("mp")
    parts = lax.axis_size("mp")
    size = lax.axis_size("dp")
    me = lax.axis_index("dp")
    rows, seq, width = layer_input.shape
    tokens = rows * seq
    cols = w_qkv.shape[-1]
    hid = w_up.shape[-1]
    experts = w_up.shape[0]
    staged = size == 16
    if staged:
        coords = jnp.stack([me // 4, (me // 2) % 2, me % 2]).astype(jnp.int32)
    else:
        coords = jnp.zeros((3,), jnp.int32)

    pa, pb = gather_pieces(w_qkv[:2], jnp.stack([w_qkv[2], w_out]), size, staged)
    hc = hid // CHUNKS
    chunks = [
        gather_pieces(w_up[:, :, c * hc : (c + 1) * hc], w_down[:, :, c * hc : (c + 1) * hc], size, staged)
        for c in range(CHUNKS)
    ]

    doc_ids = jnp.arange(modality.shape[1], dtype=jnp.int32)
    match = segments[:, :, None] == doc_ids
    mods = jnp.sum(jnp.where(match, modality[:, None, :], 0), axis=-1).reshape(tokens)
    hot_i = (mods[:, None] == jnp.arange(experts, dtype=jnp.int32)).astype(jnp.int32)
    hot = hot_i.astype(bf16)
    ids = jnp.arange(tokens, dtype=jnp.int32)
    lower = (ids[:, None] > ids[None, :]).astype(bf16)
    before = jnp.dot(lower, hot, preferred_element_type=f32).astype(jnp.int32)
    counts = jnp.sum(hot_i, axis=0)
    need = (counts + TILE - 1) // TILE
    kinds = jnp.arange(experts, dtype=jnp.int32)
    ends = jnp.sum(jnp.where(kinds[:, None] >= kinds[None, :], need[None, :], 0), axis=1)
    begins = ends - need
    pos = jnp.sum(hot_i * (before + begins[None, :] * TILE), axis=1)
    pos_row, pos_col = pos.reshape(1, tokens), pos.reshape(tokens, 1)
    tiles = (tokens + experts * (TILE - 1)) // TILE
    tile_ids = jnp.arange(tiles, dtype=jnp.int32)
    tile_expert = jnp.minimum(
        jnp.sum((tile_ids[:, None] >= ends[None, :]).astype(jnp.int32), axis=1), experts - 1
    )
    used = ends[-1:].astype(jnp.int32)

    dy = cotangent.reshape(tokens, width)
    dys, dyst = sort_tokens(pos_row, pos_col, dy, tiles)
    g_down_bias = lax.dot_general(hot, dy, (((0,), (0,)), ((), ())), preferred_element_type=f32)

    col_start = part * cols
    q_b = lax.dynamic_slice_in_dim(qv_bias[0], col_start, cols)
    v_b = lax.dynamic_slice_in_dim(qv_bias[1], col_start, cols)
    proj_bias = jnp.concatenate([q_b, jnp.zeros_like(q_b), v_b]).reshape(1, 3 * cols)
    seg_row, seg_col = segments.reshape(rows, 1, seq), segments.reshape(rows, seq, 1)
    att, *saved = attn_fwd(
        coords, layer_input, seg_row, seg_col, ln_gain[0:1], ln_bias[0:1], proj_bias, pa, pb
    )
    att = att.reshape(tokens, width)
    vec = jnp.concatenate([out_bias[None], ln_gain[1:2], ln_bias[1:2], out_bias[None]])
    x_tok = layer_input.reshape(tokens, width)
    x2, xs, xst = mid(pos_row, pos_col, x_tok, att, swap(att, parts), vec, tiles)

    up_b = lax.dynamic_slice_in_dim(up_bias, part * hid, hid, 1)
    carry = ()
    g_ffn = []
    g_upb = []
    for c in range(CHUNKS):
        ca, cb = chunks[c]
        ub = up_b[:, None, c * hc : (c + 1) * hc]
        zs, das, ga0, ga1, gb0, gb1, gub = ffn(
            c == 0, c == CHUNKS - 1, coords, tile_expert, used, xs, xst, dys, dyst, ub, ca, cb, carry
        )
        carry = (zs, das)
        g_ffn.append(scatter_pieces((ga0, ga1), (gb0, gb1), size, staged))
        g_upb.append(gub[:, 0])
    g_up = jnp.concatenate([g[0] for g in g_ffn], axis=-1)
    g_down = jnp.concatenate([g[1] for g in g_ffn], axis=-1)
    g_upb = jnp.concatenate(g_upb, axis=-1)
    da2 = unsort_tokens(pos_col, das)
    da2_other = swap(da2, parts)

    shape3 = (rows, seq, width)
    ln = jnp.concatenate([ln_gain[0:1], ln_bias[0:1], ln_gain[1:2], ln_bias[1:2]])
    da1, dx2, ga0, ga1, gb0, gb1, sums2, bsum = attn_bwd(
        coords, da2.reshape(shape3), da2_other.reshape(shape3), x2.reshape(shape3), cotangent,
        layer_input, seg_row, seg_col, ln, saved, pa, pb,
    )
    g_qk, g_vo = scatter_pieces((ga0, ga1), (gb0, gb1), size, staged)
    da1 = da1.reshape(tokens, width)
    grad_input, sums1 = input_grad(
        da1, swap(da1, parts), x_tok, dx2.reshape(tokens, width), ln_gain[0:1]
    )

    z = unsort_tokens(pos_col, zs)
    z_sum = z.astype(f32) + swap(z, parts).astype(f32)
    bias_of = jnp.zeros((tokens, width), f32)
    for e in range(experts):
        bias_of = jnp.where(mods[:, None] == e, down_bias[e][None], bias_of)
    layer_output = (x2 + (z_sum + bias_of)).astype(bf16)

    bsum = bsum.reshape(3, cols)
    g_qv = lax.dynamic_update_slice(
        jnp.zeros((2, width), f32), jnp.stack([bsum[0], bsum[2]]), (jnp.int32(0), col_start)
    )
    g_upb_full = lax.dynamic_update_slice(
        jnp.zeros((experts, up_bias.shape[1]), f32), g_upb, (jnp.int32(0), part * hid)
    )
    once = jnp.concatenate([sums1[0:2], sums2[0:3], g_down_bias]) / parts
    small = jnp.concatenate([once, g_qv, g_upb_full.reshape(-1, width)])
    small = sum_small(small, size, parts)
    g_gain = jnp.stack([small[0], small[2]])
    g_lnb = jnp.stack([small[1], small[3]])
    return (
        layer_output.reshape(shape3),
        grad_input.reshape(shape3),
        g_gain,
        g_lnb,
        jnp.concatenate([g_qk, g_vo[:1]]),
        small[5 + experts : 7 + experts],
        g_vo[1],
        small[4],
        g_up,
        small[7 + experts :].reshape(experts, up_bias.shape[1]),
        g_down,
        small[5 : 5 + experts],
    )


def solution(mesh):
    tok = P("dp", None, None)
    rep = P()
    wide = P(None, "dp", "mp")
    in_specs = (
        tok, P("dp", None), P("dp", None), rep, rep, wide, rep, P("dp", "mp"), rep, wide, rep,
        wide, rep, tok,
    )
    out_specs = (
        tok, tok, rep, rep, wide, rep, P("dp", "mp"), rep, wide, rep, wide, rep,
    )
    return jax.shard_map(body, mesh=mesh, in_specs=in_specs, out_specs=out_specs, check_vma=False)
```

```python
import functools
import math

import jax
import jax.numpy as jnp
from jax import lax
from jax.experimental import pallas as pl
from jax.experimental.pallas import tpu as pltpu
from jax.sharding import PartitionSpec as P

HD = 64
EPS = 1e-05
TILE = 256
CHUNKS = 3
SCALE = 1.0
CALLS = ((0,), (1, 2))
VMEM = 58 * 1024 * 1024
LOG2E = math.log2(math.e)
f32 = jnp.float32
bf16 = jnp.bfloat16
ANY = pl.BlockSpec(memory_space=pl.ANY)


def full_spec(shape):
    zeros = (0,) * len(shape)
    return pl.BlockSpec(shape, lambda *_: zeros)


def nt_dot(a, b):
    return lax.dot_general(a, b, (((1,), (1,)), ((), ())), preferred_element_type=f32)


def nn_dot(a, b):
    return lax.dot_general(a, b, (((1,), (0,)), ((), ())), preferred_element_type=f32)


def tn_dot(a, b):
    return lax.dot_general(a, b, (((0,), (0,)), ((), ())), preferred_element_type=f32)


def params(grid_rank):
    return pltpu.CompilerParams(
        dimension_semantics=("arbitrary",) * grid_rank, vmem_limit_bytes=VMEM
    )


def cost(flops, nbytes, trans=0):
    return pl.CostEstimate(
        flops=int(flops * SCALE), bytes_accessed=int(nbytes * SCALE), transcendentals=int(trans * SCALE)
    )


def place(c_ref, kind, outer, inner, rz):
    ry, rx = (outer, inner) if kind == "a" else (inner, outer)
    return (c_ref[0] ^ rz) * 4 + (c_ref[1] ^ ry) * 2 + (c_ref[2] ^ rx)


def load_pieces(c_ref, jobs, sems):
    copies = []
    for kind, pair, view, target in jobs:
        for outer in range(2):
            for inner in range(2):
                for rz in range(4):
                    rows = place(c_ref, kind, outer, inner, rz)
                    copies.append(
                        pltpu.make_async_copy(
                            view(pair[outer], inner, rz), target(rows), sems.at[len(copies)]
                        )
                    )
    for c in copies:
        c.start()
    return copies


def gelu_parts(u):
    mag = jnp.abs(u)
    t = 1.0 / (1.0 + (0.3275911 * math.sqrt(0.5)) * mag)
    poly = t * (
        0.254829592
        + t * (-0.284496736 + t * (1.421413741 + t * (-1.453152027 + t * 1.061405429)))
    )
    gauss = jnp.exp(-0.5 * u * u)
    half = 0.5 * poly * gauss
    cdf = jnp.where(u >= 0, 1.0 - half, half)
    return u * cdf, cdf + u * gauss * (1.0 / math.sqrt(2.0 * math.pi))


def norm_parts(v):
    mean = jnp.mean(v, axis=-1, keepdims=True)
    cent = v - mean
    var = jnp.mean(cent * cent, axis=-1, keepdims=True)
    rstd = lax.rsqrt(var + EPS)
    return cent * rstd, rstd


def norm_back(d_out, xhat, rstd, gain):
    d_hat = d_out * gain
    m1 = jnp.mean(d_hat, axis=-1, keepdims=True)
    m2 = jnp.mean(d_hat * xhat, axis=-1, keepdims=True)
    return rstd * (d_hat - m1 - xhat * m2)


def attn_fwd_kernel(
    heads, piece, c_ref, x_ref, srow_ref, scol_ref, g_ref, b_ref, pb_ref, a0, a1_, b0, b1_,
    att_ref, qkv_ref, kt_ref, o_ref, ot_ref, lse_ref,
    w_s, wo_s, bias_s, sems,
):
    cols = heads * HD
    pairs = cols // 128
    seq, width = x_ref.shape[1], x_ref.shape[2]

    def into(block, j):
        return w_s.at[pl.ds(pl.multiple_of(block * piece, 16), piece), pl.ds(j * cols, cols)]

    def into_out(block):
        return wo_s.at[pl.ds(pl.multiple_of(block * piece, 16), piece), :]

    @pl.when(pl.program_id(0) == 0)
    def _():
        jobs = [
            ("a", (a0, a1_), lambda r, i, z: r.at[i, z, 0], lambda k: into(k, 0)),
            ("a", (a0, a1_), lambda r, i, z: r.at[i, z, 1], lambda k: into(k, 1)),
            ("b", (b0, b1_), lambda r, i, z: r.at[i, z, 0], lambda k: into(k, 2)),
            ("b", (b0, b1_), lambda r, i, z: r.at[i, z, 1], into_out),
        ]
        for c in load_pieces(c_ref, jobs, sems):
            c.wait()

    xhat, _ = norm_parts(x_ref[0].astype(f32))
    a1 = (xhat * g_ref[...] + b_ref[...]).astype(bf16)
    proj = (nn_dot(a1, w_s[...]) + pb_ref[...]).astype(bf16)
    for j in range(3):
        for p in range(pairs):
            qkv_ref[0, j, p] = proj[:, j * cols + p * 128 : j * cols + (p + 1) * 128]
    for p in range(pairs):
        kt_ref[0, p] = proj[:, cols + p * 128 : cols + (p + 1) * 128].T
    bias_s[...] = jnp.where(scol_ref[0] == srow_ref[0], 0.0, -1e30)
    lane = lax.broadcasted_iota(jnp.int32, (1, 128), 1)
    scale2 = HD ** (-0.5) * LOG2E

    @pl.loop(0, pairs)
    def _(p):
        q_p = qkv_ref[0, 0, p]
        k_p = qkv_ref[0, 1, p]
        v_t = qkv_ref[0, 2, p].T
        for h in range(2):
            keep = (lane < HD) if h == 0 else (lane >= HD)
            q_h = jnp.where(keep, q_p, jnp.zeros_like(q_p))
            s_t = nt_dot(k_p, q_h) + bias_s[...]
            top = jnp.max(s_t, axis=0, keepdims=True)
            e_t = jnp.exp2((s_t - top) * scale2)
            total = jnp.sum(e_t, axis=0, keepdims=True)
            p_t = (e_t * (1.0 / total)).astype(bf16)
            o_t = nn_dot(v_t[h * HD : (h + 1) * HD], p_t)
            ot_ref[0, p, h * HD : (h + 1) * HD] = o_t.astype(bf16)
            lse_ref[0, p, pl.ds(h, 1), :] = top * scale2 + jnp.log2(total)

    for p in range(pairs):
        o_ref[0, :, p * 128 : (p + 1) * 128] = ot_ref[0, p].T
    att_ref[0] = nt_dot(o_ref[0], wo_s[...]).astype(bf16)


def attn_fwd(coords, x, seg_row, seg_col, gain, bias, proj_bias, pa, pb):
    rows, seq, width = x.shape
    cols = proj_bias.shape[-1] // 3
    heads = cols // HD
    pairs = cols // 128
    piece = pa[0].shape[-2]
    row3 = lambda r, *_: (r, 0, 0)
    row4 = lambda r, *_: (r, 0, 0, 0)
    row5 = lambda r, *_: (r, 0, 0, 0, 0)
    outs = [
        ((rows, seq, width), bf16, (1, seq, width), row3),
        ((rows, 3, pairs, seq, 128), bf16, (1, 3, pairs, seq, 128), row5),
        ((rows, pairs, 128, seq), bf16, (1, pairs, 128, seq), row4),
        ((rows, seq, cols), bf16, (1, seq, cols), row3),
        ((rows, pairs, 128, seq), bf16, (1, pairs, 128, seq), row4),
        ((rows, pairs, 2, seq), f32, (1, pairs, 2, seq), row4),
    ]
    return pl.pallas_call(
        functools.partial(attn_fwd_kernel, heads, piece),
        out_shape=[jax.ShapeDtypeStruct(s, d) for s, d, _, _ in outs],
        grid_spec=pltpu.PrefetchScalarGridSpec(
            num_scalar_prefetch=1,
            grid=(rows,),
            in_specs=[
                pl.BlockSpec((1, seq, width), row3),
                pl.BlockSpec((1, 1, seq), row3),
                pl.BlockSpec((1, seq, 1), row3),
                full_spec((1, width)),
                full_spec((1, width)),
                full_spec((1, 3 * cols)),
                ANY, ANY, ANY, ANY,
            ],
            out_specs=[pl.BlockSpec(b, m) for _, _, b, m in outs],
            scratch_shapes=[
                pltpu.VMEM((width, 3 * cols), bf16),
                pltpu.VMEM((width, cols), bf16),
                pltpu.VMEM((seq, seq), f32),
                pltpu.SemaphoreType.DMA((64,)),
            ],
        ),
        compiler_params=params(1),
        cost_estimate=cost(2e10, 1e7, 3e6),
        name="attn_fwd",
    )(coords, x, seg_row, seg_col, gain, bias, proj_bias, *pa, *pb)


def attn_bwd_kernel(
    heads, piece, c_ref, dxr_ref, dxr2_ref, x_ref, srow_ref, scol_ref, ln_ref, qkv_ref, kt_ref, o_ref, ot_ref, lse_ref, a0, a1_, b0, b1_,
    da1_ref, ga0_ref, ga1_ref, gb0_ref, gb1_ref, bsum_ref,
    w_s, wo_s, bias_s, dp_s, gw_s, go_s, sems,
):
    cols = heads * HD
    pairs = cols // 128
    step = pl.program_id(0)

    def into(block, j):
        return w_s.at[pl.ds(pl.multiple_of(block * piece, 16), piece), pl.ds(j * cols, cols)]

    def into_out(block):
        return wo_s.at[pl.ds(pl.multiple_of(block * piece, 16), piece), :]

    @pl.when(step == 0)
    def _():
        jobs = [
            ("a", (a0, a1_), lambda r, i, z: r.at[i, z, 0], lambda k: into(k, 0)),
            ("a", (a0, a1_), lambda r, i, z: r.at[i, z, 1], lambda k: into(k, 1)),
            ("b", (b0, b1_), lambda r, i, z: r.at[i, z, 0], lambda k: into(k, 2)),
            ("b", (b0, b1_), lambda r, i, z: r.at[i, z, 1], into_out),
        ]
        for c in load_pieces(c_ref, jobs, sems):
            c.wait()
        gw_s[...] = jnp.zeros_like(gw_s)
        go_s[...] = jnp.zeros_like(go_s)
        bsum_ref[...] = jnp.zeros_like(bsum_ref)

    dxr = jnp.where(step == c_ref[3], dxr_ref[...], dxr2_ref[...])
    do = nn_dot(dxr, wo_s[...]).astype(bf16)
    go_s[...] += nn_dot(dxr.T, o_ref[0])
    bias_s[...] = jnp.where(scol_ref[0] == srow_ref[0], 0.0, -1e30)
    lane = lax.broadcasted_iota(jnp.int32, (1, 128), 1)
    scale = HD ** (-0.5)
    scale2 = scale * LOG2E

    for p in range(pairs):
        q_p = qkv_ref[0, 0, p]
        k_p = qkv_ref[0, 1, p]
        v_p = qkv_ref[0, 2, p]
        do_p = do[:, p * 128 : (p + 1) * 128]
        prod = do_p.T.astype(f32) * ot_ref[0, p].astype(f32)
        dv = None
        for h in range(2):
            keep = (lane < HD) if h == 0 else (lane >= HD)
            q_h = jnp.where(keep, q_p, jnp.zeros_like(q_p))
            do_h = jnp.where(keep, do_p, jnp.zeros_like(do_p))
            row = jnp.sum(prod[h * HD : (h + 1) * HD], axis=0, keepdims=True)
            s_t = nt_dot(k_p, q_h)
            p_t = jnp.exp2(s_t * scale2 + (bias_s[...] - lse_ref[0, p, h : h + 1, :]))
            d_t = nt_dot(v_p, do_h)
            ds_t = (p_t * (d_t - row)).astype(bf16)
            dv_h = nn_dot(p_t.astype(bf16), do_h)
            dk_h = nn_dot(ds_t, q_h)
            dq_h = nn_dot(kt_ref[0, p, h * HD : (h + 1) * HD], ds_t)
            dv, dk, dq = (dv_h, dk_h, [dq_h]) if dv is None else (dv + dv_h, dk + dk_h, dq + [dq_h])
        dq = (jnp.concatenate(dq, axis=0) * scale).astype(bf16).T
        dp_s[:, p * 128 : (p + 1) * 128] = dq
        dp_s[:, cols + p * 128 : cols + (p + 1) * 128] = (dk * scale).astype(bf16)
        dp_s[:, 2 * cols + p * 128 : 2 * cols + (p + 1) * 128] = dv.astype(bf16)

    dproj = dp_s[...]
    da1_ref[0] = nt_dot(dproj, w_s[...]).astype(bf16)
    bsum_ref[...] += jnp.sum(dproj.astype(f32), axis=0, keepdims=True)
    xhat1, _ = norm_parts(x_ref[0].astype(f32))
    a1 = (xhat1 * ln_ref[0:1] + ln_ref[1:2]).astype(bf16)
    gw_s[...] += nn_dot(a1.T, dproj)

    @pl.when(step == pl.num_programs(0) - 1)
    def _():
        for outer in range(2):
            for inner in range(2):
                for rz in range(4):
                    ra = pl.ds(pl.multiple_of(place(c_ref, "a", outer, inner, rz) * piece, 16), piece)
                    rb = pl.ds(pl.multiple_of(place(c_ref, "b", outer, inner, rz) * piece, 16), piece)
                    ga, gb = ((ga0_ref, gb0_ref), (ga1_ref, gb1_ref))[outer]
                    ga[inner, rz, 0] = gw_s[ra, :cols].astype(bf16)
                    ga[inner, rz, 1] = gw_s[ra, cols : 2 * cols].astype(bf16)
                    gb[inner, rz, 0] = gw_s[rb, 2 * cols :].astype(bf16)
                    gb[inner, rz, 1] = go_s[rb, :].astype(bf16)


def attn_bwd(coords, dxr, dxr2, x, seg_row, seg_col, ln, saved, pa, pb):
    rows, seq, width = x.shape
    qkv, kt, o, ot, lse = saved
    cols = o.shape[-1]
    heads = cols // HD
    pairs = cols // 128
    piece = pa[0].shape[-2]
    row3 = lambda r, *_: (r, 0, 0)
    row4 = lambda r, *_: (r, 0, 0, 0)
    row5 = lambda r, *_: (r, 0, 0, 0, 0)
    tok = pl.BlockSpec((1, seq, width), row3)
    gshape = pa[0].shape
    return pl.pallas_call(
        functools.partial(attn_bwd_kernel, heads, piece),
        out_shape=[
            jax.ShapeDtypeStruct((rows, seq, width), bf16),
            *[jax.ShapeDtypeStruct(gshape, bf16)] * 4,
            jax.ShapeDtypeStruct((1, 3 * cols), f32),
        ],
        grid_spec=pltpu.PrefetchScalarGridSpec(
            num_scalar_prefetch=1,
            grid=(rows,),
            in_specs=[
                full_spec((seq, width)), full_spec((seq, width)), tok,
                pl.BlockSpec((1, 1, seq), row3),
                pl.BlockSpec((1, seq, 1), row3),
                full_spec((2, width)),
                pl.BlockSpec((1, 3, pairs, seq, 128), row5),
                pl.BlockSpec((1, pairs, 128, seq), row4),
                pl.BlockSpec((1, seq, cols), row3),
                pl.BlockSpec((1, pairs, 128, seq), row4),
                pl.BlockSpec((1, pairs, 2, seq), row4),
                ANY, ANY, ANY, ANY,
            ],
            out_specs=[
                tok,
                *[full_spec(gshape)] * 4,
                full_spec((1, 3 * cols)),
            ],
            scratch_shapes=[
                pltpu.VMEM((width, 3 * cols), bf16),
                pltpu.VMEM((width, cols), bf16),
                pltpu.VMEM((seq, seq), f32),
                pltpu.VMEM((seq, 3 * cols), bf16),
                pltpu.VMEM((width, 3 * cols), f32),
                pltpu.VMEM((width, cols), f32),
                pltpu.SemaphoreType.DMA((64,)),
            ],
        ),
        compiler_params=params(1),
        cost_estimate=cost(4e10, 2e7, 3e6),
        name="attn_bwd",
    )(coords, dxr, dxr2, x, seg_row, seg_col, ln, qkv, kt, o, ot, lse, *pa, *pb)


def sort_kernel(sources, *refs):
    vs_ref = refs[-1]
    block = vs_ref.shape[0]
    total = None
    for k in range(sources):
        pos_row, v_ref = refs[2 * k], refs[2 * k + 1]
        slot = lax.broadcasted_iota(jnp.int32, (block, v_ref.shape[0]), 0)
        slot = slot + pl.program_id(0) * block
        pick = (slot == pos_row[...]).astype(f32).astype(bf16)
        part = nn_dot(pick, v_ref[...])
        total = part if total is None else total + part
    vs_ref[...] = total.astype(bf16)


def sort_tokens(sources, tiles, group, groups, into=None):
    width = sources[0][1].shape[1]
    tokens = sum(v.shape[0] for _, v in sources)
    slots = tiles * TILE
    steps = 2
    block = slots // steps
    flat = [x for pair in sources for x in pair]
    return pl.pallas_call(
        functools.partial(sort_kernel, len(sources)),
        out_shape=jax.ShapeDtypeStruct((groups * slots, width), bf16),
        grid=(steps,),
        in_specs=[*[full_spec(x.shape) for x in flat], *([] if into is None else [ANY])],
        out_specs=pl.BlockSpec((block, width), lambda i: (i + group * steps, 0)),
        input_output_aliases={} if into is None else {len(flat): 0},
        compiler_params=params(1),
        cost_estimate=cost(2 * slots * tokens * width, 1e7),
        name="sort_tokens",
    )(*flat, *([] if into is None else [into]))


def unsort_kernel(targets, *refs):
    vs = refs[targets][...]
    for k in range(targets):
        pos_row, out_ref = refs[k], refs[targets + 1 + k]
        slot = lax.broadcasted_iota(jnp.int32, (vs.shape[0], out_ref.shape[0]), 0)
        pick = (slot == pos_row[...]).astype(f32).astype(bf16)
        out_ref[...] = tn_dot(pick, vs).astype(bf16)


def unsort_tokens(places, vs, group, groups):
    width = vs.shape[1]
    slots = vs.shape[0] // groups
    tokens = sum(p.shape[1] for p in places)
    return pl.pallas_call(
        functools.partial(unsort_kernel, len(places)),
        out_shape=[jax.ShapeDtypeStruct((p.shape[1], width), bf16) for p in places],
        grid=(1,),
        in_specs=[
            *[full_spec(p.shape) for p in places],
            pl.BlockSpec((slots, width), lambda i: (group, 0)),
        ],
        out_specs=[full_spec((p.shape[1], width)) for p in places],
        compiler_params=params(1),
        cost_estimate=cost(2 * slots * tokens * width, 1e7),
        name="unsort_tokens",
    )(*places, vs)


def mid_kernel(x_ref, parts_ref, vec_ref, x2_ref, a2_ref):
    att = jnp.sum(parts_ref[...].astype(f32), axis=0)
    x2 = x_ref[...].astype(f32) + att + vec_ref[0:1]
    x2_ref[...] = x2
    xhat, _ = norm_parts(x2)
    a2_ref[...] = (xhat * vec_ref[1:2] + vec_ref[2:3]).astype(bf16)


def mid(x, partial, vec):
    tokens, width = x.shape
    tile = pl.BlockSpec((TILE, width), lambda i: (i, 0))
    return pl.pallas_call(
        mid_kernel,
        out_shape=[
            jax.ShapeDtypeStruct((tokens, width), f32),
            jax.ShapeDtypeStruct((tokens, width), bf16),
        ],
        grid=(tokens // TILE,),
        in_specs=[
            tile, pl.BlockSpec((partial.shape[0], TILE, width), lambda i: (0, i, 0)),
            full_spec((3, width)),
        ],
        out_specs=[tile, tile],
        compiler_params=params(1),
        cost_estimate=cost(1e7, 5e6),
        name="mid_norm",
    )(x, partial, vec)


def ffn_kernel(first, count, piece, groups, c_ref, te_ref, n_ref, *refs):
    xs_ref, dys_ref, ub_ref, *rest = refs
    if not first:
        zin_ref, din_ref, *rest = rest
    w_refs = [rest[2 * c : 2 * c + 2] for c in range(count)]
    rest = rest[2 * count :]
    z_ref, da_ref, *rest = rest
    g_refs = [rest[2 * c : 2 * c + 2] for c in range(count)]
    gub_ref, wu_s, wd_s, gu_s, gd_s, sems = rest[2 * count :]
    experts = wu_s.shape[0]
    hc = wu_s.shape[2] // count
    i = pl.program_id(0)
    spots = [(ry, rz, rx) for ry in range(2) for rz in range(4) for rx in range(2)]

    def rows_of(ry, rz, rx):
        block = (c_ref[0] ^ rz) * 4 + (c_ref[1] ^ ry) * 2 + (c_ref[2] ^ rx)
        return pl.ds(pl.multiple_of(block * piece, 16), piece)

    @pl.when(i == 0)
    def _():
        copies = []
        for c in range(count):
            for ry, rz, rx in spots:
                for k, w_s in ((0, wu_s), (1, wd_s)):
                    copies.append(
                        pltpu.make_async_copy(
                            w_refs[c][ry].at[rz, rx, k],
                            w_s.at[:, rows_of(ry, rz, rx), pl.ds(c * hc, hc)],
                            sems.at[len(copies)],
                        )
                    )
        for c in copies:
            c.start()
        gu_s[...] = jnp.zeros_like(gu_s)
        gd_s[...] = jnp.zeros_like(gd_s)
        gub_ref[...] = jnp.zeros_like(gub_ref)
        for c in copies:
            c.wait()

    per = pl.num_programs(0) // groups
    group = i // per
    live = i - group * per < n_ref[group]

    @pl.when(live)
    def _():
        e = te_ref[i]
        x = xs_ref[...]
        dy = dys_ref[...]
        u = nn_dot(x, wu_s[e]) + ub_ref[e]
        act, slope = gelu_parts(u)
        act = act.astype(bf16)
        du = (nn_dot(dy, wd_s[e]) * slope).astype(bf16)
        z = nt_dot(act, wd_s[e])
        da = nt_dot(du, wu_s[e])
        if not first:
            z = z + zin_ref[...].astype(f32)
            da = da + din_ref[...].astype(f32)
        z_ref[...] = z.astype(bf16)
        da_ref[...] = da.astype(bf16)
        gd_s[e] += tn_dot(dy, act)
        gu_s[e] += tn_dot(x, du)
        gub_ref[e] += jnp.sum(du.astype(f32), axis=0, keepdims=True)

    @pl.when(jnp.logical_not(live))
    def _():
        z_ref[...] = jnp.zeros_like(z_ref)
        da_ref[...] = jnp.zeros_like(da_ref)

    @pl.when(i == pl.num_programs(0) - 1)
    def _():
        for c in range(count):
            lanes = pl.ds(c * hc, hc)
            for ry, rz, rx in spots:
                rows = rows_of(ry, rz, rx)
                for e in range(experts):
                    g_refs[c][ry][rz, rx, 0, e] = gu_s[e, rows, lanes].astype(bf16)
                    g_refs[c][ry][rz, rx, 1, e] = gd_s[e, rows, lanes].astype(bf16)


def ffn(coords, tile_expert, used, xs, dys, up_b, weights, carry):
    slots, width = xs.shape
    tiles = slots // TILE
    groups = used.shape[0]
    first = not carry
    count = len(weights)
    gshape = weights[0][0].shape
    experts, piece, hc = gshape[3:]
    hid = hc * count
    tile = pl.BlockSpec((TILE, width), lambda i, *_: (i, 0))
    out = pl.pallas_call(
        functools.partial(ffn_kernel, first, count, piece, groups),
        out_shape=[
            jax.ShapeDtypeStruct((slots, width), bf16),
            jax.ShapeDtypeStruct((slots, width), bf16),
            *[jax.ShapeDtypeStruct(gshape, bf16)] * (2 * count),
            jax.ShapeDtypeStruct((experts, 1, hid), f32),
        ],
        grid_spec=pltpu.PrefetchScalarGridSpec(
            num_scalar_prefetch=3,
            grid=(tiles,),
            in_specs=[
                tile, tile, full_spec((experts, 1, hid)), *([] if first else [tile, tile]),
                *[ANY] * (2 * count),
            ],
            out_specs=[
                tile, tile, *[full_spec(gshape)] * (2 * count), full_spec((experts, 1, hid)),
            ],
            scratch_shapes=[
                pltpu.VMEM((experts, width, hid), bf16),
                pltpu.VMEM((experts, width, hid), bf16),
                pltpu.VMEM((experts, width, hid), f32),
                pltpu.VMEM((experts, width, hid), f32),
                pltpu.SemaphoreType.DMA((32 * count,)),
            ],
        ),
        compiler_params=params(1),
        cost_estimate=cost(12 * slots * width * hid * 1.5, 4e7, 2 * slots * hid),
        name="ffn",
    )(coords, tile_expert, used, xs, dys, up_b, *carry, *[w for pair in weights for w in pair])
    zs, das, *rest = out
    return zs, das, [rest[2 * c : 2 * c + 2] for c in range(count)], rest[2 * count]


def norm_grad_kernel(count, low, *refs):
    parts, (v_ref, add_ref, gain_ref, out_ref, *refs) = refs[:count], refs[count:]
    sums_ref = refs[-1]

    @pl.when(pl.program_id(0) == 0)
    def _():
        sums_ref[...] = jnp.zeros_like(sums_ref)

    grad = sum(
        jnp.sum(p[...].astype(f32), axis=0) if len(p.shape) == 3 else p[...].astype(f32) for p in parts
    )
    xhat, rstd = norm_parts(v_ref[...].astype(f32))
    out = add_ref[...].astype(f32) + norm_back(grad, xhat, rstd, gain_ref[...])
    out_ref[...] = out
    if low:
        refs[0][...] = out.astype(bf16)
    sums_ref[0:1] += jnp.sum(grad * xhat, axis=0, keepdims=True)
    sums_ref[1:2] += jnp.sum(grad, axis=0, keepdims=True)
    sums_ref[2:3] += jnp.sum(out, axis=0, keepdims=True)


def norm_grad(partial, v, add, gain, low):
    tokens, width = v.shape
    tile = pl.BlockSpec((TILE, width), lambda i: (i, 0))
    return pl.pallas_call(
        functools.partial(norm_grad_kernel, len(partial), low),
        out_shape=[
            jax.ShapeDtypeStruct((tokens, width), f32),
            *([jax.ShapeDtypeStruct((tokens, width), bf16)] if low else []),
            jax.ShapeDtypeStruct((8, width), f32),
        ],
        grid=(tokens // TILE,),
        in_specs=[
            *[
                pl.BlockSpec((p.shape[0], TILE, width), lambda i: (0, i, 0)) if p.ndim == 3 else tile
                for p in partial
            ],
            tile, tile, full_spec((1, width)),
        ],
        out_specs=[tile, *([tile] if low else []), full_spec((8, width))],
        compiler_params=params(1),
        cost_estimate=cost(2e7, 8e6),
        name="norm_grad",
    )(*partial, v, add, gain)


def whole(kernel, name, outs, *args, prefetch=()):
    return pl.pallas_call(
        kernel,
        out_shape=[jax.ShapeDtypeStruct(s, d) for s, d in outs],
        grid_spec=pltpu.PrefetchScalarGridSpec(
            num_scalar_prefetch=len(prefetch),
            grid=(1,),
            in_specs=[full_spec(x.shape) for x in args],
            out_specs=[full_spec(s) for s, _ in outs],
        ),
        compiler_params=params(1),
        cost_estimate=cost(1e6, 4e6),
        name=name,
    )(*prefetch, *args)


def sums_y_kernel(keep, got, own, *sends):
    add = lambda rz: keep[rz].astype(f32) + got[rz].astype(f32)
    own[...] = add(0)
    for rz, send in zip((1, 2, 3), sends):
        send[...] = add(rz).astype(bf16)


def sums_z_kernel(own, r1, r2, r3, mine, near):
    add = lambda k: own[k] + r1[k].astype(f32) + r2[k].astype(f32) + r3[k].astype(f32)
    mine[...] = add(0)
    near[...] = add(1).astype(bf16)


def two_sums_kernel(a_keep, a_got, b_keep, b_got, a_own, a_send, b_own, b_send):
    for keep, got, own, send in ((a_keep, a_got, a_own, a_send), (b_keep, b_got, b_own, b_send)):
        own[...] = keep[0].astype(f32) + got[0].astype(f32)
        send[...] = (keep[1].astype(f32) + got[1].astype(f32)).astype(bf16)


def four_sums_kernel(a_own, a_got, b_own, b_got, own, *sends):
    add = lambda rz: (a_own[rz] + a_got[rz].astype(f32), b_own[rz] + b_got[rz].astype(f32))
    own[0], own[1] = add(0)
    for rz, send in zip((1, 2, 3), sends):
        va, vb = add(rz)
        send[0] = va.astype(bf16)
        send[1] = vb.astype(bf16)


def qkv_grad_kernel(own, r1, r2, r3, g_qkv, g_out):
    add = lambda k, j: (
        own[k, j] + r1[k, j].astype(f32) + r2[k, j].astype(f32) + r3[k, j].astype(f32)
    )
    g_qkv[0] = add(0, 0)
    g_qkv[1] = add(0, 1)
    g_qkv[2] = add(1, 0)
    g_out[...] = add(1, 1)


def rows_kernel(c_ref, *refs):
    for k in range(2):
        mine, other, out = refs[2 * k], refs[2 * k + 1], refs[4 + k]
        out[c_ref[3]] = mine[...]
        out[1 - c_ref[3]] = other[...]


def expert_grad_kernel(c_ref, *refs):
    *mines, near, g_up, g_down = refs
    hc = mines[0].shape[-1]
    half = hc * len(mines)
    here = pl.multiple_of(c_ref[2] * half, 128)
    there = pl.multiple_of((1 - c_ref[2]) * half, 128)
    for k, out in ((0, g_up), (1, g_down)):
        for c, mine in enumerate(mines):
            out[:, :, pl.ds(here + c * hc, hc)] = mine[k]
        out[:, :, pl.ds(there, half)] = near[k].astype(f32)


def flip(x, mask, size):
    return lax.ppermute(x, "dp", [(i, i ^ mask) for i in range(size)])


def after(v, *deps):
    return lax.optimization_barrier((v, deps))[0]


def deal(v):
    return lax.all_to_all(v, "mp", 0, 0)


def swap(v):
    return lax.ppermute(v, "mp", [(0, 1), (1, 0)])


def share(v):
    return deal(jnp.broadcast_to(v, (lax.axis_size("mp"),) + v.shape))


def gather_staged(a, b, size):
    both = jnp.stack([a, b])
    blocks = [both] + [flip(both, 4 * rz, size) for rz in (1, 2, 3)]
    a0 = jnp.stack([v[0] for v in blocks])
    b0 = jnp.stack([v[1] for v in blocks])
    a0 = jnp.stack([a0, flip(a0, 1, size)])
    b0 = jnp.stack([b0, flip(b0, 2, size)])
    return (a0, flip(a0, 2, size)), (b0, flip(b0, 1, size))


def attn_sums_xy(ga, gb, size):
    shape = ga[0].shape[1:]
    a_own, a_send, b_own, b_send = whole(
        two_sums_kernel, "two_sums", [(shape, f32), (shape, bf16)] * 2,
        ga[0], flip(ga[1], 2, size), gb[0], flip(gb[1], 1, size),
    )
    shape = (2,) + shape[1:]
    own, *sends = whole(
        four_sums_kernel, "four_sums", [(shape, f32), *[(shape, bf16)] * 3],
        a_own, flip(a_send, 1, size), b_own, flip(b_send, 2, size),
    )
    return own, sends


def gather_plain(w):
    full = lax.all_gather(w, "dp", axis=1, tiled=True)
    n, rows, cols = full.shape
    return full.reshape(n, 16, rows // 16, cols).swapaxes(0, 1)


def gather_pieces(a, b, size, staged):
    if staged:
        return gather_staged(a, b, size)
    blocks = [gather_plain(v) for v in (a, b)]
    blocks = [v.reshape((4, 2, 2) + v.shape[1:]) for v in blocks]
    fa = jnp.moveaxis(blocks[0], 0, 2)
    fb = jnp.swapaxes(jnp.moveaxis(blocks[1], 0, 2), 0, 1)
    return (fa[0], fa[1]), (fb[0], fb[1])


def scatter_plain(ga, gb):
    fa = jnp.moveaxis(jnp.stack(ga), 2, 0)
    fb = jnp.moveaxis(jnp.swapaxes(jnp.stack(gb), 0, 1), 2, 0)
    outs = []
    for v in (fa, fb):
        v = v.reshape((16,) + v.shape[3:]).swapaxes(0, 1)
        v = v.reshape(v.shape[0], -1, v.shape[-1]).astype(f32)
        outs.append(lax.psum_scatter(v, "dp", scatter_dimension=1, tiled=True))
    return outs


def phase(pred, f):
    shapes = jax.eval_shape(f)
    return lax.cond(
        pred, f, lambda: jax.tree.map(lambda v: jnp.zeros(v.shape, v.dtype), shapes)
    )


def along_z(p, size):
    return jnp.stack([p] + [flip(p, 4 * rz, size) for rz in (1, 2, 3)])


def sums_y(pair, size):
    shape = pair[0].shape[1:]
    return whole(
        sums_y_kernel, "sums_y", [(shape, f32), *[(shape, bf16)] * 3],
        pair[0], flip(pair[1], 2, size),
    )


def sums_z(parts_y, size):
    own, *sends = parts_y
    got = [flip(v, 4 * rz, size) for rz, v in zip((1, 2, 3), sends)]
    shape = own.shape[1:]
    return whole(sums_z_kernel, "sums_z", [(shape, f32), (shape, bf16)], own, *got)


def expert_pieces_plain(w_up, w_down):
    hc = w_up.shape[-1] // CHUNKS
    blocks = jnp.stack([gather_plain(w_up), gather_plain(w_down)], axis=1)
    blocks = blocks.reshape((4, 2, 2) + blocks.shape[1:])
    return [
        tuple(blocks[:, ry, ..., c * hc : (c + 1) * hc] for ry in range(2)) for c in range(CHUNKS)
    ]


def expert_sums_plain(pair):
    v = jnp.stack(pair, axis=1)
    v = v.reshape((16,) + v.shape[3:])
    v = jnp.moveaxis(v, 0, 2)
    v = v.reshape(v.shape[:2] + (-1, v.shape[-1])).astype(f32)
    return lax.psum_scatter(v, "dp", scatter_dimension=2, tiled=True)


def sum_small(v, size):
    if size & (size - 1):
        return lax.psum(v, ("dp", "mp"))
    v = v + swap(v)
    mask = 1
    while mask < size:
        v = v + flip(v, mask, size)
        mask *= 2
    return v


def token_plan(segments, modality, experts):
    tokens = segments.size
    doc_ids = jnp.arange(modality.shape[1], dtype=jnp.int32)
    match = segments[:, :, None] == doc_ids
    mods = jnp.sum(jnp.where(match, modality[:, None, :], 0), axis=-1).reshape(tokens)
    kinds = jnp.arange(experts, dtype=jnp.int32)
    hot = (mods[:, None] == kinds).astype(jnp.int32)
    ids = jnp.arange(tokens, dtype=jnp.int32)
    lower = (ids[:, None] > ids[None, :]).astype(bf16)
    before = jnp.dot(lower, hot.astype(bf16), preferred_element_type=f32).astype(jnp.int32)
    need = (jnp.sum(hot, axis=0) + TILE - 1) // TILE
    ends = jnp.sum(jnp.where(kinds[:, None] >= kinds[None, :], need[None, :], 0), axis=1)
    pos = jnp.sum(hot * (before + (ends - need)[None, :] * TILE), axis=1)
    tiles = (tokens + experts * (TILE - 1)) // TILE
    tile_ids = jnp.arange(tiles, dtype=jnp.int32)
    tile_expert = jnp.minimum(
        jnp.sum((tile_ids[:, None] >= ends[None, :]).astype(jnp.int32), axis=1), experts - 1
    )
    return mods, pos, tile_expert, ends[-1:]


def body(
    layer_input, segments, modality, ln_gain, ln_bias, w_qkv, qv_bias, w_out, out_bias,
    w_up, up_bias, w_down, down_bias, cotangent,
):
    part = lax.axis_index("mp")
    parts = lax.axis_size("mp")
    size = lax.axis_size("dp")
    me = lax.axis_index("dp")
    rows, seq, width = layer_input.shape
    tokens = rows * seq
    cols = w_qkv.shape[-1]
    hid = w_up.shape[-1]
    experts = w_up.shape[0]
    shape3 = (rows, seq, width)
    tiles = (tokens + experts * (TILE - 1)) // TILE
    staged = size == 16

    mine_rows = rows // parts
    mine_tokens = tokens // parts
    by_core = (parts, mine_tokens, width)
    dy = cotangent.reshape(tokens, width)
    rows_here = lambda v: lax.dynamic_slice_in_dim(v, part * mine_rows, mine_rows, 0)
    x_mine = rows_here(layer_input).reshape(mine_tokens, width)
    dy_mine = rows_here(cotangent).reshape(mine_tokens, width)
    col_start = part * cols
    q_b = lax.dynamic_slice_in_dim(qv_bias[0], col_start, cols)
    v_b = lax.dynamic_slice_in_dim(qv_bias[1], col_start, cols)
    proj_bias = jnp.concatenate([q_b, jnp.zeros_like(q_b), v_b]).reshape(1, 3 * cols)
    seg_row, seg_col = segments.reshape(rows, 1, seq), segments.reshape(rows, seq, 1)
    vec = jnp.concatenate([out_bias[None], ln_gain[1:2], ln_bias[1:2]])
    ln1 = jnp.concatenate([ln_gain[0:1], ln_bias[0:1]])
    w_ab = w_qkv[:2], jnp.stack([w_qkv[2], w_out])

    def fwd(coords, pa, pb):
        att, *saved = attn_fwd(
            coords, layer_input, seg_row, seg_col, ln_gain[0:1], ln_bias[0:1], proj_bias, pa, pb
        )
        return (saved, *mid(x_mine, deal(att.reshape(by_core)), vec))

    def bwd(coords, dxr, saved, pa, pb):
        return attn_bwd(coords, *dxr, layer_input, seg_row, seg_col, ln1, saved, pa, pb)

    def halves(v):
        take = lambda k: lax.dynamic_slice_in_dim(v, k * mine_tokens, mine_tokens, 0)
        return take(part).reshape(1, mine_tokens), take(1 - part).reshape(1, mine_tokens)

    def finish(x2, z_sum, mods):
        kinds = lax.dynamic_slice_in_dim(mods, part * mine_tokens, mine_tokens, 0)[:, None]
        bias_of = jnp.zeros((mine_tokens, width), f32)
        for e in range(experts):
            bias_of = jnp.where(kinds == e, down_bias[e][None], bias_of)
        return (x2 + (z_sum + bias_of)).astype(bf16)

    if staged:
        x_bit = me % 2
        coords = jnp.stack([me // 4, (me // 2) % 2, x_bit, part]).astype(jnp.int32)
        pred = me < size
        half = hid // 2
        hid_start = part * hid + x_bit * half
        hc = half // CHUNKS
        up_b = lax.dynamic_slice_in_dim(up_bias, hid_start, half, 1)

        def call_experts(k, xs, dys, weights, carry):
            call = CALLS[k]
            ub = up_b[:, None, call[0] * hc : (call[-1] + 1) * hc]
            return ffn(
                coords, tile_expert, used, xs, dys, ub, [weights[c] for c in call], carry
            )

        def begin():
            w = jnp.stack([w_up, w_down])
            keep = lax.dynamic_slice_in_dim(w, x_bit * half, half, 3)
            near = flip(lax.dynamic_slice_in_dim(w, (1 - x_bit) * half, half, 3), 1, size)
            pieces = [
                jnp.stack([keep[..., c * hc : (c + 1) * hc], near[..., c * hc : (c + 1) * hc]])
                for c in range(CHUNKS)
            ]
            pa, pb = gather_pieces(*w_ab, size, True)
            mods, pos, tile_expert, used = token_plan(segments, modality, experts)
            plan = flip(jnp.concatenate([pos, tile_expert, used]), 1, size)
            dys = sort_tokens([(pos.reshape(1, tokens), dy)], tiles, 0, 2)
            hot = (mods[:, None] == jnp.arange(experts, dtype=jnp.int32)).astype(bf16)
            return (
                pieces, pa, pb, mods, pos, tile_expert, used, plan,
                dys, tn_dot(hot, dy), along_z(pieces[0], size),
            )

        (pieces, pa, pb, mods, pos, tile_expert, used, plan, dys, g_down_bias,
         z0) = phase(pred, begin)
        pos_here = halves(pos)
        pos_near = halves(plan)
        tile_expert = jnp.concatenate([tile_expert, plan[tokens : tokens + tiles]])
        used = jnp.concatenate([used, plan[tokens + tiles :]])

        saved, x2, a2, y0, z1, dy_near = phase(
            pred,
            lambda: (
                *fwd(coords, pa, pb), flip(z0, 2, size), along_z(pieces[1], size),
                flip(dy_mine, 1, size),
            ),
        )

        def exchange():
            near = flip(a2, 1, size)
            y1 = flip(z1, 2, size)
            z2 = along_z(pieces[2], size)
            pos_row = pos.reshape(1, tokens)
            near_row = plan[:tokens].reshape(1, tokens)
            both = share(dy_near).reshape(tokens, width)
            d = sort_tokens([(near_row, both)], tiles, 1, 2, dys)
            xs = sort_tokens([(pos_row, share(a2).reshape(tokens, width))], tiles, 0, 2)
            near = share(after(near, d, xs)).reshape(tokens, width)
            return sort_tokens([(near_row, near)], tiles, 1, 2, xs), d, y1, z2

        xs, dys, y1, z2 = phase(pred, exchange)
        weights = [(z0, y0), (z1, y1)]
        (zs, das, grads, gub0), y2 = phase(
            pred, lambda: (call_experts(0, xs, dys, weights, ()), flip(z2, 2, size))
        )
        weights.append((z2, y2))
        def second():
            v0 = sums_y(grads[0], size)
            zs, das, more, gub = call_experts(1, xs, dys, weights, (zs0, das0))
            mine, other = unsort_tokens(pos_near, das, 1, 2)
            near = (mine.astype(f32) + swap(other).astype(f32)).astype(bf16)
            return zs, das, more, gub, near, v0

        zs0, das0 = zs, das
        zs, das, more, gub1, da_near, v0 = phase(pred, second)
        grads = grads + more
        g_upb = jnp.concatenate([gub0, gub1], axis=-1)[:, 0]
        pos_row = pos.reshape(1, tokens)
        near_row = plan[:tokens].reshape(1, tokens)

        def dealt(place, vs, group):
            return deal(unsort_tokens([place], vs, group, 2)[0].reshape(by_core))

        def back():
            near = flip(da_near, 1, size)
            g0 = sums_z(v0, size)
            v1 = sums_y(grads[1], size)
            own = dealt(pos_row, das, 0)
            z_near = jnp.sum(dealt(near_row, zs, 1).astype(f32), axis=0).astype(bf16)
            near = after(near, g0, v1, z_near)
            dx2, dxr, sums2 = norm_grad((own, near), x2, dy_mine, ln_gain[1:2], True)
            return dx2, (dxr, swap(dxr)), sums2, z_near, g0, v1

        dx2, dxr, sums2, z_near, g0, v1 = phase(pred, back)
        (da1, ga0, ga1, gb0, gb1, bsum), z_near, g1, v2 = phase(
            pred,
            lambda: (
                bwd(coords, dxr, saved, pa, pb), flip(z_near, 1, size), sums_z(v1, size),
                sums_y(grads[2], size),
            ),
        )

        def sum_up():
            own, sends = attn_sums_xy((ga0, ga1), (gb0, gb1), size)
            g2 = sums_z(v2, size)
            grad, sums1 = norm_grad((deal(da1.reshape(by_core)),), x_mine, dx2, ln_gain[0:1], False)
            z_own = dealt(pos_row, zs, 0)
            out = finish(x2, jnp.sum(z_own.astype(f32), axis=0) + z_near.astype(f32), mods)
            return own, sends, g2, grad, sums1, out

        own, sends, g2, grad, sums1, out = phase(pred, sum_up)
        got = [flip(v, 4 * rz, size) for rz, v in zip((1, 2, 3), sends)]
        near = flip(jnp.concatenate([v[1] for v in (g0, g1, g2)], axis=-1), 1, size)
        g_qkv, g_out = whole(
            qkv_grad_kernel, "qkv_grad", [(w_qkv.shape, f32), (w_out.shape, f32)], own, *got
        )
        g_up, g_down = whole(
            expert_grad_kernel, "expert_grad", [(w_up.shape, f32)] * 2,
            g0[0], g1[0], g2[0], near, prefetch=(coords,),
        )
        layer_output, grad_input = whole(
            rows_kernel, "rows", [((parts,) + v.shape, v.dtype) for v in (out, grad)],
            out, swap(out), grad, swap(grad), prefetch=(coords,),
        )
    else:
        coords = jnp.stack([0, 0, 0, part]).astype(jnp.int32)
        hid_start = part * hid
        hc = hid // CHUNKS
        up_b = lax.dynamic_slice_in_dim(up_bias, hid_start, hid, 1)
        pa, pb = gather_pieces(*w_ab, size, False)
        weights = expert_pieces_plain(w_up, w_down)
        mods, pos, tile_expert, used = token_plan(segments, modality, experts)
        pos_row = pos.reshape(1, tokens)
        hot = (mods[:, None] == jnp.arange(experts, dtype=jnp.int32)).astype(bf16)
        g_down_bias = tn_dot(hot, dy)
        dys = sort_tokens([(pos_row, dy)], tiles, 0, 1)
        saved, x2, a2 = fwd(coords, pa, pb)
        xs = sort_tokens([(pos_row, share(a2).reshape(tokens, width))], tiles, 0, 1)
        carry = ()
        grads = []
        g_upb = []
        for call in CALLS:
            ub = up_b[:, None, call[0] * hc : (call[-1] + 1) * hc]
            zs, das, pairs, gub = ffn(
                coords, tile_expert, used, xs, dys, ub, [weights[c] for c in call], carry
            )
            carry = (zs, das)
            g_upb.append(gub[:, 0])
            grads += pairs
        g_upb = jnp.concatenate(g_upb, axis=-1)
        g_up, g_down = jnp.concatenate([expert_sums_plain(pair) for pair in grads], axis=-1)
        own = deal(unsort_tokens([pos_row], das, 0, 1)[0].reshape(by_core))
        dx2, dxr, sums2 = norm_grad((own[0], own[1]), x2, dy_mine, ln_gain[1:2], True)
        da1, ga0, ga1, gb0, gb1, bsum = bwd(coords, (dxr, swap(dxr)), saved, pa, pb)
        own = deal(da1.reshape(by_core))
        grad_mine, sums1 = norm_grad((own[0], own[1]), x_mine, dx2, ln_gain[0:1], False)
        g_qk, g_vo = scatter_plain((ga0, ga1), (gb0, gb1))
        g_qkv, g_out = jnp.concatenate([g_qk, g_vo[:1]]), g_vo[1]
        own = deal(unsort_tokens([pos_row], zs, 0, 1)[0].reshape(by_core))
        layer_output = share(finish(x2, jnp.sum(own.astype(f32), axis=0), mods))
        grad_input = share(grad_mine)

    bsum = bsum.reshape(3, cols)
    g_qv = lax.dynamic_update_slice(
        jnp.zeros((2, width), f32), jnp.stack([bsum[0], bsum[2]]), (jnp.int32(0), col_start)
    )
    g_upb_full = lax.dynamic_update_slice(
        jnp.zeros((experts, up_bias.shape[1]), f32), g_upb, (jnp.int32(0), hid_start)
    )
    small = jnp.concatenate([sums1[0:2], sums2[0:3], g_down_bias / parts, g_qv, g_upb_full.reshape(-1, width)])
    small = sum_small(small, size)
    g_gain = jnp.stack([small[0], small[2]])
    g_lnb = jnp.stack([small[1], small[3]])
    return (
        layer_output.reshape(shape3),
        grad_input.reshape(shape3),
        g_gain,
        g_lnb,
        g_qkv,
        small[5 + experts : 7 + experts],
        g_out,
        small[4],
        g_up,
        small[7 + experts :].reshape(experts, up_bias.shape[1]),
        g_down,
        small[5 : 5 + experts],
    )


def solution(mesh):
    tok = P("dp", None, None)
    rep = P()
    wide = P(None, "dp", "mp")
    in_specs = (
        tok, P("dp", None), P("dp", None), rep, rep, wide, rep, P("dp", "mp"), rep, wide, rep,
        wide, rep, tok,
    )
    out_specs = (
        tok, tok, rep, rep, wide, rep, P("dp", "mp"), rep, wide, rep, wide, rep,
    )
    return jax.shard_map(body, mesh=mesh, in_specs=in_specs, out_specs=out_specs, check_vma=False)
```

```python
import functools
import math

import jax
import jax.numpy as jnp
from jax import lax
from jax.experimental import pallas as pl
from jax.experimental.pallas import tpu as pltpu
from jax.sharding import PartitionSpec as P

HD = 64
EPS = 1e-05
TILE = 256
CHUNKS = 3
SCALE = 1.0
CALLS = ((0,), (1, 2))
VMEM = 58 * 1024 * 1024
LOG2E = math.log2(math.e)
f32 = jnp.float32
bf16 = jnp.bfloat16
ANY = pl.BlockSpec(memory_space=pl.ANY)


def full_spec(shape):
    zeros = (0,) * len(shape)
    return pl.BlockSpec(shape, lambda *_: zeros)


def nt_dot(a, b):
    return lax.dot_general(a, b, (((1,), (1,)), ((), ())), preferred_element_type=f32)


def nn_dot(a, b):
    return lax.dot_general(a, b, (((1,), (0,)), ((), ())), preferred_element_type=f32)


def tn_dot(a, b):
    return lax.dot_general(a, b, (((0,), (0,)), ((), ())), preferred_element_type=f32)


def params(grid_rank):
    return pltpu.CompilerParams(
        dimension_semantics=("arbitrary",) * grid_rank, vmem_limit_bytes=VMEM
    )


def cost(flops, nbytes, trans=0):
    return pl.CostEstimate(
        flops=int(flops * SCALE), bytes_accessed=int(nbytes * SCALE), transcendentals=int(trans * SCALE)
    )


def place(c_ref, kind, outer, inner, rz):
    ry, rx = (outer, inner) if kind == "a" else (inner, outer)
    return (c_ref[0] ^ rz) * 4 + (c_ref[1] ^ ry) * 2 + (c_ref[2] ^ rx)


def load_pieces(c_ref, jobs, sems):
    copies = []
    for kind, pair, view, target in jobs:
        for outer in range(2):
            for inner in range(2):
                for rz in range(4):
                    rows = place(c_ref, kind, outer, inner, rz)
                    copies.append(
                        pltpu.make_async_copy(
                            view(pair[outer], inner, rz), target(rows), sems.at[len(copies)]
                        )
                    )
    for c in copies:
        c.start()
    return copies


def gelu_parts(u):
    mag = jnp.abs(u)
    t = 1.0 / (1.0 + (0.3275911 * math.sqrt(0.5)) * mag)
    poly = t * (
        0.254829592
        + t * (-0.284496736 + t * (1.421413741 + t * (-1.453152027 + t * 1.061405429)))
    )
    gauss = jnp.exp(-0.5 * u * u)
    half = 0.5 * poly * gauss
    cdf = jnp.where(u >= 0, 1.0 - half, half)
    return u * cdf, cdf + u * gauss * (1.0 / math.sqrt(2.0 * math.pi))


def norm_parts(v):
    mean = jnp.mean(v, axis=-1, keepdims=True)
    cent = v - mean
    var = jnp.mean(cent * cent, axis=-1, keepdims=True)
    rstd = lax.rsqrt(var + EPS)
    return cent * rstd, rstd


def norm_back(d_out, xhat, rstd, gain):
    d_hat = d_out * gain
    m1 = jnp.mean(d_hat, axis=-1, keepdims=True)
    m2 = jnp.mean(d_hat * xhat, axis=-1, keepdims=True)
    return rstd * (d_hat - m1 - xhat * m2)


def attn_fwd_kernel(
    heads, piece, c_ref, x_ref, srow_ref, scol_ref, ln_ref, pb_ref, a0, a1_, b0, b1_,
    att_ref, att_other_ref, qkv_ref, kt_ref, o_ref, ot_ref, lse_ref,
    w_s, wo_s, bias_s, sems,
):
    cols = heads * HD
    pairs = cols // 128
    seq, width = x_ref.shape[1], x_ref.shape[2]

    def into(block, j):
        return w_s.at[pl.ds(pl.multiple_of(block * piece, 16), piece), pl.ds(j * cols, cols)]

    def into_out(block):
        return wo_s.at[pl.ds(pl.multiple_of(block * piece, 16), piece), :]

    @pl.when(pl.program_id(0) == 0)
    def _():
        jobs = [
            ("a", (a0, a1_), lambda r, i, z: r.at[i, z, 0], lambda k: into(k, 0)),
            ("a", (a0, a1_), lambda r, i, z: r.at[i, z, 1], lambda k: into(k, 1)),
            ("b", (b0, b1_), lambda r, i, z: r.at[i, z, 0], lambda k: into(k, 2)),
            ("b", (b0, b1_), lambda r, i, z: r.at[i, z, 1], into_out),
        ]
        for c in load_pieces(c_ref, jobs, sems):
            c.wait()

    xhat, _ = norm_parts(x_ref[0].astype(f32))
    a1 = (xhat * ln_ref[0:1] + ln_ref[1:2]).astype(bf16)
    proj = (nn_dot(a1, w_s[...]) + pb_ref[...]).astype(bf16)
    for j in range(3):
        for p in range(pairs):
            qkv_ref[0, j, p] = proj[:, j * cols + p * 128 : j * cols + (p + 1) * 128]
    for p in range(pairs):
        kt_ref[0, p] = proj[:, cols + p * 128 : cols + (p + 1) * 128].T
    bias_s[...] = jnp.where(scol_ref[0] == srow_ref[0], 0.0, -1e30)
    lane = lax.broadcasted_iota(jnp.int32, (1, 128), 1)
    scale2 = HD ** (-0.5) * LOG2E

    @pl.loop(0, pairs)
    def _(p):
        q_p = qkv_ref[0, 0, p]
        k_p = qkv_ref[0, 1, p]
        v_t = qkv_ref[0, 2, p].T
        for h in range(2):
            keep = (lane < HD) if h == 0 else (lane >= HD)
            q_h = jnp.where(keep, q_p, jnp.zeros_like(q_p))
            s_t = nt_dot(k_p, q_h) + bias_s[...]
            top = jnp.max(s_t, axis=0, keepdims=True)
            e_t = jnp.exp2((s_t - top) * scale2)
            total = jnp.sum(e_t, axis=0, keepdims=True)
            p_t = (e_t * (1.0 / total)).astype(bf16)
            o_t = nn_dot(v_t[h * HD : (h + 1) * HD], p_t)
            ot_ref[0, p, h * HD : (h + 1) * HD] = o_t.astype(bf16)
            lse_ref[0, p, pl.ds(h, 1), :] = top * scale2 + jnp.log2(total)

    for p in range(pairs):
        o_ref[0, :, p * 128 : (p + 1) * 128] = ot_ref[0, p].T
    att = nt_dot(o_ref[0], wo_s[...]).astype(bf16)

    @pl.when(pl.program_id(0) == c_ref[3])
    def _():
        att_ref[...] = att

    @pl.when(pl.program_id(0) != c_ref[3])
    def _():
        att_other_ref[...] = att


def attn_fwd(coords, x, seg_row, seg_col, ln, proj_bias, pa, pb):
    rows, seq, width = x.shape
    cols = proj_bias.shape[-1] // 3
    heads = cols // HD
    pairs = cols // 128
    piece = pa[0].shape[-2]
    row3 = lambda r, *_: (r, 0, 0)
    row4 = lambda r, *_: (r, 0, 0, 0)
    row5 = lambda r, *_: (r, 0, 0, 0, 0)
    outs = [
        ((seq, width), bf16, (seq, width), lambda *_: (0, 0)),
        ((seq, width), bf16, (seq, width), lambda *_: (0, 0)),
        ((rows, 3, pairs, seq, 128), bf16, (1, 3, pairs, seq, 128), row5),
        ((rows, pairs, 128, seq), bf16, (1, pairs, 128, seq), row4),
        ((rows, seq, cols), bf16, (1, seq, cols), row3),
        ((rows, pairs, 128, seq), bf16, (1, pairs, 128, seq), row4),
        ((rows, pairs, 2, seq), f32, (1, pairs, 2, seq), row4),
    ]
    return pl.pallas_call(
        functools.partial(attn_fwd_kernel, heads, piece),
        out_shape=[jax.ShapeDtypeStruct(s, d) for s, d, _, _ in outs],
        grid_spec=pltpu.PrefetchScalarGridSpec(
            num_scalar_prefetch=1,
            grid=(rows,),
            in_specs=[
                pl.BlockSpec((1, seq, width), row3),
                pl.BlockSpec((1, 1, seq), row3),
                pl.BlockSpec((1, seq, 1), row3),
                full_spec((2, width)),
                full_spec((1, 3 * cols)),
                ANY, ANY, ANY, ANY,
            ],
            out_specs=[pl.BlockSpec(b, m) for _, _, b, m in outs],
            scratch_shapes=[
                pltpu.VMEM((width, 3 * cols), bf16),
                pltpu.VMEM((width, cols), bf16),
                pltpu.VMEM((seq, seq), f32),
                pltpu.SemaphoreType.DMA((64,)),
            ],
        ),
        compiler_params=params(1),
        cost_estimate=cost(2e10, 1e7, 3e6),
        name="attn_fwd",
    )(coords, x, seg_row, seg_col, ln, proj_bias, *pa, *pb)


def attn_bwd_kernel(
    heads, piece, c_ref, dxr_ref, dxr2_ref, x_ref, srow_ref, scol_ref, ln_ref, qkv_ref, kt_ref, o_ref, ot_ref, lse_ref, a0, a1_, b0, b1_,
    da1_ref, da1_other_ref, ga0_ref, ga1_ref, gb0_ref, gb1_ref, bsum_ref,
    w_s, wo_s, bias_s, dp_s, gw_s, go_s, sems,
):
    cols = heads * HD
    pairs = cols // 128
    step = pl.program_id(0)

    def into(block, j):
        return w_s.at[pl.ds(pl.multiple_of(block * piece, 16), piece), pl.ds(j * cols, cols)]

    def into_out(block):
        return wo_s.at[pl.ds(pl.multiple_of(block * piece, 16), piece), :]

    @pl.when(step == 0)
    def _():
        jobs = [
            ("a", (a0, a1_), lambda r, i, z: r.at[i, z, 0], lambda k: into(k, 0)),
            ("a", (a0, a1_), lambda r, i, z: r.at[i, z, 1], lambda k: into(k, 1)),
            ("b", (b0, b1_), lambda r, i, z: r.at[i, z, 0], lambda k: into(k, 2)),
            ("b", (b0, b1_), lambda r, i, z: r.at[i, z, 1], into_out),
        ]
        for c in load_pieces(c_ref, jobs, sems):
            c.wait()
        gw_s[...] = jnp.zeros_like(gw_s)
        go_s[...] = jnp.zeros_like(go_s)
        bsum_ref[...] = jnp.zeros_like(bsum_ref)

    dxr = jnp.where(step == c_ref[3], dxr_ref[...], dxr2_ref[...])
    do = nn_dot(dxr, wo_s[...]).astype(bf16)
    go_s[...] += nn_dot(dxr.T, o_ref[0])
    bias_s[...] = jnp.where(scol_ref[0] == srow_ref[0], 0.0, -1e30)
    lane = lax.broadcasted_iota(jnp.int32, (1, 128), 1)
    scale = HD ** (-0.5)
    scale2 = scale * LOG2E

    for p in range(pairs):
        q_p = qkv_ref[0, 0, p]
        k_p = qkv_ref[0, 1, p]
        v_p = qkv_ref[0, 2, p]
        do_p = do[:, p * 128 : (p + 1) * 128]
        prod = do_p.T.astype(f32) * ot_ref[0, p].astype(f32)
        dv = None
        for h in range(2):
            keep = (lane < HD) if h == 0 else (lane >= HD)
            q_h = jnp.where(keep, q_p, jnp.zeros_like(q_p))
            do_h = jnp.where(keep, do_p, jnp.zeros_like(do_p))
            row = jnp.sum(prod[h * HD : (h + 1) * HD], axis=0, keepdims=True)
            s_t = nt_dot(k_p, q_h)
            p_t = jnp.exp2(s_t * scale2 + (bias_s[...] - lse_ref[0, p, h : h + 1, :]))
            d_t = nt_dot(v_p, do_h)
            ds_t = (p_t * (d_t - row)).astype(bf16)
            dv_h = nn_dot(p_t.astype(bf16), do_h)
            dk_h = nn_dot(ds_t, q_h)
            dq_h = nn_dot(kt_ref[0, p, h * HD : (h + 1) * HD], ds_t)
            dv, dk, dq = (dv_h, dk_h, [dq_h]) if dv is None else (dv + dv_h, dk + dk_h, dq + [dq_h])
        dq = (jnp.concatenate(dq, axis=0) * scale).astype(bf16).T
        dp_s[:, p * 128 : (p + 1) * 128] = dq
        dp_s[:, cols + p * 128 : cols + (p + 1) * 128] = (dk * scale).astype(bf16)
        dp_s[:, 2 * cols + p * 128 : 2 * cols + (p + 1) * 128] = dv.astype(bf16)

    dproj = dp_s[...]
    da1 = nt_dot(dproj, w_s[...]).astype(bf16)

    @pl.when(step == c_ref[3])
    def _():
        da1_ref[...] = da1

    @pl.when(step != c_ref[3])
    def _():
        da1_other_ref[...] = da1

    bsum_ref[...] += jnp.sum(dproj.astype(f32), axis=0, keepdims=True)
    xhat1, _ = norm_parts(x_ref[0].astype(f32))
    a1 = (xhat1 * ln_ref[0:1] + ln_ref[1:2]).astype(bf16)
    gw_s[...] += nn_dot(a1.T, dproj)

    @pl.when(step == pl.num_programs(0) - 1)
    def _():
        for outer in range(2):
            for inner in range(2):
                for rz in range(4):
                    ra = pl.ds(pl.multiple_of(place(c_ref, "a", outer, inner, rz) * piece, 16), piece)
                    rb = pl.ds(pl.multiple_of(place(c_ref, "b", outer, inner, rz) * piece, 16), piece)
                    ga, gb = ((ga0_ref, gb0_ref), (ga1_ref, gb1_ref))[outer]
                    ga[inner, rz, 0] = gw_s[ra, :cols].astype(bf16)
                    ga[inner, rz, 1] = gw_s[ra, cols : 2 * cols].astype(bf16)
                    gb[inner, rz, 0] = gw_s[rb, 2 * cols :].astype(bf16)
                    gb[inner, rz, 1] = go_s[rb, :].astype(bf16)


def attn_bwd(coords, dxr, dxr2, x, seg_row, seg_col, ln, saved, pa, pb):
    rows, seq, width = x.shape
    qkv, kt, o, ot, lse = saved
    cols = o.shape[-1]
    heads = cols // HD
    pairs = cols // 128
    piece = pa[0].shape[-2]
    row3 = lambda r, *_: (r, 0, 0)
    row4 = lambda r, *_: (r, 0, 0, 0)
    row5 = lambda r, *_: (r, 0, 0, 0, 0)
    tok = pl.BlockSpec((1, seq, width), row3)
    gshape = pa[0].shape
    return pl.pallas_call(
        functools.partial(attn_bwd_kernel, heads, piece),
        out_shape=[
            *[jax.ShapeDtypeStruct((seq, width), bf16)] * 2,
            *[jax.ShapeDtypeStruct(gshape, bf16)] * 4,
            jax.ShapeDtypeStruct((1, 3 * cols), f32),
        ],
        grid_spec=pltpu.PrefetchScalarGridSpec(
            num_scalar_prefetch=1,
            grid=(rows,),
            in_specs=[
                full_spec((seq, width)), full_spec((seq, width)), tok,
                pl.BlockSpec((1, 1, seq), row3),
                pl.BlockSpec((1, seq, 1), row3),
                full_spec((2, width)),
                pl.BlockSpec((1, 3, pairs, seq, 128), row5),
                pl.BlockSpec((1, pairs, 128, seq), row4),
                pl.BlockSpec((1, seq, cols), row3),
                pl.BlockSpec((1, pairs, 128, seq), row4),
                pl.BlockSpec((1, pairs, 2, seq), row4),
                ANY, ANY, ANY, ANY,
            ],
            out_specs=[
                *[full_spec((seq, width))] * 2,
                *[full_spec(gshape)] * 4,
                full_spec((1, 3 * cols)),
            ],
            scratch_shapes=[
                pltpu.VMEM((width, 3 * cols), bf16),
                pltpu.VMEM((width, cols), bf16),
                pltpu.VMEM((seq, seq), f32),
                pltpu.VMEM((seq, 3 * cols), bf16),
                pltpu.VMEM((width, 3 * cols), f32),
                pltpu.VMEM((width, cols), f32),
                pltpu.SemaphoreType.DMA((64,)),
            ],
        ),
        compiler_params=params(1),
        cost_estimate=cost(4e10, 2e7, 3e6),
        name="attn_bwd",
    )(coords, dxr, dxr2, x, seg_row, seg_col, ln, qkv, kt, o, ot, lse, *pa, *pb)


def sort_kernel(sources, *refs):
    vs_ref = refs[-1]
    block = vs_ref.shape[0]
    total = None
    for k in range(sources):
        pos_row, v_ref = refs[2 * k], refs[2 * k + 1]
        slot = lax.broadcasted_iota(jnp.int32, (block, v_ref.shape[0]), 0)
        slot = slot + pl.program_id(0) * block
        pick = (slot == pos_row[...]).astype(f32).astype(bf16)
        part = nn_dot(pick, v_ref[...])
        total = part if total is None else total + part
    vs_ref[...] = total.astype(bf16)


def sort_tokens(sources, tiles, group, groups, into=None):
    width = sources[0][1].shape[1]
    tokens = sum(v.shape[0] for _, v in sources)
    slots = tiles * TILE
    steps = 2
    block = slots // steps
    flat = [x for pair in sources for x in pair]
    return pl.pallas_call(
        functools.partial(sort_kernel, len(sources)),
        out_shape=jax.ShapeDtypeStruct((groups * slots, width), bf16),
        grid=(steps,),
        in_specs=[*[full_spec(x.shape) for x in flat], *([] if into is None else [ANY])],
        out_specs=pl.BlockSpec((block, width), lambda i: (i + group * steps, 0)),
        input_output_aliases={} if into is None else {len(flat): 0},
        compiler_params=params(1),
        cost_estimate=cost(2 * slots * tokens * width, 1e7),
        name="sort_tokens",
    )(*flat, *([] if into is None else [into]))


def unsort_kernel(targets, *refs):
    vs = refs[targets][...]
    for k in range(targets):
        pos_row, out_ref = refs[k], refs[targets + 1 + k]
        slot = lax.broadcasted_iota(jnp.int32, (vs.shape[0], out_ref.shape[0]), 0)
        pick = (slot == pos_row[...]).astype(f32).astype(bf16)
        out_ref[...] = tn_dot(pick, vs).astype(bf16)


def unsort_tokens(places, vs, group, groups):
    width = vs.shape[1]
    slots = vs.shape[0] // groups
    tokens = sum(p.shape[1] for p in places)
    return pl.pallas_call(
        functools.partial(unsort_kernel, len(places)),
        out_shape=[jax.ShapeDtypeStruct((p.shape[1], width), bf16) for p in places],
        grid=(1,),
        in_specs=[
            *[full_spec(p.shape) for p in places],
            pl.BlockSpec((slots, width), lambda i: (group, 0)),
        ],
        out_specs=[full_spec((p.shape[1], width)) for p in places],
        compiler_params=params(1),
        cost_estimate=cost(2 * slots * tokens * width, 1e7),
        name="unsort_tokens",
    )(*places, vs)


def mid_kernel(x_ref, own_ref, got_ref, vec_ref, x2_ref, a2_ref):
    x2 = x_ref[...].astype(f32) + (own_ref[...].astype(f32) + got_ref[...].astype(f32)) + vec_ref[0:1]
    x2_ref[...] = x2
    xhat, _ = norm_parts(x2)
    a2_ref[...] = (xhat * vec_ref[1:2] + vec_ref[2:3]).astype(bf16)


def mid(x, own, got, vec):
    tokens, width = x.shape
    tile = pl.BlockSpec((TILE, width), lambda i: (i, 0))
    return pl.pallas_call(
        mid_kernel,
        out_shape=[
            jax.ShapeDtypeStruct((tokens, width), f32),
            jax.ShapeDtypeStruct((tokens, width), bf16),
        ],
        grid=(tokens // TILE,),
        in_specs=[tile, tile, tile, full_spec((3, width))],
        out_specs=[tile, tile],
        compiler_params=params(1),
        cost_estimate=cost(1e7, 5e6),
        name="mid_norm",
    )(x, own, got, vec)


def ffn_kernel(first, count, piece, groups, c_ref, te_ref, n_ref, *refs):
    xs_ref, dys_ref, ub_ref, *rest = refs
    if not first:
        zin_ref, din_ref, *rest = rest
    w_refs = [rest[2 * c : 2 * c + 2] for c in range(count)]
    rest = rest[2 * count :]
    z_ref, da_ref, *rest = rest
    g_refs = [rest[2 * c : 2 * c + 2] for c in range(count)]
    gub_ref, wu_s, wd_s, gu_s, gd_s, x_s, dy_s, z_s, da_s, sems, in_sems, out_sems = rest[2 * count :]
    experts = wu_s.shape[0]
    hc = wu_s.shape[2] // count
    tiles = x_s.shape[0]
    per = tiles // groups
    spots = [(ry, rz, rx) for ry in range(2) for rz in range(4) for rx in range(2)]

    def rows_of(ry, rz, rx):
        block = rz * 4 + (c_ref[1] ^ ry) * 2 + (c_ref[2] ^ rx)
        return pl.ds(pl.multiple_of(block * piece, 16), piece)

    def tile_of(ref, i):
        return ref.at[pl.ds(pl.multiple_of(i * TILE, TILE), TILE), :]

    def reads(i):
        pairs = [(xs_ref, x_s), (dys_ref, dy_s)]
        if not first:
            pairs += [(zin_ref, z_s), (din_ref, da_s)]
        return [
            pltpu.make_async_copy(tile_of(src, i), dst.at[i], in_sems.at[k, i])
            for k, (src, dst) in enumerate(pairs)
        ]

    def writes(i):
        return [
            pltpu.make_async_copy(src.at[i], tile_of(dst, i), out_sems.at[k, i])
            for k, (src, dst) in enumerate([(z_s, z_ref), (da_s, da_ref)])
        ]

    copies = []
    for c in range(count):
        for ry, rz, rx in spots:
            for k, w_s in ((0, wu_s), (1, wd_s)):
                copies.append(
                    pltpu.make_async_copy(
                        w_refs[c][ry].at[rz, rx, k],
                        w_s.at[:, rows_of(ry, rz, rx), pl.ds(c * hc, hc)],
                        sems.at[len(copies)],
                    )
                )
    for c in reads(0):
        c.start()
    for c in copies:
        c.start()

    @pl.loop(1, tiles)
    def _(i):
        for c in reads(i):
            c.start()

    gu_s[...] = jnp.zeros_like(gu_s)
    gd_s[...] = jnp.zeros_like(gd_s)
    gub_ref[...] = jnp.zeros_like(gub_ref)
    for c in copies:
        c.wait()

    @pl.loop(0, tiles)
    def _(i):
        group = i // per
        live = i - group * per < n_ref[group]
        for c in reads(i):
            c.wait()

        @pl.when(live)
        def _():
            e = te_ref[i]
            x = x_s[i]
            dy = dy_s[i]
            u = nn_dot(x, wu_s[e]) + ub_ref[e]
            act, slope = gelu_parts(u)
            act = act.astype(bf16)
            du = (nn_dot(dy, wd_s[e]) * slope).astype(bf16)
            z = nt_dot(act, wd_s[e])
            da = nt_dot(du, wu_s[e])
            if not first:
                z = z + z_s[i].astype(f32)
                da = da + da_s[i].astype(f32)
            z_s[i] = z.astype(bf16)
            da_s[i] = da.astype(bf16)
            gd_s[e] += tn_dot(dy, act)
            gu_s[e] += tn_dot(x, du)
            gub_ref[e] += jnp.sum(du.astype(f32), axis=0, keepdims=True)

        @pl.when(jnp.logical_not(live))
        def _():
            z_s[i] = jnp.zeros(z_s.shape[1:], bf16)
            da_s[i] = jnp.zeros(da_s.shape[1:], bf16)

        for c in writes(i):
            c.start()

    for c in range(count):
        lanes = pl.ds(c * hc, hc)
        for ry, rz, rx in spots:
            rows = rows_of(ry, rz, rx)
            for e in range(experts):
                g_refs[c][ry][rz, rx, 0, e] = gu_s[e, rows, lanes].astype(bf16)
                g_refs[c][ry][rz, rx, 1, e] = gd_s[e, rows, lanes].astype(bf16)

    @pl.loop(0, tiles)
    def _(i):
        for c in writes(i):
            c.wait()


def ffn(coords, tile_expert, used, xs, dys, up_b, weights, carry):
    slots, width = xs.shape
    tiles = slots // TILE
    groups = used.shape[0]
    first = not carry
    count = len(weights)
    gshape = weights[0][0].shape
    experts, piece, hc = gshape[3:]
    hid = hc * count
    out = pl.pallas_call(
        functools.partial(ffn_kernel, first, count, piece, groups),
        out_shape=[
            jax.ShapeDtypeStruct((slots, width), bf16),
            jax.ShapeDtypeStruct((slots, width), bf16),
            *[jax.ShapeDtypeStruct(gshape, bf16)] * (2 * count),
            jax.ShapeDtypeStruct((experts, 1, hid), f32),
        ],
        grid_spec=pltpu.PrefetchScalarGridSpec(
            num_scalar_prefetch=3,
            grid=(1,),
            in_specs=[
                ANY, ANY, full_spec((experts, 1, hid)), *([] if first else [ANY, ANY]),
                *[ANY] * (2 * count),
            ],
            out_specs=[ANY, ANY, *[full_spec(gshape)] * (2 * count), full_spec((experts, 1, hid))],
            scratch_shapes=[
                *[pltpu.VMEM((experts, width, hid), bf16)] * 2,
                *[pltpu.VMEM((experts, width, hid), f32)] * 2,
                *[pltpu.VMEM((tiles, TILE, width), bf16)] * 4,
                pltpu.SemaphoreType.DMA((32 * count,)),
                pltpu.SemaphoreType.DMA((2 if first else 4, tiles)),
                pltpu.SemaphoreType.DMA((2, tiles)),
            ],
        ),
        compiler_params=params(1),
        cost_estimate=cost(12 * slots * width * hid * 1.5, 4e7, 2 * slots * hid),
        name="ffn",
    )(coords, tile_expert, used, xs, dys, up_b, *carry, *[w for pair in weights for w in pair])
    zs, das, *rest = out
    return zs, das, [rest[2 * c : 2 * c + 2] for c in range(count)], rest[2 * count]


def norm_grad_kernel(count, low, *refs):
    parts, (v_ref, add_ref, gain_ref, out_ref, *refs) = refs[:count], refs[count:]
    sums_ref = refs[-1]

    @pl.when(pl.program_id(0) == 0)
    def _():
        sums_ref[...] = jnp.zeros_like(sums_ref)

    grad = sum(
        jnp.sum(p[...].astype(f32), axis=0) if len(p.shape) == 3 else p[...].astype(f32) for p in parts
    )
    xhat, rstd = norm_parts(v_ref[...].astype(f32))
    out = add_ref[...].astype(f32) + norm_back(grad, xhat, rstd, gain_ref[...])
    out_ref[...] = out
    if low:
        refs[0][...] = out.astype(bf16)
    sums_ref[0:1] += jnp.sum(grad * xhat, axis=0, keepdims=True)
    sums_ref[1:2] += jnp.sum(grad, axis=0, keepdims=True)
    sums_ref[2:3] += jnp.sum(out, axis=0, keepdims=True)


def norm_grad(partial, v, add, gain, low):
    tokens, width = v.shape
    tile = pl.BlockSpec((TILE, width), lambda i: (i, 0))
    return pl.pallas_call(
        functools.partial(norm_grad_kernel, len(partial), low),
        out_shape=[
            jax.ShapeDtypeStruct((tokens, width), f32),
            *([jax.ShapeDtypeStruct((tokens, width), bf16)] if low else []),
            jax.ShapeDtypeStruct((8, width), f32),
        ],
        grid=(tokens // TILE,),
        in_specs=[
            *[
                pl.BlockSpec((p.shape[0], TILE, width), lambda i: (0, i, 0)) if p.ndim == 3 else tile
                for p in partial
            ],
            tile, tile, full_spec((1, width)),
        ],
        out_specs=[tile, *([tile] if low else []), full_spec((8, width))],
        compiler_params=params(1),
        cost_estimate=cost(2e7, 8e6),
        name="norm_grad",
    )(*partial, v, add, gain)


def whole(kernel, name, outs, *args, prefetch=()):
    return pl.pallas_call(
        kernel,
        out_shape=[jax.ShapeDtypeStruct(s, d) for s, d in outs],
        grid_spec=pltpu.PrefetchScalarGridSpec(
            num_scalar_prefetch=len(prefetch),
            grid=(1,),
            in_specs=[full_spec(x.shape) for x in args],
            out_specs=[full_spec(s) for s, _ in outs],
        ),
        compiler_params=params(1),
        cost_estimate=cost(1e6, 4e6),
        name=name,
    )(*prefetch, *args)


def sums_y_kernel(c_ref, keep, got, own, send):
    for k in range(4):
        send[k] = (keep[k].astype(f32) + got[k].astype(f32)).astype(bf16)
    here = c_ref[0]
    own[...] = keep[here].astype(f32) + got[here].astype(f32)


def sums_z_kernel(c_ref, own, got, mine, near):
    others = [c_ref[0] ^ rz for rz in (1, 2, 3)]
    add = lambda k: own[k] + sum(got[z, k].astype(f32) for z in others)
    mine[...] = add(0)
    near[...] = add(1).astype(bf16)


def two_sums_kernel(a_keep, a_got, b_keep, b_got, a_own, a_send, b_own, b_send):
    for keep, got, own, send in ((a_keep, a_got, a_own, a_send), (b_keep, b_got, b_own, b_send)):
        own[...] = keep[0].astype(f32) + got[0].astype(f32)
        send[...] = (keep[1].astype(f32) + got[1].astype(f32)).astype(bf16)


def four_sums_kernel(c_ref, a_own, a_got, b_own, b_got, own, send):
    for rz in range(4):
        va = a_own[rz] + a_got[rz].astype(f32)
        vb = b_own[rz] + b_got[rz].astype(f32)
        if rz == 0:
            own[0], own[1] = va, vb
        send[c_ref[0] ^ rz, 0] = va.astype(bf16)
        send[c_ref[0] ^ rz, 1] = vb.astype(bf16)


def qkv_grad_kernel(c_ref, own, got, g_qkv, g_out):
    others = [c_ref[0] ^ rz for rz in (1, 2, 3)]
    add = lambda k, j: own[k, j] + sum(got[z, k, j].astype(f32) for z in others)
    g_qkv[0] = add(0, 0)
    g_qkv[1] = add(0, 1)
    g_qkv[2] = add(1, 0)
    g_out[...] = add(1, 1)


def rows_kernel(c_ref, *refs):
    n = len(refs) // 3
    for k in range(n):
        mine, other, out = refs[2 * k], refs[2 * k + 1], refs[2 * n + k]
        out[c_ref[3]] = mine[...]
        out[1 - c_ref[3]] = other[...]


def expert_grad_kernel(c_ref, *refs):
    *mines, near, g_up, g_down = refs
    hc = mines[0].shape[-1]
    half = hc * len(mines)
    here = pl.multiple_of(c_ref[2] * half, 128)
    there = pl.multiple_of((1 - c_ref[2]) * half, 128)
    for k, out in ((0, g_up), (1, g_down)):
        for c, mine in enumerate(mines):
            out[:, :, pl.ds(here + c * hc, hc)] = mine[k]
        out[:, :, pl.ds(there, half)] = near[k].astype(f32)


def flip(x, mask, size):
    return lax.ppermute(x, "dp", [(i, i ^ mask) for i in range(size)])


def after(v, *deps):
    return lax.optimization_barrier((v, deps))[0]


def deal(v):
    return lax.all_to_all(v, "mp", 0, 0)


def swap(v):
    return lax.ppermute(v, "mp", [(0, 1), (1, 0)])


def share(v):
    return deal(jnp.broadcast_to(v, (lax.axis_size("mp"),) + v.shape))


def gather_z(a, b, size):
    both = jnp.stack([a, b])
    blocks = [both] + [flip(both, 4 * rz, size) for rz in (1, 2, 3)]
    return jnp.stack([v[0] for v in blocks]), jnp.stack([v[1] for v in blocks])


def gather_xy(a0, b0, size):
    a0 = jnp.stack([a0, flip(a0, 1, size)])
    b0 = jnp.stack([b0, flip(b0, 2, size)])
    return (a0, flip(a0, 2, size)), (b0, flip(b0, 1, size))


def attn_sums_1(keep, got, dep):
    shape = keep[0].shape[1:]
    return whole(
        two_sums_kernel, "two_sums", [(shape, f32), (shape, bf16)] * 2,
        after(keep[0], dep), got[0], keep[1], got[1],
    )


def attn_sums_2(coords, own, got, dep):
    shape = (2,) + own[0].shape[1:]
    return whole(
        four_sums_kernel, "four_sums", [(shape, f32), ((4,) + shape, bf16)],
        own[0], got[0], own[1], got[1], prefetch=(after(coords, dep),),
    )


def gather_plain(w):
    full = lax.all_gather(w, "dp", axis=1, tiled=True)
    n, rows, cols = full.shape
    return full.reshape(n, 16, rows // 16, cols).swapaxes(0, 1)


def gather_pieces_plain(a, b):
    blocks = [gather_plain(v) for v in (a, b)]
    blocks = [v.reshape((4, 2, 2) + v.shape[1:]) for v in blocks]
    fa = jnp.moveaxis(blocks[0], 0, 2)
    fb = jnp.swapaxes(jnp.moveaxis(blocks[1], 0, 2), 0, 1)
    return (fa[0], fa[1]), (fb[0], fb[1])


def scatter_plain(ga, gb):
    fa = jnp.moveaxis(jnp.stack(ga), 2, 0)
    fb = jnp.moveaxis(jnp.swapaxes(jnp.stack(gb), 0, 1), 2, 0)
    outs = []
    for v in (fa, fb):
        v = v.reshape((16,) + v.shape[3:]).swapaxes(0, 1)
        v = v.reshape(v.shape[0], -1, v.shape[-1]).astype(f32)
        outs.append(lax.psum_scatter(v, "dp", scatter_dimension=1, tiled=True))
    return outs


def phase(pred, f):
    shapes = jax.eval_shape(f)
    return lax.cond(
        pred, f, lambda: jax.tree.map(lambda v: jnp.zeros(v.shape, v.dtype), shapes)
    )


def deal_z(v):
    groups = [[4 * z + k for z in range(4)] for k in range(4)]
    return lax.all_to_all(v, "dp", 0, 0, axis_index_groups=groups, tiled=True)


def along_z(p):
    return deal_z(jnp.broadcast_to(p, (4,) + p.shape))


def sums_y(coords, pair, size):
    shape = pair[0].shape
    return whole(
        sums_y_kernel, "sums_y", [(shape[1:], f32), (shape, bf16)],
        pair[0], flip(pair[1], 2, size), prefetch=(coords,),
    )


def sums_z(coords, parts_y):
    own, send = parts_y
    shape = own.shape[1:]
    return whole(
        sums_z_kernel, "sums_z", [(shape, f32), (shape, bf16)], own, deal_z(send),
        prefetch=(coords,),
    )


def expert_pieces_plain(w_up, w_down):
    hc = w_up.shape[-1] // CHUNKS
    blocks = jnp.stack([gather_plain(w_up), gather_plain(w_down)], axis=1)
    blocks = blocks.reshape((4, 2, 2) + blocks.shape[1:])
    return [
        tuple(blocks[:, ry, ..., c * hc : (c + 1) * hc] for ry in range(2)) for c in range(CHUNKS)
    ]


def expert_sums_plain(pair):
    v = jnp.stack(pair, axis=1)
    v = v.reshape((16,) + v.shape[3:])
    v = jnp.moveaxis(v, 0, 2)
    v = v.reshape(v.shape[:2] + (-1, v.shape[-1])).astype(f32)
    return lax.psum_scatter(v, "dp", scatter_dimension=2, tiled=True)


def token_plan(segments, modality, experts):
    tokens = segments.size
    doc_ids = jnp.arange(modality.shape[1], dtype=jnp.int32)
    match = segments[:, :, None] == doc_ids
    mods = jnp.sum(jnp.where(match, modality[:, None, :], 0), axis=-1).reshape(tokens)
    kinds = jnp.arange(experts, dtype=jnp.int32)
    hot = (mods[:, None] == kinds).astype(jnp.int32)
    ids = jnp.arange(tokens, dtype=jnp.int32)
    lower = (ids[:, None] > ids[None, :]).astype(bf16)
    before = jnp.dot(lower, hot.astype(bf16), preferred_element_type=f32).astype(jnp.int32)
    need = (jnp.sum(hot, axis=0) + TILE - 1) // TILE
    ends = jnp.sum(jnp.where(kinds[:, None] >= kinds[None, :], need[None, :], 0), axis=1)
    pos = jnp.sum(hot * (before + (ends - need)[None, :] * TILE), axis=1)
    tiles = (tokens + experts * (TILE - 1)) // TILE
    tile_ids = jnp.arange(tiles, dtype=jnp.int32)
    tile_expert = jnp.minimum(
        jnp.sum((tile_ids[:, None] >= ends[None, :]).astype(jnp.int32), axis=1), experts - 1
    )
    return mods, pos, tile_expert, ends[-1:]


def body(
    layer_input, segments, modality, ln_gain, ln_bias, w_qkv, qv_bias, w_out, out_bias,
    w_up, up_bias, w_down, down_bias, cotangent,
):
    part = lax.axis_index("mp")
    parts = lax.axis_size("mp")
    size = lax.axis_size("dp")
    me = lax.axis_index("dp")
    rows, seq, width = layer_input.shape
    tokens = rows * seq
    cols = w_qkv.shape[-1]
    hid = w_up.shape[-1]
    experts = w_up.shape[0]
    shape3 = (rows, seq, width)
    tiles = (tokens + experts * (TILE - 1)) // TILE
    staged = size == 16

    mine_rows = rows // parts
    mine_tokens = tokens // parts
    by_core = (parts, mine_tokens, width)
    dy = cotangent.reshape(tokens, width)
    rows_here = lambda v: lax.dynamic_slice_in_dim(v, part * mine_rows, mine_rows, 0)
    col_start = part * cols
    seg_row = segments.reshape(rows, 1, seq)

    def small_inputs():
        q_b = lax.dynamic_slice_in_dim(qv_bias[0], col_start, cols)
        v_b = lax.dynamic_slice_in_dim(qv_bias[1], col_start, cols)
        return (
            rows_here(layer_input).reshape(mine_tokens, width),
            rows_here(cotangent).reshape(mine_tokens, width),
            jnp.concatenate([q_b, jnp.zeros_like(q_b), v_b]).reshape(1, 3 * cols),
            segments.reshape(rows, seq, 1),
            jnp.concatenate([out_bias[None], ln_gain[1:2], ln_bias[1:2]]),
            jnp.concatenate([ln_gain[0:1], ln_bias[0:1]]),
        )

    def fwd(coords, pa, pb):
        own, other, *saved = attn_fwd(coords, layer_input, seg_row, seg_col, ln1, proj_bias, pa, pb)
        return (saved, *mid(x_mine, own, swap(other), vec))

    def bwd(coords, dxr, dx2, saved, pa, pb):
        own, other, *rest = attn_bwd(
            coords, *dxr, layer_input, seg_row, seg_col, ln1, saved, pa, pb
        )
        return (*norm_grad((own, swap(other)), x_mine, dx2, ln_gain[0:1], False), *rest)

    def halves(v):
        take = lambda k: lax.dynamic_slice_in_dim(v, k * mine_tokens, mine_tokens, 0)
        return take(part).reshape(1, mine_tokens), take(1 - part).reshape(1, mine_tokens)

    def finish(x2, z_sum, mods):
        kinds = lax.dynamic_slice_in_dim(mods, part * mine_tokens, mine_tokens, 0)[:, None]
        bias_of = jnp.zeros((mine_tokens, width), f32)
        for e in range(experts):
            bias_of = jnp.where(kinds == e, down_bias[e][None], bias_of)
        return (x2 + (z_sum + bias_of)).astype(bf16)

    def small_rows(sums1, sums2, bsum, g_upb, g_down_bias):
        sides = bsum.reshape(3, cols)
        g_qv = lax.dynamic_update_slice(
            jnp.zeros((2, width), f32), jnp.stack([sides[0], sides[2]]), (jnp.int32(0), col_start)
        )
        g_upb_full = lax.dynamic_update_slice(
            jnp.zeros((experts, up_bias.shape[1]), f32), g_upb, (jnp.int32(0), hid_start)
        )
        return jnp.concatenate(
            [sums1[0:2], sums2[0:3], g_down_bias / parts, g_qv, g_upb_full.reshape(-1, width)]
        )

    if staged:
        x_bit = me % 2
        coords = jnp.stack([me // 4, (me // 2) % 2, x_bit, part]).astype(jnp.int32)
        pred = me < size
        inner = part < parts
        half = hid // 2
        hid_start = part * hid + x_bit * half
        hc = half // CHUNKS
        up_b = lax.dynamic_slice_in_dim(up_bias, hid_start, half, 1)

        def call_experts(k, xs, dys, weights, carry):
            call = CALLS[k]
            ub = up_b[:, None, call[0] * hc : (call[-1] + 1) * hc]
            return ffn(
                coords, tile_expert, used, xs, dys, ub, [weights[c] for c in call], carry
            )

        def begin():
            w = jnp.stack([w_up, w_down])
            keep = lax.dynamic_slice_in_dim(w, x_bit * half, half, 3)
            near = flip(lax.dynamic_slice_in_dim(w, (1 - x_bit) * half, half, 3), 1, size)
            pieces = [
                jnp.stack([keep[..., c * hc : (c + 1) * hc], near[..., c * hc : (c + 1) * hc]])
                for c in range(CHUNKS)
            ]
            ab = gather_z(w_qkv[:2], jnp.stack([w_qkv[2], w_out]), size)
            mods, pos, tile_expert, used = token_plan(segments, modality, experts)
            plan = flip(jnp.concatenate([pos, tile_expert, used]), 1, size)
            return pieces, ab, mods, pos, plan, tile_expert, used, small_inputs()

        pieces, ab, mods, pos, plan, tile_expert, used, smalls = phase(pred, begin)
        x_mine, dy_mine, proj_bias, seg_col, vec, ln1 = smalls

        def weights_in():
            def inside():
                pos_row = pos.reshape(1, tokens)
                dys = sort_tokens([(pos_row, dy)], tiles, 0, 2)
                hot = (mods[:, None] == jnp.arange(experts, dtype=jnp.int32)).astype(bf16)
                return (
                    *gather_xy(*ab, size), halves(pos), halves(plan),
                    jnp.concatenate([tile_expert, plan[tokens : tokens + tiles]]),
                    jnp.concatenate([used, plan[tokens + tiles :]]), dys, tn_dot(hot, dy),
                )

            return along_z(pieces[0]), phase(inner, inside)

        z0, (pa, pb, pos_here, pos_near, tile_expert, used, dys, g_down_bias) = phase(
            pred, weights_in
        )

        def forward():
            return (
                *phase(inner, lambda: fwd(coords, pa, pb)), flip(z0, 2, size),
                along_z(pieces[1]), flip(dy_mine, 1, size),
            )

        saved, x2, a2, y0, z1, dy_near = phase(pred, forward)

        def sort(places, v, v2, group, into):
            return sort_tokens(list(zip(places, (v, v2))), tiles, group, 2, into)

        def exchange():
            near = flip(a2, 1, size)
            d, xs = phase(
                inner,
                lambda: (
                    sort(pos_near, dy_near, swap(dy_near), 1, dys),
                    sort(pos_here, a2, swap(a2), 0, None),
                ),
            )
            near = after(near, d, xs)
            xs = phase(inner, lambda: sort(pos_near, near, swap(near), 1, xs))
            return xs, d, flip(z1, 2, size), along_z(pieces[2])

        xs, dys, y1, z2 = phase(pred, exchange)
        weights = [(z0, y0), (z1, y1)]
        (zs0, das0, grads, gub0), y2 = phase(
            pred, lambda: (call_experts(0, xs, dys, weights, ()), flip(z2, 2, size))
        )
        weights.append((z2, y2))

        def both_cores(places, vs, group):
            mine, other = unsort_tokens(places, vs, group, 2)
            return (mine.astype(f32) + swap(other).astype(f32)).astype(bf16)

        def second():
            def inside():
                zs, das, more, gub = call_experts(1, xs, dys, weights, (zs0, das0))
                return zs, das, more, gub, both_cores(pos_near, das, 1)

            return phase(inner, inside), sums_y(coords, grads[0], size)

        (zs, das, more, gub1, da_near), v0 = phase(pred, second)
        grads = grads + more
        g_upb = jnp.concatenate([gub0, gub1], axis=-1)[:, 0]

        def back():
            def inside():
                mine, other = unsort_tokens(pos_here, das, 0, 2)
                return mine, swap(other), both_cores(pos_near, zs, 1)

            near = flip(da_near, 1, size)
            mine, other, z_near = phase(inner, inside)
            g0 = sums_z(coords, v0)
            v1 = sums_y(coords, grads[1], size)

            def to_x2():
                dx2, dxr, sums2 = norm_grad((mine, other, near), x2, dy_mine, ln_gain[1:2], True)
                return dx2, (dxr, swap(dxr)), sums2

            return *phase(inner, to_x2), z_near, g0, v1

        dx2, dxr, sums2, z_near, g0, v1 = phase(pred, back)

        def last():
            return (
                phase(inner, lambda: bwd(coords, dxr, dx2, saved, pa, pb)), flip(z_near, 1, size),
                sums_z(coords, v1), sums_y(coords, grads[2], size),
            )

        (grad, sums1, ga0, ga1, gb0, gb1, bsum), z_near, g1, v2 = phase(pred, last)
        def sum_up():
            def out_rows():
                mine, other = unsort_tokens(pos_here, zs, 0, 2)
                z_sum = mine.astype(f32) + swap(other).astype(f32) + z_near.astype(f32)
                out = finish(x2, z_sum, mods)
                return out, swap(out), swap(grad)

            def small_start():
                total = small_rows(sums1, sums2, bsum, g_upb, g_down_bias)
                total = total + swap(total)
                return total + flip(total, 1, size)

            g2 = sums_z(coords, v2)
            got_a, got_b = flip(ga1, 2, size), flip(gb1, 1, size)
            outs = phase(inner, out_rows)
            a_own, a_send, b_own, b_send = attn_sums_1((ga0, gb0), (got_a, got_b), outs)
            got_a, got_b = flip(a_send, 1, size), flip(b_send, 2, size)
            small = phase(inner, small_start)
            return attn_sums_2(coords, (a_own, b_own), (got_a, got_b), small), g2, small, outs

        (own, send), g2, small, (out, out_other, grad_other) = phase(pred, sum_up)

        def inside():
            total = small
            for mask in (2, 4, 8):
                total = total + flip(total, mask, size)
            return total

        got = deal_z(send)
        near = flip(jnp.concatenate([v[1] for v in (g0, g1, g2)], axis=-1), 1, size)
        small = phase(inner, inside)
        layer_output, grad_input = whole(
            rows_kernel, "rows", [((parts,) + v.shape, v.dtype) for v in (out, grad)],
            out, out_other, grad, grad_other, prefetch=(coords,),
        )
        g_up, g_down = whole(
            expert_grad_kernel, "expert_grad", [(w_up.shape, f32)] * 2,
            g0[0], g1[0], g2[0], near, prefetch=(coords,),
        )
        g_qkv, g_out = whole(
            qkv_grad_kernel, "qkv_grad", [(w_qkv.shape, f32), (w_out.shape, f32)], own, got,
            prefetch=(coords,),
        )
    else:
        coords = jnp.stack([0, 0, 0, part]).astype(jnp.int32)
        x_mine, dy_mine, proj_bias, seg_col, vec, ln1 = small_inputs()
        hid_start = part * hid
        hc = hid // CHUNKS
        up_b = lax.dynamic_slice_in_dim(up_bias, hid_start, hid, 1)
        pa, pb = gather_pieces_plain(w_qkv[:2], jnp.stack([w_qkv[2], w_out]))
        weights = expert_pieces_plain(w_up, w_down)
        mods, pos, tile_expert, used = token_plan(segments, modality, experts)
        pos_row = pos.reshape(1, tokens)
        hot = (mods[:, None] == jnp.arange(experts, dtype=jnp.int32)).astype(bf16)
        g_down_bias = tn_dot(hot, dy)
        dys = sort_tokens([(pos_row, dy)], tiles, 0, 1)
        saved, x2, a2 = fwd(coords, pa, pb)
        xs = sort_tokens([(pos_row, share(a2).reshape(tokens, width))], tiles, 0, 1)
        carry = ()
        grads = []
        g_upb = []
        for call in CALLS:
            ub = up_b[:, None, call[0] * hc : (call[-1] + 1) * hc]
            zs, das, pairs, gub = ffn(
                coords, tile_expert, used, xs, dys, ub, [weights[c] for c in call], carry
            )
            carry = (zs, das)
            g_upb.append(gub[:, 0])
            grads += pairs
        g_upb = jnp.concatenate(g_upb, axis=-1)
        g_up, g_down = jnp.concatenate([expert_sums_plain(pair) for pair in grads], axis=-1)
        own = deal(unsort_tokens([pos_row], das, 0, 1)[0].reshape(by_core))
        dx2, dxr, sums2 = norm_grad((own[0], own[1]), x2, dy_mine, ln_gain[1:2], True)
        grad_mine, sums1, ga0, ga1, gb0, gb1, bsum = bwd(
            coords, (dxr, swap(dxr)), dx2, saved, pa, pb
        )
        g_qk, g_vo = scatter_plain((ga0, ga1), (gb0, gb1))
        g_qkv, g_out = jnp.concatenate([g_qk, g_vo[:1]]), g_vo[1]
        own = deal(unsort_tokens([pos_row], zs, 0, 1)[0].reshape(by_core))
        layer_output = share(finish(x2, jnp.sum(own.astype(f32), axis=0), mods))
        grad_input = share(grad_mine)
        small = lax.psum(small_rows(sums1, sums2, bsum, g_upb, g_down_bias), ("dp", "mp"))

    g_gain = jnp.stack([small[0], small[2]])
    g_lnb = jnp.stack([small[1], small[3]])
    return (
        layer_output.reshape(shape3),
        grad_input.reshape(shape3),
        g_gain,
        g_lnb,
        g_qkv,
        small[5 + experts : 7 + experts],
        g_out,
        small[4],
        g_up,
        small[7 + experts :].reshape(experts, up_bias.shape[1]),
        g_down,
        small[5 : 5 + experts],
    )


def solution(mesh):
    tok = P("dp", None, None)
    rep = P()
    wide = P(None, "dp", "mp")
    in_specs = (
        tok, P("dp", None), P("dp", None), rep, rep, wide, rep, P("dp", "mp"), rep, wide, rep,
        wide, rep, tok,
    )
    out_specs = (
        tok, tok, rep, rep, wide, rep, P("dp", "mp"), rep, wide, rep, wide, rep,
    )
    return jax.shard_map(body, mesh=mesh, in_specs=in_specs, out_specs=out_specs, check_vma=False)
```

```python
import functools
import math

import jax
import jax.numpy as jnp
from jax import lax
from jax.experimental import pallas as pl
from jax.experimental.pallas import tpu as pltpu
from jax.sharding import PartitionSpec as P

HD = 64
EPS = 1e-05
TILE = 256
CHUNKS = 3
SCALE = 1.0
CALLS = ((0, 1), (2,))
VMEM = 58 * 1024 * 1024
LOG2E = math.log2(math.e)
f32 = jnp.float32
bf16 = jnp.bfloat16
ANY = pl.BlockSpec(memory_space=pl.ANY)


def full_spec(shape):
    zeros = (0,) * len(shape)
    return pl.BlockSpec(shape, lambda *_: zeros)


def nt_dot(a, b):
    return lax.dot_general(a, b, (((1,), (1,)), ((), ())), preferred_element_type=f32)


def nn_dot(a, b):
    return lax.dot_general(a, b, (((1,), (0,)), ((), ())), preferred_element_type=f32)


def tn_dot(a, b):
    return lax.dot_general(a, b, (((0,), (0,)), ((), ())), preferred_element_type=f32)


def params(grid_rank):
    return pltpu.CompilerParams(
        dimension_semantics=("arbitrary",) * grid_rank, vmem_limit_bytes=VMEM
    )


def cost(flops, nbytes, trans=0):
    return pl.CostEstimate(
        flops=int(flops * SCALE), bytes_accessed=int(nbytes * SCALE), transcendentals=int(trans * SCALE)
    )


def place(c_ref, kind, outer, inner, rz):
    ry, rx = (outer, inner) if kind == "a" else (inner, outer)
    return (c_ref[0] ^ rz) * 4 + (c_ref[1] ^ ry) * 2 + (c_ref[2] ^ rx)


def piece_copies(c_ref, jobs, sems):
    copies = []
    for kind, pair, view, target in jobs:
        for outer in range(2):
            for inner in range(2):
                for rz in range(4):
                    rows = place(c_ref, kind, outer, inner, rz)
                    copies.append(
                        pltpu.make_async_copy(
                            view(pair[outer], inner, rz), target(rows), sems.at[len(copies)]
                        )
                    )
    return copies


def gelu_parts(u):
    mag = jnp.abs(u)
    t = 1.0 / (1.0 + (0.3275911 * math.sqrt(0.5)) * mag)
    poly = t * (
        0.254829592
        + t * (-0.284496736 + t * (1.421413741 + t * (-1.453152027 + t * 1.061405429)))
    )
    gauss = jnp.exp(-0.5 * u * u)
    half = 0.5 * poly * gauss
    cdf = jnp.where(u >= 0, 1.0 - half, half)
    return u * cdf, cdf + u * gauss * (1.0 / math.sqrt(2.0 * math.pi))


def norm_parts(v):
    mean = jnp.mean(v, axis=-1, keepdims=True)
    cent = v - mean
    var = jnp.mean(cent * cent, axis=-1, keepdims=True)
    rstd = lax.rsqrt(var + EPS)
    return cent * rstd, rstd


def norm_back(d_out, xhat, rstd, gain):
    d_hat = d_out * gain
    m1 = jnp.mean(d_hat, axis=-1, keepdims=True)
    m2 = jnp.mean(d_hat * xhat, axis=-1, keepdims=True)
    return rstd * (d_hat - m1 - xhat * m2)


def two_heads(v):
    lane = lax.broadcasted_iota(jnp.int32, v.shape, 1)
    none = jnp.zeros_like(v)
    return jnp.concatenate([jnp.where(lane < HD, v, none), jnp.where(lane >= HD, v, none)], axis=0)


def fill_bias(srow_ref, bias_s):
    seq = bias_s.shape[0]
    column = jnp.broadcast_to(srow_ref[0], (128, seq)).T
    for k in range(0, seq, 128):
        bias_s[:, k : k + 128] = jnp.where(column == srow_ref[0, :, k : k + 128], 0.0, -1e30)


def each_window(win_ref, row, blocks, f):
    @pl.loop(0, blocks)
    def _(j):
        first = win_ref[(row * blocks + j) * 2]
        n = win_ref[(row * blocks + j) * 2 + 1]
        for size in range(1, blocks + 1):

            @pl.when(n == size)
            def _():
                f(j, first, size)


def key_windows(segments):
    first, last = segments[:, ::128], segments[:, 127::128]
    low = jnp.sum((last[:, None, :] < first[:, :, None]).astype(jnp.int32), axis=-1)
    high = jnp.sum((first[:, None, :] <= last[:, :, None]).astype(jnp.int32), axis=-1)
    return jnp.stack([low, high - low], axis=-1).reshape(-1)


def attn_fwd_kernel(
    heads, piece, c_ref, win_ref, x_ref, srow_ref, ln_ref, pb_ref, a0, a1_, b0, b1_,
    att_ref, att_other_ref, qkv_ref, kt_ref, o_ref, ot_ref, lse_ref,
    w_s, wo_s, bias_s, vt_s, a1_s, sems,
):
    cols = heads * HD
    pairs = cols // 128
    seq, width = x_ref.shape[1], x_ref.shape[2]

    def into(block, j):
        return w_s.at[pl.ds(pl.multiple_of(block * piece, 16), piece), pl.ds(j * cols, cols)]

    def into_out(block):
        return wo_s.at[pl.ds(pl.multiple_of(block * piece, 16), piece), :]

    jobs = [
        ("a", (a0, a1_), lambda r, i, z: r.at[i, z, 0], lambda k: into(k, 0)),
        ("a", (a0, a1_), lambda r, i, z: r.at[i, z, 1], lambda k: into(k, 1)),
        ("b", (b0, b1_), lambda r, i, z: r.at[i, z, 0], lambda k: into(k, 2)),
        ("b", (b0, b1_), lambda r, i, z: r.at[i, z, 1], into_out),
    ]
    copies = piece_copies(c_ref, jobs, sems)

    @pl.when(pl.program_id(0) == 0)
    def _():
        for c in copies:
            c.start()

    xhat, _ = norm_parts(x_ref[0].astype(f32))
    a1_s[...] = (xhat * ln_ref[0:1] + ln_ref[1:2]).astype(bf16)
    fill_bias(srow_ref, bias_s)

    @pl.when(pl.program_id(0) == 0)
    def _():
        for c in copies:
            c.wait()

    a1 = a1_s[...]
    proj = (nn_dot(a1, w_s[...]) + pb_ref[...]).astype(bf16)
    for j in range(3):
        for p in range(pairs):
            qkv_ref[0, j, p] = proj[:, j * cols + p * 128 : j * cols + (p + 1) * 128]
    for p in range(pairs):
        kt_ref[0, p] = proj[:, cols + p * 128 : cols + (p + 1) * 128].T
        vt_s[p] = proj[:, 2 * cols + p * 128 : 2 * cols + (p + 1) * 128].T
    scale2 = HD ** (-0.5) * LOG2E

    def block(j, start, n):
        keys = pl.ds(pl.multiple_of(start * 128, 128), n * 128)
        mine = pl.ds(pl.multiple_of(j * 128, 128), 128)
        bias = bias_s[keys, mine]
        bias = jnp.concatenate([bias, bias], axis=1)
        every = range(pairs)
        s_t = [
            nt_dot(qkv_ref[0, 1, p, keys, :], two_heads(qkv_ref[0, 0, p, mine, :])) + bias
            for p in every
        ]
        top = [jnp.max(v, axis=0, keepdims=True) for v in s_t]
        e_t = [jnp.exp2((v - m) * scale2) for v, m in zip(s_t, top)]
        total = [jnp.sum(v, axis=0, keepdims=True) for v in e_t]
        p_t = [(v * (1.0 / t)).astype(bf16) for v, t in zip(e_t, total)]
        o_t = [nn_dot(vt_s[p, :, keys], p_t[p]).astype(bf16) for p in every]
        for p in every:
            ot_ref[0, p, :HD, mine] = o_t[p][:HD, :128]
            ot_ref[0, p, HD:, mine] = o_t[p][HD:, 128:]
            lse = top[p] * scale2 + jnp.log2(total[p])
            lse_ref[0, p, 0:1, mine] = lse[:, :128]
            lse_ref[0, p, 1:2, mine] = lse[:, 128:]

    each_window(win_ref, pl.program_id(0), seq // 128, block)

    for p in range(pairs):
        o_ref[0, :, p * 128 : (p + 1) * 128] = ot_ref[0, p].T
    att = nt_dot(o_ref[0], wo_s[...]).astype(bf16)

    @pl.when(pl.program_id(0) == c_ref[3])
    def _():
        att_ref[...] = att

    @pl.when(pl.program_id(0) != c_ref[3])
    def _():
        att_other_ref[...] = att


def attn_fwd(coords, windows, x, seg_row, ln, proj_bias, pa, pb):
    rows, seq, width = x.shape
    cols = proj_bias.shape[-1] // 3
    heads = cols // HD
    pairs = cols // 128
    piece = pa[0].shape[-2]
    row3 = lambda r, *_: (r, 0, 0)
    row4 = lambda r, *_: (r, 0, 0, 0)
    row5 = lambda r, *_: (r, 0, 0, 0, 0)
    outs = [
        ((seq, width), bf16, (seq, width), lambda *_: (0, 0)),
        ((seq, width), bf16, (seq, width), lambda *_: (0, 0)),
        ((rows, 3, pairs, seq, 128), bf16, (1, 3, pairs, seq, 128), row5),
        ((rows, pairs, 128, seq), bf16, (1, pairs, 128, seq), row4),
        ((rows, seq, cols), bf16, (1, seq, cols), row3),
        ((rows, pairs, 128, seq), bf16, (1, pairs, 128, seq), row4),
        ((rows, pairs, 2, seq), f32, (1, pairs, 2, seq), row4),
    ]
    return pl.pallas_call(
        functools.partial(attn_fwd_kernel, heads, piece),
        out_shape=[jax.ShapeDtypeStruct(s, d) for s, d, _, _ in outs],
        grid_spec=pltpu.PrefetchScalarGridSpec(
            num_scalar_prefetch=2,
            grid=(rows,),
            in_specs=[
                pl.BlockSpec((1, seq, width), row3),
                pl.BlockSpec((1, 1, seq), row3),
                full_spec((2, width)),
                full_spec((1, 3 * cols)),
                ANY, ANY, ANY, ANY,
            ],
            out_specs=[pl.BlockSpec(b, m) for _, _, b, m in outs],
            scratch_shapes=[
                pltpu.VMEM((width, 3 * cols), bf16),
                pltpu.VMEM((width, cols), bf16),
                pltpu.VMEM((seq, seq), f32),
                pltpu.VMEM((pairs, 128, seq), bf16),
                pltpu.VMEM((seq, width), bf16),
                pltpu.SemaphoreType.DMA((64,)),
            ],
        ),
        compiler_params=params(1),
        cost_estimate=cost(2e10, 1e7, 3e6),
        name="attn_fwd",
    )(coords, windows, x, seg_row, ln, proj_bias, *pa, *pb)


def attn_bwd_kernel(
    heads, piece, c_ref, win_ref, dxr_ref, dxr2_ref, x_ref, srow_ref, ln_ref, qkv_ref, kt_ref, o_ref, ot_ref, lse_ref, a0, a1_, b0, b1_,
    da1_ref, da1_other_ref, ga0_ref, ga1_ref, gb0_ref, gb1_ref, bsum_ref,
    w_s, wo_s, bias_s, dp_s, gw_s, go_s, do_s, row_s, dk_s, dv_s, dqt_s, a1t_s, sems,
):
    cols = heads * HD
    pairs = cols // 128
    seq = x_ref.shape[1]
    step = pl.program_id(0)

    def into(block, j):
        return w_s.at[pl.ds(pl.multiple_of(block * piece, 16), piece), pl.ds(j * cols, cols)]

    def into_out(block):
        return wo_s.at[pl.ds(pl.multiple_of(block * piece, 16), piece), :]

    jobs = [
        ("a", (a0, a1_), lambda r, i, z: r.at[i, z, 0], lambda k: into(k, 0)),
        ("a", (a0, a1_), lambda r, i, z: r.at[i, z, 1], lambda k: into(k, 1)),
        ("b", (b0, b1_), lambda r, i, z: r.at[i, z, 0], lambda k: into(k, 2)),
        ("b", (b0, b1_), lambda r, i, z: r.at[i, z, 1], into_out),
    ]
    copies = piece_copies(c_ref, jobs, sems)

    @pl.when(step == 0)
    def _():
        for c in copies:
            c.start()
        gw_s[...] = jnp.zeros_like(gw_s)
        go_s[...] = jnp.zeros_like(go_s)
        bsum_ref[...] = jnp.zeros_like(bsum_ref)

    xhat1, _ = norm_parts(x_ref[0].astype(f32))
    a1t_s[...] = (xhat1 * ln_ref[0:1] + ln_ref[1:2]).astype(bf16).T
    fill_bias(srow_ref, bias_s)

    @pl.when(step == 0)
    def _():
        for c in copies:
            c.wait()

    dxr = jnp.where(step == c_ref[3], dxr_ref[...], dxr2_ref[...])
    do = nn_dot(dxr, wo_s[...]).astype(bf16)
    go_s[...] += nn_dot(dxr.T, o_ref[0])
    scale = HD ** (-0.5)
    scale2 = scale * LOG2E
    do_s[...] = do
    for p in range(pairs):
        prod = do[:, p * 128 : (p + 1) * 128].T.astype(f32) * ot_ref[0, p].astype(f32)
        for h in range(2):
            row_s[p, h : h + 1] = jnp.sum(prod[h * HD : (h + 1) * HD], axis=0, keepdims=True)
    dk_s[...] = jnp.zeros_like(dk_s)
    dv_s[...] = jnp.zeros_like(dv_s)

    def block(j, start, n):
        keys = pl.ds(pl.multiple_of(start * 128, 128), n * 128)
        mine = pl.ds(pl.multiple_of(j * 128, 128), 128)
        pair = lambda ref: jnp.concatenate([ref[0:1, mine], ref[1:2, mine]], axis=1)
        every = range(pairs)
        bias = bias_s[keys, mine]
        bias = jnp.concatenate([bias, bias], axis=1)
        q_2 = [two_heads(qkv_ref[0, 0, p, mine, :]) for p in every]
        do_2 = [two_heads(do_s[mine, p * 128 : (p + 1) * 128]) for p in every]
        s_t = [nt_dot(qkv_ref[0, 1, p, keys, :], q_2[p]) * scale2 for p in every]
        d_t = [nt_dot(qkv_ref[0, 2, p, keys, :], do_2[p]) - pair(row_s.at[p]) for p in every]
        p_t = [jnp.exp2(s_t[p] + (bias - pair(lse_ref.at[0, p]))) for p in every]
        for p in every:
            dv_s[p, keys, :] += nn_dot(p_t[p].astype(bf16), do_2[p])
        ds_t = [(p_t[p] * d_t[p]).astype(bf16) for p in every]
        for p in every:
            dk_s[p, keys, :] += nn_dot(ds_t[p], q_2[p])
            dq_t = (nn_dot(kt_ref[0, p, :, keys], ds_t[p]) * scale).astype(bf16)
            dqt_s[p, :HD, mine] = dq_t[:HD, :128]
            dqt_s[p, HD:, mine] = dq_t[HD:, 128:]

    each_window(win_ref, step, seq // 128, block)

    for p in range(pairs):
        dp_s[:, p * 128 : (p + 1) * 128] = dqt_s[p].T
        dp_s[:, cols + p * 128 : cols + (p + 1) * 128] = (dk_s[p] * scale).astype(bf16)
        dp_s[:, 2 * cols + p * 128 : 2 * cols + (p + 1) * 128] = dv_s[p].astype(bf16)

    dproj = dp_s[...]
    da1 = nt_dot(dproj, w_s[...]).astype(bf16)

    @pl.when(step == c_ref[3])
    def _():
        da1_ref[...] = da1

    @pl.when(step != c_ref[3])
    def _():
        da1_other_ref[...] = da1

    bsum_ref[...] += jnp.sum(dproj.astype(f32), axis=0, keepdims=True)
    gw_s[...] += nn_dot(a1t_s[...], dproj)

    @pl.when(step == pl.num_programs(0) - 1)
    def _():
        for outer in range(2):
            for inner in range(2):
                for rz in range(4):
                    ra = pl.ds(pl.multiple_of(place(c_ref, "a", outer, inner, rz) * piece, 16), piece)
                    rb = pl.ds(pl.multiple_of(place(c_ref, "b", outer, inner, rz) * piece, 16), piece)
                    ga, gb = ((ga0_ref, gb0_ref), (ga1_ref, gb1_ref))[outer]
                    ga[inner, rz, 0] = gw_s[ra, :cols].astype(bf16)
                    ga[inner, rz, 1] = gw_s[ra, cols : 2 * cols].astype(bf16)
                    gb[inner, rz, 0] = gw_s[rb, 2 * cols :].astype(bf16)
                    gb[inner, rz, 1] = go_s[rb, :].astype(bf16)


def attn_bwd(coords, windows, dxr, dxr2, x, seg_row, ln, saved, pa, pb):
    rows, seq, width = x.shape
    qkv, kt, o, ot, lse = saved
    cols = o.shape[-1]
    heads = cols // HD
    pairs = cols // 128
    piece = pa[0].shape[-2]
    row3 = lambda r, *_: (r, 0, 0)
    row4 = lambda r, *_: (r, 0, 0, 0)
    row5 = lambda r, *_: (r, 0, 0, 0, 0)
    tok = pl.BlockSpec((1, seq, width), row3)
    gshape = pa[0].shape
    return pl.pallas_call(
        functools.partial(attn_bwd_kernel, heads, piece),
        out_shape=[
            *[jax.ShapeDtypeStruct((seq, width), bf16)] * 2,
            *[jax.ShapeDtypeStruct(gshape, bf16)] * 4,
            jax.ShapeDtypeStruct((1, 3 * cols), f32),
        ],
        grid_spec=pltpu.PrefetchScalarGridSpec(
            num_scalar_prefetch=2,
            grid=(rows,),
            in_specs=[
                full_spec((seq, width)), full_spec((seq, width)), tok,
                pl.BlockSpec((1, 1, seq), row3),
                full_spec((2, width)),
                pl.BlockSpec((1, 3, pairs, seq, 128), row5),
                pl.BlockSpec((1, pairs, 128, seq), row4),
                pl.BlockSpec((1, seq, cols), row3),
                pl.BlockSpec((1, pairs, 128, seq), row4),
                pl.BlockSpec((1, pairs, 2, seq), row4),
                ANY, ANY, ANY, ANY,
            ],
            out_specs=[
                *[full_spec((seq, width))] * 2,
                *[full_spec(gshape)] * 4,
                full_spec((1, 3 * cols)),
            ],
            scratch_shapes=[
                pltpu.VMEM((width, 3 * cols), bf16),
                pltpu.VMEM((width, cols), bf16),
                pltpu.VMEM((seq, seq), f32),
                pltpu.VMEM((seq, 3 * cols), bf16),
                pltpu.VMEM((width, 3 * cols), f32),
                pltpu.VMEM((width, cols), f32),
                pltpu.VMEM((seq, cols), bf16),
                pltpu.VMEM((pairs, 2, seq), f32),
                pltpu.VMEM((pairs, seq, 128), f32),
                pltpu.VMEM((pairs, seq, 128), f32),
                pltpu.VMEM((pairs, 128, seq), bf16),
                pltpu.VMEM((width, seq), bf16),
                pltpu.SemaphoreType.DMA((64,)),
            ],
        ),
        compiler_params=params(1),
        cost_estimate=cost(4e10, 2e7, 3e6),
        name="attn_bwd",
    )(coords, windows, dxr, dxr2, x, seg_row, ln, qkv, kt, o, ot, lse, *pa, *pb)


def sort_kernel(sources, *refs):
    vs_ref = refs[-1]
    block = vs_ref.shape[0]
    total = None
    for k in range(sources):
        pos_row, v_ref = refs[2 * k], refs[2 * k + 1]
        slot = lax.broadcasted_iota(jnp.int32, (block, v_ref.shape[0]), 0)
        slot = slot + pl.program_id(0) * block
        pick = (slot == pos_row[...]).astype(f32).astype(bf16)
        part = nn_dot(pick, v_ref[...])
        total = part if total is None else total + part
    vs_ref[...] = total.astype(bf16)


def sort_tokens(sources, tiles, group, groups, into=None):
    width = sources[0][1].shape[1]
    tokens = sum(v.shape[0] for _, v in sources)
    slots = tiles * TILE
    steps = 2
    block = slots // steps
    flat = [x for pair in sources for x in pair]
    return pl.pallas_call(
        functools.partial(sort_kernel, len(sources)),
        out_shape=jax.ShapeDtypeStruct((groups * slots, width), bf16),
        grid=(steps,),
        in_specs=[*[full_spec(x.shape) for x in flat], *([] if into is None else [ANY])],
        out_specs=pl.BlockSpec((block, width), lambda i: (i + group * steps, 0)),
        input_output_aliases={} if into is None else {len(flat): 0},
        compiler_params=params(1),
        cost_estimate=cost(2 * slots * tokens * width, 1e7),
        name="sort_tokens",
    )(*flat, *([] if into is None else [into]))


def unsort_kernel(targets, *refs):
    vs = refs[targets][...]
    for k in range(targets):
        pos_row, out_ref = refs[k], refs[targets + 1 + k]
        slot = lax.broadcasted_iota(jnp.int32, (vs.shape[0], out_ref.shape[0]), 0)
        pick = (slot == pos_row[...]).astype(f32).astype(bf16)
        out_ref[...] = tn_dot(pick, vs).astype(bf16)


def unsort_tokens(places, vs, group, groups):
    width = vs.shape[1]
    slots = vs.shape[0] // groups
    tokens = sum(p.shape[1] for p in places)
    return pl.pallas_call(
        functools.partial(unsort_kernel, len(places)),
        out_shape=[jax.ShapeDtypeStruct((p.shape[1], width), bf16) for p in places],
        grid=(1,),
        in_specs=[
            *[full_spec(p.shape) for p in places],
            pl.BlockSpec((slots, width), lambda i: (group, 0)),
        ],
        out_specs=[full_spec((p.shape[1], width)) for p in places],
        compiler_params=params(1),
        cost_estimate=cost(2 * slots * tokens * width, 1e7),
        name="unsort_tokens",
    )(*places, vs)


def mid_kernel(x_ref, own_ref, got_ref, vec_ref, x2_ref, a2_ref):
    x2 = x_ref[...].astype(f32) + (own_ref[...].astype(f32) + got_ref[...].astype(f32)) + vec_ref[0:1]
    x2_ref[...] = x2
    xhat, _ = norm_parts(x2)
    a2_ref[...] = (xhat * vec_ref[1:2] + vec_ref[2:3]).astype(bf16)


def mid(x, own, got, vec):
    tokens, width = x.shape
    tile = pl.BlockSpec((TILE, width), lambda i: (i, 0))
    return pl.pallas_call(
        mid_kernel,
        out_shape=[
            jax.ShapeDtypeStruct((tokens, width), f32),
            jax.ShapeDtypeStruct((tokens, width), bf16),
        ],
        grid=(tokens // TILE,),
        in_specs=[tile, tile, tile, full_spec((3, width))],
        out_specs=[tile, tile],
        compiler_params=params(1),
        cost_estimate=cost(1e7, 5e6),
        name="mid_norm",
    )(x, own, got, vec)


def ffn_kernel(first, count, piece, groups, c_ref, plan0_ref, plan1_ref, *refs):
    xs_ref, dys_ref, ub_ref, *rest = refs
    if not first:
        zin_ref, din_ref, *rest = rest
    w_refs = [rest[2 * c : 2 * c + 2] for c in range(count)]
    rest = rest[2 * count :]
    z_ref, da_ref, *rest = rest
    g_refs = [rest[2 * c : 2 * c + 2] for c in range(count)]
    gub_ref, wu_s, wd_s, gu_s, gd_s, x_s, dy_s, z_s, da_s, sems, in_sems, out_sems = rest[2 * count :]
    experts = wu_s.shape[0]
    hc = wu_s.shape[2] // count
    tiles = x_s.shape[0]
    per = tiles // groups
    spots = [(ry, rz, rx) for ry in range(2) for rz in range(4) for rx in range(2)]

    def rows_of(ry, rz, rx):
        block = rz * 4 + (c_ref[1] ^ ry) * 2 + (c_ref[2] ^ rx)
        return pl.ds(pl.multiple_of(block * piece, 16), piece)

    def tile_of(ref, i):
        return ref.at[pl.ds(pl.multiple_of(i * TILE, TILE), TILE), :]

    def reads(i):
        pairs = [(xs_ref, x_s), (dys_ref, dy_s)]
        if not first:
            pairs += [(zin_ref, z_s), (din_ref, da_s)]
        return [
            pltpu.make_async_copy(tile_of(src, i), dst.at[i], in_sems.at[k, i])
            for k, (src, dst) in enumerate(pairs)
        ]

    def writes(i):
        return [
            pltpu.make_async_copy(src.at[i], tile_of(dst, i), out_sems.at[k, i])
            for k, (src, dst) in enumerate([(z_s, z_ref), (da_s, da_ref)])
        ]

    copies = []
    for c in range(count):
        for ry, rz, rx in spots:
            for k, w_s in ((0, wu_s), (1, wd_s)):
                copies.append(
                    pltpu.make_async_copy(
                        w_refs[c][ry].at[rz, rx, k],
                        w_s.at[:, rows_of(ry, rz, rx), pl.ds(c * hc, hc)],
                        sems.at[len(copies)],
                    )
                )
    for c in reads(0):
        c.start()
    for c in copies:
        c.start()

    @pl.loop(1, tiles)
    def _(i):
        for c in reads(i):
            c.start()

    gu_s[...] = jnp.zeros_like(gu_s)
    gd_s[...] = jnp.zeros_like(gd_s)
    gub_ref[...] = jnp.zeros_like(gub_ref)
    for c in copies:
        c.wait()

    @pl.loop(0, tiles)
    def _(i):
        group = i // per
        k = i - group * per
        info = lambda at: jnp.where(group == 0, plan0_ref[at], plan1_ref[at])
        tokens = plan0_ref.shape[0] - per - 1
        live = k < info(tokens + per)
        for c in reads(i):
            c.wait()

        @pl.when(live)
        def _():
            e = info(tokens + k)
            x = x_s[i]
            dy = dy_s[i]
            u = nn_dot(x, wu_s[e]) + ub_ref[e]
            act, slope = gelu_parts(u)
            act = act.astype(bf16)
            du = (nn_dot(dy, wd_s[e]) * slope).astype(bf16)
            z = nt_dot(act, wd_s[e])
            da = nt_dot(du, wu_s[e])
            if not first:
                z = z + z_s[i].astype(f32)
                da = da + da_s[i].astype(f32)
            z_s[i] = z.astype(bf16)
            da_s[i] = da.astype(bf16)
            gd_s[e] += tn_dot(dy, act)
            gu_s[e] += tn_dot(x, du)
            gub_ref[e] += jnp.sum(du.astype(f32), axis=0, keepdims=True)

        @pl.when(jnp.logical_not(live))
        def _():
            z_s[i] = jnp.zeros(z_s.shape[1:], bf16)
            da_s[i] = jnp.zeros(da_s.shape[1:], bf16)

        for c in writes(i):
            c.start()

    for c in range(count):
        lanes = pl.ds(c * hc, hc)
        for ry, rz, rx in spots:
            rows = rows_of(ry, rz, rx)
            for e in range(experts):
                g_refs[c][ry][rz, rx, 0, e] = gu_s[e, rows, lanes].astype(bf16)
                g_refs[c][ry][rz, rx, 1, e] = gd_s[e, rows, lanes].astype(bf16)

    @pl.loop(0, tiles)
    def _(i):
        for c in writes(i):
            c.wait()


def ffn(coords, plans, xs, dys, up_b, weights, carry):
    slots, width = xs.shape
    tiles = slots // TILE
    groups = len(plans)
    first = not carry
    count = len(weights)
    gshape = weights[0][0].shape
    experts, piece, hc = gshape[3:]
    hid = hc * count
    out = pl.pallas_call(
        functools.partial(ffn_kernel, first, count, piece, groups),
        out_shape=[
            jax.ShapeDtypeStruct((slots, width), bf16),
            jax.ShapeDtypeStruct((slots, width), bf16),
            *[jax.ShapeDtypeStruct(gshape, bf16)] * (2 * count),
            jax.ShapeDtypeStruct((experts, 1, hid), f32),
        ],
        grid_spec=pltpu.PrefetchScalarGridSpec(
            num_scalar_prefetch=3,
            grid=(1,),
            in_specs=[
                ANY, ANY, full_spec((experts, 1, hid)), *([] if first else [ANY, ANY]),
                *[ANY] * (2 * count),
            ],
            out_specs=[ANY, ANY, *[full_spec(gshape)] * (2 * count), full_spec((experts, 1, hid))],
            scratch_shapes=[
                *[pltpu.VMEM((experts, width, hid), bf16)] * 2,
                *[pltpu.VMEM((experts, width, hid), f32)] * 2,
                *[pltpu.VMEM((tiles, TILE, width), bf16)] * 4,
                pltpu.SemaphoreType.DMA((32 * count,)),
                pltpu.SemaphoreType.DMA((2 if first else 4, tiles)),
                pltpu.SemaphoreType.DMA((2, tiles)),
            ],
        ),
        compiler_params=params(1),
        cost_estimate=cost(12 * slots * width * hid * 1.5, 4e7, 2 * slots * hid),
        name="ffn",
    )(coords, plans[0], plans[-1], xs, dys, up_b, *carry, *[w for pair in weights for w in pair])
    zs, das, *rest = out
    return zs, das, [rest[2 * c : 2 * c + 2] for c in range(count)], rest[2 * count]


def norm_grad_kernel(count, low, *refs):
    parts, (v_ref, add_ref, gain_ref, out_ref, *refs) = refs[:count], refs[count:]
    sums_ref = refs[-1]

    @pl.when(pl.program_id(0) == 0)
    def _():
        sums_ref[...] = jnp.zeros_like(sums_ref)

    grad = sum(
        jnp.sum(p[...].astype(f32), axis=0) if len(p.shape) == 3 else p[...].astype(f32) for p in parts
    )
    xhat, rstd = norm_parts(v_ref[...].astype(f32))
    out = add_ref[...].astype(f32) + norm_back(grad, xhat, rstd, gain_ref[...])
    out_ref[...] = out
    if low:
        refs[0][...] = out.astype(bf16)
    sums_ref[0:1] += jnp.sum(grad * xhat, axis=0, keepdims=True)
    sums_ref[1:2] += jnp.sum(grad, axis=0, keepdims=True)
    sums_ref[2:3] += jnp.sum(out, axis=0, keepdims=True)


def norm_grad(partial, v, add, gain, low):
    tokens, width = v.shape
    tile = pl.BlockSpec((TILE, width), lambda i: (i, 0))
    return pl.pallas_call(
        functools.partial(norm_grad_kernel, len(partial), low),
        out_shape=[
            jax.ShapeDtypeStruct((tokens, width), f32),
            *([jax.ShapeDtypeStruct((tokens, width), bf16)] if low else []),
            jax.ShapeDtypeStruct((8, width), f32),
        ],
        grid=(tokens // TILE,),
        in_specs=[
            *[
                pl.BlockSpec((p.shape[0], TILE, width), lambda i: (0, i, 0)) if p.ndim == 3 else tile
                for p in partial
            ],
            tile, tile, full_spec((1, width)),
        ],
        out_specs=[tile, *([tile] if low else []), full_spec((8, width))],
        compiler_params=params(1),
        cost_estimate=cost(2e7, 8e6),
        name="norm_grad",
    )(*partial, v, add, gain)


def whole(kernel, name, outs, *args, prefetch=()):
    return pl.pallas_call(
        kernel,
        out_shape=[jax.ShapeDtypeStruct(s, d) for s, d in outs],
        grid_spec=pltpu.PrefetchScalarGridSpec(
            num_scalar_prefetch=len(prefetch),
            grid=(1,),
            in_specs=[full_spec(x.shape) for x in args],
            out_specs=[full_spec(s) for s, _ in outs],
        ),
        compiler_params=params(1),
        cost_estimate=cost(1e6, 4e6),
        name=name,
    )(*prefetch, *args)


def sums_y_kernel(c_ref, keep, got, own, send):
    for k in range(4):
        send[k] = (keep[k].astype(f32) + got[k].astype(f32)).astype(bf16)
    here = c_ref[0]
    own[...] = keep[here].astype(f32) + got[here].astype(f32)


def sums_z_kernel(c_ref, own, got, mine, near):
    others = [c_ref[0] ^ rz for rz in (1, 2, 3)]
    add = lambda k: own[k] + sum(got[z, k].astype(f32) for z in others)
    mine[...] = add(0)
    near[...] = add(1).astype(bf16)


def two_sums_kernel(a_keep, a_got, b_keep, b_got, a_own, a_send, b_own, b_send):
    for keep, got, own, send in ((a_keep, a_got, a_own, a_send), (b_keep, b_got, b_own, b_send)):
        own[...] = keep[0].astype(f32) + got[0].astype(f32)
        send[...] = (keep[1].astype(f32) + got[1].astype(f32)).astype(bf16)


def four_sums_kernel(c_ref, a_own, a_got, b_own, b_got, own, send):
    for rz in range(4):
        va = a_own[rz] + a_got[rz].astype(f32)
        vb = b_own[rz] + b_got[rz].astype(f32)
        if rz == 0:
            own[0], own[1] = va, vb
        send[c_ref[0] ^ rz, 0] = va.astype(bf16)
        send[c_ref[0] ^ rz, 1] = vb.astype(bf16)


def qkv_grad_kernel(c_ref, own, got, g_qkv, g_out):
    others = [c_ref[0] ^ rz for rz in (1, 2, 3)]
    add = lambda k, j: own[k, j] + sum(got[z, k, j].astype(f32) for z in others)
    g_qkv[0] = add(0, 0)
    g_qkv[1] = add(0, 1)
    g_qkv[2] = add(1, 0)
    g_out[...] = add(1, 1)


def rows_kernel(c_ref, *refs):
    n = len(refs) // 3
    for k in range(n):
        mine, other, out = refs[2 * k], refs[2 * k + 1], refs[2 * n + k]
        out[c_ref[3]] = mine[...]
        out[1 - c_ref[3]] = other[...]


def expert_grad_kernel(c_ref, *refs):
    *mines, near, g_up, g_down = refs
    hc = mines[0].shape[-1]
    half = hc * len(mines)
    here = pl.multiple_of(c_ref[2] * half, 128)
    there = pl.multiple_of((1 - c_ref[2]) * half, 128)
    for k, out in ((0, g_up), (1, g_down)):
        for c, mine in enumerate(mines):
            out[:, :, pl.ds(here + c * hc, hc)] = mine[k]
        out[:, :, pl.ds(there, half)] = near[k].astype(f32)


def flip(x, mask, size):
    return lax.ppermute(x, "dp", [(i, i ^ mask) for i in range(size)])


def after(v, *deps):
    return lax.optimization_barrier((v, deps))[0]


def deal(v):
    return lax.all_to_all(v, "mp", 0, 0)


def swap(v):
    return lax.ppermute(v, "mp", [(0, 1), (1, 0)])


def share(v):
    return deal(jnp.broadcast_to(v, (lax.axis_size("mp"),) + v.shape))


def gather_z(a, b, size):
    both = jnp.stack([a, b])
    blocks = [both] + [flip(both, 4 * rz, size) for rz in (1, 2, 3)]
    return jnp.stack([v[0] for v in blocks]), jnp.stack([v[1] for v in blocks])


def gather_xy(a0, b0, dep, size):
    a0 = jnp.stack([after(a0, dep), flip(a0, 1, size)])
    b0 = jnp.stack([b0, flip(b0, 2, size)])
    return (a0, flip(a0, 2, size)), (b0, flip(b0, 1, size))


def attn_sums_1(keep, got, dep):
    shape = keep[0].shape[1:]
    return whole(
        two_sums_kernel, "two_sums", [(shape, f32), (shape, bf16)] * 2,
        after(keep[0], dep), got[0], keep[1], got[1],
    )


def attn_sums_2(coords, own, got, dep):
    shape = (2,) + own[0].shape[1:]
    return whole(
        four_sums_kernel, "four_sums", [(shape, f32), ((4,) + shape, bf16)],
        own[0], got[0], own[1], got[1], prefetch=(after(coords, dep),),
    )


def gather_plain(w):
    full = lax.all_gather(w, "dp", axis=1, tiled=True)
    n, rows, cols = full.shape
    return full.reshape(n, 16, rows // 16, cols).swapaxes(0, 1)


def gather_pieces_plain(a, b):
    blocks = [gather_plain(v) for v in (a, b)]
    blocks = [v.reshape((4, 2, 2) + v.shape[1:]) for v in blocks]
    fa = jnp.moveaxis(blocks[0], 0, 2)
    fb = jnp.swapaxes(jnp.moveaxis(blocks[1], 0, 2), 0, 1)
    return (fa[0], fa[1]), (fb[0], fb[1])


def scatter_plain(ga, gb):
    fa = jnp.moveaxis(jnp.stack(ga), 2, 0)
    fb = jnp.moveaxis(jnp.swapaxes(jnp.stack(gb), 0, 1), 2, 0)
    outs = []
    for v in (fa, fb):
        v = v.reshape((16,) + v.shape[3:]).swapaxes(0, 1)
        v = v.reshape(v.shape[0], -1, v.shape[-1]).astype(f32)
        outs.append(lax.psum_scatter(v, "dp", scatter_dimension=1, tiled=True))
    return outs


def phase(pred, f):
    shapes = jax.eval_shape(f)
    return lax.cond(
        pred, f, lambda: jax.tree.map(lambda v: jnp.zeros(v.shape, v.dtype), shapes)
    )


def deal_z(v):
    groups = [[4 * z + k for z in range(4)] for k in range(4)]
    return lax.all_to_all(v, "dp", 0, 0, axis_index_groups=groups, tiled=True)


def four_times(p):
    return jnp.broadcast_to(p, (4,) + p.shape)


def sums_y(coords, pair, size):
    shape = pair[0].shape
    return whole(
        sums_y_kernel, "sums_y", [(shape[1:], f32), (shape, bf16)],
        pair[0], flip(pair[1], 2, size), prefetch=(coords,),
    )


def sums_z(coords, parts_y):
    own, send = parts_y
    return add_z(coords, own, deal_z(send))


def add_z(coords, own, got):
    shape = own.shape[1:]
    return whole(
        sums_z_kernel, "sums_z", [(shape, f32), (shape, bf16)], own, got, prefetch=(coords,)
    )


def expert_pieces_plain(w_up, w_down):
    hc = w_up.shape[-1] // CHUNKS
    blocks = jnp.stack([gather_plain(w_up), gather_plain(w_down)], axis=1)
    blocks = blocks.reshape((4, 2, 2) + blocks.shape[1:])
    return [
        tuple(blocks[:, ry, ..., c * hc : (c + 1) * hc] for ry in range(2)) for c in range(CHUNKS)
    ]


def expert_sums_plain(pair):
    v = jnp.stack(pair, axis=1)
    v = v.reshape((16,) + v.shape[3:])
    v = jnp.moveaxis(v, 0, 2)
    v = v.reshape(v.shape[:2] + (-1, v.shape[-1])).astype(f32)
    return lax.psum_scatter(v, "dp", scatter_dimension=2, tiled=True)


def token_plan(segments, modality, experts):
    tokens = segments.size
    doc_ids = jnp.arange(modality.shape[1], dtype=jnp.int32)
    match = segments[:, :, None] == doc_ids
    mods = jnp.sum(jnp.where(match, modality[:, None, :], 0), axis=-1).reshape(tokens)
    kinds = jnp.arange(experts, dtype=jnp.int32)
    hot = (mods[:, None] == kinds).astype(jnp.int32)
    ids = jnp.arange(tokens, dtype=jnp.int32)
    lower = (ids[:, None] > ids[None, :]).astype(bf16)
    before = jnp.dot(lower, hot.astype(bf16), preferred_element_type=f32).astype(jnp.int32)
    need = (jnp.sum(hot, axis=0) + TILE - 1) // TILE
    ends = jnp.sum(jnp.where(kinds[:, None] >= kinds[None, :], need[None, :], 0), axis=1)
    pos = jnp.sum(hot * (before + (ends - need)[None, :] * TILE), axis=1)
    tiles = (tokens + experts * (TILE - 1)) // TILE
    tile_ids = jnp.arange(tiles, dtype=jnp.int32)
    tile_expert = jnp.minimum(
        jnp.sum((tile_ids[:, None] >= ends[None, :]).astype(jnp.int32), axis=1), experts - 1
    )
    return mods, pos, jnp.concatenate([pos, tile_expert, ends[-1:]])


def body(
    layer_input, segments, modality, ln_gain, ln_bias, w_qkv, qv_bias, w_out, out_bias,
    w_up, up_bias, w_down, down_bias, cotangent,
):
    part = lax.axis_index("mp")
    parts = lax.axis_size("mp")
    size = lax.axis_size("dp")
    me = lax.axis_index("dp")
    rows, seq, width = layer_input.shape
    tokens = rows * seq
    cols = w_qkv.shape[-1]
    hid = w_up.shape[-1]
    experts = w_up.shape[0]
    shape3 = (rows, seq, width)
    tiles = (tokens + experts * (TILE - 1)) // TILE
    staged = size == 16

    mine_rows = rows // parts
    mine_tokens = tokens // parts
    by_core = (parts, mine_tokens, width)
    dy = cotangent.reshape(tokens, width)
    rows_here = lambda v: lax.dynamic_slice_in_dim(v, part * mine_rows, mine_rows, 0)
    col_start = part * cols

    def small_inputs():
        q_b = lax.dynamic_slice_in_dim(qv_bias[0], col_start, cols)
        v_b = lax.dynamic_slice_in_dim(qv_bias[1], col_start, cols)
        return (
            rows_here(layer_input).reshape(mine_tokens, width),
            rows_here(cotangent).reshape(mine_tokens, width),
            jnp.concatenate([q_b, jnp.zeros_like(q_b), v_b]).reshape(1, 3 * cols),
            segments.reshape(rows, 1, seq),
            key_windows(segments),
            jnp.concatenate([out_bias[None], ln_gain[1:2], ln_bias[1:2]]),
            jnp.concatenate([ln_gain[0:1], ln_bias[0:1]]),
        )

    def fwd(coords, pa, pb):
        own, other, *saved = attn_fwd(coords, windows, layer_input, seg_row, ln1, proj_bias, pa, pb)
        return (saved, *mid(x_mine, own, swap(other), vec))

    def bwd(coords, dxr, dx2, saved, pa, pb):
        own, other, *rest = attn_bwd(
            coords, windows, *dxr, layer_input, seg_row, ln1, saved, pa, pb
        )
        return (*norm_grad((own, swap(other)), x_mine, dx2, ln_gain[0:1], False), *rest)

    def halves(v):
        take = lambda k: lax.dynamic_slice_in_dim(v, k * mine_tokens, mine_tokens, 0)
        return take(part).reshape(1, mine_tokens), take(1 - part).reshape(1, mine_tokens)

    def finish(x2, z_sum, mods):
        kinds = lax.dynamic_slice_in_dim(mods, part * mine_tokens, mine_tokens, 0)[:, None]
        bias_of = jnp.zeros((mine_tokens, width), f32)
        for e in range(experts):
            bias_of = jnp.where(kinds == e, down_bias[e][None], bias_of)
        return (x2 + (z_sum + bias_of)).astype(bf16)

    def small_rows(sums1, sums2, bsum, g_upb, g_down_bias):
        sides = bsum.reshape(3, cols)
        g_qv = lax.dynamic_update_slice(
            jnp.zeros((2, width), f32), jnp.stack([sides[0], sides[2]]), (jnp.int32(0), col_start)
        )
        g_upb_full = lax.dynamic_update_slice(
            jnp.zeros((experts, up_bias.shape[1]), f32), g_upb, (jnp.int32(0), hid_start)
        )
        return jnp.concatenate(
            [sums1[0:2], sums2[0:3], g_down_bias / parts, g_qv, g_upb_full.reshape(-1, width)]
        )

    if staged:
        x_bit = me % 2
        coords = jnp.stack([me // 4, (me // 2) % 2, x_bit, part]).astype(jnp.int32)
        pred = me < size
        inner = part < parts
        half = hid // 2
        hid_start = part * hid + x_bit * half
        hc = half // CHUNKS
        up_b = lax.dynamic_slice_in_dim(up_bias, hid_start, half, 1)

        def call_experts(k, xs, dys, weights, carry):
            call = CALLS[k]
            ub = up_b[:, None, call[0] * hc : (call[-1] + 1) * hc]
            return ffn(
                coords, (plan_own, plan), xs, dys, ub, [weights[c] for c in call], carry
            )

        def begin():
            w = jnp.stack([w_up, w_down])
            keep = lax.dynamic_slice_in_dim(w, x_bit * half, half, 3)
            send = lax.dynamic_slice_in_dim(w, (1 - x_bit) * half, half, 3)
            near = flip(send, 1, size)
            pieces = [
                jnp.stack([keep[..., c * hc : (c + 1) * hc], near[..., c * hc : (c + 1) * hc]])
                for c in range(CHUNKS)
            ]
            pieces[0] = four_times(pieces[0])
            ab = gather_z(w_qkv[:2], jnp.stack([w_qkv[2], w_out]), size)
            mods, pos, plan_own = token_plan(segments, modality, experts)
            return pieces, ab, mods, pos, plan_own, flip(plan_own, 1, size), small_inputs()

        pieces, ab, mods, pos, plan_own, plan, smalls = phase(pred, begin)
        x_mine, dy_mine, proj_bias, seg_row, windows, vec, ln1 = smalls

        def weights_in():
            def inside():
                pos_row = pos.reshape(1, tokens)
                dys = sort_tokens([(pos_row, dy)], tiles, 0, 2)
                later = [four_times(v) for v in pieces[1:]]
                hot = (mods[:, None] == jnp.arange(experts, dtype=jnp.int32)).astype(bf16)
                return (
                    *gather_xy(*ab, later, size), halves(pos), halves(plan),
                    dys, tn_dot(hot, dy),
                    later,
                )

            return deal_z(pieces[0]), phase(inner, inside)

        z0, (pa, pb, pos_here, pos_near, dys, g_down_bias, later) = phase(pred, weights_in)

        def forward():
            return (
                *phase(inner, lambda: fwd(coords, pa, pb)), flip(z0, 2, size),
                deal_z(later[0]), flip(dy_mine, 1, size),
            )

        saved, x2, a2, y0, z1, dy_near = phase(pred, forward)

        def sort(places, v, v2, group, into):
            return sort_tokens(list(zip(places, (v, v2))), tiles, group, 2, into)

        def exchange():
            near = flip(a2, 1, size)
            d, xs = phase(
                inner,
                lambda: (
                    sort(pos_near, dy_near, swap(dy_near), 1, dys),
                    sort(pos_here, a2, swap(a2), 0, None),
                ),
            )
            near = after(near, d, xs)
            xs = phase(inner, lambda: sort(pos_near, near, swap(near), 1, xs))
            return xs, d, flip(z1, 2, size), deal_z(later[1])

        xs, dys, y1, z2 = phase(pred, exchange)
        weights = [(z0, y0), (z1, y1)]
        (zs0, das0, grads, gub0), y2 = phase(
            pred, lambda: (call_experts(0, xs, dys, weights, ()), flip(z2, 2, size))
        )
        weights.append((z2, y2))

        def both_cores(places, vs, group):
            mine, other = unsort_tokens(places, vs, group, 2)
            return (mine.astype(f32) + swap(other).astype(f32)).astype(bf16)

        def second():
            def inside():
                zs, das, more, gub = call_experts(1, xs, dys, weights, (zs0, das0))
                return zs, das, more, gub, both_cores(pos_near, das, 1)

            return phase(inner, inside), sums_y(coords, grads[0], size)

        (zs, das, more, gub1, da_near), v0 = phase(pred, second)
        grads = grads + more
        g_upb = jnp.concatenate([gub0, gub1], axis=-1)[:, 0]

        def back():
            def inside():
                mine, other = unsort_tokens(pos_here, das, 0, 2)
                return mine, swap(other), both_cores(pos_near, zs, 1)

            near = flip(da_near, 1, size)
            mine, other, z_near = phase(inner, inside)
            g0 = sums_z(coords, v0)
            v1 = sums_y(coords, grads[1], size)

            def to_x2():
                dx2, dxr, sums2 = norm_grad((mine, other, near), x2, dy_mine, ln_gain[1:2], True)
                return dx2, (dxr, swap(dxr)), sums2

            return *phase(inner, to_x2), z_near, g0, v1

        dx2, dxr, sums2, z_near, g0, v1 = phase(pred, back)

        def last():
            return (
                phase(inner, lambda: bwd(coords, dxr, dx2, saved, pa, pb)), flip(z_near, 1, size),
                sums_z(coords, v1), sums_y(coords, grads[2], size),
            )

        (grad, sums1, ga0, ga1, gb0, gb1, bsum), z_near, g1, v2 = phase(pred, last)
        def sum_up():
            def out_rows():
                mine, other = unsort_tokens(pos_here, zs, 0, 2)
                z_sum = mine.astype(f32) + swap(other).astype(f32) + z_near.astype(f32)
                out = finish(x2, z_sum, mods)
                return out, swap(out), swap(grad)

            rows_all = phase(inner, lambda: small_rows(sums1, sums2, bsum, g_upb, g_down_bias))

            def small_start():
                total = rows_all + swap(rows_all)
                return total + flip(total, 1, size)

            got2 = deal_z(after(v2[1], rows_all))
            got_a, got_b = flip(ga1, 2, size), flip(gb1, 1, size)
            outs = phase(inner, out_rows)
            a_own, a_send, b_own, b_send = attn_sums_1((ga0, gb0), (got_a, got_b), outs)
            got_a, got_b = flip(a_send, 1, size), flip(b_send, 2, size)
            small = phase(inner, small_start)
            return attn_sums_2(coords, (a_own, b_own), (got_a, got_b), small), got2, small, outs

        (own, send), got2, small, (out, out_other, grad_other) = phase(pred, sum_up)

        got = deal_z(send)
        g2 = add_z(coords, v2[0], got2)
        near = flip(jnp.concatenate([v[1] for v in (g0, g1, g2)], axis=-1), 1, size)
        total = phase(inner, lambda: small + flip(small, 2, size))
        rows_z = jnp.stack([total] + [flip(total, 4 * rz, size) for rz in (1, 2, 3)])
        pick = lambda z: lax.dynamic_index_in_dim(rows_z, coords[0] ^ z, 0, False)
        small = pick(0) + pick(1) + pick(2) + pick(3)
        layer_output, grad_input = whole(
            rows_kernel, "rows", [((parts,) + v.shape, v.dtype) for v in (out, grad)],
            out, out_other, grad, grad_other, prefetch=(coords,),
        )
        g_up, g_down = whole(
            expert_grad_kernel, "expert_grad", [(w_up.shape, f32)] * 2,
            g0[0], g1[0], g2[0], near, prefetch=(coords,),
        )
        g_qkv, g_out = whole(
            qkv_grad_kernel, "qkv_grad", [(w_qkv.shape, f32), (w_out.shape, f32)], own, got,
            prefetch=(coords,),
        )
    else:
        coords = jnp.stack([0, 0, 0, part]).astype(jnp.int32)
        x_mine, dy_mine, proj_bias, seg_row, windows, vec, ln1 = small_inputs()
        hid_start = part * hid
        hc = hid // CHUNKS
        up_b = lax.dynamic_slice_in_dim(up_bias, hid_start, hid, 1)
        pa, pb = gather_pieces_plain(w_qkv[:2], jnp.stack([w_qkv[2], w_out]))
        weights = expert_pieces_plain(w_up, w_down)
        mods, pos, plan_own = token_plan(segments, modality, experts)
        pos_row = pos.reshape(1, tokens)
        hot = (mods[:, None] == jnp.arange(experts, dtype=jnp.int32)).astype(bf16)
        g_down_bias = tn_dot(hot, dy)
        dys = sort_tokens([(pos_row, dy)], tiles, 0, 1)
        saved, x2, a2 = fwd(coords, pa, pb)
        xs = sort_tokens([(pos_row, share(a2).reshape(tokens, width))], tiles, 0, 1)
        carry = ()
        grads = []
        g_upb = []
        for call in CALLS:
            ub = up_b[:, None, call[0] * hc : (call[-1] + 1) * hc]
            zs, das, pairs, gub = ffn(
                coords, (plan_own,), xs, dys, ub, [weights[c] for c in call], carry
            )
            carry = (zs, das)
            g_upb.append(gub[:, 0])
            grads += pairs
        g_upb = jnp.concatenate(g_upb, axis=-1)
        g_up, g_down = jnp.concatenate([expert_sums_plain(pair) for pair in grads], axis=-1)
        own = deal(unsort_tokens([pos_row], das, 0, 1)[0].reshape(by_core))
        dx2, dxr, sums2 = norm_grad((own[0], own[1]), x2, dy_mine, ln_gain[1:2], True)
        grad_mine, sums1, ga0, ga1, gb0, gb1, bsum = bwd(
            coords, (dxr, swap(dxr)), dx2, saved, pa, pb
        )
        g_qk, g_vo = scatter_plain((ga0, ga1), (gb0, gb1))
        g_qkv, g_out = jnp.concatenate([g_qk, g_vo[:1]]), g_vo[1]
        own = deal(unsort_tokens([pos_row], zs, 0, 1)[0].reshape(by_core))
        layer_output = share(finish(x2, jnp.sum(own.astype(f32), axis=0), mods))
        grad_input = share(grad_mine)
        small = lax.psum(small_rows(sums1, sums2, bsum, g_upb, g_down_bias), ("dp", "mp"))

    g_gain = jnp.stack([small[0], small[2]])
    g_lnb = jnp.stack([small[1], small[3]])
    return (
        layer_output.reshape(shape3),
        grad_input.reshape(shape3),
        g_gain,
        g_lnb,
        g_qkv,
        small[5 + experts : 7 + experts],
        g_out,
        small[4],
        g_up,
        small[7 + experts :].reshape(experts, up_bias.shape[1]),
        g_down,
        small[5 : 5 + experts],
    )


def solution(mesh):
    tok = P("dp", None, None)
    rep = P()
    wide = P(None, "dp", "mp")
    in_specs = (
        tok, P("dp", None), P("dp", None), rep, rep, wide, rep, P("dp", "mp"), rep, wide, rep,
        wide, rep, tok,
    )
    out_specs = (
        tok, tok, rep, rep, wide, rep, P("dp", "mp"), rep, wide, rep, wide, rep,
    )
    return jax.shard_map(body, mesh=mesh, in_specs=in_specs, out_specs=out_specs, check_vma=False)
```

```python
import functools
import math

import jax
import jax.numpy as jnp
from jax import lax
from jax.experimental import pallas as pl
from jax.experimental.pallas import tpu as pltpu
from jax.sharding import PartitionSpec as P

HD = 64
EPS = 1e-05
TILE = 256
CHUNKS = 3
SCALE = 1.0
CALLS = ((0, 1), (2,))
VMEM = 58 * 1024 * 1024
LOG2E = math.log2(math.e)
f32 = jnp.float32
bf16 = jnp.bfloat16
ANY = pl.BlockSpec(memory_space=pl.ANY)


def full_spec(shape):
    zeros = (0,) * len(shape)
    return pl.BlockSpec(shape, lambda *_: zeros)


def nt_dot(a, b):
    return lax.dot_general(a, b, (((1,), (1,)), ((), ())), preferred_element_type=f32)


def nn_dot(a, b):
    return lax.dot_general(a, b, (((1,), (0,)), ((), ())), preferred_element_type=f32)


def tn_dot(a, b):
    return lax.dot_general(a, b, (((0,), (0,)), ((), ())), preferred_element_type=f32)


def params(grid_rank):
    return pltpu.CompilerParams(
        dimension_semantics=("arbitrary",) * grid_rank, vmem_limit_bytes=VMEM
    )


def cost(flops, nbytes, trans=0):
    return pl.CostEstimate(
        flops=int(flops * SCALE), bytes_accessed=int(nbytes * SCALE), transcendentals=int(trans * SCALE)
    )


def place(c_ref, kind, outer, inner, rz):
    ry, rx = (outer, inner) if kind == "a" else (inner, outer)
    return (c_ref[0] ^ rz) * 4 + (c_ref[1] ^ ry) * 2 + (c_ref[2] ^ rx)


def piece_copies(c_ref, jobs, sems):
    copies = []
    for kind, pair, view, target in jobs:
        for outer in range(2):
            for inner in range(2):
                for rz in range(4):
                    rows = place(c_ref, kind, outer, inner, rz)
                    copies.append(
                        pltpu.make_async_copy(
                            view(pair[outer], inner, rz), target(rows), sems.at[len(copies)]
                        )
                    )
    return copies


def gelu_parts(u):
    mag = jnp.abs(u)
    t = 1.0 / (1.0 + (0.3275911 * math.sqrt(0.5)) * mag)
    poly = t * (
        0.254829592
        + t * (-0.284496736 + t * (1.421413741 + t * (-1.453152027 + t * 1.061405429)))
    )
    gauss = jnp.exp(-0.5 * u * u)
    half = 0.5 * poly * gauss
    cdf = jnp.where(u >= 0, 1.0 - half, half)
    return u * cdf, cdf + u * gauss * (1.0 / math.sqrt(2.0 * math.pi))


def norm_parts(v):
    mean = jnp.mean(v, axis=-1, keepdims=True)
    cent = v - mean
    var = jnp.mean(cent * cent, axis=-1, keepdims=True)
    rstd = lax.rsqrt(var + EPS)
    return cent * rstd, rstd


def norm_back(d_out, xhat, rstd, gain):
    d_hat = d_out * gain
    m1 = jnp.mean(d_hat, axis=-1, keepdims=True)
    m2 = jnp.mean(d_hat * xhat, axis=-1, keepdims=True)
    return rstd * (d_hat - m1 - xhat * m2)


def two_heads(v):
    lane = lax.broadcasted_iota(jnp.int32, v.shape, 1)
    none = jnp.zeros_like(v)
    return jnp.concatenate([jnp.where(lane < HD, v, none), jnp.where(lane >= HD, v, none)], axis=0)


def fill_bias(srow_ref, bias_s):
    seq = bias_s.shape[0]
    column = jnp.broadcast_to(srow_ref[0], (128, seq)).T
    for k in range(0, seq, 128):
        bias_s[:, k : k + 128] = jnp.where(column == srow_ref[0, :, k : k + 128], 0.0, -1e30)


def each_window(win_ref, row, blocks, f):
    @pl.loop(0, blocks)
    def _(j):
        first = win_ref[(row * blocks + j) * 2]
        n = win_ref[(row * blocks + j) * 2 + 1]
        for size in range(1, blocks + 1):

            @pl.when(n == size)
            def _():
                f(j, first, size)


def key_windows(segments):
    first, last = segments[:, ::128], segments[:, 127::128]
    low = jnp.sum((last[:, None, :] < first[:, :, None]).astype(jnp.int32), axis=-1)
    high = jnp.sum((first[:, None, :] <= last[:, :, None]).astype(jnp.int32), axis=-1)
    return jnp.stack([low, high - low], axis=-1).reshape(-1)


def attn_fwd_kernel(
    heads, piece, c_ref, win_ref, x_ref, srow_ref, ln_ref, pb_ref, a0, a1_, b0, b1_,
    att_ref, att_other_ref, qkv_ref, kt_ref, o_ref, ot_ref, lse_ref,
    w_s, wo_s, bias_s, vt_s, a1_s, sems,
):
    cols = heads * HD
    pairs = cols // 128
    seq, width = x_ref.shape[1], x_ref.shape[2]

    def into(block, j):
        return w_s.at[pl.ds(pl.multiple_of(block * piece, 16), piece), pl.ds(j * cols, cols)]

    def into_out(block):
        return wo_s.at[pl.ds(pl.multiple_of(block * piece, 16), piece), :]

    jobs = [
        ("a", (a0, a1_), lambda r, i, z: r.at[i, z, 0], lambda k: into(k, 0)),
        ("a", (a0, a1_), lambda r, i, z: r.at[i, z, 1], lambda k: into(k, 1)),
        ("b", (b0, b1_), lambda r, i, z: r.at[i, z, 0], lambda k: into(k, 2)),
        ("b", (b0, b1_), lambda r, i, z: r.at[i, z, 1], into_out),
    ]
    copies = piece_copies(c_ref, jobs, sems)

    @pl.when(pl.program_id(0) == 0)
    def _():
        for c in copies:
            c.start()

    xhat, _ = norm_parts(x_ref[0].astype(f32))
    a1_s[...] = (xhat * ln_ref[0:1] + ln_ref[1:2]).astype(bf16)
    fill_bias(srow_ref, bias_s)

    @pl.when(pl.program_id(0) == 0)
    def _():
        for c in copies:
            c.wait()

    a1 = a1_s[...]
    proj = (nn_dot(a1, w_s[...]) + pb_ref[...]).astype(bf16)
    for j in range(3):
        for p in range(pairs):
            qkv_ref[0, j, p] = proj[:, j * cols + p * 128 : j * cols + (p + 1) * 128]
    for p in range(pairs):
        kt_ref[0, p] = proj[:, cols + p * 128 : cols + (p + 1) * 128].T
        vt_s[p] = proj[:, 2 * cols + p * 128 : 2 * cols + (p + 1) * 128].T
    scale2 = HD ** (-0.5) * LOG2E

    def block(j, start, n):
        keys = pl.ds(pl.multiple_of(start * 128, 128), n * 128)
        mine = pl.ds(pl.multiple_of(j * 128, 128), 128)
        bias = bias_s[keys, mine]
        bias = jnp.concatenate([bias, bias], axis=1)
        every = range(pairs)
        s_t = [
            nt_dot(qkv_ref[0, 1, p, keys, :], two_heads(qkv_ref[0, 0, p, mine, :])) + bias
            for p in every
        ]
        top = [jnp.max(v, axis=0, keepdims=True) for v in s_t]
        e_t = [jnp.exp2((v - m) * scale2) for v, m in zip(s_t, top)]
        total = [jnp.sum(v, axis=0, keepdims=True) for v in e_t]
        p_t = [(v * (1.0 / t)).astype(bf16) for v, t in zip(e_t, total)]
        o_t = [nn_dot(vt_s[p, :, keys], p_t[p]).astype(bf16) for p in every]
        for p in every:
            ot_ref[0, p, :HD, mine] = o_t[p][:HD, :128]
            ot_ref[0, p, HD:, mine] = o_t[p][HD:, 128:]
            lse = top[p] * scale2 + jnp.log2(total[p])
            lse_ref[0, p, 0:1, mine] = lse[:, :128]
            lse_ref[0, p, 1:2, mine] = lse[:, 128:]

    each_window(win_ref, pl.program_id(0), seq // 128, block)

    for p in range(pairs):
        o_ref[0, :, p * 128 : (p + 1) * 128] = ot_ref[0, p].T
    att = nt_dot(o_ref[0], wo_s[...]).astype(bf16)

    @pl.when(pl.program_id(0) == c_ref[3])
    def _():
        att_ref[...] = att

    @pl.when(pl.program_id(0) != c_ref[3])
    def _():
        att_other_ref[...] = att


def attn_fwd(coords, windows, x, seg_row, ln, proj_bias, pa, pb):
    rows, seq, width = x.shape
    cols = proj_bias.shape[-1] // 3
    heads = cols // HD
    pairs = cols // 128
    piece = pa[0].shape[-2]
    row3 = lambda r, *_: (r, 0, 0)
    row4 = lambda r, *_: (r, 0, 0, 0)
    row5 = lambda r, *_: (r, 0, 0, 0, 0)
    outs = [
        ((seq, width), bf16, (seq, width), lambda *_: (0, 0)),
        ((seq, width), bf16, (seq, width), lambda *_: (0, 0)),
        ((rows, 3, pairs, seq, 128), bf16, (1, 3, pairs, seq, 128), row5),
        ((rows, pairs, 128, seq), bf16, (1, pairs, 128, seq), row4),
        ((rows, seq, cols), bf16, (1, seq, cols), row3),
        ((rows, pairs, 128, seq), bf16, (1, pairs, 128, seq), row4),
        ((rows, pairs, 2, seq), f32, (1, pairs, 2, seq), row4),
    ]
    return pl.pallas_call(
        functools.partial(attn_fwd_kernel, heads, piece),
        out_shape=[jax.ShapeDtypeStruct(s, d) for s, d, _, _ in outs],
        grid_spec=pltpu.PrefetchScalarGridSpec(
            num_scalar_prefetch=2,
            grid=(rows,),
            in_specs=[
                pl.BlockSpec((1, seq, width), row3),
                pl.BlockSpec((1, 1, seq), row3),
                full_spec((2, width)),
                full_spec((1, 3 * cols)),
                ANY, ANY, ANY, ANY,
            ],
            out_specs=[pl.BlockSpec(b, m) for _, _, b, m in outs],
            scratch_shapes=[
                pltpu.VMEM((width, 3 * cols), bf16),
                pltpu.VMEM((width, cols), bf16),
                pltpu.VMEM((seq, seq), f32),
                pltpu.VMEM((pairs, 128, seq), bf16),
                pltpu.VMEM((seq, width), bf16),
                pltpu.SemaphoreType.DMA((64,)),
            ],
        ),
        compiler_params=params(1),
        cost_estimate=cost(2e10, 1e7, 3e6),
        name="attn_fwd",
    )(coords, windows, x, seg_row, ln, proj_bias, *pa, *pb)


def attn_bwd_kernel(
    heads, piece, c_ref, win_ref, dxr_ref, dxr2_ref, x_ref, srow_ref, ln_ref, qkv_ref, kt_ref, o_ref, ot_ref, lse_ref, a0, a1_, b0, b1_,
    da1_ref, da1_other_ref, ga0_ref, ga1_ref, gb0_ref, gb1_ref, bsum_ref,
    w_s, wo_s, bias_s, dp_s, gw_s, go_s, do_s, row_s, dk_s, dv_s, dqt_s, a1t_s, sems,
):
    cols = heads * HD
    pairs = cols // 128
    seq = x_ref.shape[1]
    step = pl.program_id(0)

    def into(block, j):
        return w_s.at[pl.ds(pl.multiple_of(block * piece, 16), piece), pl.ds(j * cols, cols)]

    def into_out(block):
        return wo_s.at[pl.ds(pl.multiple_of(block * piece, 16), piece), :]

    jobs = [
        ("a", (a0, a1_), lambda r, i, z: r.at[i, z, 0], lambda k: into(k, 0)),
        ("a", (a0, a1_), lambda r, i, z: r.at[i, z, 1], lambda k: into(k, 1)),
        ("b", (b0, b1_), lambda r, i, z: r.at[i, z, 0], lambda k: into(k, 2)),
        ("b", (b0, b1_), lambda r, i, z: r.at[i, z, 1], into_out),
    ]
    copies = piece_copies(c_ref, jobs, sems)

    @pl.when(step == 0)
    def _():
        for c in copies:
            c.start()
        gw_s[...] = jnp.zeros_like(gw_s)
        go_s[...] = jnp.zeros_like(go_s)
        bsum_ref[...] = jnp.zeros_like(bsum_ref)

    xhat1, _ = norm_parts(x_ref[0].astype(f32))
    a1t_s[...] = (xhat1 * ln_ref[0:1] + ln_ref[1:2]).astype(bf16).T
    fill_bias(srow_ref, bias_s)

    @pl.when(step == 0)
    def _():
        for c in copies:
            c.wait()

    dxr = jnp.where(step == c_ref[3], dxr_ref[...], dxr2_ref[...])
    do = nn_dot(dxr, wo_s[...]).astype(bf16)
    go_s[...] += nn_dot(dxr.T, o_ref[0])
    scale = HD ** (-0.5)
    scale2 = scale * LOG2E
    do_s[...] = do
    for p in range(pairs):
        prod = do[:, p * 128 : (p + 1) * 128].T.astype(f32) * ot_ref[0, p].astype(f32)
        for h in range(2):
            row_s[p, h : h + 1] = jnp.sum(prod[h * HD : (h + 1) * HD], axis=0, keepdims=True)
    dk_s[...] = jnp.zeros_like(dk_s)
    dv_s[...] = jnp.zeros_like(dv_s)

    def block(j, start, n):
        keys = pl.ds(pl.multiple_of(start * 128, 128), n * 128)
        mine = pl.ds(pl.multiple_of(j * 128, 128), 128)
        pair = lambda ref: jnp.concatenate([ref[0:1, mine], ref[1:2, mine]], axis=1)
        every = range(pairs)
        bias = bias_s[keys, mine]
        bias = jnp.concatenate([bias, bias], axis=1)
        q_2 = [two_heads(qkv_ref[0, 0, p, mine, :]) for p in every]
        do_2 = [two_heads(do_s[mine, p * 128 : (p + 1) * 128]) for p in every]
        s_t = [nt_dot(qkv_ref[0, 1, p, keys, :], q_2[p]) * scale2 for p in every]
        d_t = [nt_dot(qkv_ref[0, 2, p, keys, :], do_2[p]) - pair(row_s.at[p]) for p in every]
        p_t = [jnp.exp2(s_t[p] + (bias - pair(lse_ref.at[0, p]))) for p in every]
        for p in every:
            dv_s[p, keys, :] += nn_dot(p_t[p].astype(bf16), do_2[p])
        ds_t = [(p_t[p] * d_t[p]).astype(bf16) for p in every]
        for p in every:
            dk_s[p, keys, :] += nn_dot(ds_t[p], q_2[p])
            dq_t = (nn_dot(kt_ref[0, p, :, keys], ds_t[p]) * scale).astype(bf16)
            dqt_s[p, :HD, mine] = dq_t[:HD, :128]
            dqt_s[p, HD:, mine] = dq_t[HD:, 128:]

    each_window(win_ref, step, seq // 128, block)

    for p in range(pairs):
        dp_s[:, p * 128 : (p + 1) * 128] = dqt_s[p].T
        dp_s[:, cols + p * 128 : cols + (p + 1) * 128] = (dk_s[p] * scale).astype(bf16)
        dp_s[:, 2 * cols + p * 128 : 2 * cols + (p + 1) * 128] = dv_s[p].astype(bf16)

    dproj = dp_s[...]
    da1 = nt_dot(dproj, w_s[...]).astype(bf16)

    @pl.when(step == c_ref[3])
    def _():
        da1_ref[...] = da1

    @pl.when(step != c_ref[3])
    def _():
        da1_other_ref[...] = da1

    bsum_ref[...] += jnp.sum(dproj.astype(f32), axis=0, keepdims=True)
    gw_s[...] += nn_dot(a1t_s[...], dproj)

    @pl.when(step == pl.num_programs(0) - 1)
    def _():
        for outer in range(2):
            for inner in range(2):
                for rz in range(4):
                    ra = pl.ds(pl.multiple_of(place(c_ref, "a", outer, inner, rz) * piece, 16), piece)
                    rb = pl.ds(pl.multiple_of(place(c_ref, "b", outer, inner, rz) * piece, 16), piece)
                    ga, gb = ((ga0_ref, gb0_ref), (ga1_ref, gb1_ref))[outer]
                    ga[inner, rz, 0] = gw_s[ra, :cols].astype(bf16)
                    ga[inner, rz, 1] = gw_s[ra, cols : 2 * cols].astype(bf16)
                    gb[inner, rz, 0] = gw_s[rb, 2 * cols :].astype(bf16)
                    gb[inner, rz, 1] = go_s[rb, :].astype(bf16)


def attn_bwd(coords, windows, dxr, dxr2, x, seg_row, ln, saved, pa, pb):
    rows, seq, width = x.shape
    qkv, kt, o, ot, lse = saved
    cols = o.shape[-1]
    heads = cols // HD
    pairs = cols // 128
    piece = pa[0].shape[-2]
    row3 = lambda r, *_: (r, 0, 0)
    row4 = lambda r, *_: (r, 0, 0, 0)
    row5 = lambda r, *_: (r, 0, 0, 0, 0)
    tok = pl.BlockSpec((1, seq, width), row3)
    gshape = pa[0].shape
    return pl.pallas_call(
        functools.partial(attn_bwd_kernel, heads, piece),
        out_shape=[
            *[jax.ShapeDtypeStruct((seq, width), bf16)] * 2,
            *[jax.ShapeDtypeStruct(gshape, bf16)] * 4,
            jax.ShapeDtypeStruct((1, 3 * cols), f32),
        ],
        grid_spec=pltpu.PrefetchScalarGridSpec(
            num_scalar_prefetch=2,
            grid=(rows,),
            in_specs=[
                full_spec((seq, width)), full_spec((seq, width)), tok,
                pl.BlockSpec((1, 1, seq), row3),
                full_spec((2, width)),
                pl.BlockSpec((1, 3, pairs, seq, 128), row5),
                pl.BlockSpec((1, pairs, 128, seq), row4),
                pl.BlockSpec((1, seq, cols), row3),
                pl.BlockSpec((1, pairs, 128, seq), row4),
                pl.BlockSpec((1, pairs, 2, seq), row4),
                ANY, ANY, ANY, ANY,
            ],
            out_specs=[
                *[full_spec((seq, width))] * 2,
                *[full_spec(gshape)] * 4,
                full_spec((1, 3 * cols)),
            ],
            scratch_shapes=[
                pltpu.VMEM((width, 3 * cols), bf16),
                pltpu.VMEM((width, cols), bf16),
                pltpu.VMEM((seq, seq), f32),
                pltpu.VMEM((seq, 3 * cols), bf16),
                pltpu.VMEM((width, 3 * cols), f32),
                pltpu.VMEM((width, cols), f32),
                pltpu.VMEM((seq, cols), bf16),
                pltpu.VMEM((pairs, 2, seq), f32),
                pltpu.VMEM((pairs, seq, 128), f32),
                pltpu.VMEM((pairs, seq, 128), f32),
                pltpu.VMEM((pairs, 128, seq), bf16),
                pltpu.VMEM((width, seq), bf16),
                pltpu.SemaphoreType.DMA((64,)),
            ],
        ),
        compiler_params=params(1),
        cost_estimate=cost(4e10, 2e7, 3e6),
        name="attn_bwd",
    )(coords, windows, dxr, dxr2, x, seg_row, ln, qkv, kt, o, ot, lse, *pa, *pb)


def sort_kernel(sources, *refs):
    vs_ref = refs[-1]
    block = vs_ref.shape[0]
    total = None
    for k in range(sources):
        pos_row, v_ref = refs[2 * k], refs[2 * k + 1]
        slot = lax.broadcasted_iota(jnp.int32, (block, v_ref.shape[0]), 0)
        slot = slot + pl.program_id(0) * block
        pick = (slot == pos_row[...]).astype(f32).astype(bf16)
        part = nn_dot(pick, v_ref[...])
        total = part if total is None else total + part
    vs_ref[...] = total.astype(bf16)


def sort_tokens(sources, tiles, group, groups, into=None):
    width = sources[0][1].shape[1]
    tokens = sum(v.shape[0] for _, v in sources)
    slots = tiles * TILE
    steps = 2
    block = slots // steps
    flat = [x for pair in sources for x in pair]
    return pl.pallas_call(
        functools.partial(sort_kernel, len(sources)),
        out_shape=jax.ShapeDtypeStruct((groups * slots, width), bf16),
        grid=(steps,),
        in_specs=[*[full_spec(x.shape) for x in flat], *([] if into is None else [ANY])],
        out_specs=pl.BlockSpec((block, width), lambda i: (i + group * steps, 0)),
        input_output_aliases={} if into is None else {len(flat): 0},
        compiler_params=params(1),
        cost_estimate=cost(2 * slots * tokens * width, 1e7),
        name="sort_tokens",
    )(*flat, *([] if into is None else [into]))


def unsort_kernel(targets, *refs):
    vs = refs[targets][...]
    for k in range(targets):
        pos_row, out_ref = refs[k], refs[targets + 1 + k]
        slot = lax.broadcasted_iota(jnp.int32, (vs.shape[0], out_ref.shape[0]), 0)
        pick = (slot == pos_row[...]).astype(f32).astype(bf16)
        out_ref[...] = tn_dot(pick, vs).astype(bf16)


def unsort_tokens(places, vs, group, groups):
    width = vs.shape[1]
    slots = vs.shape[0] // groups
    tokens = sum(p.shape[1] for p in places)
    return pl.pallas_call(
        functools.partial(unsort_kernel, len(places)),
        out_shape=[jax.ShapeDtypeStruct((p.shape[1], width), bf16) for p in places],
        grid=(1,),
        in_specs=[
            *[full_spec(p.shape) for p in places],
            pl.BlockSpec((slots, width), lambda i: (group, 0)),
        ],
        out_specs=[full_spec((p.shape[1], width)) for p in places],
        compiler_params=params(1),
        cost_estimate=cost(2 * slots * tokens * width, 1e7),
        name="unsort_tokens",
    )(*places, vs)


def mid_kernel(x_ref, own_ref, got_ref, vec_ref, x2_ref, a2_ref):
    x2 = x_ref[...].astype(f32) + (own_ref[...].astype(f32) + got_ref[...].astype(f32)) + vec_ref[0:1]
    x2_ref[...] = x2
    xhat, _ = norm_parts(x2)
    a2_ref[...] = (xhat * vec_ref[1:2] + vec_ref[2:3]).astype(bf16)


def mid(x, own, got, vec):
    tokens, width = x.shape
    tile = pl.BlockSpec((TILE, width), lambda i: (i, 0))
    return pl.pallas_call(
        mid_kernel,
        out_shape=[
            jax.ShapeDtypeStruct((tokens, width), f32),
            jax.ShapeDtypeStruct((tokens, width), bf16),
        ],
        grid=(tokens // TILE,),
        in_specs=[tile, tile, tile, full_spec((3, width))],
        out_specs=[tile, tile],
        compiler_params=params(1),
        cost_estimate=cost(1e7, 5e6),
        name="mid_norm",
    )(x, own, got, vec)


def ffn_kernel(first, count, piece, groups, near, c_ref, plan0_ref, plan1_ref, *refs):
    xs_ref, dys_ref, ub_ref, *rest = refs
    if near:
        pos_refs, rest = rest[:2], rest[2:]
    if not first:
        zin_ref, din_ref, *rest = rest
    w_refs = [rest[2 * c : 2 * c + 2] for c in range(count)]
    rest = rest[2 * count :]
    z_ref, da_ref, *rest = rest
    if near:
        near_refs, rest = rest[:2], rest[2:]
    g_refs = [rest[2 * c : 2 * c + 2] for c in range(count)]
    gub_ref, wu_s, wd_s, gu_s, gd_s, x_s, dy_s, z_s, da_s, sems, in_sems, out_sems = rest[2 * count :]
    experts = wu_s.shape[0]
    hc = wu_s.shape[2] // count
    tiles = x_s.shape[0]
    per = tiles // groups
    spots = [(ry, rz, rx) for ry in range(2) for rz in range(4) for rx in range(2)]

    def rows_of(ry, rz, rx):
        block = rz * 4 + (c_ref[1] ^ ry) * 2 + (c_ref[2] ^ rx)
        return pl.ds(pl.multiple_of(block * piece, 16), piece)

    def tile_of(ref, i):
        return ref.at[pl.ds(pl.multiple_of(i * TILE, TILE), TILE), :]

    def reads(i):
        pairs = [(xs_ref, x_s), (dys_ref, dy_s)]
        if not first:
            pairs += [(zin_ref, z_s), (din_ref, da_s)]
        return [
            pltpu.make_async_copy(tile_of(src, i), dst.at[i], in_sems.at[k, i])
            for k, (src, dst) in enumerate(pairs)
        ]

    def writes(i):
        return [
            pltpu.make_async_copy(src.at[i], tile_of(dst, i), out_sems.at[k, i])
            for k, (src, dst) in enumerate([(z_s, z_ref), (da_s, da_ref)])
        ]

    copies = []
    for c in range(count):
        for ry, rz, rx in spots:
            for k, w_s in ((0, wu_s), (1, wd_s)):
                copies.append(
                    pltpu.make_async_copy(
                        w_refs[c][ry].at[rz, rx, k],
                        w_s.at[:, rows_of(ry, rz, rx), pl.ds(c * hc, hc)],
                        sems.at[len(copies)],
                    )
                )
    for c in reads(0):
        c.start()
    for c in copies:
        c.start()

    @pl.loop(1, tiles)
    def _(i):
        for c in reads(i):
            c.start()

    gu_s[...] = jnp.zeros_like(gu_s)
    gd_s[...] = jnp.zeros_like(gd_s)
    gub_ref[...] = jnp.zeros_like(gub_ref)
    for c in copies:
        c.wait()

    @pl.loop(0, tiles)
    def _(i):
        group = i // per
        k = i - group * per
        info = lambda at: jnp.where(group == 0, plan0_ref[at], plan1_ref[at])
        tokens = plan0_ref.shape[0] - per - 1
        live = k < info(tokens + per)
        for c in reads(i):
            c.wait()

        @pl.when(live)
        def _():
            e = info(tokens + k)
            x = x_s[i]
            dy = dy_s[i]
            u = nn_dot(x, wu_s[e]) + ub_ref[e]
            act, slope = gelu_parts(u)
            act = act.astype(bf16)
            du = (nn_dot(dy, wd_s[e]) * slope).astype(bf16)
            z = nt_dot(act, wd_s[e])
            da = nt_dot(du, wu_s[e])
            if not first:
                z = z + z_s[i].astype(f32)
                da = da + da_s[i].astype(f32)
            z_s[i] = z.astype(bf16)
            da_s[i] = da.astype(bf16)
            gd_s[e] += tn_dot(dy, act)
            gu_s[e] += tn_dot(x, du)
            gub_ref[e] += jnp.sum(du.astype(f32), axis=0, keepdims=True)

        @pl.when(jnp.logical_not(live))
        def _():
            z_s[i] = jnp.zeros(z_s.shape[1:], bf16)
            da_s[i] = jnp.zeros(da_s.shape[1:], bf16)

        for c in writes(i):
            c.start()

    if near:
        rows = da_s[per:].reshape(per * TILE, da_s.shape[2])
        for pos_ref, out_ref in zip(pos_refs, near_refs):
            slot = lax.broadcasted_iota(jnp.int32, (per * TILE, out_ref.shape[0]), 0)
            pick = (slot == pos_ref[...]).astype(f32).astype(bf16)
            out_ref[...] = tn_dot(pick, rows).astype(bf16)

    for c in range(count):
        lanes = pl.ds(c * hc, hc)
        for ry, rz, rx in spots:
            rows = rows_of(ry, rz, rx)
            for e in range(experts):
                g_refs[c][ry][rz, rx, 0, e] = gu_s[e, rows, lanes].astype(bf16)
                g_refs[c][ry][rz, rx, 1, e] = gd_s[e, rows, lanes].astype(bf16)

    @pl.loop(0, tiles)
    def _(i):
        for c in writes(i):
            c.wait()


def ffn(coords, plans, xs, dys, up_b, weights, carry, places=()):
    slots, width = xs.shape
    tiles = slots // TILE
    groups = len(plans)
    first = not carry
    count = len(weights)
    gshape = weights[0][0].shape
    experts, piece, hc = gshape[3:]
    hid = hc * count
    out = pl.pallas_call(
        functools.partial(ffn_kernel, first, count, piece, groups, bool(places)),
        out_shape=[
            jax.ShapeDtypeStruct((slots, width), bf16),
            jax.ShapeDtypeStruct((slots, width), bf16),
            *[jax.ShapeDtypeStruct((p.shape[1], width), bf16) for p in places],
            *[jax.ShapeDtypeStruct(gshape, bf16)] * (2 * count),
            jax.ShapeDtypeStruct((experts, 1, hid), f32),
        ],
        grid_spec=pltpu.PrefetchScalarGridSpec(
            num_scalar_prefetch=3,
            grid=(1,),
            in_specs=[
                ANY, ANY, full_spec((experts, 1, hid)), *[full_spec(p.shape) for p in places],
                *([] if first else [ANY, ANY]), *[ANY] * (2 * count),
            ],
            out_specs=[
                ANY, ANY, *[full_spec((p.shape[1], width)) for p in places], *[full_spec(gshape)] * (2 * count),
                full_spec((experts, 1, hid)),
            ],
            scratch_shapes=[
                *[pltpu.VMEM((experts, width, hid), bf16)] * 2,
                *[pltpu.VMEM((experts, width, hid), f32)] * 2,
                *[pltpu.VMEM((tiles, TILE, width), bf16)] * 4,
                pltpu.SemaphoreType.DMA((32 * count,)),
                pltpu.SemaphoreType.DMA((2 if first else 4, tiles)),
                pltpu.SemaphoreType.DMA((2, tiles)),
            ],
        ),
        compiler_params=params(1),
        cost_estimate=cost(12 * slots * width * hid * 1.5, 4e7, 2 * slots * hid),
        name="ffn",
    )(coords, plans[0], plans[-1], xs, dys, up_b, *places, *carry, *[w for pair in weights for w in pair])
    zs, das, *rest = out
    rows, rest = rest[: len(places)], rest[len(places) :]
    if places:
        return zs, das, [rest[2 * c : 2 * c + 2] for c in range(count)], rest[2 * count], rows
    return zs, das, [rest[2 * c : 2 * c + 2] for c in range(count)], rest[2 * count]


def norm_grad_kernel(count, low, *refs):
    parts, (v_ref, add_ref, gain_ref, out_ref, *refs) = refs[:count], refs[count:]
    sums_ref = refs[-1]

    @pl.when(pl.program_id(0) == 0)
    def _():
        sums_ref[...] = jnp.zeros_like(sums_ref)

    grad = sum(
        jnp.sum(p[...].astype(f32), axis=0) if len(p.shape) == 3 else p[...].astype(f32) for p in parts
    )
    xhat, rstd = norm_parts(v_ref[...].astype(f32))
    out = add_ref[...].astype(f32) + norm_back(grad, xhat, rstd, gain_ref[...])
    out_ref[...] = out
    if low:
        refs[0][...] = out.astype(bf16)
    sums_ref[0:1] += jnp.sum(grad * xhat, axis=0, keepdims=True)
    sums_ref[1:2] += jnp.sum(grad, axis=0, keepdims=True)
    sums_ref[2:3] += jnp.sum(out, axis=0, keepdims=True)


def norm_grad(partial, v, add, gain, low):
    tokens, width = v.shape
    tile = pl.BlockSpec((TILE, width), lambda i: (i, 0))
    return pl.pallas_call(
        functools.partial(norm_grad_kernel, len(partial), low),
        out_shape=[
            jax.ShapeDtypeStruct((tokens, width), f32),
            *([jax.ShapeDtypeStruct((tokens, width), bf16)] if low else []),
            jax.ShapeDtypeStruct((8, width), f32),
        ],
        grid=(tokens // TILE,),
        in_specs=[
            *[
                pl.BlockSpec((p.shape[0], TILE, width), lambda i: (0, i, 0)) if p.ndim == 3 else tile
                for p in partial
            ],
            tile, tile, full_spec((1, width)),
        ],
        out_specs=[tile, *([tile] if low else []), full_spec((8, width))],
        compiler_params=params(1),
        cost_estimate=cost(2e7, 8e6),
        name="norm_grad",
    )(*partial, v, add, gain)


def whole(kernel, name, outs, *args, prefetch=()):
    return pl.pallas_call(
        kernel,
        out_shape=[jax.ShapeDtypeStruct(s, d) for s, d in outs],
        grid_spec=pltpu.PrefetchScalarGridSpec(
            num_scalar_prefetch=len(prefetch),
            grid=(1,),
            in_specs=[full_spec(x.shape) for x in args],
            out_specs=[full_spec(s) for s, _ in outs],
        ),
        compiler_params=params(1),
        cost_estimate=cost(1e6, 4e6),
        name=name,
    )(*prefetch, *args)


def sums_y_kernel(c_ref, keep, got, own, send):
    for k in range(4):
        send[k] = (keep[k].astype(f32) + got[k].astype(f32)).astype(bf16)
    here = c_ref[0]
    own[...] = keep[here].astype(f32) + got[here].astype(f32)


def sums_z_kernel(c_ref, own, got, mine, near):
    others = [c_ref[0] ^ rz for rz in (1, 2, 3)]
    add = lambda k: own[k] + sum(got[z, k].astype(f32) for z in others)
    mine[...] = add(0)
    near[...] = add(1).astype(bf16)


def two_sums_kernel(a_keep, a_got, b_keep, b_got, a_own, a_send, b_own, b_send):
    for keep, got, own, send in ((a_keep, a_got, a_own, a_send), (b_keep, b_got, b_own, b_send)):
        own[...] = keep[0].astype(f32) + got[0].astype(f32)
        send[...] = (keep[1].astype(f32) + got[1].astype(f32)).astype(bf16)


def four_sums_kernel(c_ref, a_own, a_got, b_own, b_got, own, send):
    for rz in range(4):
        va = a_own[rz] + a_got[rz].astype(f32)
        vb = b_own[rz] + b_got[rz].astype(f32)
        if rz == 0:
            own[0], own[1] = va, vb
        send[c_ref[0] ^ rz, 0] = va.astype(bf16)
        send[c_ref[0] ^ rz, 1] = vb.astype(bf16)


def qkv_grad_kernel(c_ref, own, got, g_qkv, g_out):
    others = [c_ref[0] ^ rz for rz in (1, 2, 3)]
    add = lambda k, j: own[k, j] + sum(got[z, k, j].astype(f32) for z in others)
    g_qkv[0] = add(0, 0)
    g_qkv[1] = add(0, 1)
    g_qkv[2] = add(1, 0)
    g_out[...] = add(1, 1)


def rows_kernel(c_ref, *refs):
    n = len(refs) // 3
    for k in range(n):
        mine, other, out = refs[2 * k], refs[2 * k + 1], refs[2 * n + k]
        out[c_ref[3]] = mine[...]
        out[1 - c_ref[3]] = other[...]


def expert_grad_kernel(c_ref, *refs):
    *mines, near, g_up, g_down = refs
    hc = mines[0].shape[-1]
    half = hc * len(mines)
    here = pl.multiple_of(c_ref[2] * half, 128)
    there = pl.multiple_of((1 - c_ref[2]) * half, 128)
    for k, out in ((0, g_up), (1, g_down)):
        for c, mine in enumerate(mines):
            out[:, :, pl.ds(here + c * hc, hc)] = mine[k]
        out[:, :, pl.ds(there, half)] = near[k].astype(f32)


def flip(x, mask, size):
    return lax.ppermute(x, "dp", [(i, i ^ mask) for i in range(size)])


def after(v, *deps):
    return lax.optimization_barrier((v, deps))[0]


def deal(v):
    return lax.all_to_all(v, "mp", 0, 0)


def swap(v):
    return lax.ppermute(v, "mp", [(0, 1), (1, 0)])


def share(v):
    return deal(jnp.broadcast_to(v, (lax.axis_size("mp"),) + v.shape))


def gather_z(a, b, size):
    both = jnp.stack([a, b])
    blocks = [both] + [flip(both, 4 * rz, size) for rz in (1, 2, 3)]
    return jnp.stack([v[0] for v in blocks]), jnp.stack([v[1] for v in blocks])


def gather_xy(a0, b0, dep, size):
    a0 = jnp.stack([after(a0, dep), flip(a0, 1, size)])
    b0 = jnp.stack([b0, flip(b0, 2, size)])
    return (a0, flip(a0, 2, size)), (b0, flip(b0, 1, size))


def attn_sums_1(keep, got, dep):
    shape = keep[0].shape[1:]
    return whole(
        two_sums_kernel, "two_sums", [(shape, f32), (shape, bf16)] * 2,
        after(keep[0], dep), got[0], keep[1], got[1],
    )


def attn_sums_2(coords, own, got, dep):
    shape = (2,) + own[0].shape[1:]
    return whole(
        four_sums_kernel, "four_sums", [(shape, f32), ((4,) + shape, bf16)],
        own[0], got[0], own[1], got[1], prefetch=(after(coords, dep),),
    )


def gather_plain(w):
    full = lax.all_gather(w, "dp", axis=1, tiled=True)
    n, rows, cols = full.shape
    return full.reshape(n, 16, rows // 16, cols).swapaxes(0, 1)


def gather_pieces_plain(a, b):
    blocks = [gather_plain(v) for v in (a, b)]
    blocks = [v.reshape((4, 2, 2) + v.shape[1:]) for v in blocks]
    fa = jnp.moveaxis(blocks[0], 0, 2)
    fb = jnp.swapaxes(jnp.moveaxis(blocks[1], 0, 2), 0, 1)
    return (fa[0], fa[1]), (fb[0], fb[1])


def scatter_plain(ga, gb):
    fa = jnp.moveaxis(jnp.stack(ga), 2, 0)
    fb = jnp.moveaxis(jnp.swapaxes(jnp.stack(gb), 0, 1), 2, 0)
    outs = []
    for v in (fa, fb):
        v = v.reshape((16,) + v.shape[3:]).swapaxes(0, 1)
        v = v.reshape(v.shape[0], -1, v.shape[-1]).astype(f32)
        outs.append(lax.psum_scatter(v, "dp", scatter_dimension=1, tiled=True))
    return outs


def phase(pred, f):
    shapes = jax.eval_shape(f)
    return lax.cond(
        pred, f, lambda: jax.tree.map(lambda v: jnp.zeros(v.shape, v.dtype), shapes)
    )


def deal_z(v):
    groups = [[4 * z + k for z in range(4)] for k in range(4)]
    return lax.all_to_all(v, "dp", 0, 0, axis_index_groups=groups, tiled=True)


def four_times(p):
    return jnp.broadcast_to(p, (4,) + p.shape)


def sums_y(coords, pair, size):
    shape = pair[0].shape
    return whole(
        sums_y_kernel, "sums_y", [(shape[1:], f32), (shape, bf16)],
        pair[0], flip(pair[1], 2, size), prefetch=(coords,),
    )


def sums_z(coords, parts_y):
    own, send = parts_y
    return add_z(coords, own, deal_z(send))


def add_z(coords, own, got):
    shape = own.shape[1:]
    return whole(
        sums_z_kernel, "sums_z", [(shape, f32), (shape, bf16)], own, got, prefetch=(coords,)
    )


def expert_pieces_plain(w_up, w_down):
    hc = w_up.shape[-1] // CHUNKS
    blocks = jnp.stack([gather_plain(w_up), gather_plain(w_down)], axis=1)
    blocks = blocks.reshape((4, 2, 2) + blocks.shape[1:])
    return [
        tuple(blocks[:, ry, ..., c * hc : (c + 1) * hc] for ry in range(2)) for c in range(CHUNKS)
    ]


def expert_sums_plain(pair):
    v = jnp.stack(pair, axis=1)
    v = v.reshape((16,) + v.shape[3:])
    v = jnp.moveaxis(v, 0, 2)
    v = v.reshape(v.shape[:2] + (-1, v.shape[-1])).astype(f32)
    return lax.psum_scatter(v, "dp", scatter_dimension=2, tiled=True)


def token_plan(segments, modality, experts):
    tokens = segments.size
    doc_ids = jnp.arange(modality.shape[1], dtype=jnp.int32)
    match = segments[:, :, None] == doc_ids
    mods = jnp.sum(jnp.where(match, modality[:, None, :], 0), axis=-1).reshape(tokens)
    kinds = jnp.arange(experts, dtype=jnp.int32)
    hot = (mods[:, None] == kinds).astype(jnp.int32)
    ids = jnp.arange(tokens, dtype=jnp.int32)
    lower = (ids[:, None] > ids[None, :]).astype(bf16)
    before = jnp.dot(lower, hot.astype(bf16), preferred_element_type=f32).astype(jnp.int32)
    need = (jnp.sum(hot, axis=0) + TILE - 1) // TILE
    ends = jnp.sum(jnp.where(kinds[:, None] >= kinds[None, :], need[None, :], 0), axis=1)
    pos = jnp.sum(hot * (before + (ends - need)[None, :] * TILE), axis=1)
    tiles = (tokens + experts * (TILE - 1)) // TILE
    tile_ids = jnp.arange(tiles, dtype=jnp.int32)
    tile_expert = jnp.minimum(
        jnp.sum((tile_ids[:, None] >= ends[None, :]).astype(jnp.int32), axis=1), experts - 1
    )
    return mods, pos, jnp.concatenate([pos, tile_expert, ends[-1:]])


def body(
    layer_input, segments, modality, ln_gain, ln_bias, w_qkv, qv_bias, w_out, out_bias,
    w_up, up_bias, w_down, down_bias, cotangent,
):
    part = lax.axis_index("mp")
    parts = lax.axis_size("mp")
    size = lax.axis_size("dp")
    me = lax.axis_index("dp")
    rows, seq, width = layer_input.shape
    tokens = rows * seq
    cols = w_qkv.shape[-1]
    hid = w_up.shape[-1]
    experts = w_up.shape[0]
    shape3 = (rows, seq, width)
    tiles = (tokens + experts * (TILE - 1)) // TILE
    staged = size == 16

    mine_rows = rows // parts
    mine_tokens = tokens // parts
    by_core = (parts, mine_tokens, width)
    dy = cotangent.reshape(tokens, width)
    rows_here = lambda v: lax.dynamic_slice_in_dim(v, part * mine_rows, mine_rows, 0)
    col_start = part * cols

    def small_inputs():
        q_b = lax.dynamic_slice_in_dim(qv_bias[0], col_start, cols)
        v_b = lax.dynamic_slice_in_dim(qv_bias[1], col_start, cols)
        return (
            rows_here(layer_input).reshape(mine_tokens, width),
            rows_here(cotangent).reshape(mine_tokens, width),
            jnp.concatenate([q_b, jnp.zeros_like(q_b), v_b]).reshape(1, 3 * cols),
            segments.reshape(rows, 1, seq),
            key_windows(segments),
            jnp.concatenate([out_bias[None], ln_gain[1:2], ln_bias[1:2]]),
            jnp.concatenate([ln_gain[0:1], ln_bias[0:1]]),
        )

    def fwd(coords, pa, pb):
        own, other, *saved = attn_fwd(coords, windows, layer_input, seg_row, ln1, proj_bias, pa, pb)
        return (saved, *mid(x_mine, own, swap(other), vec))

    def bwd(coords, dxr, dx2, saved, pa, pb):
        own, other, *rest = attn_bwd(
            coords, windows, *dxr, layer_input, seg_row, ln1, saved, pa, pb
        )
        return (*norm_grad((own, swap(other)), x_mine, dx2, ln_gain[0:1], False), *rest)

    def halves(v):
        take = lambda k: lax.dynamic_slice_in_dim(v, k * mine_tokens, mine_tokens, 0)
        return take(part).reshape(1, mine_tokens), take(1 - part).reshape(1, mine_tokens)

    def bias_rows(mods):
        kinds = lax.dynamic_slice_in_dim(mods, part * mine_tokens, mine_tokens, 0)[:, None]
        bias_of = jnp.zeros((mine_tokens, width), f32)
        for e in range(experts):
            bias_of = jnp.where(kinds == e, down_bias[e][None], bias_of)
        return bias_of

    def finish(x2, z_sum, bias_of):
        return (x2 + (z_sum + bias_of)).astype(bf16)

    def small_rows(sums1, sums2, bsum, g_upb, g_down_bias):
        sides = bsum.reshape(3, cols)
        g_qv = lax.dynamic_update_slice(
            jnp.zeros((2, width), f32), jnp.stack([sides[0], sides[2]]), (jnp.int32(0), col_start)
        )
        g_upb_full = lax.dynamic_update_slice(
            jnp.zeros((experts, up_bias.shape[1]), f32), g_upb, (jnp.int32(0), hid_start)
        )
        return jnp.concatenate(
            [sums1[0:2], sums2[0:3], g_down_bias / parts, g_qv, g_upb_full.reshape(-1, width)]
        )

    if staged:
        x_bit = me % 2
        coords = jnp.stack([me // 4, (me // 2) % 2, x_bit, part]).astype(jnp.int32)
        pred = me < size
        inner = part < parts
        half = hid // 2
        hid_start = part * hid + x_bit * half
        hc = half // CHUNKS
        up_b = lax.dynamic_slice_in_dim(up_bias, hid_start, half, 1)

        def call_experts(k, xs, dys, weights, carry, places=()):
            call = CALLS[k]
            ub = up_b[:, None, call[0] * hc : (call[-1] + 1) * hc]
            return ffn(
                coords, (plan_own, plan), xs, dys, ub, [weights[c] for c in call], carry, places
            )

        def begin():
            w = jnp.stack([w_up, w_down])
            keep = lax.dynamic_slice_in_dim(w, x_bit * half, half, 3)
            send = lax.dynamic_slice_in_dim(w, (1 - x_bit) * half, half, 3)
            near = flip(send, 1, size)
            pieces = [
                jnp.stack([keep[..., c * hc : (c + 1) * hc], near[..., c * hc : (c + 1) * hc]])
                for c in range(CHUNKS)
            ]
            pieces[0] = four_times(pieces[0])
            ab = gather_z(w_qkv[:2], jnp.stack([w_qkv[2], w_out]), size)
            mods, pos, plan_own = token_plan(segments, modality, experts)
            plan = flip(plan_own, 1, size)
            return pieces, ab, mods, pos, plan_own, plan, bias_rows(mods), small_inputs()

        pieces, ab, mods, pos, plan_own, plan, bias_of, smalls = phase(pred, begin)
        x_mine, dy_mine, proj_bias, seg_row, windows, vec, ln1 = smalls

        def weights_in():
            def inside():
                pos_row = pos.reshape(1, tokens)
                dys = sort_tokens([(pos_row, dy)], tiles, 0, 2)
                later = [four_times(v) for v in pieces[1:]]
                hot = (mods[:, None] == jnp.arange(experts, dtype=jnp.int32)).astype(bf16)
                return (
                    *gather_xy(*ab, later, size), halves(pos), halves(plan),
                    dys, tn_dot(hot, dy),
                    later,
                )

            return deal_z(pieces[0]), phase(inner, inside)

        z0, (pa, pb, pos_here, pos_near, dys, g_down_bias, later) = phase(pred, weights_in)

        def forward():
            return (
                *phase(inner, lambda: fwd(coords, pa, pb)), flip(z0, 2, size),
                deal_z(later[0]), flip(dy_mine, 1, size),
            )

        saved, x2, a2, y0, z1, dy_near = phase(pred, forward)

        def sort(places, v, v2, group, into):
            return sort_tokens(list(zip(places, (v, v2))), tiles, group, 2, into)

        def exchange():
            near = flip(a2, 1, size)
            d, xs = phase(
                inner,
                lambda: (
                    sort(pos_near, dy_near, swap(dy_near), 1, dys),
                    sort(pos_here, a2, swap(a2), 0, None),
                ),
            )
            near = after(near, d, xs)
            xs = phase(inner, lambda: sort(pos_near, near, swap(near), 1, xs))
            return xs, d, flip(z1, 2, size), deal_z(later[1])

        xs, dys, y1, z2 = phase(pred, exchange)
        weights = [(z0, y0), (z1, y1)]
        (zs0, das0, grads, gub0), y2 = phase(
            pred, lambda: (call_experts(0, xs, dys, weights, ()), flip(z2, 2, size))
        )
        weights.append((z2, y2))

        def both_cores(places, vs, group):
            mine, other = unsort_tokens(places, vs, group, 2)
            return (mine.astype(f32) + swap(other).astype(f32)).astype(bf16)

        def second():
            def inside():
                zs, das, more, gub, (mine, other) = call_experts(
                    1, xs, dys, weights, (zs0, das0), pos_near
                )
                near = (mine.astype(f32) + swap(other).astype(f32)).astype(bf16)
                return zs, das, more, gub, near

            return phase(inner, inside), sums_y(coords, grads[0], size)

        (zs, das, more, gub1, da_near), v0 = phase(pred, second)
        grads = grads + more
        g_upb = jnp.concatenate([gub0, gub1], axis=-1)[:, 0]

        def back():
            def inside():
                mine, other = unsort_tokens(pos_here, das, 0, 2)
                return mine, swap(other), both_cores(pos_near, zs, 1)

            near = flip(da_near, 1, size)
            mine, other, z_near = phase(inner, inside)
            g0 = sums_z(coords, v0)
            v1 = sums_y(coords, grads[1], size)

            def to_x2():
                dx2, dxr, sums2 = norm_grad((mine, other, near), x2, dy_mine, ln_gain[1:2], True)
                return dx2, (dxr, swap(dxr)), sums2

            return *phase(inner, to_x2), z_near, g0, v1

        dx2, dxr, sums2, z_near, g0, v1 = phase(pred, back)

        def last():
            return (
                phase(inner, lambda: bwd(coords, dxr, dx2, saved, pa, pb)), flip(z_near, 1, size),
                sums_z(coords, v1), sums_y(coords, grads[2], size),
            )

        (grad, sums1, ga0, ga1, gb0, gb1, bsum), z_near, g1, v2 = phase(pred, last)
        def sum_up():
            def out_rows():
                mine, other = unsort_tokens(pos_here, zs, 0, 2)
                z_sum = mine.astype(f32) + swap(other).astype(f32) + z_near.astype(f32)
                out = finish(x2, z_sum, bias_of)
                return out, swap(out), swap(grad)

            rows_all = phase(inner, lambda: small_rows(sums1, sums2, bsum, g_upb, g_down_bias))

            def small_start():
                total = rows_all + swap(rows_all)
                return total + flip(total, 1, size)

            got2 = deal_z(after(v2[1], rows_all))
            got_a, got_b = flip(ga1, 2, size), flip(gb1, 1, size)
            outs = phase(inner, out_rows)
            a_own, a_send, b_own, b_send = attn_sums_1((ga0, gb0), (got_a, got_b), outs)
            got_a, got_b = flip(a_send, 1, size), flip(b_send, 2, size)
            small = phase(inner, small_start)
            return attn_sums_2(coords, (a_own, b_own), (got_a, got_b), small), got2, small, outs

        (own, send), got2, small, (out, out_other, grad_other) = phase(pred, sum_up)

        got = deal_z(send)
        g2 = add_z(coords, v2[0], got2)
        near = flip(jnp.concatenate([v[1] for v in (g0, g1, g2)], axis=-1), 1, size)
        total = phase(inner, lambda: small + flip(small, 2, size))
        rows_z = [flip(total, 4 * rz, size) for rz in (1, 2, 3)]
        layer_output, grad_input = whole(
            rows_kernel, "rows", [((parts,) + v.shape, v.dtype) for v in (out, grad)],
            out, out_other, grad, grad_other, prefetch=(coords,),
        )
        g_qkv, g_out = whole(
            qkv_grad_kernel, "qkv_grad", [(w_qkv.shape, f32), (w_out.shape, f32)], own, got,
            prefetch=(after(coords, layer_output),),
        )
        last = after(coords, g_out)
        g_up, g_down = whole(
            expert_grad_kernel, "expert_grad", [(w_up.shape, f32)] * 2,
            g0[0], g1[0], g2[0], near, prefetch=(last,),
        )
        rows_z = jnp.stack([after(total, g_up)] + rows_z)
        pick = lambda z: lax.dynamic_index_in_dim(rows_z, last[0] ^ z, 0, False)
        small = pick(0) + pick(1) + pick(2) + pick(3)
    else:
        coords = jnp.stack([0, 0, 0, part]).astype(jnp.int32)
        x_mine, dy_mine, proj_bias, seg_row, windows, vec, ln1 = small_inputs()
        hid_start = part * hid
        hc = hid // CHUNKS
        up_b = lax.dynamic_slice_in_dim(up_bias, hid_start, hid, 1)
        pa, pb = gather_pieces_plain(w_qkv[:2], jnp.stack([w_qkv[2], w_out]))
        weights = expert_pieces_plain(w_up, w_down)
        mods, pos, plan_own = token_plan(segments, modality, experts)
        pos_row = pos.reshape(1, tokens)
        hot = (mods[:, None] == jnp.arange(experts, dtype=jnp.int32)).astype(bf16)
        g_down_bias = tn_dot(hot, dy)
        dys = sort_tokens([(pos_row, dy)], tiles, 0, 1)
        saved, x2, a2 = fwd(coords, pa, pb)
        xs = sort_tokens([(pos_row, share(a2).reshape(tokens, width))], tiles, 0, 1)
        carry = ()
        grads = []
        g_upb = []
        for call in CALLS:
            ub = up_b[:, None, call[0] * hc : (call[-1] + 1) * hc]
            zs, das, pairs, gub = ffn(
                coords, (plan_own,), xs, dys, ub, [weights[c] for c in call], carry
            )
            carry = (zs, das)
            g_upb.append(gub[:, 0])
            grads += pairs
        g_upb = jnp.concatenate(g_upb, axis=-1)
        g_up, g_down = jnp.concatenate([expert_sums_plain(pair) for pair in grads], axis=-1)
        own = deal(unsort_tokens([pos_row], das, 0, 1)[0].reshape(by_core))
        dx2, dxr, sums2 = norm_grad((own[0], own[1]), x2, dy_mine, ln_gain[1:2], True)
        grad_mine, sums1, ga0, ga1, gb0, gb1, bsum = bwd(
            coords, (dxr, swap(dxr)), dx2, saved, pa, pb
        )
        g_qk, g_vo = scatter_plain((ga0, ga1), (gb0, gb1))
        g_qkv, g_out = jnp.concatenate([g_qk, g_vo[:1]]), g_vo[1]
        own = deal(unsort_tokens([pos_row], zs, 0, 1)[0].reshape(by_core))
        layer_output = share(finish(x2, jnp.sum(own.astype(f32), axis=0), bias_rows(mods)))
        grad_input = share(grad_mine)
        small = lax.psum(small_rows(sums1, sums2, bsum, g_upb, g_down_bias), ("dp", "mp"))

    g_gain = jnp.stack([small[0], small[2]])
    g_lnb = jnp.stack([small[1], small[3]])
    return (
        layer_output.reshape(shape3),
        grad_input.reshape(shape3),
        g_gain,
        g_lnb,
        g_qkv,
        small[5 + experts : 7 + experts],
        g_out,
        small[4],
        g_up,
        small[7 + experts :].reshape(experts, up_bias.shape[1]),
        g_down,
        small[5 : 5 + experts],
    )


def solution(mesh):
    tok = P("dp", None, None)
    rep = P()
    wide = P(None, "dp", "mp")
    in_specs = (
        tok, P("dp", None), P("dp", None), rep, rep, wide, rep, P("dp", "mp"), rep, wide, rep,
        wide, rep, tok,
    )
    out_specs = (
        tok, tok, rep, rep, wide, rep, P("dp", "mp"), rep, wide, rep, wide, rep,
    )
    return jax.shard_map(body, mesh=mesh, in_specs=in_specs, out_specs=out_specs, check_vma=False)
```

```python
import functools
import math

import jax
import jax.numpy as jnp
from jax import lax
from jax.experimental import pallas as pl
from jax.experimental.pallas import tpu as pltpu
from jax.sharding import PartitionSpec as P

HD = 64
EPS = 1e-05
TILE = 256
CHUNKS = 3
SCALE = 1.0
CALLS = ((0, 1), (2,))
MIB = 1024 * 1024
LOG2E = math.log2(math.e)
f32 = jnp.float32
bf16 = jnp.bfloat16
ANY = pl.BlockSpec(memory_space=pl.ANY)


def full_spec(shape):
    zeros = (0,) * len(shape)
    return pl.BlockSpec(shape, lambda *_: zeros)


def nt_dot(a, b):
    return lax.dot_general(a, b, (((1,), (1,)), ((), ())), preferred_element_type=f32)


def nn_dot(a, b):
    return lax.dot_general(a, b, (((1,), (0,)), ((), ())), preferred_element_type=f32)


def tn_dot(a, b):
    return lax.dot_general(a, b, (((0,), (0,)), ((), ())), preferred_element_type=f32)


def params(grid_rank, mib=20):
    return pltpu.CompilerParams(
        dimension_semantics=("arbitrary",) * grid_rank, vmem_limit_bytes=mib * MIB
    )


def cost(flops, nbytes, trans=0):
    return pl.CostEstimate(
        flops=int(flops * SCALE), bytes_accessed=int(nbytes * SCALE), transcendentals=int(trans * SCALE)
    )


def place(c_ref, kind, outer, inner, rz):
    ry, rx = (outer, inner) if kind == "a" else (inner, outer)
    return (c_ref[0] ^ rz) * 4 + (c_ref[1] ^ ry) * 2 + (c_ref[2] ^ rx)


def piece_copies(c_ref, jobs, sems):
    copies = []
    for kind, pair, view, target in jobs:
        for outer in range(2):
            for inner in range(2):
                for rz in range(4):
                    rows = place(c_ref, kind, outer, inner, rz)
                    copies.append(
                        pltpu.make_async_copy(
                            view(pair[outer], inner, rz), target(rows), sems.at[len(copies)]
                        )
                    )
    return copies


def gelu_parts(u):
    mag = jnp.abs(u)
    t = 1.0 / (1.0 + (0.3275911 * math.sqrt(0.5)) * mag)
    poly = t * (
        0.254829592
        + t * (-0.284496736 + t * (1.421413741 + t * (-1.453152027 + t * 1.061405429)))
    )
    gauss = jnp.exp(-0.5 * u * u)
    half = 0.5 * poly * gauss
    cdf = jnp.where(u >= 0, 1.0 - half, half)
    return u * cdf, cdf + u * gauss * (1.0 / math.sqrt(2.0 * math.pi))


def norm_parts(v):
    mean = jnp.mean(v, axis=-1, keepdims=True)
    cent = v - mean
    var = jnp.mean(cent * cent, axis=-1, keepdims=True)
    rstd = lax.rsqrt(var + EPS)
    return cent * rstd, rstd


def norm_back(d_out, xhat, rstd, gain):
    d_hat = d_out * gain
    m1 = jnp.mean(d_hat, axis=-1, keepdims=True)
    m2 = jnp.mean(d_hat * xhat, axis=-1, keepdims=True)
    return rstd * (d_hat - m1 - xhat * m2)


def two_heads(v):
    lane = lax.broadcasted_iota(jnp.int32, v.shape, 1)
    none = jnp.zeros_like(v)
    return jnp.concatenate([jnp.where(lane < HD, v, none), jnp.where(lane >= HD, v, none)], axis=0)


def fill_bias(srow_ref, bias_s):
    seq = bias_s.shape[0]
    column = jnp.broadcast_to(srow_ref[0], (128, seq)).T
    for k in range(0, seq, 128):
        bias_s[:, k : k + 128] = jnp.where(column == srow_ref[0, :, k : k + 128], 0.0, -1e30)


def each_window(win_ref, row, blocks, f):
    @pl.loop(0, blocks)
    def _(j):
        first = win_ref[(row * blocks + j) * 2]
        n = win_ref[(row * blocks + j) * 2 + 1]
        for size in range(1, blocks + 1):

            @pl.when(n == size)
            def _():
                f(j, first, size)


def key_windows(segments):
    first, last = segments[:, ::128], segments[:, 127::128]
    low = jnp.sum((last[:, None, :] < first[:, :, None]).astype(jnp.int32), axis=-1)
    high = jnp.sum((first[:, None, :] <= last[:, :, None]).astype(jnp.int32), axis=-1)
    return jnp.stack([low, high - low], axis=-1).reshape(-1)


def attn_fwd_kernel(
    heads, piece, c_ref, win_ref, x_ref, srow_ref, ln_ref, pb_ref, a0, a1_, b0, b1_,
    att_ref, att_other_ref, qkv_ref, kt_ref, o_ref, ot_ref, lse_ref,
    w_s, wo_s, bias_s, vt_s, a1_s, sems,
):
    cols = heads * HD
    pairs = cols // 128
    seq, width = x_ref.shape[1], x_ref.shape[2]

    def into(block, j):
        return w_s.at[pl.ds(pl.multiple_of(block * piece, 16), piece), pl.ds(j * cols, cols)]

    def into_out(block):
        return wo_s.at[pl.ds(pl.multiple_of(block * piece, 16), piece), :]

    jobs = [
        ("a", (a0, a1_), lambda r, i, z: r.at[i, z, 0], lambda k: into(k, 0)),
        ("a", (a0, a1_), lambda r, i, z: r.at[i, z, 1], lambda k: into(k, 1)),
        ("b", (b0, b1_), lambda r, i, z: r.at[i, z, 0], lambda k: into(k, 2)),
        ("b", (b0, b1_), lambda r, i, z: r.at[i, z, 1], into_out),
    ]
    copies = piece_copies(c_ref, jobs, sems)

    @pl.when(pl.program_id(0) == 0)
    def _():
        for c in copies:
            c.start()

    xhat, _ = norm_parts(x_ref[0].astype(f32))
    a1_s[...] = (xhat * ln_ref[0:1] + ln_ref[1:2]).astype(bf16)
    fill_bias(srow_ref, bias_s)

    @pl.when(pl.program_id(0) == 0)
    def _():
        for c in copies:
            c.wait()

    a1 = a1_s[...]
    proj = (nn_dot(a1, w_s[...]) + pb_ref[...]).astype(bf16)
    for j in range(3):
        for p in range(pairs):
            qkv_ref[0, j, p] = proj[:, j * cols + p * 128 : j * cols + (p + 1) * 128]
    for p in range(pairs):
        kt_ref[0, p] = proj[:, cols + p * 128 : cols + (p + 1) * 128].T
        vt_s[p] = proj[:, 2 * cols + p * 128 : 2 * cols + (p + 1) * 128].T
    scale2 = HD ** (-0.5) * LOG2E

    def block(j, start, n):
        keys = pl.ds(pl.multiple_of(start * 128, 128), n * 128)
        mine = pl.ds(pl.multiple_of(j * 128, 128), 128)
        bias = bias_s[keys, mine]
        bias = jnp.concatenate([bias, bias], axis=1)
        every = range(pairs)
        s_t = [
            nt_dot(qkv_ref[0, 1, p, keys, :], two_heads(qkv_ref[0, 0, p, mine, :])) + bias
            for p in every
        ]
        top = [jnp.max(v, axis=0, keepdims=True) for v in s_t]
        e_t = [jnp.exp2((v - m) * scale2) for v, m in zip(s_t, top)]
        total = [jnp.sum(v, axis=0, keepdims=True) for v in e_t]
        p_t = [(v * (1.0 / t)).astype(bf16) for v, t in zip(e_t, total)]
        o_t = [nn_dot(vt_s[p, :, keys], p_t[p]).astype(bf16) for p in every]
        for p in every:
            ot_ref[0, p, :HD, mine] = o_t[p][:HD, :128]
            ot_ref[0, p, HD:, mine] = o_t[p][HD:, 128:]
            lse = top[p] * scale2 + jnp.log2(total[p])
            lse_ref[0, p, 0:1, mine] = lse[:, :128]
            lse_ref[0, p, 1:2, mine] = lse[:, 128:]

    each_window(win_ref, pl.program_id(0), seq // 128, block)

    for p in range(pairs):
        o_ref[0, :, p * 128 : (p + 1) * 128] = ot_ref[0, p].T
    att = nt_dot(o_ref[0], wo_s[...]).astype(bf16)

    @pl.when(pl.program_id(0) == c_ref[3])
    def _():
        att_ref[...] = att

    @pl.when(pl.program_id(0) != c_ref[3])
    def _():
        att_other_ref[...] = att


def attn_fwd(coords, windows, x, seg_row, ln, proj_bias, pa, pb):
    rows, seq, width = x.shape
    cols = proj_bias.shape[-1] // 3
    heads = cols // HD
    pairs = cols // 128
    piece = pa[0].shape[-2]
    row3 = lambda r, *_: (r, 0, 0)
    row4 = lambda r, *_: (r, 0, 0, 0)
    row5 = lambda r, *_: (r, 0, 0, 0, 0)
    outs = [
        ((seq, width), bf16, (seq, width), lambda *_: (0, 0)),
        ((seq, width), bf16, (seq, width), lambda *_: (0, 0)),
        ((rows, 3, pairs, seq, 128), bf16, (1, 3, pairs, seq, 128), row5),
        ((rows, pairs, 128, seq), bf16, (1, pairs, 128, seq), row4),
        ((rows, seq, cols), bf16, (1, seq, cols), row3),
        ((rows, pairs, 128, seq), bf16, (1, pairs, 128, seq), row4),
        ((rows, pairs, 2, seq), f32, (1, pairs, 2, seq), row4),
    ]
    return pl.pallas_call(
        functools.partial(attn_fwd_kernel, heads, piece),
        out_shape=[jax.ShapeDtypeStruct(s, d) for s, d, _, _ in outs],
        grid_spec=pltpu.PrefetchScalarGridSpec(
            num_scalar_prefetch=2,
            grid=(rows,),
            in_specs=[
                pl.BlockSpec((1, seq, width), row3),
                pl.BlockSpec((1, 1, seq), row3),
                full_spec((2, width)),
                full_spec((1, 3 * cols)),
                ANY, ANY, ANY, ANY,
            ],
            out_specs=[pl.BlockSpec(b, m) for _, _, b, m in outs],
            scratch_shapes=[
                pltpu.VMEM((width, 3 * cols), bf16),
                pltpu.VMEM((width, cols), bf16),
                pltpu.VMEM((seq, seq), f32),
                pltpu.VMEM((pairs, 128, seq), bf16),
                pltpu.VMEM((seq, width), bf16),
                pltpu.SemaphoreType.DMA((64,)),
            ],
        ),
        compiler_params=params(1, 26),
        cost_estimate=cost(2e10, 1e7, 3e6),
        name="attn_fwd",
    )(coords, windows, x, seg_row, ln, proj_bias, *pa, *pb)


def attn_bwd_kernel(
    heads, piece, c_ref, win_ref, dxr_ref, dxr2_ref, x_ref, srow_ref, ln_ref, qkv_ref, kt_ref, o_ref, ot_ref, lse_ref, a0, a1_, b0, b1_,
    da1_ref, da1_other_ref, ga0_ref, ga1_ref, gb0_ref, gb1_ref, bsum_ref,
    w_s, wo_s, bias_s, dp_s, gw_s, go_s, do_s, row_s, dk_s, dv_s, dqt_s, a1_s, dxr_s, o_s, sems,
):
    cols = heads * HD
    pairs = cols // 128
    seq = x_ref.shape[1]
    step = pl.program_id(0)

    def into(block, j):
        return w_s.at[pl.ds(pl.multiple_of(block * piece, 16), piece), pl.ds(j * cols, cols)]

    def into_out(block):
        return wo_s.at[pl.ds(pl.multiple_of(block * piece, 16), piece), :]

    jobs = [
        ("a", (a0, a1_), lambda r, i, z: r.at[i, z, 0], lambda k: into(k, 0)),
        ("a", (a0, a1_), lambda r, i, z: r.at[i, z, 1], lambda k: into(k, 1)),
        ("b", (b0, b1_), lambda r, i, z: r.at[i, z, 0], lambda k: into(k, 2)),
        ("b", (b0, b1_), lambda r, i, z: r.at[i, z, 1], into_out),
    ]
    copies = piece_copies(c_ref, jobs, sems)

    @pl.when(step == 0)
    def _():
        for c in copies:
            c.start()
        bsum_ref[...] = jnp.zeros_like(bsum_ref)

    xhat1, _ = norm_parts(x_ref[0].astype(f32))
    here = pl.ds(pl.multiple_of(step * seq, 128), seq)
    a1_s[here, :] = (xhat1 * ln_ref[0:1] + ln_ref[1:2]).astype(bf16)
    o_s[here, :] = o_ref[0]
    fill_bias(srow_ref, bias_s)

    @pl.when(step == 0)
    def _():
        for c in copies:
            c.wait()

    dxr = jnp.where(step == c_ref[3], dxr_ref[...], dxr2_ref[...])
    do = nn_dot(dxr, wo_s[...]).astype(bf16)
    dxr_s[here, :] = dxr
    scale = HD ** (-0.5)
    scale2 = scale * LOG2E
    do_s[...] = do
    for p in range(pairs):
        prod = do[:, p * 128 : (p + 1) * 128].T.astype(f32) * ot_ref[0, p].astype(f32)
        for h in range(2):
            row_s[p, h : h + 1] = jnp.sum(prod[h * HD : (h + 1) * HD], axis=0, keepdims=True)
    dk_s[...] = jnp.zeros_like(dk_s)
    dv_s[...] = jnp.zeros_like(dv_s)

    def block(j, start, n):
        keys = pl.ds(pl.multiple_of(start * 128, 128), n * 128)
        mine = pl.ds(pl.multiple_of(j * 128, 128), 128)
        pair = lambda ref: jnp.concatenate([ref[0:1, mine], ref[1:2, mine]], axis=1)
        every = range(pairs)
        bias = bias_s[keys, mine]
        bias = jnp.concatenate([bias, bias], axis=1)
        q_2 = [two_heads(qkv_ref[0, 0, p, mine, :]) for p in every]
        do_2 = [two_heads(do_s[mine, p * 128 : (p + 1) * 128]) for p in every]
        s_t = [nt_dot(qkv_ref[0, 1, p, keys, :], q_2[p]) * scale2 for p in every]
        d_t = [nt_dot(qkv_ref[0, 2, p, keys, :], do_2[p]) - pair(row_s.at[p]) for p in every]
        p_t = [jnp.exp2(s_t[p] + (bias - pair(lse_ref.at[0, p]))) for p in every]
        for p in every:
            dv_s[p, keys, :] += nn_dot(p_t[p].astype(bf16), do_2[p])
        ds_t = [(p_t[p] * d_t[p]).astype(bf16) for p in every]
        for p in every:
            dk_s[p, keys, :] += nn_dot(ds_t[p], q_2[p])
            dq_t = (nn_dot(kt_ref[0, p, :, keys], ds_t[p]) * scale).astype(bf16)
            dqt_s[p, :HD, mine] = dq_t[:HD, :128]
            dqt_s[p, HD:, mine] = dq_t[HD:, 128:]

    each_window(win_ref, step, seq // 128, block)

    for p in range(pairs):
        dp_s[here, p * 128 : (p + 1) * 128] = dqt_s[p].T
        dp_s[here, cols + p * 128 : cols + (p + 1) * 128] = (dk_s[p] * scale).astype(bf16)
        dp_s[here, 2 * cols + p * 128 : 2 * cols + (p + 1) * 128] = dv_s[p].astype(bf16)

    dproj = dp_s[here, :]
    da1 = nt_dot(dproj, w_s[...]).astype(bf16)

    @pl.when(step == c_ref[3])
    def _():
        da1_ref[...] = da1

    @pl.when(step != c_ref[3])
    def _():
        da1_other_ref[...] = da1

    bsum_ref[...] += jnp.sum(dproj.astype(f32), axis=0, keepdims=True)

    @pl.when(step == pl.num_programs(0) - 1)
    def _():
        gw_s[...] = tn_dot(a1_s[...], dp_s[...]).astype(bf16)
        go_s[...] = tn_dot(dxr_s[...], o_s[...]).astype(bf16)
        for outer in range(2):
            for inner in range(2):
                for rz in range(4):
                    ra = pl.ds(pl.multiple_of(place(c_ref, "a", outer, inner, rz) * piece, 16), piece)
                    rb = pl.ds(pl.multiple_of(place(c_ref, "b", outer, inner, rz) * piece, 16), piece)
                    ga, gb = ((ga0_ref, gb0_ref), (ga1_ref, gb1_ref))[outer]
                    ga[inner, rz, 0] = gw_s[ra, :cols]
                    ga[inner, rz, 1] = gw_s[ra, cols : 2 * cols]
                    gb[inner, rz, 0] = gw_s[rb, 2 * cols :]
                    gb[inner, rz, 1] = go_s[rb, :]


def attn_bwd(coords, windows, dxr, dxr2, x, seg_row, ln, saved, pa, pb):
    rows, seq, width = x.shape
    qkv, kt, o, ot, lse = saved
    cols = o.shape[-1]
    heads = cols // HD
    pairs = cols // 128
    piece = pa[0].shape[-2]
    row3 = lambda r, *_: (r, 0, 0)
    row4 = lambda r, *_: (r, 0, 0, 0)
    row5 = lambda r, *_: (r, 0, 0, 0, 0)
    tok = pl.BlockSpec((1, seq, width), row3)
    gshape = pa[0].shape
    return pl.pallas_call(
        functools.partial(attn_bwd_kernel, heads, piece),
        out_shape=[
            *[jax.ShapeDtypeStruct((seq, width), bf16)] * 2,
            *[jax.ShapeDtypeStruct(gshape, bf16)] * 4,
            jax.ShapeDtypeStruct((1, 3 * cols), f32),
        ],
        grid_spec=pltpu.PrefetchScalarGridSpec(
            num_scalar_prefetch=2,
            grid=(rows,),
            in_specs=[
                full_spec((seq, width)), full_spec((seq, width)), tok,
                pl.BlockSpec((1, 1, seq), row3),
                full_spec((2, width)),
                pl.BlockSpec((1, 3, pairs, seq, 128), row5),
                pl.BlockSpec((1, pairs, 128, seq), row4),
                pl.BlockSpec((1, seq, cols), row3),
                pl.BlockSpec((1, pairs, 128, seq), row4),
                pl.BlockSpec((1, pairs, 2, seq), row4),
                ANY, ANY, ANY, ANY,
            ],
            out_specs=[
                *[full_spec((seq, width))] * 2,
                *[full_spec(gshape)] * 4,
                full_spec((1, 3 * cols)),
            ],
            scratch_shapes=[
                pltpu.VMEM((width, 3 * cols), bf16),
                pltpu.VMEM((width, cols), bf16),
                pltpu.VMEM((seq, seq), f32),
                pltpu.VMEM((rows * seq, 3 * cols), bf16),
                pltpu.VMEM((width, 3 * cols), bf16),
                pltpu.VMEM((width, cols), bf16),
                pltpu.VMEM((seq, cols), bf16),
                pltpu.VMEM((pairs, 2, seq), f32),
                pltpu.VMEM((pairs, seq, 128), f32),
                pltpu.VMEM((pairs, seq, 128), f32),
                pltpu.VMEM((pairs, 128, seq), bf16),
                pltpu.VMEM((rows * seq, width), bf16),
                pltpu.VMEM((rows * seq, width), bf16),
                pltpu.VMEM((rows * seq, cols), bf16),
                pltpu.SemaphoreType.DMA((64,)),
            ],
        ),
        compiler_params=params(1, 34),
        cost_estimate=cost(4e10, 2e7, 3e6),
        name="attn_bwd",
    )(coords, windows, dxr, dxr2, x, seg_row, ln, qkv, kt, o, ot, lse, *pa, *pb)


def sort_kernel(sources, *refs):
    vs_ref = refs[-1]
    block = vs_ref.shape[0]
    total = None
    for k in range(sources):
        pos_row, v_ref = refs[2 * k], refs[2 * k + 1]
        slot = lax.broadcasted_iota(jnp.int32, (block, v_ref.shape[0]), 0)
        slot = slot + pl.program_id(0) * block
        pick = (slot == pos_row[...]).astype(f32).astype(bf16)
        part = nn_dot(pick, v_ref[...])
        total = part if total is None else total + part
    vs_ref[...] = total.astype(bf16)


def sort_tokens(sources, tiles, group, groups, into=None):
    width = sources[0][1].shape[1]
    tokens = sum(v.shape[0] for _, v in sources)
    slots = tiles * TILE
    steps = 2
    block = slots // steps
    flat = [x for pair in sources for x in pair]
    return pl.pallas_call(
        functools.partial(sort_kernel, len(sources)),
        out_shape=jax.ShapeDtypeStruct((groups * slots, width), bf16),
        grid=(steps,),
        in_specs=[*[full_spec(x.shape) for x in flat], *([] if into is None else [ANY])],
        out_specs=pl.BlockSpec((block, width), lambda i: (i + group * steps, 0)),
        input_output_aliases={} if into is None else {len(flat): 0},
        compiler_params=params(1),
        cost_estimate=cost(2 * slots * tokens * width, 1e7),
        name="sort_tokens",
    )(*flat, *([] if into is None else [into]))


def unsort_kernel(targets, *refs):
    vs = refs[targets][...]
    for k in range(targets):
        pos_row, out_ref = refs[k], refs[targets + 1 + k]
        slot = lax.broadcasted_iota(jnp.int32, (vs.shape[0], out_ref.shape[0]), 0)
        pick = (slot == pos_row[...]).astype(f32).astype(bf16)
        out_ref[...] = tn_dot(pick, vs).astype(bf16)


def unsort_tokens(places, vs, group, groups):
    width = vs.shape[1]
    slots = vs.shape[0] // groups
    tokens = sum(p.shape[1] for p in places)
    return pl.pallas_call(
        functools.partial(unsort_kernel, len(places)),
        out_shape=[jax.ShapeDtypeStruct((p.shape[1], width), bf16) for p in places],
        grid=(1,),
        in_specs=[
            *[full_spec(p.shape) for p in places],
            pl.BlockSpec((slots, width), lambda i: (group, 0)),
        ],
        out_specs=[full_spec((p.shape[1], width)) for p in places],
        compiler_params=params(1),
        cost_estimate=cost(2 * slots * tokens * width, 1e7),
        name="unsort_tokens",
    )(*places, vs)


def mid_kernel(x_ref, own_ref, got_ref, vec_ref, x2_ref, a2_ref):
    x2 = x_ref[...].astype(f32) + (own_ref[...].astype(f32) + got_ref[...].astype(f32)) + vec_ref[0:1]
    x2_ref[...] = x2
    xhat, _ = norm_parts(x2)
    a2_ref[...] = (xhat * vec_ref[1:2] + vec_ref[2:3]).astype(bf16)


def mid(x, own, got, vec):
    tokens, width = x.shape
    tile = pl.BlockSpec((TILE, width), lambda i: (i, 0))
    return pl.pallas_call(
        mid_kernel,
        out_shape=[
            jax.ShapeDtypeStruct((tokens, width), f32),
            jax.ShapeDtypeStruct((tokens, width), bf16),
        ],
        grid=(tokens // TILE,),
        in_specs=[tile, tile, tile, full_spec((3, width))],
        out_specs=[tile, tile],
        compiler_params=params(1),
        cost_estimate=cost(1e7, 5e6),
        name="mid_norm",
    )(x, own, got, vec)


def ffn_kernel(first, count, piece, groups, near, c_ref, plan0_ref, plan1_ref, *refs):
    xs_ref, dys_ref, ub_ref, *rest = refs
    if near:
        pos_refs, rest = rest[:2], rest[2:]
    if not first:
        zin_ref, din_ref, *rest = rest
    w_refs = [rest[2 * c : 2 * c + 2] for c in range(count)]
    rest = rest[2 * count :]
    z_ref, da_ref, *rest = rest
    if near:
        near_refs, rest = rest[:2], rest[2:]
    g_refs = [rest[2 * c : 2 * c + 2] for c in range(count)]
    gub_ref, wu_s, wd_s, gu_s, gd_s, x_s, dy_s, z_s, da_s, sems, in_sems, out_sems = rest[2 * count :]
    experts = wu_s.shape[0]
    hc = wu_s.shape[2] // count
    tiles = x_s.shape[0]
    per = tiles // groups
    spots = [(ry, rz, rx) for ry in range(2) for rz in range(4) for rx in range(2)]

    def rows_of(ry, rz, rx):
        block = rz * 4 + (c_ref[1] ^ ry) * 2 + (c_ref[2] ^ rx)
        return pl.ds(pl.multiple_of(block * piece, 16), piece)

    def tile_of(ref, i):
        return ref.at[pl.ds(pl.multiple_of(i * TILE, TILE), TILE), :]

    def reads(i):
        pairs = [(xs_ref, x_s), (dys_ref, dy_s)]
        if not first:
            pairs += [(zin_ref, z_s), (din_ref, da_s)]
        return [
            pltpu.make_async_copy(tile_of(src, i), dst.at[i], in_sems.at[k, i])
            for k, (src, dst) in enumerate(pairs)
        ]

    def writes(i):
        return [
            pltpu.make_async_copy(src.at[i], tile_of(dst, i), out_sems.at[k, i])
            for k, (src, dst) in enumerate([(z_s, z_ref), (da_s, da_ref)])
        ]

    copies = []
    for c in range(count):
        for ry, rz, rx in spots:
            for k, w_s in ((0, wu_s), (1, wd_s)):
                copies.append(
                    pltpu.make_async_copy(
                        w_refs[c][ry].at[rz, rx, k],
                        w_s.at[:, rows_of(ry, rz, rx), pl.ds(c * hc, hc)],
                        sems.at[len(copies)],
                    )
                )
    for c in reads(0):
        c.start()
    for c in copies:
        c.start()

    @pl.loop(1, tiles)
    def _(i):
        for c in reads(i):
            c.start()

    gu_s[...] = jnp.zeros_like(gu_s)
    gd_s[...] = jnp.zeros_like(gd_s)
    gub_ref[...] = jnp.zeros_like(gub_ref)
    for c in copies:
        c.wait()

    @pl.loop(0, tiles)
    def _(i):
        group = i // per
        k = i - group * per
        info = lambda at: jnp.where(group == 0, plan0_ref[at], plan1_ref[at])
        tokens = plan0_ref.shape[0] - per - 1
        live = k < info(tokens + per)
        for c in reads(i):
            c.wait()

        @pl.when(live)
        def _():
            e = info(tokens + k)
            x = x_s[i]
            dy = dy_s[i]
            u = nn_dot(x, wu_s[e]) + ub_ref[e]
            act, slope = gelu_parts(u)
            act = act.astype(bf16)
            du = (nn_dot(dy, wd_s[e]) * slope).astype(bf16)
            z = nt_dot(act, wd_s[e])
            da = nt_dot(du, wu_s[e])
            if not first:
                z = z + z_s[i].astype(f32)
                da = da + da_s[i].astype(f32)
            z_s[i] = z.astype(bf16)
            da_s[i] = da.astype(bf16)
            gd_s[e] += tn_dot(dy, act)
            gu_s[e] += tn_dot(x, du)
            gub_ref[e] += jnp.sum(du.astype(f32), axis=0, keepdims=True)

        @pl.when(jnp.logical_not(live))
        def _():
            z_s[i] = jnp.zeros(z_s.shape[1:], bf16)
            da_s[i] = jnp.zeros(da_s.shape[1:], bf16)

        for c in writes(i):
            c.start()

    if near:
        rows = da_s[per:].reshape(per * TILE, da_s.shape[2])
        for pos_ref, out_ref in zip(pos_refs, near_refs):
            slot = lax.broadcasted_iota(jnp.int32, (per * TILE, out_ref.shape[0]), 0)
            pick = (slot == pos_ref[...]).astype(f32).astype(bf16)
            out_ref[...] = tn_dot(pick, rows).astype(bf16)

    for c in range(count):
        lanes = pl.ds(c * hc, hc)
        for ry, rz, rx in spots:
            rows = rows_of(ry, rz, rx)
            for e in range(experts):
                g_refs[c][ry][rz, rx, 0, e] = gu_s[e, rows, lanes].astype(bf16)
                g_refs[c][ry][rz, rx, 1, e] = gd_s[e, rows, lanes].astype(bf16)

    @pl.loop(0, tiles)
    def _(i):
        for c in writes(i):
            c.wait()


def ffn(coords, plans, xs, dys, up_b, weights, carry, places=()):
    slots, width = xs.shape
    tiles = slots // TILE
    groups = len(plans)
    first = not carry
    count = len(weights)
    gshape = weights[0][0].shape
    experts, piece, hc = gshape[3:]
    hid = hc * count
    out = pl.pallas_call(
        functools.partial(ffn_kernel, first, count, piece, groups, bool(places)),
        out_shape=[
            jax.ShapeDtypeStruct((slots, width), bf16),
            jax.ShapeDtypeStruct((slots, width), bf16),
            *[jax.ShapeDtypeStruct((p.shape[1], width), bf16) for p in places],
            *[jax.ShapeDtypeStruct(gshape, bf16)] * (2 * count),
            jax.ShapeDtypeStruct((experts, 1, hid), f32),
        ],
        grid_spec=pltpu.PrefetchScalarGridSpec(
            num_scalar_prefetch=3,
            grid=(1,),
            in_specs=[
                ANY, ANY, full_spec((experts, 1, hid)), *[full_spec(p.shape) for p in places],
                *([] if first else [ANY, ANY]), *[ANY] * (2 * count),
            ],
            out_specs=[
                ANY, ANY, *[full_spec((p.shape[1], width)) for p in places], *[full_spec(gshape)] * (2 * count),
                full_spec((experts, 1, hid)),
            ],
            scratch_shapes=[
                *[pltpu.VMEM((experts, width, hid), bf16)] * 2,
                *[pltpu.VMEM((experts, width, hid), f32)] * 2,
                *[pltpu.VMEM((tiles, TILE, width), bf16)] * 4,
                pltpu.SemaphoreType.DMA((32 * count,)),
                pltpu.SemaphoreType.DMA((2 if first else 4, tiles)),
                pltpu.SemaphoreType.DMA((2, tiles)),
            ],
        ),
        compiler_params=params(1, 46 if groups == 2 else 60),
        cost_estimate=cost(12 * slots * width * hid * 1.5, 4e7, 2 * slots * hid),
        name="ffn",
    )(coords, plans[0], plans[-1], xs, dys, up_b, *places, *carry, *[w for pair in weights for w in pair])
    zs, das, *rest = out
    rows, rest = rest[: len(places)], rest[len(places) :]
    if places:
        return zs, das, [rest[2 * c : 2 * c + 2] for c in range(count)], rest[2 * count], rows
    return zs, das, [rest[2 * c : 2 * c + 2] for c in range(count)], rest[2 * count]


def norm_grad_kernel(count, low, *refs):
    parts, (v_ref, add_ref, gain_ref, out_ref, *refs) = refs[:count], refs[count:]
    sums_ref = refs[-1]

    @pl.when(pl.program_id(0) == 0)
    def _():
        sums_ref[...] = jnp.zeros_like(sums_ref)

    grad = sum(
        jnp.sum(p[...].astype(f32), axis=0) if len(p.shape) == 3 else p[...].astype(f32) for p in parts
    )
    xhat, rstd = norm_parts(v_ref[...].astype(f32))
    out = add_ref[...].astype(f32) + norm_back(grad, xhat, rstd, gain_ref[...])
    out_ref[...] = out
    if low:
        refs[0][...] = out.astype(bf16)
    sums_ref[0:1] += jnp.sum(grad * xhat, axis=0, keepdims=True)
    sums_ref[1:2] += jnp.sum(grad, axis=0, keepdims=True)
    sums_ref[2:3] += jnp.sum(out, axis=0, keepdims=True)


def norm_grad(partial, v, add, gain, low):
    tokens, width = v.shape
    tile = pl.BlockSpec((TILE, width), lambda i: (i, 0))
    return pl.pallas_call(
        functools.partial(norm_grad_kernel, len(partial), low),
        out_shape=[
            jax.ShapeDtypeStruct((tokens, width), f32),
            *([jax.ShapeDtypeStruct((tokens, width), bf16)] if low else []),
            jax.ShapeDtypeStruct((8, width), f32),
        ],
        grid=(tokens // TILE,),
        in_specs=[
            *[
                pl.BlockSpec((p.shape[0], TILE, width), lambda i: (0, i, 0)) if p.ndim == 3 else tile
                for p in partial
            ],
            tile, tile, full_spec((1, width)),
        ],
        out_specs=[tile, *([tile] if low else []), full_spec((8, width))],
        compiler_params=params(1),
        cost_estimate=cost(2e7, 8e6),
        name="norm_grad",
    )(*partial, v, add, gain)


def whole(kernel, name, outs, *args, prefetch=()):
    return pl.pallas_call(
        kernel,
        out_shape=[jax.ShapeDtypeStruct(s, d) for s, d in outs],
        grid_spec=pltpu.PrefetchScalarGridSpec(
            num_scalar_prefetch=len(prefetch),
            grid=(1,),
            in_specs=[full_spec(x.shape) for x in args],
            out_specs=[full_spec(s) for s, _ in outs],
        ),
        compiler_params=params(1),
        cost_estimate=cost(1e6, 4e6),
        name=name,
    )(*prefetch, *args)


def sums_y_kernel(c_ref, keep, got, own, send):
    for k in range(4):
        send[k] = (keep[k].astype(f32) + got[k].astype(f32)).astype(bf16)
    here = c_ref[0]
    own[...] = keep[here].astype(f32) + got[here].astype(f32)


def sums_z_kernel(c_ref, own, got, mine, near):
    others = [c_ref[0] ^ rz for rz in (1, 2, 3)]
    add = lambda k: own[k] + sum(got[z, k].astype(f32) for z in others)
    mine[...] = add(0)
    near[...] = add(1).astype(bf16)


def two_sums_kernel(a_keep, a_got, b_keep, b_got, a_own, a_send, b_own, b_send):
    for keep, got, own, send in ((a_keep, a_got, a_own, a_send), (b_keep, b_got, b_own, b_send)):
        own[...] = keep[0].astype(f32) + got[0].astype(f32)
        send[...] = (keep[1].astype(f32) + got[1].astype(f32)).astype(bf16)


def four_sums_kernel(c_ref, a_own, a_got, b_own, b_got, own, send):
    for rz in range(4):
        va = a_own[rz] + a_got[rz].astype(f32)
        vb = b_own[rz] + b_got[rz].astype(f32)
        if rz == 0:
            own[0], own[1] = va, vb
        send[c_ref[0] ^ rz, 0] = va.astype(bf16)
        send[c_ref[0] ^ rz, 1] = vb.astype(bf16)


def qkv_grad_kernel(c_ref, own, got, g_qkv, g_out):
    others = [c_ref[0] ^ rz for rz in (1, 2, 3)]
    add = lambda k, j: own[k, j] + sum(got[z, k, j].astype(f32) for z in others)
    g_qkv[0] = add(0, 0)
    g_qkv[1] = add(0, 1)
    g_qkv[2] = add(1, 0)
    g_out[...] = add(1, 1)


def rows_kernel(c_ref, *refs):
    n = len(refs) // 3
    for k in range(n):
        mine, other, out = refs[2 * k], refs[2 * k + 1], refs[2 * n + k]
        out[c_ref[3]] = mine[...]
        out[1 - c_ref[3]] = other[...]


def expert_grad_kernel(c_ref, *refs):
    *mines, near, g_up, g_down = refs
    hc = mines[0].shape[-1]
    half = hc * len(mines)
    here = pl.multiple_of(c_ref[2] * half, 128)
    there = pl.multiple_of((1 - c_ref[2]) * half, 128)
    for k, out in ((0, g_up), (1, g_down)):
        for c, mine in enumerate(mines):
            out[:, :, pl.ds(here + c * hc, hc)] = mine[k]
        out[:, :, pl.ds(there, half)] = near[k].astype(f32)


def flip(x, mask, size):
    return lax.ppermute(x, "dp", [(i, i ^ mask) for i in range(size)])


def after(v, *deps):
    return lax.optimization_barrier((v, deps))[0]


def deal(v):
    return lax.all_to_all(v, "mp", 0, 0)


def swap(v):
    return lax.ppermute(v, "mp", [(0, 1), (1, 0)])


def share(v):
    return deal(jnp.broadcast_to(v, (lax.axis_size("mp"),) + v.shape))


def gather_z(a, b, size):
    both = jnp.stack([a, b])
    blocks = [both] + [flip(both, 4 * rz, size) for rz in (1, 2, 3)]
    return jnp.stack([v[0] for v in blocks]), jnp.stack([v[1] for v in blocks])


def gather_xy(a0, b0, dep, size):
    a0 = jnp.stack([after(a0, dep), flip(a0, 1, size)])
    b0 = jnp.stack([b0, flip(b0, 2, size)])
    return (a0, flip(a0, 2, size)), (b0, flip(b0, 1, size))


def attn_sums_1(keep, got, dep):
    shape = keep[0].shape[1:]
    return whole(
        two_sums_kernel, "two_sums", [(shape, f32), (shape, bf16)] * 2,
        after(keep[0], dep), got[0], keep[1], got[1],
    )


def attn_sums_2(coords, own, got, dep):
    shape = (2,) + own[0].shape[1:]
    return whole(
        four_sums_kernel, "four_sums", [(shape, f32), ((4,) + shape, bf16)],
        own[0], got[0], own[1], got[1], prefetch=(after(coords, dep),),
    )


def gather_plain(w):
    full = lax.all_gather(w, "dp", axis=1, tiled=True)
    n, rows, cols = full.shape
    return full.reshape(n, 16, rows // 16, cols).swapaxes(0, 1)


def gather_pieces_plain(a, b):
    blocks = [gather_plain(v) for v in (a, b)]
    blocks = [v.reshape((4, 2, 2) + v.shape[1:]) for v in blocks]
    fa = jnp.moveaxis(blocks[0], 0, 2)
    fb = jnp.swapaxes(jnp.moveaxis(blocks[1], 0, 2), 0, 1)
    return (fa[0], fa[1]), (fb[0], fb[1])


def scatter_plain(ga, gb):
    fa = jnp.moveaxis(jnp.stack(ga), 2, 0)
    fb = jnp.moveaxis(jnp.swapaxes(jnp.stack(gb), 0, 1), 2, 0)
    outs = []
    for v in (fa, fb):
        v = v.reshape((16,) + v.shape[3:]).swapaxes(0, 1)
        v = v.reshape(v.shape[0], -1, v.shape[-1]).astype(f32)
        outs.append(lax.psum_scatter(v, "dp", scatter_dimension=1, tiled=True))
    return outs


def phase(pred, f):
    shapes = jax.eval_shape(f)
    return lax.cond(
        pred, f, lambda: jax.tree.map(lambda v: jnp.zeros(v.shape, v.dtype), shapes)
    )


def deal_z(v):
    groups = [[4 * z + k for z in range(4)] for k in range(4)]
    return lax.all_to_all(v, "dp", 0, 0, axis_index_groups=groups, tiled=True)


def four_times(p):
    return jnp.broadcast_to(p, (4,) + p.shape)


def sums_y(coords, pair, size):
    shape = pair[0].shape
    return whole(
        sums_y_kernel, "sums_y", [(shape[1:], f32), (shape, bf16)],
        pair[0], flip(pair[1], 2, size), prefetch=(coords,),
    )


def sums_z(coords, parts_y):
    own, send = parts_y
    return add_z(coords, own, deal_z(send))


def add_z(coords, own, got):
    shape = own.shape[1:]
    return whole(
        sums_z_kernel, "sums_z", [(shape, f32), (shape, bf16)], own, got, prefetch=(coords,)
    )


def expert_pieces_plain(w_up, w_down):
    hc = w_up.shape[-1] // CHUNKS
    blocks = jnp.stack([gather_plain(w_up), gather_plain(w_down)], axis=1)
    blocks = blocks.reshape((4, 2, 2) + blocks.shape[1:])
    return [
        tuple(blocks[:, ry, ..., c * hc : (c + 1) * hc] for ry in range(2)) for c in range(CHUNKS)
    ]


def expert_sums_plain(pair):
    v = jnp.stack(pair, axis=1)
    v = v.reshape((16,) + v.shape[3:])
    v = jnp.moveaxis(v, 0, 2)
    v = v.reshape(v.shape[:2] + (-1, v.shape[-1])).astype(f32)
    return lax.psum_scatter(v, "dp", scatter_dimension=2, tiled=True)


def token_plan(segments, modality, experts):
    tokens = segments.size
    doc_ids = jnp.arange(modality.shape[1], dtype=jnp.int32)
    match = segments[:, :, None] == doc_ids
    mods = jnp.sum(jnp.where(match, modality[:, None, :], 0), axis=-1).reshape(tokens)
    kinds = jnp.arange(experts, dtype=jnp.int32)
    hot = (mods[:, None] == kinds).astype(jnp.int32)
    ids = jnp.arange(tokens, dtype=jnp.int32)
    lower = (ids[:, None] > ids[None, :]).astype(bf16)
    before = jnp.dot(lower, hot.astype(bf16), preferred_element_type=f32).astype(jnp.int32)
    need = (jnp.sum(hot, axis=0) + TILE - 1) // TILE
    ends = jnp.sum(jnp.where(kinds[:, None] >= kinds[None, :], need[None, :], 0), axis=1)
    pos = jnp.sum(hot * (before + (ends - need)[None, :] * TILE), axis=1)
    tiles = (tokens + experts * (TILE - 1)) // TILE
    tile_ids = jnp.arange(tiles, dtype=jnp.int32)
    tile_expert = jnp.minimum(
        jnp.sum((tile_ids[:, None] >= ends[None, :]).astype(jnp.int32), axis=1), experts - 1
    )
    return mods, pos, jnp.concatenate([pos, tile_expert, ends[-1:]])


def body(
    layer_input, segments, modality, ln_gain, ln_bias, w_qkv, qv_bias, w_out, out_bias,
    w_up, up_bias, w_down, down_bias, cotangent,
):
    part = lax.axis_index("mp")
    parts = lax.axis_size("mp")
    size = lax.axis_size("dp")
    me = lax.axis_index("dp")
    rows, seq, width = layer_input.shape
    tokens = rows * seq
    cols = w_qkv.shape[-1]
    hid = w_up.shape[-1]
    experts = w_up.shape[0]
    shape3 = (rows, seq, width)
    tiles = (tokens + experts * (TILE - 1)) // TILE
    staged = size == 16

    mine_rows = rows // parts
    mine_tokens = tokens // parts
    by_core = (parts, mine_tokens, width)
    dy = cotangent.reshape(tokens, width)
    rows_here = lambda v: lax.dynamic_slice_in_dim(v, part * mine_rows, mine_rows, 0)
    col_start = part * cols

    def small_inputs():
        q_b = lax.dynamic_slice_in_dim(qv_bias[0], col_start, cols)
        v_b = lax.dynamic_slice_in_dim(qv_bias[1], col_start, cols)
        return (
            rows_here(layer_input).reshape(mine_tokens, width),
            rows_here(cotangent).reshape(mine_tokens, width),
            jnp.concatenate([q_b, jnp.zeros_like(q_b), v_b]).reshape(1, 3 * cols),
            segments.reshape(rows, 1, seq),
            key_windows(segments),
            jnp.concatenate([out_bias[None], ln_gain[1:2], ln_bias[1:2]]),
            jnp.concatenate([ln_gain[0:1], ln_bias[0:1]]),
        )

    def fwd(coords, pa, pb):
        own, other, *saved = attn_fwd(coords, windows, layer_input, seg_row, ln1, proj_bias, pa, pb)
        return (saved, *mid(x_mine, own, swap(other), vec))

    def bwd(coords, dxr, dx2, saved, pa, pb):
        own, other, *rest = attn_bwd(
            coords, windows, *dxr, layer_input, seg_row, ln1, saved, pa, pb
        )
        return (*norm_grad((own, swap(other)), x_mine, dx2, ln_gain[0:1], False), *rest)

    def halves(v):
        take = lambda k: lax.dynamic_slice_in_dim(v, k * mine_tokens, mine_tokens, 0)
        return take(part).reshape(1, mine_tokens), take(1 - part).reshape(1, mine_tokens)

    def bias_rows(mods):
        kinds = lax.dynamic_slice_in_dim(mods, part * mine_tokens, mine_tokens, 0)[:, None]
        bias_of = jnp.zeros((mine_tokens, width), f32)
        for e in range(experts):
            bias_of = jnp.where(kinds == e, down_bias[e][None], bias_of)
        return bias_of

    def finish(x2, z_sum, bias_of):
        return (x2 + (z_sum + bias_of)).astype(bf16)

    def small_rows(sums1, sums2, bsum, g_upb, g_down_bias):
        sides = bsum.reshape(3, cols)
        g_qv = lax.dynamic_update_slice(
            jnp.zeros((2, width), f32), jnp.stack([sides[0], sides[2]]), (jnp.int32(0), col_start)
        )
        g_upb_full = lax.dynamic_update_slice(
            jnp.zeros((experts, up_bias.shape[1]), f32), g_upb, (jnp.int32(0), hid_start)
        )
        return jnp.concatenate(
            [sums1[0:2], sums2[0:3], g_down_bias / parts, g_qv, g_upb_full.reshape(-1, width)]
        )

    if staged:
        x_bit = me % 2
        coords = jnp.stack([me // 4, (me // 2) % 2, x_bit, part]).astype(jnp.int32)
        pred = me < size
        inner = part < parts
        half = hid // 2
        hid_start = part * hid + x_bit * half
        hc = half // CHUNKS
        up_b = lax.dynamic_slice_in_dim(up_bias, hid_start, half, 1)

        def call_experts(k, xs, dys, weights, carry, places=()):
            call = CALLS[k]
            ub = up_b[:, None, call[0] * hc : (call[-1] + 1) * hc]
            return ffn(
                coords, (plan_own, plan), xs, dys, ub, [weights[c] for c in call], carry, places
            )

        def begin():
            w = jnp.stack([w_up, w_down])
            keep = lax.dynamic_slice_in_dim(w, x_bit * half, half, 3)
            send = lax.dynamic_slice_in_dim(w, (1 - x_bit) * half, half, 3)
            near = flip(send, 1, size)
            pieces = [
                jnp.stack([keep[..., c * hc : (c + 1) * hc], near[..., c * hc : (c + 1) * hc]])
                for c in range(CHUNKS)
            ]
            pieces[0] = four_times(pieces[0])
            ab = gather_z(w_qkv[:2], jnp.stack([w_qkv[2], w_out]), size)
            mods, pos, plan_own = token_plan(segments, modality, experts)
            plan = flip(plan_own, 1, size)
            return pieces, ab, mods, pos, plan_own, plan, bias_rows(mods), small_inputs()

        pieces, ab, mods, pos, plan_own, plan, bias_of, smalls = phase(pred, begin)
        x_mine, dy_mine, proj_bias, seg_row, windows, vec, ln1 = smalls

        def weights_in():
            def inside():
                pos_row = pos.reshape(1, tokens)
                dys = sort_tokens([(pos_row, dy)], tiles, 0, 2)
                later = [four_times(v) for v in pieces[1:]]
                hot = (mods[:, None] == jnp.arange(experts, dtype=jnp.int32)).astype(bf16)
                return (
                    *gather_xy(*ab, later, size), halves(pos), halves(plan),
                    dys, tn_dot(hot, dy),
                    later,
                )

            return deal_z(pieces[0]), phase(inner, inside)

        z0, (pa, pb, pos_here, pos_near, dys, g_down_bias, later) = phase(pred, weights_in)

        def forward():
            return (
                *phase(inner, lambda: fwd(coords, pa, pb)), flip(z0, 2, size),
                deal_z(later[0]), flip(dy_mine, 1, size),
            )

        saved, x2, a2, y0, z1, dy_near = phase(pred, forward)

        def sort(places, v, v2, group, into):
            return sort_tokens(list(zip(places, (v, v2))), tiles, group, 2, into)

        def exchange():
            near = flip(a2, 1, size)
            d, xs = phase(
                inner,
                lambda: (
                    sort(pos_near, dy_near, swap(dy_near), 1, dys),
                    sort(pos_here, a2, swap(a2), 0, None),
                ),
            )
            near = after(near, d, xs)
            xs = phase(inner, lambda: sort(pos_near, near, swap(near), 1, xs))
            return xs, d, flip(z1, 2, size), deal_z(later[1])

        xs, dys, y1, z2 = phase(pred, exchange)
        weights = [(z0, y0), (z1, y1)]
        (zs0, das0, grads, gub0), y2 = phase(
            pred, lambda: (call_experts(0, xs, dys, weights, ()), flip(z2, 2, size))
        )
        weights.append((z2, y2))

        def both_cores(places, vs, group):
            mine, other = unsort_tokens(places, vs, group, 2)
            return (mine.astype(f32) + swap(other).astype(f32)).astype(bf16)

        def second():
            def inside():
                zs, das, more, gub, (mine, other) = call_experts(
                    1, xs, dys, weights, (zs0, das0), pos_near
                )
                near = (mine.astype(f32) + swap(other).astype(f32)).astype(bf16)
                return zs, das, more, gub, near

            return phase(inner, inside), sums_y(coords, grads[0], size)

        (zs, das, more, gub1, da_near), v0 = phase(pred, second)
        grads = grads + more
        g_upb = jnp.concatenate([gub0, gub1], axis=-1)[:, 0]

        def back():
            def inside():
                mine, other = unsort_tokens(pos_here, das, 0, 2)
                return mine, swap(other), both_cores(pos_near, zs, 1)

            near = flip(da_near, 1, size)
            mine, other, z_near = phase(inner, inside)
            g0 = sums_z(coords, v0)
            v1 = sums_y(coords, grads[1], size)

            def to_x2():
                dx2, dxr, sums2 = norm_grad((mine, other, near), x2, dy_mine, ln_gain[1:2], True)
                return dx2, (dxr, swap(dxr)), sums2

            return *phase(inner, to_x2), z_near, g0, v1

        dx2, dxr, sums2, z_near, g0, v1 = phase(pred, back)

        def last():
            return (
                phase(inner, lambda: bwd(coords, dxr, dx2, saved, pa, pb)), flip(z_near, 1, size),
                sums_z(coords, v1), sums_y(coords, grads[2], size),
            )

        (grad, sums1, ga0, ga1, gb0, gb1, bsum), z_near, g1, v2 = phase(pred, last)
        def sum_up():
            def out_rows():
                mine, other = unsort_tokens(pos_here, zs, 0, 2)
                z_sum = mine.astype(f32) + swap(other).astype(f32) + z_near.astype(f32)
                out = finish(x2, z_sum, bias_of)
                return out, swap(out), swap(grad)

            rows_all = phase(inner, lambda: small_rows(sums1, sums2, bsum, g_upb, g_down_bias))

            def small_start():
                total = rows_all + swap(rows_all)
                return total + flip(total, 1, size)

            got2 = deal_z(after(v2[1], rows_all))
            got_a, got_b = flip(ga1, 2, size), flip(gb1, 1, size)
            outs = phase(inner, out_rows)
            a_own, a_send, b_own, b_send = attn_sums_1((ga0, gb0), (got_a, got_b), outs)
            got_a, got_b = flip(a_send, 1, size), flip(b_send, 2, size)
            small = phase(inner, small_start)
            return attn_sums_2(coords, (a_own, b_own), (got_a, got_b), small), got2, small, outs

        (own, send), got2, small, (out, out_other, grad_other) = phase(pred, sum_up)

        got = deal_z(send)
        g2 = add_z(coords, v2[0], got2)
        near = flip(jnp.concatenate([v[1] for v in (g0, g1, g2)], axis=-1), 1, size)
        total = phase(inner, lambda: small + flip(small, 2, size))
        rows_z = [flip(total, 4 * rz, size) for rz in (1, 2, 3)]
        layer_output, grad_input = whole(
            rows_kernel, "rows", [((parts,) + v.shape, v.dtype) for v in (out, grad)],
            out, out_other, grad, grad_other, prefetch=(coords,),
        )
        g_qkv, g_out = whole(
            qkv_grad_kernel, "qkv_grad", [(w_qkv.shape, f32), (w_out.shape, f32)], own, got,
            prefetch=(after(coords, layer_output),),
        )
        last = after(coords, g_out)
        g_up, g_down = whole(
            expert_grad_kernel, "expert_grad", [(w_up.shape, f32)] * 2,
            g0[0], g1[0], g2[0], near, prefetch=(last,),
        )
        rows_z = jnp.stack([after(total, g_up)] + rows_z)
        pick = lambda z: lax.dynamic_index_in_dim(rows_z, last[0] ^ z, 0, False)
        small = pick(0) + pick(1) + pick(2) + pick(3)
    else:
        coords = jnp.stack([0, 0, 0, part]).astype(jnp.int32)
        x_mine, dy_mine, proj_bias, seg_row, windows, vec, ln1 = small_inputs()
        hid_start = part * hid
        hc = hid // CHUNKS
        up_b = lax.dynamic_slice_in_dim(up_bias, hid_start, hid, 1)
        pa, pb = gather_pieces_plain(w_qkv[:2], jnp.stack([w_qkv[2], w_out]))
        weights = expert_pieces_plain(w_up, w_down)
        mods, pos, plan_own = token_plan(segments, modality, experts)
        pos_row = pos.reshape(1, tokens)
        hot = (mods[:, None] == jnp.arange(experts, dtype=jnp.int32)).astype(bf16)
        g_down_bias = tn_dot(hot, dy)
        dys = sort_tokens([(pos_row, dy)], tiles, 0, 1)
        saved, x2, a2 = fwd(coords, pa, pb)
        xs = sort_tokens([(pos_row, share(a2).reshape(tokens, width))], tiles, 0, 1)
        carry = ()
        grads = []
        g_upb = []
        for call in CALLS:
            ub = up_b[:, None, call[0] * hc : (call[-1] + 1) * hc]
            zs, das, pairs, gub = ffn(
                coords, (plan_own,), xs, dys, ub, [weights[c] for c in call], carry
            )
            carry = (zs, das)
            g_upb.append(gub[:, 0])
            grads += pairs
        g_upb = jnp.concatenate(g_upb, axis=-1)
        g_up, g_down = jnp.concatenate([expert_sums_plain(pair) for pair in grads], axis=-1)
        own = deal(unsort_tokens([pos_row], das, 0, 1)[0].reshape(by_core))
        dx2, dxr, sums2 = norm_grad((own[0], own[1]), x2, dy_mine, ln_gain[1:2], True)
        grad_mine, sums1, ga0, ga1, gb0, gb1, bsum = bwd(
            coords, (dxr, swap(dxr)), dx2, saved, pa, pb
        )
        g_qk, g_vo = scatter_plain((ga0, ga1), (gb0, gb1))
        g_qkv, g_out = jnp.concatenate([g_qk, g_vo[:1]]), g_vo[1]
        own = deal(unsort_tokens([pos_row], zs, 0, 1)[0].reshape(by_core))
        layer_output = share(finish(x2, jnp.sum(own.astype(f32), axis=0), bias_rows(mods)))
        grad_input = share(grad_mine)
        small = lax.psum(small_rows(sums1, sums2, bsum, g_upb, g_down_bias), ("dp", "mp"))

    g_gain = jnp.stack([small[0], small[2]])
    g_lnb = jnp.stack([small[1], small[3]])
    return (
        layer_output.reshape(shape3),
        grad_input.reshape(shape3),
        g_gain,
        g_lnb,
        g_qkv,
        small[5 + experts : 7 + experts],
        g_out,
        small[4],
        g_up,
        small[7 + experts :].reshape(experts, up_bias.shape[1]),
        g_down,
        small[5 : 5 + experts],
    )


def solution(mesh):
    tok = P("dp", None, None)
    rep = P()
    wide = P(None, "dp", "mp")
    in_specs = (
        tok, P("dp", None), P("dp", None), rep, rep, wide, rep, P("dp", "mp"), rep, wide, rep,
        wide, rep, tok,
    )
    out_specs = (
        tok, tok, rep, rep, wide, rep, P("dp", "mp"), rep, wide, rep, wide, rep,
    )
    return jax.shard_map(body, mesh=mesh, in_specs=in_specs, out_specs=out_specs, check_vma=False)
```

```python
import functools
import math

import jax
import jax.numpy as jnp
from jax import lax
from jax.experimental import pallas as pl
from jax.experimental.pallas import tpu as pltpu
from jax.sharding import PartitionSpec as P

HD = 64
EPS = 1e-05
TILE = 256
CHUNKS = 3
SCALE = 1.0
CALLS = ((0, 1), (2,))
MIB = 1024 * 1024
LOG2E = math.log2(math.e)
f32 = jnp.float32
bf16 = jnp.bfloat16
ANY = pl.BlockSpec(memory_space=pl.ANY)


def full_spec(shape):
    zeros = (0,) * len(shape)
    return pl.BlockSpec(shape, lambda *_: zeros)


def nt_dot(a, b):
    return lax.dot_general(a, b, (((1,), (1,)), ((), ())), preferred_element_type=f32)


def nn_dot(a, b):
    return lax.dot_general(a, b, (((1,), (0,)), ((), ())), preferred_element_type=f32)


def tn_dot(a, b):
    return lax.dot_general(a, b, (((0,), (0,)), ((), ())), preferred_element_type=f32)


def params(grid_rank, mib=14):
    return pltpu.CompilerParams(
        dimension_semantics=("arbitrary",) * grid_rank, vmem_limit_bytes=mib * MIB
    )


def cost(flops, nbytes, trans=0):
    return pl.CostEstimate(
        flops=int(flops * SCALE), bytes_accessed=int(nbytes * SCALE), transcendentals=int(trans * SCALE)
    )


def place(c_ref, kind, outer, inner, rz):
    ry, rx = (outer, inner) if kind == "a" else (inner, outer)
    return (c_ref[0] ^ rz) * 4 + (c_ref[1] ^ ry) * 2 + (c_ref[2] ^ rx)


def piece_copies(c_ref, jobs, sems):
    copies = []
    for kind, pair, view, target in jobs:
        for outer in range(2):
            for inner in range(2):
                for rz in range(4):
                    rows = place(c_ref, kind, outer, inner, rz)
                    copies.append(
                        pltpu.make_async_copy(
                            view(pair[outer], inner, rz), target(rows), sems.at[len(copies)]
                        )
                    )
    return copies


def gelu_parts(u):
    mag = jnp.abs(u)
    t = 1.0 / (1.0 + (0.3275911 * math.sqrt(0.5)) * mag)
    poly = t * (
        0.254829592
        + t * (-0.284496736 + t * (1.421413741 + t * (-1.453152027 + t * 1.061405429)))
    )
    gauss = jnp.exp(-0.5 * u * u)
    half = 0.5 * poly * gauss
    cdf = jnp.where(u >= 0, 1.0 - half, half)
    return u * cdf, cdf + u * gauss * (1.0 / math.sqrt(2.0 * math.pi))


def norm_parts(v):
    mean = jnp.mean(v, axis=-1, keepdims=True)
    cent = v - mean
    var = jnp.mean(cent * cent, axis=-1, keepdims=True)
    rstd = lax.rsqrt(var + EPS)
    return cent * rstd, rstd


def norm_back(d_out, xhat, rstd, gain):
    d_hat = d_out * gain
    m1 = jnp.mean(d_hat, axis=-1, keepdims=True)
    m2 = jnp.mean(d_hat * xhat, axis=-1, keepdims=True)
    return rstd * (d_hat - m1 - xhat * m2)


def two_heads(v):
    lane = lax.broadcasted_iota(jnp.int32, v.shape, 1)
    none = jnp.zeros_like(v)
    return jnp.concatenate([jnp.where(lane < HD, v, none), jnp.where(lane >= HD, v, none)], axis=0)


def fill_bias(srow_ref, bias_s):
    seq = bias_s.shape[0]
    column = jnp.broadcast_to(srow_ref[0], (128, seq)).T
    for k in range(0, seq, 128):
        bias_s[:, k : k + 128] = jnp.where(column == srow_ref[0, :, k : k + 128], 0.0, -1e30)


def each_window(win_ref, row, blocks, f):
    @pl.loop(0, blocks)
    def _(j):
        first = win_ref[(row * blocks + j) * 2]
        n = win_ref[(row * blocks + j) * 2 + 1]
        for size in range(1, blocks + 1):

            @pl.when(n == size)
            def _():
                f(j, first, size)


def key_windows(segments):
    first, last = segments[:, ::128], segments[:, 127::128]
    low = jnp.sum((last[:, None, :] < first[:, :, None]).astype(jnp.int32), axis=-1)
    high = jnp.sum((first[:, None, :] <= last[:, :, None]).astype(jnp.int32), axis=-1)
    return jnp.stack([low, high - low], axis=-1).reshape(-1)


def attn_fwd_kernel(
    heads, piece, c_ref, win_ref, x_ref, srow_ref, ln_ref, pb_ref, a0, a1_, b0, b1_,
    att_ref, att_other_ref, qkv_ref, kt_ref, o_ref, ot_ref, lse_ref,
    w_s, wo_s, bias_s, vt_s, a1_s, sems,
):
    cols = heads * HD
    pairs = cols // 128
    seq, width = x_ref.shape[1], x_ref.shape[2]

    def into(block, j):
        return w_s.at[pl.ds(pl.multiple_of(block * piece, 16), piece), pl.ds(j * cols, cols)]

    def into_out(block):
        return wo_s.at[pl.ds(pl.multiple_of(block * piece, 16), piece), :]

    jobs = [
        ("a", (a0, a1_), lambda r, i, z: r.at[i, z, 0], lambda k: into(k, 0)),
        ("a", (a0, a1_), lambda r, i, z: r.at[i, z, 1], lambda k: into(k, 1)),
        ("b", (b0, b1_), lambda r, i, z: r.at[i, z, 0], lambda k: into(k, 2)),
        ("b", (b0, b1_), lambda r, i, z: r.at[i, z, 1], into_out),
    ]
    copies = piece_copies(c_ref, jobs, sems)

    @pl.when(pl.program_id(0) == 0)
    def _():
        for c in copies:
            c.start()

    xhat, _ = norm_parts(x_ref[0].astype(f32))
    a1_s[...] = (xhat * ln_ref[0:1] + ln_ref[1:2]).astype(bf16)
    fill_bias(srow_ref, bias_s)

    @pl.when(pl.program_id(0) == 0)
    def _():
        for c in copies:
            c.wait()

    a1 = a1_s[...]
    proj = (nn_dot(a1, w_s[...]) + pb_ref[...]).astype(bf16)
    for j in range(3):
        for p in range(pairs):
            qkv_ref[0, j, p] = proj[:, j * cols + p * 128 : j * cols + (p + 1) * 128]
    for p in range(pairs):
        kt_ref[0, p] = proj[:, cols + p * 128 : cols + (p + 1) * 128].T
        vt_s[p] = proj[:, 2 * cols + p * 128 : 2 * cols + (p + 1) * 128].T
    scale2 = HD ** (-0.5) * LOG2E

    def block(j, start, n):
        keys = pl.ds(pl.multiple_of(start * 128, 128), n * 128)
        mine = pl.ds(pl.multiple_of(j * 128, 128), 128)
        bias = bias_s[keys, mine]
        bias = jnp.concatenate([bias, bias], axis=1)
        every = range(pairs)
        s_t = [
            nt_dot(qkv_ref[0, 1, p, keys, :], two_heads(qkv_ref[0, 0, p, mine, :])) + bias
            for p in every
        ]
        top = [jnp.max(v, axis=0, keepdims=True) for v in s_t]
        e_t = [jnp.exp2((v - m) * scale2) for v, m in zip(s_t, top)]
        total = [jnp.sum(v, axis=0, keepdims=True) for v in e_t]
        p_t = [(v * (1.0 / t)).astype(bf16) for v, t in zip(e_t, total)]
        o_t = [nn_dot(vt_s[p, :, keys], p_t[p]).astype(bf16) for p in every]
        for p in every:
            ot_ref[0, p, :HD, mine] = o_t[p][:HD, :128]
            ot_ref[0, p, HD:, mine] = o_t[p][HD:, 128:]
            lse = top[p] * scale2 + jnp.log2(total[p])
            lse_ref[0, p, 0:1, mine] = lse[:, :128]
            lse_ref[0, p, 1:2, mine] = lse[:, 128:]

    each_window(win_ref, pl.program_id(0), seq // 128, block)

    for p in range(pairs):
        o_ref[0, :, p * 128 : (p + 1) * 128] = ot_ref[0, p].T
    att = nt_dot(o_ref[0], wo_s[...]).astype(bf16)

    @pl.when(pl.program_id(0) == c_ref[3])
    def _():
        att_ref[...] = att

    @pl.when(pl.program_id(0) != c_ref[3])
    def _():
        att_other_ref[...] = att


def attn_fwd(coords, windows, x, seg_row, ln, proj_bias, pa, pb):
    rows, seq, width = x.shape
    cols = proj_bias.shape[-1] // 3
    heads = cols // HD
    pairs = cols // 128
    piece = pa[0].shape[-2]
    row3 = lambda r, *_: (r, 0, 0)
    row4 = lambda r, *_: (r, 0, 0, 0)
    row5 = lambda r, *_: (r, 0, 0, 0, 0)
    outs = [
        ((seq, width), bf16, (seq, width), lambda *_: (0, 0)),
        ((seq, width), bf16, (seq, width), lambda *_: (0, 0)),
        ((rows, 3, pairs, seq, 128), bf16, (1, 3, pairs, seq, 128), row5),
        ((rows, pairs, 128, seq), bf16, (1, pairs, 128, seq), row4),
        ((rows, seq, cols), bf16, (1, seq, cols), row3),
        ((rows, pairs, 128, seq), bf16, (1, pairs, 128, seq), row4),
        ((rows, pairs, 2, seq), f32, (1, pairs, 2, seq), row4),
    ]
    return pl.pallas_call(
        functools.partial(attn_fwd_kernel, heads, piece),
        out_shape=[jax.ShapeDtypeStruct(s, d) for s, d, _, _ in outs],
        grid_spec=pltpu.PrefetchScalarGridSpec(
            num_scalar_prefetch=2,
            grid=(rows,),
            in_specs=[
                pl.BlockSpec((1, seq, width), row3),
                pl.BlockSpec((1, 1, seq), row3),
                full_spec((2, width)),
                full_spec((1, 3 * cols)),
                ANY, ANY, ANY, ANY,
            ],
            out_specs=[pl.BlockSpec(b, m) for _, _, b, m in outs],
            scratch_shapes=[
                pltpu.VMEM((width, 3 * cols), bf16),
                pltpu.VMEM((width, cols), bf16),
                pltpu.VMEM((seq, seq), f32),
                pltpu.VMEM((pairs, 128, seq), bf16),
                pltpu.VMEM((seq, width), bf16),
                pltpu.SemaphoreType.DMA((64,)),
            ],
        ),
        compiler_params=params(1, 22),
        cost_estimate=cost(2e10, 1e7, 3e6),
        name="attn_fwd",
    )(coords, windows, x, seg_row, ln, proj_bias, *pa, *pb)


def attn_bwd_kernel(
    heads, piece, c_ref, win_ref, dxr_ref, dxr2_ref, x_ref, srow_ref, ln_ref, qkv_ref, kt_ref, o_ref, ot_ref, lse_ref, a0, a1_, b0, b1_,
    da1_ref, da1_other_ref, ga0_ref, ga1_ref, gb0_ref, gb1_ref, bsum_ref,
    w_s, wo_s, bias_s, dp_s, gw_s, go_s, do_s, row_s, dk_s, dv_s, dqt_s, a1_s, dxr_s, o_s, sems,
):
    cols = heads * HD
    pairs = cols // 128
    seq = x_ref.shape[1]
    step = pl.program_id(0)

    def into(block, j):
        return w_s.at[pl.ds(pl.multiple_of(block * piece, 16), piece), pl.ds(j * cols, cols)]

    def into_out(block):
        return wo_s.at[pl.ds(pl.multiple_of(block * piece, 16), piece), :]

    jobs = [
        ("a", (a0, a1_), lambda r, i, z: r.at[i, z, 0], lambda k: into(k, 0)),
        ("a", (a0, a1_), lambda r, i, z: r.at[i, z, 1], lambda k: into(k, 1)),
        ("b", (b0, b1_), lambda r, i, z: r.at[i, z, 0], lambda k: into(k, 2)),
        ("b", (b0, b1_), lambda r, i, z: r.at[i, z, 1], into_out),
    ]
    copies = piece_copies(c_ref, jobs, sems)

    @pl.when(step == 0)
    def _():
        for c in copies:
            c.start()
        bsum_ref[...] = jnp.zeros_like(bsum_ref)

    xhat1, _ = norm_parts(x_ref[0].astype(f32))
    here = pl.ds(pl.multiple_of(step * seq, 128), seq)
    a1_s[here, :] = (xhat1 * ln_ref[0:1] + ln_ref[1:2]).astype(bf16)
    o_s[here, :] = o_ref[0]
    fill_bias(srow_ref, bias_s)

    @pl.when(step == 0)
    def _():
        for c in copies:
            c.wait()

    dxr = jnp.where(step == c_ref[3], dxr_ref[...], dxr2_ref[...])
    do = nn_dot(dxr, wo_s[...]).astype(bf16)
    dxr_s[here, :] = dxr
    scale = HD ** (-0.5)
    scale2 = scale * LOG2E
    do_s[...] = do
    for p in range(pairs):
        prod = do[:, p * 128 : (p + 1) * 128].T.astype(f32) * ot_ref[0, p].astype(f32)
        for h in range(2):
            row_s[p, h : h + 1] = jnp.sum(prod[h * HD : (h + 1) * HD], axis=0, keepdims=True)
    dk_s[...] = jnp.zeros_like(dk_s)
    dv_s[...] = jnp.zeros_like(dv_s)

    def block(j, start, n):
        keys = pl.ds(pl.multiple_of(start * 128, 128), n * 128)
        mine = pl.ds(pl.multiple_of(j * 128, 128), 128)
        pair = lambda ref: jnp.concatenate([ref[0:1, mine], ref[1:2, mine]], axis=1)
        every = range(pairs)
        bias = bias_s[keys, mine]
        bias = jnp.concatenate([bias, bias], axis=1)
        q_2 = [two_heads(qkv_ref[0, 0, p, mine, :]) for p in every]
        do_2 = [two_heads(do_s[mine, p * 128 : (p + 1) * 128]) for p in every]
        s_t = [nt_dot(qkv_ref[0, 1, p, keys, :], q_2[p]) * scale2 for p in every]
        d_t = [nt_dot(qkv_ref[0, 2, p, keys, :], do_2[p]) - pair(row_s.at[p]) for p in every]
        p_t = [jnp.exp2(s_t[p] + (bias - pair(lse_ref.at[0, p]))) for p in every]
        for p in every:
            dv_s[p, keys, :] += nn_dot(p_t[p].astype(bf16), do_2[p])
        ds_t = [(p_t[p] * d_t[p]).astype(bf16) for p in every]
        for p in every:
            dk_s[p, keys, :] += nn_dot(ds_t[p], q_2[p])
            dq_t = (nn_dot(kt_ref[0, p, :, keys], ds_t[p]) * scale).astype(bf16)
            dqt_s[p, :HD, mine] = dq_t[:HD, :128]
            dqt_s[p, HD:, mine] = dq_t[HD:, 128:]

    each_window(win_ref, step, seq // 128, block)

    for p in range(pairs):
        dp_s[here, p * 128 : (p + 1) * 128] = dqt_s[p].T
        dp_s[here, cols + p * 128 : cols + (p + 1) * 128] = (dk_s[p] * scale).astype(bf16)
        dp_s[here, 2 * cols + p * 128 : 2 * cols + (p + 1) * 128] = dv_s[p].astype(bf16)

    dproj = dp_s[here, :]
    da1 = nt_dot(dproj, w_s[...]).astype(bf16)

    @pl.when(step == c_ref[3])
    def _():
        da1_ref[...] = da1

    @pl.when(step != c_ref[3])
    def _():
        da1_other_ref[...] = da1

    bsum_ref[...] += jnp.sum(dproj.astype(f32), axis=0, keepdims=True)

    @pl.when(step == pl.num_programs(0) - 1)
    def _():
        gw_s[...] = tn_dot(a1_s[...], dp_s[...]).astype(bf16)
        go_s[...] = tn_dot(dxr_s[...], o_s[...]).astype(bf16)
        for outer in range(2):
            for inner in range(2):
                for rz in range(4):
                    ra = pl.ds(pl.multiple_of(place(c_ref, "a", outer, inner, rz) * piece, 16), piece)
                    rb = pl.ds(pl.multiple_of(place(c_ref, "b", outer, inner, rz) * piece, 16), piece)
                    ga, gb = ((ga0_ref, gb0_ref), (ga1_ref, gb1_ref))[outer]
                    ga[inner, rz, 0] = gw_s[ra, :cols]
                    ga[inner, rz, 1] = gw_s[ra, cols : 2 * cols]
                    gb[inner, rz, 0] = gw_s[rb, 2 * cols :]
                    gb[inner, rz, 1] = go_s[rb, :]


def attn_bwd(coords, windows, dxr, dxr2, x, seg_row, ln, saved, pa, pb):
    rows, seq, width = x.shape
    qkv, kt, o, ot, lse = saved
    cols = o.shape[-1]
    heads = cols // HD
    pairs = cols // 128
    piece = pa[0].shape[-2]
    row3 = lambda r, *_: (r, 0, 0)
    row4 = lambda r, *_: (r, 0, 0, 0)
    row5 = lambda r, *_: (r, 0, 0, 0, 0)
    tok = pl.BlockSpec((1, seq, width), row3)
    gshape = pa[0].shape
    return pl.pallas_call(
        functools.partial(attn_bwd_kernel, heads, piece),
        out_shape=[
            *[jax.ShapeDtypeStruct((seq, width), bf16)] * 2,
            *[jax.ShapeDtypeStruct(gshape, bf16)] * 4,
            jax.ShapeDtypeStruct((1, 3 * cols), f32),
        ],
        grid_spec=pltpu.PrefetchScalarGridSpec(
            num_scalar_prefetch=2,
            grid=(rows,),
            in_specs=[
                full_spec((seq, width)), full_spec((seq, width)), tok,
                pl.BlockSpec((1, 1, seq), row3),
                full_spec((2, width)),
                pl.BlockSpec((1, 3, pairs, seq, 128), row5),
                pl.BlockSpec((1, pairs, 128, seq), row4),
                pl.BlockSpec((1, seq, cols), row3),
                pl.BlockSpec((1, pairs, 128, seq), row4),
                pl.BlockSpec((1, pairs, 2, seq), row4),
                ANY, ANY, ANY, ANY,
            ],
            out_specs=[
                *[full_spec((seq, width))] * 2,
                *[full_spec(gshape)] * 4,
                full_spec((1, 3 * cols)),
            ],
            scratch_shapes=[
                pltpu.VMEM((width, 3 * cols), bf16),
                pltpu.VMEM((width, cols), bf16),
                pltpu.VMEM((seq, seq), f32),
                pltpu.VMEM((rows * seq, 3 * cols), bf16),
                pltpu.VMEM((width, 3 * cols), bf16),
                pltpu.VMEM((width, cols), bf16),
                pltpu.VMEM((seq, cols), bf16),
                pltpu.VMEM((pairs, 2, seq), f32),
                pltpu.VMEM((pairs, seq, 128), f32),
                pltpu.VMEM((pairs, seq, 128), f32),
                pltpu.VMEM((pairs, 128, seq), bf16),
                pltpu.VMEM((rows * seq, width), bf16),
                pltpu.VMEM((rows * seq, width), bf16),
                pltpu.VMEM((rows * seq, cols), bf16),
                pltpu.SemaphoreType.DMA((64,)),
            ],
        ),
        compiler_params=params(1, 30),
        cost_estimate=cost(4e10, 2e7, 3e6),
        name="attn_bwd",
    )(coords, windows, dxr, dxr2, x, seg_row, ln, qkv, kt, o, ot, lse, *pa, *pb)


def sort_kernel(sources, *refs):
    vs_ref = refs[-1]
    block = vs_ref.shape[0]
    total = None
    for k in range(sources):
        pos_row, v_ref = refs[2 * k], refs[2 * k + 1]
        slot = lax.broadcasted_iota(jnp.int32, (block, v_ref.shape[0]), 0)
        slot = slot + pl.program_id(0) * block
        pick = (slot == pos_row[...]).astype(f32).astype(bf16)
        part = nn_dot(pick, v_ref[...])
        total = part if total is None else total + part
    vs_ref[...] = total.astype(bf16)


def sort_tokens(sources, tiles, group, groups, into=None):
    width = sources[0][1].shape[1]
    tokens = sum(v.shape[0] for _, v in sources)
    slots = tiles * TILE
    steps = 2
    block = slots // steps
    flat = [x for pair in sources for x in pair]
    return pl.pallas_call(
        functools.partial(sort_kernel, len(sources)),
        out_shape=jax.ShapeDtypeStruct((groups * slots, width), bf16),
        grid=(steps,),
        in_specs=[*[full_spec(x.shape) for x in flat], *([] if into is None else [ANY])],
        out_specs=pl.BlockSpec((block, width), lambda i: (i + group * steps, 0)),
        input_output_aliases={} if into is None else {len(flat): 0},
        compiler_params=params(1),
        cost_estimate=cost(2 * slots * tokens * width, 1e7),
        name="sort_tokens",
    )(*flat, *([] if into is None else [into]))


def unsort_kernel(targets, *refs):
    vs = refs[targets][...]
    for k in range(targets):
        pos_row, out_ref = refs[k], refs[targets + 1 + k]
        slot = lax.broadcasted_iota(jnp.int32, (vs.shape[0], out_ref.shape[0]), 0)
        pick = (slot == pos_row[...]).astype(f32).astype(bf16)
        out_ref[...] = tn_dot(pick, vs).astype(bf16)


def unsort_tokens(places, vs, group, groups):
    width = vs.shape[1]
    slots = vs.shape[0] // groups
    tokens = sum(p.shape[1] for p in places)
    return pl.pallas_call(
        functools.partial(unsort_kernel, len(places)),
        out_shape=[jax.ShapeDtypeStruct((p.shape[1], width), bf16) for p in places],
        grid=(1,),
        in_specs=[
            *[full_spec(p.shape) for p in places],
            pl.BlockSpec((slots, width), lambda i: (group, 0)),
        ],
        out_specs=[full_spec((p.shape[1], width)) for p in places],
        compiler_params=params(1),
        cost_estimate=cost(2 * slots * tokens * width, 1e7),
        name="unsort_tokens",
    )(*places, vs)


def mid_kernel(x_ref, own_ref, got_ref, vec_ref, x2_ref, a2_ref):
    x2 = x_ref[...].astype(f32) + (own_ref[...].astype(f32) + got_ref[...].astype(f32)) + vec_ref[0:1]
    x2_ref[...] = x2
    xhat, _ = norm_parts(x2)
    a2_ref[...] = (xhat * vec_ref[1:2] + vec_ref[2:3]).astype(bf16)


def mid(x, own, got, vec):
    tokens, width = x.shape
    tile = pl.BlockSpec((TILE, width), lambda i: (i, 0))
    return pl.pallas_call(
        mid_kernel,
        out_shape=[
            jax.ShapeDtypeStruct((tokens, width), f32),
            jax.ShapeDtypeStruct((tokens, width), bf16),
        ],
        grid=(tokens // TILE,),
        in_specs=[tile, tile, tile, full_spec((3, width))],
        out_specs=[tile, tile],
        compiler_params=params(1),
        cost_estimate=cost(1e7, 5e6),
        name="mid_norm",
    )(x, own, got, vec)


def ffn_kernel(first, count, piece, groups, near, c_ref, plan0_ref, plan1_ref, *refs):
    xs_ref, dys_ref, ub_ref, *rest = refs
    if near:
        pos_refs, rest = rest[:2], rest[2:]
    if not first:
        zin_ref, din_ref, *rest = rest
    w_refs = [rest[2 * c : 2 * c + 2] for c in range(count)]
    rest = rest[2 * count :]
    z_ref, da_ref, *rest = rest
    if near:
        near_refs, rest = rest[:2], rest[2:]
    g_refs = [rest[2 * c : 2 * c + 2] for c in range(count)]
    gub_ref, wu_s, wd_s, gu_s, gd_s, x_s, dy_s, z_s, da_s, sems, in_sems, out_sems = rest[2 * count :]
    experts = wu_s.shape[0]
    hc = wu_s.shape[2] // count
    tiles = x_s.shape[0]
    per = tiles // groups
    spots = [(ry, rz, rx) for ry in range(2) for rz in range(4) for rx in range(2)]

    def rows_of(ry, rz, rx):
        block = rz * 4 + (c_ref[1] ^ ry) * 2 + (c_ref[2] ^ rx)
        return pl.ds(pl.multiple_of(block * piece, 16), piece)

    def tile_of(ref, i):
        return ref.at[pl.ds(pl.multiple_of(i * TILE, TILE), TILE), :]

    def reads(i):
        pairs = [(xs_ref, x_s), (dys_ref, dy_s)]
        if not first:
            pairs += [(zin_ref, z_s), (din_ref, da_s)]
        return [
            pltpu.make_async_copy(tile_of(src, i), dst.at[i], in_sems.at[k, i])
            for k, (src, dst) in enumerate(pairs)
        ]

    def writes(i):
        return [
            pltpu.make_async_copy(src.at[i], tile_of(dst, i), out_sems.at[k, i])
            for k, (src, dst) in enumerate([(z_s, z_ref), (da_s, da_ref)])
        ]

    copies = []
    for c in range(count):
        for ry, rz, rx in spots:
            for k, w_s in ((0, wu_s), (1, wd_s)):
                copies.append(
                    pltpu.make_async_copy(
                        w_refs[c][ry].at[rz, rx, k],
                        w_s.at[:, rows_of(ry, rz, rx), pl.ds(c * hc, hc)],
                        sems.at[len(copies)],
                    )
                )
    for c in reads(0):
        c.start()
    for c in copies:
        c.start()

    @pl.loop(1, tiles)
    def _(i):
        for c in reads(i):
            c.start()

    gu_s[...] = jnp.zeros_like(gu_s)
    gd_s[...] = jnp.zeros_like(gd_s)
    gub_ref[...] = jnp.zeros_like(gub_ref)
    for c in copies:
        c.wait()

    @pl.loop(0, tiles)
    def _(i):
        group = i // per
        k = i - group * per
        info = lambda at: jnp.where(group == 0, plan0_ref[at], plan1_ref[at])
        tokens = plan0_ref.shape[0] - per - 1
        live = k < info(tokens + per)
        for c in reads(i):
            c.wait()

        @pl.when(live)
        def _():
            e = info(tokens + k)
            x = x_s[i]
            dy = dy_s[i]
            u = nn_dot(x, wu_s[e]) + ub_ref[e]
            act, slope = gelu_parts(u)
            act = act.astype(bf16)
            du = (nn_dot(dy, wd_s[e]) * slope).astype(bf16)
            z = nt_dot(act, wd_s[e])
            da = nt_dot(du, wu_s[e])
            if not first:
                z = z + z_s[i].astype(f32)
                da = da + da_s[i].astype(f32)
            z_s[i] = z.astype(bf16)
            da_s[i] = da.astype(bf16)
            gd_s[e] += tn_dot(dy, act)
            gu_s[e] += tn_dot(x, du)
            gub_ref[e] += jnp.sum(du.astype(f32), axis=0, keepdims=True)

        @pl.when(jnp.logical_not(live))
        def _():
            z_s[i] = jnp.zeros(z_s.shape[1:], bf16)
            da_s[i] = jnp.zeros(da_s.shape[1:], bf16)

        for c in writes(i):
            c.start()

    if near:
        rows = da_s[per:].reshape(per * TILE, da_s.shape[2])
        for pos_ref, out_ref in zip(pos_refs, near_refs):
            slot = lax.broadcasted_iota(jnp.int32, (per * TILE, out_ref.shape[0]), 0)
            pick = (slot == pos_ref[...]).astype(f32).astype(bf16)
            out_ref[...] = tn_dot(pick, rows).astype(bf16)

    for c in range(count):
        lanes = pl.ds(c * hc, hc)
        for ry, rz, rx in spots:
            rows = rows_of(ry, rz, rx)
            for e in range(experts):
                g_refs[c][ry][rz, rx, 0, e] = gu_s[e, rows, lanes].astype(bf16)
                g_refs[c][ry][rz, rx, 1, e] = gd_s[e, rows, lanes].astype(bf16)

    @pl.loop(0, tiles)
    def _(i):
        for c in writes(i):
            c.wait()


def ffn(coords, plans, xs, dys, up_b, weights, carry, places=()):
    slots, width = xs.shape
    tiles = slots // TILE
    groups = len(plans)
    first = not carry
    count = len(weights)
    gshape = weights[0][0].shape
    experts, piece, hc = gshape[3:]
    hid = hc * count
    out = pl.pallas_call(
        functools.partial(ffn_kernel, first, count, piece, groups, bool(places)),
        out_shape=[
            jax.ShapeDtypeStruct((slots, width), bf16),
            jax.ShapeDtypeStruct((slots, width), bf16),
            *[jax.ShapeDtypeStruct((p.shape[1], width), bf16) for p in places],
            *[jax.ShapeDtypeStruct(gshape, bf16)] * (2 * count),
            jax.ShapeDtypeStruct((experts, 1, hid), f32),
        ],
        grid_spec=pltpu.PrefetchScalarGridSpec(
            num_scalar_prefetch=3,
            grid=(1,),
            in_specs=[
                ANY, ANY, full_spec((experts, 1, hid)), *[full_spec(p.shape) for p in places],
                *([] if first else [ANY, ANY]), *[ANY] * (2 * count),
            ],
            out_specs=[
                ANY, ANY, *[full_spec((p.shape[1], width)) for p in places], *[full_spec(gshape)] * (2 * count),
                full_spec((experts, 1, hid)),
            ],
            scratch_shapes=[
                *[pltpu.VMEM((experts, width, hid), bf16)] * 2,
                *[pltpu.VMEM((experts, width, hid), f32)] * 2,
                *[pltpu.VMEM((tiles, TILE, width), bf16)] * 4,
                pltpu.SemaphoreType.DMA((32 * count,)),
                pltpu.SemaphoreType.DMA((2 if first else 4, tiles)),
                pltpu.SemaphoreType.DMA((2, tiles)),
            ],
        ),
        compiler_params=params(1, 42 if groups == 2 else 60),
        cost_estimate=cost(12 * slots * width * hid * 1.5, 4e7, 2 * slots * hid),
        name="ffn",
    )(coords, plans[0], plans[-1], xs, dys, up_b, *places, *carry, *[w for pair in weights for w in pair])
    zs, das, *rest = out
    rows, rest = rest[: len(places)], rest[len(places) :]
    if places:
        return zs, das, [rest[2 * c : 2 * c + 2] for c in range(count)], rest[2 * count], rows
    return zs, das, [rest[2 * c : 2 * c + 2] for c in range(count)], rest[2 * count]


def norm_grad_kernel(count, low, *refs):
    parts, (v_ref, add_ref, gain_ref, out_ref, *refs) = refs[:count], refs[count:]
    sums_ref = refs[-1]

    @pl.when(pl.program_id(0) == 0)
    def _():
        sums_ref[...] = jnp.zeros_like(sums_ref)

    grad = sum(
        jnp.sum(p[...].astype(f32), axis=0) if len(p.shape) == 3 else p[...].astype(f32) for p in parts
    )
    xhat, rstd = norm_parts(v_ref[...].astype(f32))
    out = add_ref[...].astype(f32) + norm_back(grad, xhat, rstd, gain_ref[...])
    out_ref[...] = out
    if low:
        refs[0][...] = out.astype(bf16)
    sums_ref[0:1] += jnp.sum(grad * xhat, axis=0, keepdims=True)
    sums_ref[1:2] += jnp.sum(grad, axis=0, keepdims=True)
    sums_ref[2:3] += jnp.sum(out, axis=0, keepdims=True)


def norm_grad(partial, v, add, gain, low):
    tokens, width = v.shape
    tile = pl.BlockSpec((TILE, width), lambda i: (i, 0))
    return pl.pallas_call(
        functools.partial(norm_grad_kernel, len(partial), low),
        out_shape=[
            jax.ShapeDtypeStruct((tokens, width), f32),
            *([jax.ShapeDtypeStruct((tokens, width), bf16)] if low else []),
            jax.ShapeDtypeStruct((8, width), f32),
        ],
        grid=(tokens // TILE,),
        in_specs=[
            *[
                pl.BlockSpec((p.shape[0], TILE, width), lambda i: (0, i, 0)) if p.ndim == 3 else tile
                for p in partial
            ],
            tile, tile, full_spec((1, width)),
        ],
        out_specs=[tile, *([tile] if low else []), full_spec((8, width))],
        compiler_params=params(1),
        cost_estimate=cost(2e7, 8e6),
        name="norm_grad",
    )(*partial, v, add, gain)


def whole(kernel, name, outs, *args, prefetch=()):
    return pl.pallas_call(
        kernel,
        out_shape=[jax.ShapeDtypeStruct(s, d) for s, d in outs],
        grid_spec=pltpu.PrefetchScalarGridSpec(
            num_scalar_prefetch=len(prefetch),
            grid=(1,),
            in_specs=[full_spec(x.shape) for x in args],
            out_specs=[full_spec(s) for s, _ in outs],
        ),
        compiler_params=params(1),
        cost_estimate=cost(1e6, 4e6),
        name=name,
    )(*prefetch, *args)


def sums_y_kernel(c_ref, keep, got, own, send):
    for k in range(4):
        send[k] = (keep[k].astype(f32) + got[k].astype(f32)).astype(bf16)
    here = c_ref[0]
    own[...] = keep[here].astype(f32) + got[here].astype(f32)


def sums_z_kernel(c_ref, own, got, mine, near):
    others = [c_ref[0] ^ rz for rz in (1, 2, 3)]
    add = lambda k: own[k] + sum(got[z, k].astype(f32) for z in others)
    mine[...] = add(0)
    near[...] = add(1).astype(bf16)


def two_sums_kernel(a_keep, a_got, b_keep, b_got, a_own, a_send, b_own, b_send):
    for keep, got, own, send in ((a_keep, a_got, a_own, a_send), (b_keep, b_got, b_own, b_send)):
        own[...] = keep[0].astype(f32) + got[0].astype(f32)
        send[...] = (keep[1].astype(f32) + got[1].astype(f32)).astype(bf16)


def four_sums_kernel(c_ref, a_own, a_got, b_own, b_got, own, send):
    for rz in range(4):
        va = a_own[rz] + a_got[rz].astype(f32)
        vb = b_own[rz] + b_got[rz].astype(f32)
        if rz == 0:
            own[0], own[1] = va, vb
        send[c_ref[0] ^ rz, 0] = va.astype(bf16)
        send[c_ref[0] ^ rz, 1] = vb.astype(bf16)


def qkv_grad_kernel(c_ref, own, got, g_qkv, g_out):
    others = [c_ref[0] ^ rz for rz in (1, 2, 3)]
    add = lambda k, j: own[k, j] + sum(got[z, k, j].astype(f32) for z in others)
    g_qkv[0] = add(0, 0)
    g_qkv[1] = add(0, 1)
    g_qkv[2] = add(1, 0)
    g_out[...] = add(1, 1)


def rows_kernel(c_ref, *refs):
    n = len(refs) // 3
    for k in range(n):
        mine, other, out = refs[2 * k], refs[2 * k + 1], refs[2 * n + k]
        out[c_ref[3]] = mine[...]
        out[1 - c_ref[3]] = other[...]


def expert_grad_kernel(c_ref, *refs):
    *mines, near, g_up, g_down = refs
    hc = mines[0].shape[-1]
    half = hc * len(mines)
    here = pl.multiple_of(c_ref[2] * half, 128)
    there = pl.multiple_of((1 - c_ref[2]) * half, 128)
    for k, out in ((0, g_up), (1, g_down)):
        for c, mine in enumerate(mines):
            out[:, :, pl.ds(here + c * hc, hc)] = mine[k]
        out[:, :, pl.ds(there, half)] = near[k].astype(f32)


def flip(x, mask, size):
    return lax.ppermute(x, "dp", [(i, i ^ mask) for i in range(size)])


def after(v, *deps):
    return lax.optimization_barrier((v, deps))[0]


def deal(v):
    return lax.all_to_all(v, "mp", 0, 0)


def swap(v):
    return lax.ppermute(v, "mp", [(0, 1), (1, 0)])


def share(v):
    return deal(jnp.broadcast_to(v, (lax.axis_size("mp"),) + v.shape))


def gather_z(a, b, size):
    both = jnp.stack([a, b])
    blocks = [both] + [flip(both, 4 * rz, size) for rz in (1, 2, 3)]
    return jnp.stack([v[0] for v in blocks]), jnp.stack([v[1] for v in blocks])


def gather_xy(a0, b0, dep, size):
    a0 = jnp.stack([after(a0, dep), flip(a0, 1, size)])
    b0 = jnp.stack([b0, flip(b0, 2, size)])
    return (a0, flip(a0, 2, size)), (b0, flip(b0, 1, size))


def attn_sums_1(keep, got, dep):
    shape = keep[0].shape[1:]
    return whole(
        two_sums_kernel, "two_sums", [(shape, f32), (shape, bf16)] * 2,
        after(keep[0], dep), got[0], keep[1], got[1],
    )


def attn_sums_2(coords, own, got, dep):
    shape = (2,) + own[0].shape[1:]
    return whole(
        four_sums_kernel, "four_sums", [(shape, f32), ((4,) + shape, bf16)],
        own[0], got[0], own[1], got[1], prefetch=(after(coords, dep),),
    )


def gather_plain(w):
    full = lax.all_gather(w, "dp", axis=1, tiled=True)
    n, rows, cols = full.shape
    return full.reshape(n, 16, rows // 16, cols).swapaxes(0, 1)


def gather_pieces_plain(a, b):
    blocks = [gather_plain(v) for v in (a, b)]
    blocks = [v.reshape((4, 2, 2) + v.shape[1:]) for v in blocks]
    fa = jnp.moveaxis(blocks[0], 0, 2)
    fb = jnp.swapaxes(jnp.moveaxis(blocks[1], 0, 2), 0, 1)
    return (fa[0], fa[1]), (fb[0], fb[1])


def scatter_plain(ga, gb):
    fa = jnp.moveaxis(jnp.stack(ga), 2, 0)
    fb = jnp.moveaxis(jnp.swapaxes(jnp.stack(gb), 0, 1), 2, 0)
    outs = []
    for v in (fa, fb):
        v = v.reshape((16,) + v.shape[3:]).swapaxes(0, 1)
        v = v.reshape(v.shape[0], -1, v.shape[-1]).astype(f32)
        outs.append(lax.psum_scatter(v, "dp", scatter_dimension=1, tiled=True))
    return outs


def phase(pred, f):
    shapes = jax.eval_shape(f)
    return lax.cond(
        pred, f, lambda: jax.tree.map(lambda v: jnp.zeros(v.shape, v.dtype), shapes)
    )


def deal_z(v):
    groups = [[4 * z + k for z in range(4)] for k in range(4)]
    return lax.all_to_all(v, "dp", 0, 0, axis_index_groups=groups, tiled=True)


def four_times(p):
    return jnp.broadcast_to(p, (4,) + p.shape)


def sums_y(coords, pair, size):
    shape = pair[0].shape
    return whole(
        sums_y_kernel, "sums_y", [(shape[1:], f32), (shape, bf16)],
        pair[0], flip(pair[1], 2, size), prefetch=(coords,),
    )


def sums_z(coords, parts_y):
    own, send = parts_y
    return add_z(coords, own, deal_z(send))


def add_z(coords, own, got):
    shape = own.shape[1:]
    return whole(
        sums_z_kernel, "sums_z", [(shape, f32), (shape, bf16)], own, got, prefetch=(coords,)
    )


def expert_pieces_plain(w_up, w_down):
    hc = w_up.shape[-1] // CHUNKS
    blocks = jnp.stack([gather_plain(w_up), gather_plain(w_down)], axis=1)
    blocks = blocks.reshape((4, 2, 2) + blocks.shape[1:])
    return [
        tuple(blocks[:, ry, ..., c * hc : (c + 1) * hc] for ry in range(2)) for c in range(CHUNKS)
    ]


def expert_sums_plain(pair):
    v = jnp.stack(pair, axis=1)
    v = v.reshape((16,) + v.shape[3:])
    v = jnp.moveaxis(v, 0, 2)
    v = v.reshape(v.shape[:2] + (-1, v.shape[-1])).astype(f32)
    return lax.psum_scatter(v, "dp", scatter_dimension=2, tiled=True)


def token_plan(segments, modality, experts):
    tokens = segments.size
    doc_ids = jnp.arange(modality.shape[1], dtype=jnp.int32)
    match = segments[:, :, None] == doc_ids
    mods = jnp.sum(jnp.where(match, modality[:, None, :], 0), axis=-1).reshape(tokens)
    kinds = jnp.arange(experts, dtype=jnp.int32)
    hot = (mods[:, None] == kinds).astype(jnp.int32)
    ids = jnp.arange(tokens, dtype=jnp.int32)
    lower = (ids[:, None] > ids[None, :]).astype(bf16)
    before = jnp.dot(lower, hot.astype(bf16), preferred_element_type=f32).astype(jnp.int32)
    need = (jnp.sum(hot, axis=0) + TILE - 1) // TILE
    ends = jnp.sum(jnp.where(kinds[:, None] >= kinds[None, :], need[None, :], 0), axis=1)
    pos = jnp.sum(hot * (before + (ends - need)[None, :] * TILE), axis=1)
    tiles = (tokens + experts * (TILE - 1)) // TILE
    tile_ids = jnp.arange(tiles, dtype=jnp.int32)
    tile_expert = jnp.minimum(
        jnp.sum((tile_ids[:, None] >= ends[None, :]).astype(jnp.int32), axis=1), experts - 1
    )
    return mods, pos, jnp.concatenate([pos, tile_expert, ends[-1:]])


def body(
    layer_input, segments, modality, ln_gain, ln_bias, w_qkv, qv_bias, w_out, out_bias,
    w_up, up_bias, w_down, down_bias, cotangent,
):
    part = lax.axis_index("mp")
    parts = lax.axis_size("mp")
    size = lax.axis_size("dp")
    me = lax.axis_index("dp")
    rows, seq, width = layer_input.shape
    tokens = rows * seq
    cols = w_qkv.shape[-1]
    hid = w_up.shape[-1]
    experts = w_up.shape[0]
    shape3 = (rows, seq, width)
    tiles = (tokens + experts * (TILE - 1)) // TILE
    staged = size == 16

    mine_rows = rows // parts
    mine_tokens = tokens // parts
    by_core = (parts, mine_tokens, width)
    dy = cotangent.reshape(tokens, width)
    rows_here = lambda v: lax.dynamic_slice_in_dim(v, part * mine_rows, mine_rows, 0)
    col_start = part * cols

    def small_inputs():
        q_b = lax.dynamic_slice_in_dim(qv_bias[0], col_start, cols)
        v_b = lax.dynamic_slice_in_dim(qv_bias[1], col_start, cols)
        return (
            rows_here(layer_input).reshape(mine_tokens, width),
            rows_here(cotangent).reshape(mine_tokens, width),
            jnp.concatenate([q_b, jnp.zeros_like(q_b), v_b]).reshape(1, 3 * cols),
            segments.reshape(rows, 1, seq),
            key_windows(segments),
            jnp.concatenate([out_bias[None], ln_gain[1:2], ln_bias[1:2]]),
            jnp.concatenate([ln_gain[0:1], ln_bias[0:1]]),
        )

    def fwd(coords, pa, pb):
        own, other, *saved = attn_fwd(coords, windows, layer_input, seg_row, ln1, proj_bias, pa, pb)
        return (saved, *mid(x_mine, own, swap(other), vec))

    def bwd(coords, dxr, dx2, saved, pa, pb):
        own, other, *rest = attn_bwd(
            coords, windows, *dxr, layer_input, seg_row, ln1, saved, pa, pb
        )
        return (*norm_grad((own, swap(other)), x_mine, dx2, ln_gain[0:1], False), *rest)

    def halves(v):
        take = lambda k: lax.dynamic_slice_in_dim(v, k * mine_tokens, mine_tokens, 0)
        return take(part).reshape(1, mine_tokens), take(1 - part).reshape(1, mine_tokens)

    def bias_rows(mods):
        kinds = lax.dynamic_slice_in_dim(mods, part * mine_tokens, mine_tokens, 0)[:, None]
        bias_of = jnp.zeros((mine_tokens, width), f32)
        for e in range(experts):
            bias_of = jnp.where(kinds == e, down_bias[e][None], bias_of)
        return bias_of

    def finish(x2, z_sum, bias_of):
        return (x2 + (z_sum + bias_of)).astype(bf16)

    def small_rows(sums1, sums2, bsum, g_upb, g_down_bias):
        sides = bsum.reshape(3, cols)
        g_qv = lax.dynamic_update_slice(
            jnp.zeros((2, width), f32), jnp.stack([sides[0], sides[2]]), (jnp.int32(0), col_start)
        )
        g_upb_full = lax.dynamic_update_slice(
            jnp.zeros((experts, up_bias.shape[1]), f32), g_upb, (jnp.int32(0), hid_start)
        )
        return jnp.concatenate(
            [sums1[0:2], sums2[0:3], g_down_bias / parts, g_qv, g_upb_full.reshape(-1, width)]
        )

    if staged:
        x_bit = me % 2
        coords = jnp.stack([me // 4, (me // 2) % 2, x_bit, part]).astype(jnp.int32)
        pred = me < size
        inner = part < parts
        half = hid // 2
        hid_start = part * hid + x_bit * half
        hc = half // CHUNKS
        up_b = lax.dynamic_slice_in_dim(up_bias, hid_start, half, 1)

        def call_experts(k, xs, dys, weights, carry, places=()):
            call = CALLS[k]
            ub = up_b[:, None, call[0] * hc : (call[-1] + 1) * hc]
            return ffn(
                coords, (plan_own, plan), xs, dys, ub, [weights[c] for c in call], carry, places
            )

        def begin():
            w = jnp.stack([w_up, w_down])
            keep = lax.dynamic_slice_in_dim(w, x_bit * half, half, 3)
            send = lax.dynamic_slice_in_dim(w, (1 - x_bit) * half, half, 3)
            near = flip(send, 1, size)
            pieces = [
                jnp.stack([keep[..., c * hc : (c + 1) * hc], near[..., c * hc : (c + 1) * hc]])
                for c in range(CHUNKS)
            ]
            pieces[0] = four_times(pieces[0])
            ab = gather_z(w_qkv[:2], jnp.stack([w_qkv[2], w_out]), size)
            mods, pos, plan_own = token_plan(segments, modality, experts)
            plan = flip(plan_own, 1, size)
            return pieces, ab, mods, pos, plan_own, plan, bias_rows(mods), small_inputs()

        pieces, ab, mods, pos, plan_own, plan, bias_of, smalls = phase(pred, begin)
        x_mine, dy_mine, proj_bias, seg_row, windows, vec, ln1 = smalls

        def weights_in():
            def inside():
                pos_row = pos.reshape(1, tokens)
                dys = sort_tokens([(pos_row, dy)], tiles, 0, 2)
                later = [four_times(v) for v in pieces[1:]]
                hot = (mods[:, None] == jnp.arange(experts, dtype=jnp.int32)).astype(bf16)
                return (
                    *gather_xy(*ab, later, size), halves(pos), halves(plan),
                    dys, tn_dot(hot, dy),
                    later,
                )

            return deal_z(pieces[0]), phase(inner, inside)

        z0, (pa, pb, pos_here, pos_near, dys, g_down_bias, later) = phase(pred, weights_in)

        def forward():
            return (
                *phase(inner, lambda: fwd(coords, pa, pb)), flip(z0, 2, size),
                deal_z(later[0]), flip(dy_mine, 1, size),
            )

        saved, x2, a2, y0, z1, dy_near = phase(pred, forward)

        def sort(places, v, v2, group, into):
            return sort_tokens(list(zip(places, (v, v2))), tiles, group, 2, into)

        def exchange():
            near = flip(a2, 1, size)
            d, xs = phase(
                inner,
                lambda: (
                    sort(pos_near, dy_near, swap(dy_near), 1, dys),
                    sort(pos_here, a2, swap(a2), 0, None),
                ),
            )
            near = after(near, d, xs)
            xs = phase(inner, lambda: sort(pos_near, near, swap(near), 1, xs))
            return xs, d, flip(z1, 2, size), deal_z(later[1])

        xs, dys, y1, z2 = phase(pred, exchange)
        weights = [(z0, y0), (z1, y1)]
        (zs0, das0, grads, gub0), y2 = phase(
            pred, lambda: (call_experts(0, xs, dys, weights, ()), flip(z2, 2, size))
        )
        weights.append((z2, y2))

        def both_cores(places, vs, group):
            mine, other = unsort_tokens(places, vs, group, 2)
            return (mine.astype(f32) + swap(other).astype(f32)).astype(bf16)

        def second():
            def inside():
                zs, das, more, gub, (mine, other) = call_experts(
                    1, xs, dys, weights, (zs0, das0), pos_near
                )
                near = (mine.astype(f32) + swap(other).astype(f32)).astype(bf16)
                return zs, das, more, gub, near

            return phase(inner, inside), sums_y(coords, grads[0], size)

        (zs, das, more, gub1, da_near), v0 = phase(pred, second)
        grads = grads + more
        g_upb = jnp.concatenate([gub0, gub1], axis=-1)[:, 0]

        def back():
            def inside():
                mine, other = unsort_tokens(pos_here, das, 0, 2)
                return mine, swap(other), both_cores(pos_near, zs, 1)

            near = flip(da_near, 1, size)
            mine, other, z_near = phase(inner, inside)
            g0 = sums_z(coords, v0)
            v1 = sums_y(coords, grads[1], size)

            def to_x2():
                dx2, dxr, sums2 = norm_grad((mine, other, near), x2, dy_mine, ln_gain[1:2], True)
                return dx2, (dxr, swap(dxr)), sums2

            return *phase(inner, to_x2), z_near, g0, v1

        dx2, dxr, sums2, z_near, g0, v1 = phase(pred, back)

        def last():
            return (
                phase(inner, lambda: bwd(coords, dxr, dx2, saved, pa, pb)), flip(z_near, 1, size),
                sums_z(coords, v1), sums_y(coords, grads[2], size),
            )

        (grad, sums1, ga0, ga1, gb0, gb1, bsum), z_near, g1, v2 = phase(pred, last)
        def sum_up():
            def out_rows():
                mine, other = unsort_tokens(pos_here, zs, 0, 2)
                z_sum = mine.astype(f32) + swap(other).astype(f32) + z_near.astype(f32)
                out = finish(x2, z_sum, bias_of)
                return out, swap(out), swap(grad)

            rows_all = phase(inner, lambda: small_rows(sums1, sums2, bsum, g_upb, g_down_bias))

            def small_start():
                total = rows_all + swap(rows_all)
                return total + flip(total, 1, size)

            got2 = deal_z(after(v2[1], rows_all))
            got_a, got_b = flip(ga1, 2, size), flip(gb1, 1, size)
            outs = phase(inner, out_rows)
            a_own, a_send, b_own, b_send = attn_sums_1((ga0, gb0), (got_a, got_b), outs)
            got_a, got_b = flip(a_send, 1, size), flip(b_send, 2, size)
            small = phase(inner, small_start)
            return attn_sums_2(coords, (a_own, b_own), (got_a, got_b), small), got2, small, outs

        (own, send), got2, small, (out, out_other, grad_other) = phase(pred, sum_up)

        got = deal_z(send)
        g2 = add_z(coords, v2[0], got2)
        near = flip(jnp.concatenate([v[1] for v in (g0, g1, g2)], axis=-1), 1, size)
        total = phase(inner, lambda: small + flip(small, 2, size))
        rows_z = [flip(total, 4 * rz, size) for rz in (1, 2, 3)]
        layer_output, grad_input = whole(
            rows_kernel, "rows", [((parts,) + v.shape, v.dtype) for v in (out, grad)],
            out, out_other, grad, grad_other, prefetch=(coords,),
        )
        g_qkv, g_out = whole(
            qkv_grad_kernel, "qkv_grad", [(w_qkv.shape, f32), (w_out.shape, f32)], own, got,
            prefetch=(after(coords, layer_output),),
        )
        last = after(coords, g_out)
        g_up, g_down = whole(
            expert_grad_kernel, "expert_grad", [(w_up.shape, f32)] * 2,
            g0[0], g1[0], g2[0], near, prefetch=(last,),
        )
        rows_z = jnp.stack([after(total, g_up)] + rows_z)
        pick = lambda z: lax.dynamic_index_in_dim(rows_z, last[0] ^ z, 0, False)
        small = pick(0) + pick(1) + pick(2) + pick(3)
    else:
        coords = jnp.stack([0, 0, 0, part]).astype(jnp.int32)
        x_mine, dy_mine, proj_bias, seg_row, windows, vec, ln1 = small_inputs()
        hid_start = part * hid
        hc = hid // CHUNKS
        up_b = lax.dynamic_slice_in_dim(up_bias, hid_start, hid, 1)
        pa, pb = gather_pieces_plain(w_qkv[:2], jnp.stack([w_qkv[2], w_out]))
        weights = expert_pieces_plain(w_up, w_down)
        mods, pos, plan_own = token_plan(segments, modality, experts)
        pos_row = pos.reshape(1, tokens)
        hot = (mods[:, None] == jnp.arange(experts, dtype=jnp.int32)).astype(bf16)
        g_down_bias = tn_dot(hot, dy)
        dys = sort_tokens([(pos_row, dy)], tiles, 0, 1)
        saved, x2, a2 = fwd(coords, pa, pb)
        xs = sort_tokens([(pos_row, share(a2).reshape(tokens, width))], tiles, 0, 1)
        carry = ()
        grads = []
        g_upb = []
        for call in CALLS:
            ub = up_b[:, None, call[0] * hc : (call[-1] + 1) * hc]
            zs, das, pairs, gub = ffn(
                coords, (plan_own,), xs, dys, ub, [weights[c] for c in call], carry
            )
            carry = (zs, das)
            g_upb.append(gub[:, 0])
            grads += pairs
        g_upb = jnp.concatenate(g_upb, axis=-1)
        g_up, g_down = jnp.concatenate([expert_sums_plain(pair) for pair in grads], axis=-1)
        own = deal(unsort_tokens([pos_row], das, 0, 1)[0].reshape(by_core))
        dx2, dxr, sums2 = norm_grad((own[0], own[1]), x2, dy_mine, ln_gain[1:2], True)
        grad_mine, sums1, ga0, ga1, gb0, gb1, bsum = bwd(
            coords, (dxr, swap(dxr)), dx2, saved, pa, pb
        )
        g_qk, g_vo = scatter_plain((ga0, ga1), (gb0, gb1))
        g_qkv, g_out = jnp.concatenate([g_qk, g_vo[:1]]), g_vo[1]
        own = deal(unsort_tokens([pos_row], zs, 0, 1)[0].reshape(by_core))
        layer_output = share(finish(x2, jnp.sum(own.astype(f32), axis=0), bias_rows(mods)))
        grad_input = share(grad_mine)
        small = lax.psum(small_rows(sums1, sums2, bsum, g_upb, g_down_bias), ("dp", "mp"))

    g_gain = jnp.stack([small[0], small[2]])
    g_lnb = jnp.stack([small[1], small[3]])
    return (
        layer_output.reshape(shape3),
        grad_input.reshape(shape3),
        g_gain,
        g_lnb,
        g_qkv,
        small[5 + experts : 7 + experts],
        g_out,
        small[4],
        g_up,
        small[7 + experts :].reshape(experts, up_bias.shape[1]),
        g_down,
        small[5 : 5 + experts],
    )


def solution(mesh):
    tok = P("dp", None, None)
    rep = P()
    wide = P(None, "dp", "mp")
    in_specs = (
        tok, P("dp", None), P("dp", None), rep, rep, wide, rep, P("dp", "mp"), rep, wide, rep,
        wide, rep, tok,
    )
    out_specs = (
        tok, tok, rep, rep, wide, rep, P("dp", "mp"), rep, wide, rep, wide, rep,
    )
    return jax.shard_map(body, mesh=mesh, in_specs=in_specs, out_specs=out_specs, check_vma=False)
```

```python
import functools
import math

import jax
import jax.numpy as jnp
from jax import lax
from jax.experimental import pallas as pl
from jax.experimental.pallas import tpu as pltpu
from jax.sharding import PartitionSpec as P

HD = 64
EPS = 1e-05
TILE = 256
CHUNKS = 3
SCALE = 1.0
CALLS = ((0, 1), (2,))
MIB = 1024 * 1024
LOG2E = math.log2(math.e)
f32 = jnp.float32
bf16 = jnp.bfloat16
ANY = pl.BlockSpec(memory_space=pl.ANY)


def full_spec(shape):
    zeros = (0,) * len(shape)
    return pl.BlockSpec(shape, lambda *_: zeros)


def nt_dot(a, b):
    return lax.dot_general(a, b, (((1,), (1,)), ((), ())), preferred_element_type=f32)


def nn_dot(a, b):
    return lax.dot_general(a, b, (((1,), (0,)), ((), ())), preferred_element_type=f32)


def tn_dot(a, b):
    return lax.dot_general(a, b, (((0,), (0,)), ((), ())), preferred_element_type=f32)


def params(grid_rank, mib=20):
    return pltpu.CompilerParams(
        dimension_semantics=("arbitrary",) * grid_rank, vmem_limit_bytes=mib * MIB
    )


def cost(flops, nbytes, trans=0):
    return pl.CostEstimate(
        flops=int(flops * SCALE), bytes_accessed=int(nbytes * SCALE), transcendentals=int(trans * SCALE)
    )


def place(c_ref, kind, outer, inner, rz):
    ry, rx = (outer, inner) if kind == "a" else (inner, outer)
    return (c_ref[0] ^ rz) * 4 + (c_ref[1] ^ ry) * 2 + (c_ref[2] ^ rx)


def piece_copies(c_ref, jobs, sems):
    copies = []
    for kind, pair, view, target in jobs:
        for outer in range(2):
            for inner in range(2):
                for rz in range(4):
                    rows = place(c_ref, kind, outer, inner, rz)
                    copies.append(
                        pltpu.make_async_copy(
                            view(pair[outer], inner, rz), target(rows), sems.at[len(copies)]
                        )
                    )
    return copies


def gelu_parts(u):
    mag = jnp.abs(u)
    t = 1.0 / (1.0 + (0.3275911 * math.sqrt(0.5)) * mag)
    poly = t * (
        0.254829592
        + t * (-0.284496736 + t * (1.421413741 + t * (-1.453152027 + t * 1.061405429)))
    )
    gauss = jnp.exp(-0.5 * u * u)
    half = 0.5 * poly * gauss
    cdf = jnp.where(u >= 0, 1.0 - half, half)
    return u * cdf, cdf + u * gauss * (1.0 / math.sqrt(2.0 * math.pi))


def norm_parts(v):
    mean = jnp.mean(v, axis=-1, keepdims=True)
    cent = v - mean
    var = jnp.mean(cent * cent, axis=-1, keepdims=True)
    rstd = lax.rsqrt(var + EPS)
    return cent * rstd, rstd


def norm_back(d_out, xhat, rstd, gain):
    d_hat = d_out * gain
    m1 = jnp.mean(d_hat, axis=-1, keepdims=True)
    m2 = jnp.mean(d_hat * xhat, axis=-1, keepdims=True)
    return rstd * (d_hat - m1 - xhat * m2)


def two_heads(v):
    lane = lax.broadcasted_iota(jnp.int32, v.shape, 1)
    none = jnp.zeros_like(v)
    return jnp.concatenate([jnp.where(lane < HD, v, none), jnp.where(lane >= HD, v, none)], axis=0)


def fill_bias(srow_ref, bias_s):
    seq = bias_s.shape[0]
    column = jnp.broadcast_to(srow_ref[0], (128, seq)).T
    for k in range(0, seq, 128):
        bias_s[:, k : k + 128] = jnp.where(column == srow_ref[0, :, k : k + 128], 0.0, -1e30)


def each_window(win_ref, row, blocks, f):
    @pl.loop(0, blocks)
    def _(j):
        first = win_ref[(row * blocks + j) * 2]
        n = win_ref[(row * blocks + j) * 2 + 1]
        for size in range(1, blocks + 1):

            @pl.when(n == size)
            def _():
                f(j, first, size)


def key_windows(segments):
    first, last = segments[:, ::128], segments[:, 127::128]
    low = jnp.sum((last[:, None, :] < first[:, :, None]).astype(jnp.int32), axis=-1)
    high = jnp.sum((first[:, None, :] <= last[:, :, None]).astype(jnp.int32), axis=-1)
    return jnp.stack([low, high - low], axis=-1).reshape(-1)


def attn_fwd_kernel(
    heads, piece, c_ref, win_ref, x_ref, srow_ref, ln_ref, pb_ref, a0, a1_, b0, b1_,
    att_ref, att_other_ref, qkv_ref, kt_ref, o_ref, ot_ref, lse_ref,
    w_s, wo_s, bias_s, vt_s, a1_s, sems,
):
    cols = heads * HD
    pairs = cols // 128
    seq, width = x_ref.shape[1], x_ref.shape[2]

    def into(block, j):
        return w_s.at[pl.ds(pl.multiple_of(block * piece, 16), piece), pl.ds(j * cols, cols)]

    def into_out(block):
        return wo_s.at[pl.ds(pl.multiple_of(block * piece, 16), piece), :]

    jobs = [
        ("a", (a0, a1_), lambda r, i, z: r.at[i, z, 0], lambda k: into(k, 0)),
        ("a", (a0, a1_), lambda r, i, z: r.at[i, z, 1], lambda k: into(k, 1)),
        ("b", (b0, b1_), lambda r, i, z: r.at[i, z, 0], lambda k: into(k, 2)),
        ("b", (b0, b1_), lambda r, i, z: r.at[i, z, 1], into_out),
    ]
    copies = piece_copies(c_ref, jobs, sems)

    @pl.when(pl.program_id(0) == 0)
    def _():
        for c in copies:
            c.start()

    xhat, _ = norm_parts(x_ref[0].astype(f32))
    a1_s[...] = (xhat * ln_ref[0:1] + ln_ref[1:2]).astype(bf16)
    fill_bias(srow_ref, bias_s)

    @pl.when(pl.program_id(0) == 0)
    def _():
        for c in copies:
            c.wait()

    a1 = a1_s[...]
    proj = (nn_dot(a1, w_s[...]) + pb_ref[...]).astype(bf16)
    for j in range(3):
        for p in range(pairs):
            qkv_ref[0, j, p] = proj[:, j * cols + p * 128 : j * cols + (p + 1) * 128]
    for p in range(pairs):
        kt_ref[0, p] = proj[:, cols + p * 128 : cols + (p + 1) * 128].T
        vt_s[p] = proj[:, 2 * cols + p * 128 : 2 * cols + (p + 1) * 128].T
    scale2 = HD ** (-0.5) * LOG2E

    def block(j, start, n):
        keys = pl.ds(pl.multiple_of(start * 128, 128), n * 128)
        mine = pl.ds(pl.multiple_of(j * 128, 128), 128)
        bias = bias_s[keys, mine]
        bias = jnp.concatenate([bias, bias], axis=1)
        every = range(pairs)
        s_t = [
            nt_dot(qkv_ref[0, 1, p, keys, :], two_heads(qkv_ref[0, 0, p, mine, :])) + bias
            for p in every
        ]
        top = [jnp.max(v, axis=0, keepdims=True) for v in s_t]
        e_t = [jnp.exp2((v - m) * scale2) for v, m in zip(s_t, top)]
        total = [jnp.sum(v, axis=0, keepdims=True) for v in e_t]
        p_t = [(v * (1.0 / t)).astype(bf16) for v, t in zip(e_t, total)]
        o_t = [nn_dot(vt_s[p, :, keys], p_t[p]).astype(bf16) for p in every]
        for p in every:
            ot_ref[0, p, :HD, mine] = o_t[p][:HD, :128]
            ot_ref[0, p, HD:, mine] = o_t[p][HD:, 128:]
            lse = top[p] * scale2 + jnp.log2(total[p])
            lse_ref[0, p, 0:1, mine] = lse[:, :128]
            lse_ref[0, p, 1:2, mine] = lse[:, 128:]

    each_window(win_ref, pl.program_id(0), seq // 128, block)

    for p in range(pairs):
        o_ref[0, :, p * 128 : (p + 1) * 128] = ot_ref[0, p].T
    att = nt_dot(o_ref[0], wo_s[...]).astype(bf16)

    @pl.when(pl.program_id(0) == c_ref[3])
    def _():
        att_ref[...] = att

    @pl.when(pl.program_id(0) != c_ref[3])
    def _():
        att_other_ref[...] = att


def attn_fwd(coords, windows, x, seg_row, ln, proj_bias, pa, pb):
    rows, seq, width = x.shape
    cols = proj_bias.shape[-1] // 3
    heads = cols // HD
    pairs = cols // 128
    piece = pa[0].shape[-2]
    row3 = lambda r, *_: (r, 0, 0)
    row4 = lambda r, *_: (r, 0, 0, 0)
    row5 = lambda r, *_: (r, 0, 0, 0, 0)
    outs = [
        ((seq, width), bf16, (seq, width), lambda *_: (0, 0)),
        ((seq, width), bf16, (seq, width), lambda *_: (0, 0)),
        ((rows, 3, pairs, seq, 128), bf16, (1, 3, pairs, seq, 128), row5),
        ((rows, pairs, 128, seq), bf16, (1, pairs, 128, seq), row4),
        ((rows, seq, cols), bf16, (1, seq, cols), row3),
        ((rows, pairs, 128, seq), bf16, (1, pairs, 128, seq), row4),
        ((rows, pairs, 2, seq), f32, (1, pairs, 2, seq), row4),
    ]
    return pl.pallas_call(
        functools.partial(attn_fwd_kernel, heads, piece),
        out_shape=[jax.ShapeDtypeStruct(s, d) for s, d, _, _ in outs],
        grid_spec=pltpu.PrefetchScalarGridSpec(
            num_scalar_prefetch=2,
            grid=(rows,),
            in_specs=[
                pl.BlockSpec((1, seq, width), row3),
                pl.BlockSpec((1, 1, seq), row3),
                full_spec((2, width)),
                full_spec((1, 3 * cols)),
                ANY, ANY, ANY, ANY,
            ],
            out_specs=[pl.BlockSpec(b, m) for _, _, b, m in outs],
            scratch_shapes=[
                pltpu.VMEM((width, 3 * cols), bf16),
                pltpu.VMEM((width, cols), bf16),
                pltpu.VMEM((seq, seq), f32),
                pltpu.VMEM((pairs, 128, seq), bf16),
                pltpu.VMEM((seq, width), bf16),
                pltpu.SemaphoreType.DMA((64,)),
            ],
        ),
        compiler_params=params(1, 26),
        cost_estimate=cost(2e10, 1e7, 3e6),
        name="attn_fwd",
    )(coords, windows, x, seg_row, ln, proj_bias, *pa, *pb)


def attn_bwd_kernel(
    heads, piece, c_ref, win_ref, dxr_ref, dxr2_ref, x_ref, srow_ref, ln_ref, qkv_ref, kt_ref, o_ref, ot_ref, lse_ref, a0, a1_, b0, b1_,
    da1_ref, da1_other_ref, ga0_ref, ga1_ref, gb0_ref, gb1_ref, bsum_ref,
    w_s, wo_s, bias_s, dp_s, gw_s, go_s, do_s, row_s, dk_s, dv_s, dqt_s, a1_s, dxr_s, o_s, sems,
):
    cols = heads * HD
    pairs = cols // 128
    seq = x_ref.shape[1]
    step = pl.program_id(0)

    def into(block, j):
        return w_s.at[pl.ds(pl.multiple_of(block * piece, 16), piece), pl.ds(j * cols, cols)]

    def into_out(block):
        return wo_s.at[pl.ds(pl.multiple_of(block * piece, 16), piece), :]

    jobs = [
        ("a", (a0, a1_), lambda r, i, z: r.at[i, z, 0], lambda k: into(k, 0)),
        ("a", (a0, a1_), lambda r, i, z: r.at[i, z, 1], lambda k: into(k, 1)),
        ("b", (b0, b1_), lambda r, i, z: r.at[i, z, 0], lambda k: into(k, 2)),
        ("b", (b0, b1_), lambda r, i, z: r.at[i, z, 1], into_out),
    ]
    copies = piece_copies(c_ref, jobs, sems)

    @pl.when(step == 0)
    def _():
        for c in copies:
            c.start()
        bsum_ref[...] = jnp.zeros_like(bsum_ref)

    xhat1, _ = norm_parts(x_ref[0].astype(f32))
    here = pl.ds(pl.multiple_of(step * seq, 128), seq)
    a1_s[here, :] = (xhat1 * ln_ref[0:1] + ln_ref[1:2]).astype(bf16)
    o_s[here, :] = o_ref[0]
    fill_bias(srow_ref, bias_s)

    @pl.when(step == 0)
    def _():
        for c in copies:
            c.wait()

    dxr = jnp.where(step == c_ref[3], dxr_ref[...], dxr2_ref[...])
    do = nn_dot(dxr, wo_s[...]).astype(bf16)
    dxr_s[here, :] = dxr
    scale = HD ** (-0.5)
    scale2 = scale * LOG2E
    do_s[...] = do
    for p in range(pairs):
        prod = do[:, p * 128 : (p + 1) * 128].T.astype(f32) * ot_ref[0, p].astype(f32)
        for h in range(2):
            row_s[p, h : h + 1] = jnp.sum(prod[h * HD : (h + 1) * HD], axis=0, keepdims=True)
    dk_s[...] = jnp.zeros_like(dk_s)
    dv_s[...] = jnp.zeros_like(dv_s)

    def block(j, start, n):
        keys = pl.ds(pl.multiple_of(start * 128, 128), n * 128)
        mine = pl.ds(pl.multiple_of(j * 128, 128), 128)
        pair = lambda ref: jnp.concatenate([ref[0:1, mine], ref[1:2, mine]], axis=1)
        every = range(pairs)
        bias = bias_s[keys, mine]
        bias = jnp.concatenate([bias, bias], axis=1)
        q_2 = [two_heads(qkv_ref[0, 0, p, mine, :]) for p in every]
        do_2 = [two_heads(do_s[mine, p * 128 : (p + 1) * 128]) for p in every]
        s_t = [nt_dot(qkv_ref[0, 1, p, keys, :], q_2[p]) * scale2 for p in every]
        d_t = [nt_dot(qkv_ref[0, 2, p, keys, :], do_2[p]) - pair(row_s.at[p]) for p in every]
        p_t = [jnp.exp2(s_t[p] + (bias - pair(lse_ref.at[0, p]))) for p in every]
        for p in every:
            dv_s[p, keys, :] += nn_dot(p_t[p].astype(bf16), do_2[p])
        ds_t = [(p_t[p] * d_t[p]).astype(bf16) for p in every]
        for p in every:
            dk_s[p, keys, :] += nn_dot(ds_t[p], q_2[p])
            dq_t = (nn_dot(kt_ref[0, p, :, keys], ds_t[p]) * scale).astype(bf16)
            dqt_s[p, :HD, mine] = dq_t[:HD, :128]
            dqt_s[p, HD:, mine] = dq_t[HD:, 128:]

    each_window(win_ref, step, seq // 128, block)

    for p in range(pairs):
        dp_s[here, p * 128 : (p + 1) * 128] = dqt_s[p].T
        dp_s[here, cols + p * 128 : cols + (p + 1) * 128] = (dk_s[p] * scale).astype(bf16)
        dp_s[here, 2 * cols + p * 128 : 2 * cols + (p + 1) * 128] = dv_s[p].astype(bf16)

    dproj = dp_s[here, :]
    da1 = nt_dot(dproj, w_s[...]).astype(bf16)

    @pl.when(step == c_ref[3])
    def _():
        da1_ref[...] = da1

    @pl.when(step != c_ref[3])
    def _():
        da1_other_ref[...] = da1

    bsum_ref[...] += jnp.sum(dproj.astype(f32), axis=0, keepdims=True)

    @pl.when(step == pl.num_programs(0) - 1)
    def _():
        gw_s[...] = tn_dot(a1_s[...], dp_s[...]).astype(bf16)
        go_s[...] = tn_dot(dxr_s[...], o_s[...]).astype(bf16)
        for outer in range(2):
            for inner in range(2):
                for rz in range(4):
                    ra = pl.ds(pl.multiple_of(place(c_ref, "a", outer, inner, rz) * piece, 16), piece)
                    rb = pl.ds(pl.multiple_of(place(c_ref, "b", outer, inner, rz) * piece, 16), piece)
                    ga, gb = ((ga0_ref, gb0_ref), (ga1_ref, gb1_ref))[outer]
                    ga[inner, rz, 0] = gw_s[ra, :cols]
                    ga[inner, rz, 1] = gw_s[ra, cols : 2 * cols]
                    gb[inner, rz, 0] = gw_s[rb, 2 * cols :]
                    gb[inner, rz, 1] = go_s[rb, :]


def attn_bwd(coords, windows, dxr, dxr2, x, seg_row, ln, saved, pa, pb):
    rows, seq, width = x.shape
    qkv, kt, o, ot, lse = saved
    cols = o.shape[-1]
    heads = cols // HD
    pairs = cols // 128
    piece = pa[0].shape[-2]
    row3 = lambda r, *_: (r, 0, 0)
    row4 = lambda r, *_: (r, 0, 0, 0)
    row5 = lambda r, *_: (r, 0, 0, 0, 0)
    tok = pl.BlockSpec((1, seq, width), row3)
    gshape = pa[0].shape
    return pl.pallas_call(
        functools.partial(attn_bwd_kernel, heads, piece),
        out_shape=[
            *[jax.ShapeDtypeStruct((seq, width), bf16)] * 2,
            *[jax.ShapeDtypeStruct(gshape, bf16)] * 4,
            jax.ShapeDtypeStruct((1, 3 * cols), f32),
        ],
        grid_spec=pltpu.PrefetchScalarGridSpec(
            num_scalar_prefetch=2,
            grid=(rows,),
            in_specs=[
                full_spec((seq, width)), full_spec((seq, width)), tok,
                pl.BlockSpec((1, 1, seq), row3),
                full_spec((2, width)),
                pl.BlockSpec((1, 3, pairs, seq, 128), row5),
                pl.BlockSpec((1, pairs, 128, seq), row4),
                pl.BlockSpec((1, seq, cols), row3),
                pl.BlockSpec((1, pairs, 128, seq), row4),
                pl.BlockSpec((1, pairs, 2, seq), row4),
                ANY, ANY, ANY, ANY,
            ],
            out_specs=[
                *[full_spec((seq, width))] * 2,
                *[full_spec(gshape)] * 4,
                full_spec((1, 3 * cols)),
            ],
            scratch_shapes=[
                pltpu.VMEM((width, 3 * cols), bf16),
                pltpu.VMEM((width, cols), bf16),
                pltpu.VMEM((seq, seq), f32),
                pltpu.VMEM((rows * seq, 3 * cols), bf16),
                pltpu.VMEM((width, 3 * cols), bf16),
                pltpu.VMEM((width, cols), bf16),
                pltpu.VMEM((seq, cols), bf16),
                pltpu.VMEM((pairs, 2, seq), f32),
                pltpu.VMEM((pairs, seq, 128), f32),
                pltpu.VMEM((pairs, seq, 128), f32),
                pltpu.VMEM((pairs, 128, seq), bf16),
                pltpu.VMEM((rows * seq, width), bf16),
                pltpu.VMEM((rows * seq, width), bf16),
                pltpu.VMEM((rows * seq, cols), bf16),
                pltpu.SemaphoreType.DMA((64,)),
            ],
        ),
        compiler_params=params(1, 34),
        cost_estimate=cost(4e10, 2e7, 3e6),
        name="attn_bwd",
    )(coords, windows, dxr, dxr2, x, seg_row, ln, qkv, kt, o, ot, lse, *pa, *pb)


def sort_kernel(sources, *refs):
    vs_ref = refs[-1]
    block = vs_ref.shape[0]
    total = None
    for k in range(sources):
        pos_row, v_ref = refs[2 * k], refs[2 * k + 1]
        slot = lax.broadcasted_iota(jnp.int32, (block, v_ref.shape[0]), 0)
        slot = slot + pl.program_id(0) * block
        pick = (slot == pos_row[...]).astype(f32).astype(bf16)
        part = nn_dot(pick, v_ref[...])
        total = part if total is None else total + part
    vs_ref[...] = total.astype(bf16)


def sort_tokens(sources, tiles, group, groups, into=None):
    width = sources[0][1].shape[1]
    tokens = sum(v.shape[0] for _, v in sources)
    slots = tiles * TILE
    steps = 2
    block = slots // steps
    flat = [x for pair in sources for x in pair]
    return pl.pallas_call(
        functools.partial(sort_kernel, len(sources)),
        out_shape=jax.ShapeDtypeStruct((groups * slots, width), bf16),
        grid=(steps,),
        in_specs=[*[full_spec(x.shape) for x in flat], *([] if into is None else [ANY])],
        out_specs=pl.BlockSpec((block, width), lambda i: (i + group * steps, 0)),
        input_output_aliases={} if into is None else {len(flat): 0},
        compiler_params=params(1),
        cost_estimate=cost(2 * slots * tokens * width, 1e7),
        name="sort_tokens",
    )(*flat, *([] if into is None else [into]))


def unsort_kernel(targets, *refs):
    vs = refs[targets][...]
    for k in range(targets):
        pos_row, out_ref = refs[k], refs[targets + 1 + k]
        slot = lax.broadcasted_iota(jnp.int32, (vs.shape[0], out_ref.shape[0]), 0)
        pick = (slot == pos_row[...]).astype(f32).astype(bf16)
        out_ref[...] = tn_dot(pick, vs).astype(bf16)


def unsort_tokens(places, vs, group, groups):
    width = vs.shape[1]
    slots = vs.shape[0] // groups
    tokens = sum(p.shape[1] for p in places)
    return pl.pallas_call(
        functools.partial(unsort_kernel, len(places)),
        out_shape=[jax.ShapeDtypeStruct((p.shape[1], width), bf16) for p in places],
        grid=(1,),
        in_specs=[
            *[full_spec(p.shape) for p in places],
            pl.BlockSpec((slots, width), lambda i: (group, 0)),
        ],
        out_specs=[full_spec((p.shape[1], width)) for p in places],
        compiler_params=params(1),
        cost_estimate=cost(2 * slots * tokens * width, 1e7),
        name="unsort_tokens",
    )(*places, vs)


def mid_kernel(x_ref, own_ref, got_ref, vec_ref, x2_ref, a2_ref):
    x2 = x_ref[...].astype(f32) + (own_ref[...].astype(f32) + got_ref[...].astype(f32)) + vec_ref[0:1]
    x2_ref[...] = x2
    xhat, _ = norm_parts(x2)
    a2_ref[...] = (xhat * vec_ref[1:2] + vec_ref[2:3]).astype(bf16)


def mid(x, own, got, vec):
    tokens, width = x.shape
    tile = pl.BlockSpec((tokens, width), lambda i: (i, 0))
    return pl.pallas_call(
        mid_kernel,
        out_shape=[
            jax.ShapeDtypeStruct((tokens, width), f32),
            jax.ShapeDtypeStruct((tokens, width), bf16),
        ],
        grid=(tokens // tokens,),
        in_specs=[tile, tile, tile, full_spec((3, width))],
        out_specs=[tile, tile],
        compiler_params=params(1),
        cost_estimate=cost(1e7, 5e6),
        name="mid_norm",
    )(x, own, got, vec)


def ffn_kernel(first, count, piece, groups, near, c_ref, plan0_ref, plan1_ref, *refs):
    xs_ref, dys_ref, ub_ref, *rest = refs
    if near:
        pos_refs, rest = rest[:2], rest[2:]
    if not first:
        zin_ref, din_ref, *rest = rest
    w_refs = [rest[2 * c : 2 * c + 2] for c in range(count)]
    rest = rest[2 * count :]
    z_ref, da_ref, *rest = rest
    if near:
        near_refs, rest = rest[:2], rest[2:]
    g_refs = [rest[2 * c : 2 * c + 2] for c in range(count)]
    gub_ref, wu_s, wd_s, gu_s, gd_s, x_s, dy_s, z_s, da_s, sems, in_sems, out_sems = rest[2 * count :]
    experts = wu_s.shape[0]
    hc = wu_s.shape[2] // count
    tiles = x_s.shape[0]
    per = tiles // groups
    spots = [(ry, rz, rx) for ry in range(2) for rz in range(4) for rx in range(2)]

    def rows_of(ry, rz, rx):
        block = rz * 4 + (c_ref[1] ^ ry) * 2 + (c_ref[2] ^ rx)
        return pl.ds(pl.multiple_of(block * piece, 16), piece)

    def tile_of(ref, i):
        return ref.at[pl.ds(pl.multiple_of(i * TILE, TILE), TILE), :]

    def reads(i):
        pairs = [(xs_ref, x_s), (dys_ref, dy_s)]
        if not first:
            pairs += [(zin_ref, z_s), (din_ref, da_s)]
        return [
            pltpu.make_async_copy(tile_of(src, i), dst.at[i], in_sems.at[k, i])
            for k, (src, dst) in enumerate(pairs)
        ]

    def writes(i):
        return [
            pltpu.make_async_copy(src.at[i], tile_of(dst, i), out_sems.at[k, i])
            for k, (src, dst) in enumerate([(z_s, z_ref), (da_s, da_ref)])
        ]

    copies = []
    for c in range(count):
        for ry, rz, rx in spots:
            for k, w_s in ((0, wu_s), (1, wd_s)):
                copies.append(
                    pltpu.make_async_copy(
                        w_refs[c][ry].at[rz, rx, k],
                        w_s.at[:, rows_of(ry, rz, rx), pl.ds(c * hc, hc)],
                        sems.at[len(copies)],
                    )
                )
    for c in reads(0):
        c.start()
    for c in copies:
        c.start()

    @pl.loop(1, tiles)
    def _(i):
        for c in reads(i):
            c.start()

    gu_s[...] = jnp.zeros_like(gu_s)
    gd_s[...] = jnp.zeros_like(gd_s)
    gub_ref[...] = jnp.zeros_like(gub_ref)
    for c in copies:
        c.wait()

    @pl.loop(0, tiles)
    def _(i):
        group = i // per
        k = i - group * per
        info = lambda at: jnp.where(group == 0, plan0_ref[at], plan1_ref[at])
        tokens = plan0_ref.shape[0] - per - 1
        live = k < info(tokens + per)
        for c in reads(i):
            c.wait()

        @pl.when(live)
        def _():
            e = info(tokens + k)
            x = x_s[i]
            dy = dy_s[i]
            u = nn_dot(x, wu_s[e]) + ub_ref[e]
            act, slope = gelu_parts(u)
            act = act.astype(bf16)
            du = (nn_dot(dy, wd_s[e]) * slope).astype(bf16)
            z = nt_dot(act, wd_s[e])
            da = nt_dot(du, wu_s[e])
            if not first:
                z = z + z_s[i].astype(f32)
                da = da + da_s[i].astype(f32)
            z_s[i] = z.astype(bf16)
            da_s[i] = da.astype(bf16)
            gd_s[e] += tn_dot(dy, act)
            gu_s[e] += tn_dot(x, du)
            gub_ref[e] += jnp.sum(du.astype(f32), axis=0, keepdims=True)

        @pl.when(jnp.logical_not(live))
        def _():
            z_s[i] = jnp.zeros(z_s.shape[1:], bf16)
            da_s[i] = jnp.zeros(da_s.shape[1:], bf16)

        for c in writes(i):
            c.start()

    if near:
        rows = da_s[per:].reshape(per * TILE, da_s.shape[2])
        for pos_ref, out_ref in zip(pos_refs, near_refs):
            slot = lax.broadcasted_iota(jnp.int32, (per * TILE, out_ref.shape[0]), 0)
            pick = (slot == pos_ref[...]).astype(f32).astype(bf16)
            out_ref[...] = tn_dot(pick, rows).astype(bf16)

    for c in range(count):
        lanes = pl.ds(c * hc, hc)
        for ry, rz, rx in spots:
            rows = rows_of(ry, rz, rx)
            for e in range(experts):
                g_refs[c][ry][rz, rx, 0, e] = gu_s[e, rows, lanes].astype(bf16)
                g_refs[c][ry][rz, rx, 1, e] = gd_s[e, rows, lanes].astype(bf16)

    @pl.loop(0, tiles)
    def _(i):
        for c in writes(i):
            c.wait()


def ffn(coords, plans, xs, dys, up_b, weights, carry, places=()):
    slots, width = xs.shape
    tiles = slots // TILE
    groups = len(plans)
    first = not carry
    count = len(weights)
    gshape = weights[0][0].shape
    experts, piece, hc = gshape[3:]
    hid = hc * count
    out = pl.pallas_call(
        functools.partial(ffn_kernel, first, count, piece, groups, bool(places)),
        out_shape=[
            jax.ShapeDtypeStruct((slots, width), bf16),
            jax.ShapeDtypeStruct((slots, width), bf16),
            *[jax.ShapeDtypeStruct((p.shape[1], width), bf16) for p in places],
            *[jax.ShapeDtypeStruct(gshape, bf16)] * (2 * count),
            jax.ShapeDtypeStruct((experts, 1, hid), f32),
        ],
        grid_spec=pltpu.PrefetchScalarGridSpec(
            num_scalar_prefetch=3,
            grid=(1,),
            in_specs=[
                ANY, ANY, full_spec((experts, 1, hid)), *[full_spec(p.shape) for p in places],
                *([] if first else [ANY, ANY]), *[ANY] * (2 * count),
            ],
            out_specs=[
                ANY, ANY, *[full_spec((p.shape[1], width)) for p in places], *[full_spec(gshape)] * (2 * count),
                full_spec((experts, 1, hid)),
            ],
            scratch_shapes=[
                *[pltpu.VMEM((experts, width, hid), bf16)] * 2,
                *[pltpu.VMEM((experts, width, hid), f32)] * 2,
                *[pltpu.VMEM((tiles, TILE, width), bf16)] * 4,
                pltpu.SemaphoreType.DMA((32 * count,)),
                pltpu.SemaphoreType.DMA((2 if first else 4, tiles)),
                pltpu.SemaphoreType.DMA((2, tiles)),
            ],
        ),
        compiler_params=params(1, 46 if groups == 2 else 60),
        cost_estimate=cost(12 * slots * width * hid * 1.5, 4e7, 2 * slots * hid),
        name="ffn",
    )(coords, plans[0], plans[-1], xs, dys, up_b, *places, *carry, *[w for pair in weights for w in pair])
    zs, das, *rest = out
    rows, rest = rest[: len(places)], rest[len(places) :]
    if places:
        return zs, das, [rest[2 * c : 2 * c + 2] for c in range(count)], rest[2 * count], rows
    return zs, das, [rest[2 * c : 2 * c + 2] for c in range(count)], rest[2 * count]


def norm_grad_kernel(count, low, *refs):
    parts, (v_ref, add_ref, gain_ref, out_ref, *refs) = refs[:count], refs[count:]
    sums_ref = refs[-1]

    @pl.when(pl.program_id(0) == 0)
    def _():
        sums_ref[...] = jnp.zeros_like(sums_ref)

    grad = sum(
        jnp.sum(p[...].astype(f32), axis=0) if len(p.shape) == 3 else p[...].astype(f32) for p in parts
    )
    xhat, rstd = norm_parts(v_ref[...].astype(f32))
    out = add_ref[...].astype(f32) + norm_back(grad, xhat, rstd, gain_ref[...])
    out_ref[...] = out
    if low:
        refs[0][...] = out.astype(bf16)
    sums_ref[0:1] += jnp.sum(grad * xhat, axis=0, keepdims=True)
    sums_ref[1:2] += jnp.sum(grad, axis=0, keepdims=True)
    sums_ref[2:3] += jnp.sum(out, axis=0, keepdims=True)


def norm_grad(partial, v, add, gain, low):
    tokens, width = v.shape
    tile = pl.BlockSpec((tokens, width), lambda i: (i, 0))
    return pl.pallas_call(
        functools.partial(norm_grad_kernel, len(partial), low),
        out_shape=[
            jax.ShapeDtypeStruct((tokens, width), f32),
            *([jax.ShapeDtypeStruct((tokens, width), bf16)] if low else []),
            jax.ShapeDtypeStruct((8, width), f32),
        ],
        grid=(tokens // tokens,),
        in_specs=[
            *[
                pl.BlockSpec((p.shape[0], tokens, width), lambda i: (0, i, 0)) if p.ndim == 3 else tile
                for p in partial
            ],
            tile, tile, full_spec((1, width)),
        ],
        out_specs=[tile, *([tile] if low else []), full_spec((8, width))],
        compiler_params=params(1),
        cost_estimate=cost(2e7, 8e6),
        name="norm_grad",
    )(*partial, v, add, gain)


def whole(kernel, name, outs, *args, prefetch=()):
    return pl.pallas_call(
        kernel,
        out_shape=[jax.ShapeDtypeStruct(s, d) for s, d in outs],
        grid_spec=pltpu.PrefetchScalarGridSpec(
            num_scalar_prefetch=len(prefetch),
            grid=(1,),
            in_specs=[full_spec(x.shape) for x in args],
            out_specs=[full_spec(s) for s, _ in outs],
        ),
        compiler_params=params(1),
        cost_estimate=cost(1e6, 4e6),
        name=name,
    )(*prefetch, *args)


def sums_y_kernel(c_ref, keep, got, own, send):
    for k in range(4):
        send[k] = (keep[k].astype(f32) + got[k].astype(f32)).astype(bf16)
    here = c_ref[0]
    own[...] = keep[here].astype(f32) + got[here].astype(f32)


def sums_z_kernel(c_ref, own, got, mine, near):
    others = [c_ref[0] ^ rz for rz in (1, 2, 3)]
    add = lambda k: own[k] + sum(got[z, k].astype(f32) for z in others)
    mine[...] = add(0)
    near[...] = add(1).astype(bf16)


def two_sums_kernel(a_keep, a_got, b_keep, b_got, a_own, a_send, b_own, b_send):
    for keep, got, own, send in ((a_keep, a_got, a_own, a_send), (b_keep, b_got, b_own, b_send)):
        own[...] = keep[0].astype(f32) + got[0].astype(f32)
        send[...] = (keep[1].astype(f32) + got[1].astype(f32)).astype(bf16)


def four_sums_kernel(c_ref, a_own, a_got, b_own, b_got, own, send):
    for rz in range(4):
        va = a_own[rz] + a_got[rz].astype(f32)
        vb = b_own[rz] + b_got[rz].astype(f32)
        if rz == 0:
            own[0], own[1] = va, vb
        send[c_ref[0] ^ rz, 0] = va.astype(bf16)
        send[c_ref[0] ^ rz, 1] = vb.astype(bf16)


def qkv_grad_kernel(c_ref, own, got, g_qkv, g_out):
    others = [c_ref[0] ^ rz for rz in (1, 2, 3)]
    add = lambda k, j: own[k, j] + sum(got[z, k, j].astype(f32) for z in others)
    g_qkv[0] = add(0, 0)
    g_qkv[1] = add(0, 1)
    g_qkv[2] = add(1, 0)
    g_out[...] = add(1, 1)


def rows_kernel(c_ref, *refs):
    n = len(refs) // 3
    for k in range(n):
        mine, other, out = refs[2 * k], refs[2 * k + 1], refs[2 * n + k]
        out[c_ref[3]] = mine[...]
        out[1 - c_ref[3]] = other[...]


def expert_grad_kernel(c_ref, *refs):
    *mines, near, g_up, g_down = refs
    hc = mines[0].shape[-1]
    half = hc * len(mines)
    here = pl.multiple_of(c_ref[2] * half, 128)
    there = pl.multiple_of((1 - c_ref[2]) * half, 128)
    for k, out in ((0, g_up), (1, g_down)):
        for c, mine in enumerate(mines):
            out[:, :, pl.ds(here + c * hc, hc)] = mine[k]
        out[:, :, pl.ds(there, half)] = near[k].astype(f32)


def flip(x, mask, size):
    return lax.ppermute(x, "dp", [(i, i ^ mask) for i in range(size)])


def after(v, *deps):
    return lax.optimization_barrier((v, deps))[0]


def deal(v):
    return lax.all_to_all(v, "mp", 0, 0)


def swap(v):
    return lax.ppermute(v, "mp", [(0, 1), (1, 0)])


def share(v):
    return deal(jnp.broadcast_to(v, (lax.axis_size("mp"),) + v.shape))


def gather_z(a, b, size):
    both = jnp.stack([a, b])
    blocks = [both] + [flip(both, 4 * rz, size) for rz in (1, 2, 3)]
    return jnp.stack([v[0] for v in blocks]), jnp.stack([v[1] for v in blocks])


def gather_xy(a0, b0, dep, size):
    a0 = jnp.stack([after(a0, dep), flip(a0, 1, size)])
    b0 = jnp.stack([b0, flip(b0, 2, size)])
    return (a0, flip(a0, 2, size)), (b0, flip(b0, 1, size))


def attn_sums_1(keep, got, dep):
    shape = keep[0].shape[1:]
    return whole(
        two_sums_kernel, "two_sums", [(shape, f32), (shape, bf16)] * 2,
        after(keep[0], dep), got[0], keep[1], got[1],
    )


def attn_sums_2(coords, own, got, dep):
    shape = (2,) + own[0].shape[1:]
    return whole(
        four_sums_kernel, "four_sums", [(shape, f32), ((4,) + shape, bf16)],
        own[0], got[0], own[1], got[1], prefetch=(after(coords, dep),),
    )


def gather_plain(w):
    full = lax.all_gather(w, "dp", axis=1, tiled=True)
    n, rows, cols = full.shape
    return full.reshape(n, 16, rows // 16, cols).swapaxes(0, 1)


def gather_pieces_plain(a, b):
    blocks = [gather_plain(v) for v in (a, b)]
    blocks = [v.reshape((4, 2, 2) + v.shape[1:]) for v in blocks]
    fa = jnp.moveaxis(blocks[0], 0, 2)
    fb = jnp.swapaxes(jnp.moveaxis(blocks[1], 0, 2), 0, 1)
    return (fa[0], fa[1]), (fb[0], fb[1])


def scatter_plain(ga, gb):
    fa = jnp.moveaxis(jnp.stack(ga), 2, 0)
    fb = jnp.moveaxis(jnp.swapaxes(jnp.stack(gb), 0, 1), 2, 0)
    outs = []
    for v in (fa, fb):
        v = v.reshape((16,) + v.shape[3:]).swapaxes(0, 1)
        v = v.reshape(v.shape[0], -1, v.shape[-1]).astype(f32)
        outs.append(lax.psum_scatter(v, "dp", scatter_dimension=1, tiled=True))
    return outs


def phase(pred, f):
    shapes = jax.eval_shape(f)
    return lax.cond(
        pred, f, lambda: jax.tree.map(lambda v: jnp.zeros(v.shape, v.dtype), shapes)
    )


def deal_z(v):
    groups = [[4 * z + k for z in range(4)] for k in range(4)]
    return lax.all_to_all(v, "dp", 0, 0, axis_index_groups=groups, tiled=True)


def four_times(p):
    return jnp.broadcast_to(p, (4,) + p.shape)


def sums_y(coords, pair, size):
    shape = pair[0].shape
    return whole(
        sums_y_kernel, "sums_y", [(shape[1:], f32), (shape, bf16)],
        pair[0], flip(pair[1], 2, size), prefetch=(coords,),
    )


def sums_z(coords, parts_y):
    own, send = parts_y
    return add_z(coords, own, deal_z(send))


def add_z(coords, own, got):
    shape = own.shape[1:]
    return whole(
        sums_z_kernel, "sums_z", [(shape, f32), (shape, bf16)], own, got, prefetch=(coords,)
    )


def expert_pieces_plain(w_up, w_down):
    hc = w_up.shape[-1] // CHUNKS
    blocks = jnp.stack([gather_plain(w_up), gather_plain(w_down)], axis=1)
    blocks = blocks.reshape((4, 2, 2) + blocks.shape[1:])
    return [
        tuple(blocks[:, ry, ..., c * hc : (c + 1) * hc] for ry in range(2)) for c in range(CHUNKS)
    ]


def expert_sums_plain(pair):
    v = jnp.stack(pair, axis=1)
    v = v.reshape((16,) + v.shape[3:])
    v = jnp.moveaxis(v, 0, 2)
    v = v.reshape(v.shape[:2] + (-1, v.shape[-1])).astype(f32)
    return lax.psum_scatter(v, "dp", scatter_dimension=2, tiled=True)


def token_plan(segments, modality, experts):
    tokens = segments.size
    doc_ids = jnp.arange(modality.shape[1], dtype=jnp.int32)
    match = segments[:, :, None] == doc_ids
    mods = jnp.sum(jnp.where(match, modality[:, None, :], 0), axis=-1).reshape(tokens)
    kinds = jnp.arange(experts, dtype=jnp.int32)
    hot = (mods[:, None] == kinds).astype(jnp.int32)
    ids = jnp.arange(tokens, dtype=jnp.int32)
    lower = (ids[:, None] > ids[None, :]).astype(bf16)
    before = jnp.dot(lower, hot.astype(bf16), preferred_element_type=f32).astype(jnp.int32)
    need = (jnp.sum(hot, axis=0) + TILE - 1) // TILE
    ends = jnp.sum(jnp.where(kinds[:, None] >= kinds[None, :], need[None, :], 0), axis=1)
    pos = jnp.sum(hot * (before + (ends - need)[None, :] * TILE), axis=1)
    tiles = (tokens + experts * (TILE - 1)) // TILE
    tile_ids = jnp.arange(tiles, dtype=jnp.int32)
    tile_expert = jnp.minimum(
        jnp.sum((tile_ids[:, None] >= ends[None, :]).astype(jnp.int32), axis=1), experts - 1
    )
    return mods, pos, jnp.concatenate([pos, tile_expert, ends[-1:]])


def body(
    layer_input, segments, modality, ln_gain, ln_bias, w_qkv, qv_bias, w_out, out_bias,
    w_up, up_bias, w_down, down_bias, cotangent,
):
    part = lax.axis_index("mp")
    parts = lax.axis_size("mp")
    size = lax.axis_size("dp")
    me = lax.axis_index("dp")
    rows, seq, width = layer_input.shape
    tokens = rows * seq
    cols = w_qkv.shape[-1]
    hid = w_up.shape[-1]
    experts = w_up.shape[0]
    shape3 = (rows, seq, width)
    tiles = (tokens + experts * (TILE - 1)) // TILE
    staged = size == 16

    mine_rows = rows // parts
    mine_tokens = tokens // parts
    by_core = (parts, mine_tokens, width)
    dy = cotangent.reshape(tokens, width)
    rows_here = lambda v: lax.dynamic_slice_in_dim(v, part * mine_rows, mine_rows, 0)
    col_start = part * cols

    def small_inputs():
        q_b = lax.dynamic_slice_in_dim(qv_bias[0], col_start, cols)
        v_b = lax.dynamic_slice_in_dim(qv_bias[1], col_start, cols)
        return (
            rows_here(layer_input).reshape(mine_tokens, width),
            rows_here(cotangent).reshape(mine_tokens, width),
            jnp.concatenate([q_b, jnp.zeros_like(q_b), v_b]).reshape(1, 3 * cols),
            segments.reshape(rows, 1, seq),
            key_windows(segments),
            jnp.concatenate([out_bias[None], ln_gain[1:2], ln_bias[1:2]]),
            jnp.concatenate([ln_gain[0:1], ln_bias[0:1]]),
        )

    def fwd(coords, pa, pb):
        own, other, *saved = attn_fwd(coords, windows, layer_input, seg_row, ln1, proj_bias, pa, pb)
        return (saved, *mid(x_mine, own, swap(other), vec))

    def bwd(coords, dxr, dx2, saved, pa, pb):
        own, other, *rest = attn_bwd(
            coords, windows, *dxr, layer_input, seg_row, ln1, saved, pa, pb
        )
        return (*norm_grad((own, swap(other)), x_mine, dx2, ln_gain[0:1], False), *rest)

    def halves(v):
        take = lambda k: lax.dynamic_slice_in_dim(v, k * mine_tokens, mine_tokens, 0)
        return take(part).reshape(1, mine_tokens), take(1 - part).reshape(1, mine_tokens)

    def bias_rows(mods):
        kinds = lax.dynamic_slice_in_dim(mods, part * mine_tokens, mine_tokens, 0)[:, None]
        bias_of = jnp.zeros((mine_tokens, width), f32)
        for e in range(experts):
            bias_of = jnp.where(kinds == e, down_bias[e][None], bias_of)
        return bias_of

    def finish(x2, z_sum, bias_of):
        return (x2 + (z_sum + bias_of)).astype(bf16)

    def small_rows(sums1, sums2, bsum, g_upb, g_down_bias):
        sides = bsum.reshape(3, cols)
        g_qv = lax.dynamic_update_slice(
            jnp.zeros((2, width), f32), jnp.stack([sides[0], sides[2]]), (jnp.int32(0), col_start)
        )
        g_upb_full = lax.dynamic_update_slice(
            jnp.zeros((experts, up_bias.shape[1]), f32), g_upb, (jnp.int32(0), hid_start)
        )
        return jnp.concatenate(
            [sums1[0:2], sums2[0:3], g_down_bias / parts, g_qv, g_upb_full.reshape(-1, width)]
        )

    if staged:
        x_bit = me % 2
        coords = jnp.stack([me // 4, (me // 2) % 2, x_bit, part]).astype(jnp.int32)
        pred = me < size
        inner = part < parts
        half = hid // 2
        hid_start = part * hid + x_bit * half
        hc = half // CHUNKS
        up_b = lax.dynamic_slice_in_dim(up_bias, hid_start, half, 1)

        def call_experts(k, xs, dys, weights, carry, places=()):
            call = CALLS[k]
            ub = up_b[:, None, call[0] * hc : (call[-1] + 1) * hc]
            return ffn(
                coords, (plan_own, plan), xs, dys, ub, [weights[c] for c in call], carry, places
            )

        def begin():
            w = jnp.stack([w_up, w_down])
            keep = lax.dynamic_slice_in_dim(w, x_bit * half, half, 3)
            send = lax.dynamic_slice_in_dim(w, (1 - x_bit) * half, half, 3)
            near = flip(send, 1, size)
            pieces = [
                jnp.stack([keep[..., c * hc : (c + 1) * hc], near[..., c * hc : (c + 1) * hc]])
                for c in range(CHUNKS)
            ]
            pieces[0] = four_times(pieces[0])
            ab = gather_z(w_qkv[:2], jnp.stack([w_qkv[2], w_out]), size)
            mods, pos, plan_own = token_plan(segments, modality, experts)
            plan = flip(plan_own, 1, size)
            return pieces, ab, mods, pos, plan_own, plan, bias_rows(mods), small_inputs()

        pieces, ab, mods, pos, plan_own, plan, bias_of, smalls = phase(pred, begin)
        x_mine, dy_mine, proj_bias, seg_row, windows, vec, ln1 = smalls

        def weights_in():
            def inside():
                pos_row = pos.reshape(1, tokens)
                dys = sort_tokens([(pos_row, dy)], tiles, 0, 2)
                later = [four_times(v) for v in pieces[1:]]
                hot = (mods[:, None] == jnp.arange(experts, dtype=jnp.int32)).astype(bf16)
                return (
                    *gather_xy(*ab, later, size), halves(pos), halves(plan),
                    dys, tn_dot(hot, dy),
                    later,
                )

            return deal_z(pieces[0]), phase(inner, inside)

        z0, (pa, pb, pos_here, pos_near, dys, g_down_bias, later) = phase(pred, weights_in)

        def forward():
            return (
                *phase(inner, lambda: fwd(coords, pa, pb)), flip(z0, 2, size),
                deal_z(later[0]), flip(dy_mine, 1, size),
            )

        saved, x2, a2, y0, z1, dy_near = phase(pred, forward)

        def sort(places, v, v2, group, into):
            return sort_tokens(list(zip(places, (v, v2))), tiles, group, 2, into)

        def exchange():
            near = flip(a2, 1, size)
            d, xs = phase(
                inner,
                lambda: (
                    sort(pos_near, dy_near, swap(dy_near), 1, dys),
                    sort(pos_here, a2, swap(a2), 0, None),
                ),
            )
            near = after(near, d, xs)
            xs = phase(inner, lambda: sort(pos_near, near, swap(near), 1, xs))
            return xs, d, flip(z1, 2, size), deal_z(later[1])

        xs, dys, y1, z2 = phase(pred, exchange)
        weights = [(z0, y0), (z1, y1)]
        (zs0, das0, grads, gub0), y2 = phase(
            pred, lambda: (call_experts(0, xs, dys, weights, ()), flip(z2, 2, size))
        )
        weights.append((z2, y2))

        def both_cores(places, vs, group):
            mine, other = unsort_tokens(places, vs, group, 2)
            return (mine.astype(f32) + swap(other).astype(f32)).astype(bf16)

        def second():
            def inside():
                zs, das, more, gub, (mine, other) = call_experts(
                    1, xs, dys, weights, (zs0, das0), pos_near
                )
                near = (mine.astype(f32) + swap(other).astype(f32)).astype(bf16)
                return zs, das, more, gub, near

            return phase(inner, inside), sums_y(coords, grads[0], size)

        (zs, das, more, gub1, da_near), v0 = phase(pred, second)
        grads = grads + more
        g_upb = jnp.concatenate([gub0, gub1], axis=-1)[:, 0]

        def back():
            def inside():
                mine, other = unsort_tokens(pos_here, das, 0, 2)
                return mine, swap(other), both_cores(pos_near, zs, 1)

            near = flip(da_near, 1, size)
            mine, other, z_near = phase(inner, inside)
            g0 = sums_z(coords, v0)
            v1 = sums_y(coords, grads[1], size)

            def to_x2():
                dx2, dxr, sums2 = norm_grad((mine, other, near), x2, dy_mine, ln_gain[1:2], True)
                return dx2, (dxr, swap(dxr)), sums2

            return *phase(inner, to_x2), z_near, g0, v1

        dx2, dxr, sums2, z_near, g0, v1 = phase(pred, back)

        def last():
            return (
                phase(inner, lambda: bwd(coords, dxr, dx2, saved, pa, pb)), flip(z_near, 1, size),
                sums_z(coords, v1), sums_y(coords, grads[2], size),
            )

        (grad, sums1, ga0, ga1, gb0, gb1, bsum), z_near, g1, v2 = phase(pred, last)
        def sum_up():
            def out_rows():
                mine, other = unsort_tokens(pos_here, zs, 0, 2)
                z_sum = mine.astype(f32) + swap(other).astype(f32) + z_near.astype(f32)
                out = finish(x2, z_sum, bias_of)
                return out, swap(out), swap(grad)

            rows_all = phase(inner, lambda: small_rows(sums1, sums2, bsum, g_upb, g_down_bias))

            def small_start():
                total = rows_all + swap(rows_all)
                return total + flip(total, 1, size)

            got2 = deal_z(after(v2[1], rows_all))
            got_a, got_b = flip(ga1, 2, size), flip(gb1, 1, size)
            outs = phase(inner, out_rows)
            a_own, a_send, b_own, b_send = attn_sums_1((ga0, gb0), (got_a, got_b), outs)
            got_a, got_b = flip(a_send, 1, size), flip(b_send, 2, size)
            small = phase(inner, small_start)
            return attn_sums_2(coords, (a_own, b_own), (got_a, got_b), small), got2, small, outs

        (own, send), got2, small, (out, out_other, grad_other) = phase(pred, sum_up)

        got = deal_z(send)
        g2 = add_z(coords, v2[0], got2)
        near = flip(jnp.concatenate([v[1] for v in (g0, g1, g2)], axis=-1), 1, size)
        total = phase(inner, lambda: small + flip(small, 2, size))
        rows_z = [flip(total, 4 * rz, size) for rz in (1, 2, 3)]
        layer_output, grad_input = whole(
            rows_kernel, "rows", [((parts,) + v.shape, v.dtype) for v in (out, grad)],
            out, out_other, grad, grad_other, prefetch=(coords,),
        )
        g_qkv, g_out = whole(
            qkv_grad_kernel, "qkv_grad", [(w_qkv.shape, f32), (w_out.shape, f32)], own, got,
            prefetch=(after(coords, layer_output),),
        )
        last = after(coords, g_out)
        g_up, g_down = whole(
            expert_grad_kernel, "expert_grad", [(w_up.shape, f32)] * 2,
            g0[0], g1[0], g2[0], near, prefetch=(last,),
        )
        rows_z = jnp.stack([after(total, g_up)] + rows_z)
        pick = lambda z: lax.dynamic_index_in_dim(rows_z, last[0] ^ z, 0, False)
        small = pick(0) + pick(1) + pick(2) + pick(3)
    else:
        coords = jnp.stack([0, 0, 0, part]).astype(jnp.int32)
        x_mine, dy_mine, proj_bias, seg_row, windows, vec, ln1 = small_inputs()
        hid_start = part * hid
        hc = hid // CHUNKS
        up_b = lax.dynamic_slice_in_dim(up_bias, hid_start, hid, 1)
        pa, pb = gather_pieces_plain(w_qkv[:2], jnp.stack([w_qkv[2], w_out]))
        weights = expert_pieces_plain(w_up, w_down)
        mods, pos, plan_own = token_plan(segments, modality, experts)
        pos_row = pos.reshape(1, tokens)
        hot = (mods[:, None] == jnp.arange(experts, dtype=jnp.int32)).astype(bf16)
        g_down_bias = tn_dot(hot, dy)
        dys = sort_tokens([(pos_row, dy)], tiles, 0, 1)
        saved, x2, a2 = fwd(coords, pa, pb)
        xs = sort_tokens([(pos_row, share(a2).reshape(tokens, width))], tiles, 0, 1)
        carry = ()
        grads = []
        g_upb = []
        for call in CALLS:
            ub = up_b[:, None, call[0] * hc : (call[-1] + 1) * hc]
            zs, das, pairs, gub = ffn(
                coords, (plan_own,), xs, dys, ub, [weights[c] for c in call], carry
            )
            carry = (zs, das)
            g_upb.append(gub[:, 0])
            grads += pairs
        g_upb = jnp.concatenate(g_upb, axis=-1)
        g_up, g_down = jnp.concatenate([expert_sums_plain(pair) for pair in grads], axis=-1)
        own = deal(unsort_tokens([pos_row], das, 0, 1)[0].reshape(by_core))
        dx2, dxr, sums2 = norm_grad((own[0], own[1]), x2, dy_mine, ln_gain[1:2], True)
        grad_mine, sums1, ga0, ga1, gb0, gb1, bsum = bwd(
            coords, (dxr, swap(dxr)), dx2, saved, pa, pb
        )
        g_qk, g_vo = scatter_plain((ga0, ga1), (gb0, gb1))
        g_qkv, g_out = jnp.concatenate([g_qk, g_vo[:1]]), g_vo[1]
        own = deal(unsort_tokens([pos_row], zs, 0, 1)[0].reshape(by_core))
        layer_output = share(finish(x2, jnp.sum(own.astype(f32), axis=0), bias_rows(mods)))
        grad_input = share(grad_mine)
        small = lax.psum(small_rows(sums1, sums2, bsum, g_upb, g_down_bias), ("dp", "mp"))

    g_gain = jnp.stack([small[0], small[2]])
    g_lnb = jnp.stack([small[1], small[3]])
    return (
        layer_output.reshape(shape3),
        grad_input.reshape(shape3),
        g_gain,
        g_lnb,
        g_qkv,
        small[5 + experts : 7 + experts],
        g_out,
        small[4],
        g_up,
        small[7 + experts :].reshape(experts, up_bias.shape[1]),
        g_down,
        small[5 : 5 + experts],
    )


def solution(mesh):
    tok = P("dp", None, None)
    rep = P()
    wide = P(None, "dp", "mp")
    in_specs = (
        tok, P("dp", None), P("dp", None), rep, rep, wide, rep, P("dp", "mp"), rep, wide, rep,
        wide, rep, tok,
    )
    out_specs = (
        tok, tok, rep, rep, wide, rep, P("dp", "mp"), rep, wide, rep, wide, rep,
    )
    return jax.shard_map(body, mesh=mesh, in_specs=in_specs, out_specs=out_specs, check_vma=False)
```
